32 devices in a mesh: dp: 4 (over y, x), seq: 4 (over z), mp: 2 (over core).
Axes of the slice: x: 2, y: 2, z: 4, core: 2. Of those that a mesh axis runs over, the one named last changes fastest.
Arguments:
- inputs: bfloat16 [8, 1024, 2304], P('dp', 'seq', 'mp'), may hold values from -6 to 6
- starts: int32 [8, 1024], P('dp', 'seq'), may hold values from 0 to 1, as said below
- init_state: float32 [2, 8, 2304], P(None, 'dp', 'mp'), may hold values from -4 to 4
- weight_one: bfloat16 [2, 2304, 3, 2304], P(None, None, None, 'mp'), may hold values from -0.09375 to 0.09375
- bias_one: float32 [3, 2304], P(None, 'mp'), may hold values from -1.5 to 8.5
- weight_two: bfloat16 [2304, 3, 2304], P(None, None, 'mp'), may hold values from -0.25 to 0.25
- bias_two: float32 [3, 2304], P(None, 'mp'), may hold values from -1.5 to 8.5
- cotangent: bfloat16 [8, 1024, 2304], P('dp', 'seq', 'mp'), may hold values from -6 to 6
Outputs:
- pooled_two: bfloat16 [8, 1024, 2304], P('dp', 'seq', 'mp')
- input_grad: float32 [8, 1024, 2304], P('dp', 'seq', 'mp')
- weight_one_grad: float32 [2, 2304, 3, 2304], P(None, None, None, 'mp')
- bias_one_grad: float32 [3, 2304], P(None, 'mp')
- weight_two_grad: float32 [2304, 3, 2304], P(None, None, 'mp')
- bias_two_grad: float32 [3, 2304], P(None, 'mp')
The draws below stay inside these ranges and needn't reach their ends.
Inputs may be any that keep to these rules, and one draw needn't show every extreme that they name: `starts`: 1 marks a token that begins a new document; among the 2 sequences of each index of dp one has no mark.
All inputs are finite; a program needn't handle non-finite values.
Results may differ from the reference program's by a relative error of at most 0.0047.
Values may be sent and summed in bfloat16 or wider, within the bound.
A program may use at most 704 MiB of HBM per device.

```python
import jax
import jax.numpy as jnp
from jax import lax

D = 2304
SEQS_DEV = 2
SEQS = 8
SEQ_LEN = 1024


def bias_rows(key, forget_low, forget_high):
    first, second, third = jax.random.split(key, 3)
    update = 0.3 * jax.random.truncated_normal(first, -3.0, 3.0, (D,), jnp.float32)
    forget = jax.random.uniform(second, (D,), jnp.float32, forget_low, forget_high)
    output = 0.5 * jax.random.truncated_normal(third, -3.0, 3.0, (D,), jnp.float32)
    return jnp.stack([update, forget, output])


def draw_bias_one(key, part):
    key = jax.random.fold_in(key, 11)
    return bias_rows(key, 1.0, 7.5)


def draw_bias_two(key, part):
    key = jax.random.fold_in(key, 12)
    return bias_rows(key, 1.0, 7.5)


def draw_starts(key, part):
    key = jax.random.fold_in(key, 5)
    first, second, third = jax.random.split(key, 3)
    rates = jax.random.randint(first, (SEQS, 1), 1, 33)
    values = jax.random.randint(second, (SEQS, SEQ_LEN), 0, 4 * SEQ_LEN)
    marks = (values < rates).astype(jnp.int32)
    picks = jax.random.randint(third, (SEQS // SEQS_DEV,), 0, SEQS_DEV)
    numbers = jnp.arange(SEQS)
    chosen = picks[numbers // SEQS_DEV]
    clear = numbers % SEQS_DEV == chosen
    return jnp.where(clear[:, None], 0, marks).astype(jnp.int32)


def steps_of(stream_key, shape, shards, low, high):
    gain = 1.0
    for axis_at, blocks in shards:
        steps = jax.random.uniform(jax.random.fold_in(jax.random.fold_in(stream_key, 6), axis_at), (blocks,), jnp.float32, low / len(shards), high / len(shards))
        gain = gain * jnp.repeat(jnp.exp(steps), shape[axis_at] // blocks).reshape((-1,) + (1,) * (len(shape) - 1 - axis_at))
    return gain


def bell_draw(stream_key, extent, spread, reach, cuts=(), dtype=jnp.bfloat16):
    level = steps_of(stream_key, extent, cuts, -0.22, 0.18) if cuts else 1.0
    drawn = jax.random.normal(stream_key, extent, jnp.float32) * spread * level
    return jnp.minimum(jnp.maximum(drawn, -reach), reach).astype(dtype)


def setup_inputs(seed: int = 0) -> dict:
    key_list = jax.random.split(jax.random.key(seed), 9)
    return {
        "inputs": bell_draw(key_list[0], (SEQS, SEQ_LEN, D), 1.0, 6.0, ((0, 4), (1, 4), (2, 2))),
        "starts": draw_starts(jax.random.fold_in(key_list[8], 71), 0),
        "init_state": bell_draw(key_list[2], (2, SEQS, D), 1.0, 4.0, ((1, 4), (2, 2)), jnp.float32),
        "weight_one": bell_draw(key_list[3], (2, D, 3, D), (2 * D) ** -0.5, 0.09375, ((3, 2),)),
        "bias_one": draw_bias_one(jax.random.fold_in(key_list[8], 71), 0),
        "weight_two": bell_draw(key_list[5], (D, 3, D), (D // 4) ** -0.5, 0.25, ((2, 2),)),
        "bias_two": draw_bias_two(jax.random.fold_in(key_list[8], 71), 0),
        "cotangent": bell_draw(key_list[7], (SEQS, SEQ_LEN, D), 1.0, 6.0, ((0, 4), (1, 4), (2, 2))),
    }


@jax.custom_vjp
def low(v):
    return lax.optimization_barrier(v.astype(jnp.bfloat16)).astype(jnp.float32)

@jax.custom_vjp
def low_back(v):
    return v

def low_keep(v):
    return (low(v), None)

def low_pass(kept, grad):
    return (grad,)

def back_keep(v):
    return (v, None)

def back_low(kept, grad):
    return (low(grad),)
low.defvjp(low_keep, low_pass)
low_back.defvjp(back_keep, back_low)
highest = lax.Precision.HIGHEST

def pool_layer(gates, resets, initial):
    update = jnp.tanh(gates[:, 0])
    forget = jax.nn.sigmoid(gates[:, 1])
    output = jax.nn.sigmoid(gates[:, 2])
    retain = forget * resets[:, None]
    inflow = (1.0 - forget) * update

    def advance(carried, factors):
        carried = factors[0] * carried + factors[1]
        return (carried, carried)
    unused, states = lax.scan(advance, initial, (retain, inflow))
    return output * states

def sequence_forward(sequence_in, conv_weights, conv_biases, mix_weights, mix_biases, resets, init_one, init_two):
    features = sequence_in.shape[1]
    previous = jnp.concatenate([jnp.zeros((1, features), jnp.float32), sequence_in[:-1]], 0)
    gates_one = jnp.einsum('td,dgc->tgc', sequence_in, conv_weights[0], precision=highest)
    gates_one = gates_one + jnp.einsum('td,dgc->tgc', previous, conv_weights[1], precision=highest) + conv_biases
    gates_one = low_back(gates_one)
    pooled_one = pool_layer(gates_one, resets, init_one)
    hidden_one = low(pooled_one)
    gates_two = jnp.einsum('td,dgc->tgc', hidden_one, mix_weights, precision=highest) + mix_biases
    gates_two = low_back(gates_two)
    return pool_layer(gates_two, resets, init_two)

def reference(inputs, starts, init_state, weight_one, bias_one, weight_two, bias_two, cotangent):
    first_weight = weight_one.astype(jnp.float32)
    second_weight = weight_two.astype(jnp.float32)

    def per_sequence(totals, sliced):
        sequence, doc_marks, init_one, init_two, upstream = sliced
        resets = 1.0 - doc_marks.astype(jnp.float32)

        def forward(sequence_in, conv_weights, conv_biases, mix_weights, mix_biases):
            return sequence_forward(sequence_in, conv_weights, conv_biases, mix_weights, mix_biases, resets, init_one, init_two)
        pooled, pullback = jax.vjp(forward, sequence.astype(jnp.float32), first_weight, bias_one, second_weight, bias_two)
        gradients = pullback(upstream.astype(jnp.float32))
        totals = (totals[0] + gradients[1], totals[1] + gradients[2], totals[2] + gradients[3], totals[3] + gradients[4])
        return (totals, (pooled.astype(jnp.bfloat16), gradients[0]))
    zeros_start = (jnp.zeros_like(first_weight), jnp.zeros((3, D), jnp.float32), jnp.zeros_like(second_weight), jnp.zeros((3, D), jnp.float32))
    totals, outputs = lax.scan(per_sequence, zeros_start, (inputs, starts, init_state[0], init_state[1], cotangent))
    return (outputs[0], outputs[1], totals[0], totals[1], totals[2], totals[3])
```

```python
import functools

import jax
import jax.numpy as jnp
from jax import lax
from jax.experimental import pallas as pl
from jax.experimental.pallas import tpu as pltpu
from jax.sharding import PartitionSpec as P

F32 = jnp.float32
BF16 = jnp.bfloat16
SUB = 8
STEP = 16
VMEM = pl.BlockSpec(memory_space=pltpu.VMEM)


def sigmoid(x):
    return 0.5 * jnp.tanh(0.5 * x) + 0.5


def lane_blocks(channels):
    width = 384 if channels % 384 == 0 else channels
    return [slice(at, at + width) for at in range(0, channels, width)]


def scan_down(scale, shift):
    row = lax.broadcasted_iota(jnp.int32, scale.shape, 0)
    for step in (1, 2, 4):
        earlier = row >= step
        scale_before = jnp.where(earlier, pltpu.roll(scale, step, 0), 1.0)
        shift_before = jnp.where(earlier, pltpu.roll(shift, step, 0), 0.0)
        shift = scale * shift_before + shift
        scale = scale * scale_before
    return scale, shift


def scan_up(scale, shift):
    row = lax.broadcasted_iota(jnp.int32, scale.shape, 0)
    for step in (1, 2, 4):
        later = row < SUB - step
        scale_after = jnp.where(later, pltpu.roll(scale, SUB - step, 0), 1.0)
        shift_after = jnp.where(later, pltpu.roll(shift, SUB - step, 0), 0.0)
        shift = scale * shift_after + shift
        scale = scale * scale_after
    return scale, shift


def greet(axis):
    count = lax.axis_size(axis)
    me = lax.axis_index(axis)
    barrier = pltpu.get_barrier_semaphore()
    for step in range(1, count):
        pl.semaphore_signal(
            barrier, inc=1, device_id={axis: lax.rem(me + step, count)}, device_id_type=pl.DeviceIdType.MESH
        )
    pl.semaphore_wait(barrier, count - 1)


def to_all(src, slots, send_sems, recv_sems, axis):
    count = lax.axis_size(axis)
    me = lax.axis_index(axis)
    copies = []
    for step in range(1, count):
        copies.append(
            pltpu.make_async_remote_copy(
                src_ref=src,
                dst_ref=slots.at[step - 1],
                send_sem=send_sems.at[step - 1],
                recv_sem=recv_sems.at[step - 1],
                device_id={axis: lax.rem(me + step, count)},
                device_id_type=pl.DeviceIdType.MESH,
            )
        )
    for copy in copies:
        copy.start()
    return copies


def from_earlier(slots, initial, scale_rows, shift_rows, axis):
    count = lax.axis_size(axis)
    me = lax.axis_index(axis)
    state = initial
    for block in range(count - 1):
        slot = jnp.maximum(me - block - 1, 0)
        after = slots[slot, scale_rows, :] * state + slots[slot, shift_rows, :]
        state = jnp.where(block < me, after, state)
    return state


def from_later(slots, shape, scale_rows, shift_rows, axis):
    count = lax.axis_size(axis)
    me = lax.axis_index(axis)
    message = jnp.zeros(shape, F32)
    for block in range(count - 1, 0, -1):
        slot = jnp.minimum(me + count - block - 1, count - 2)
        after = slots[slot, scale_rows, :] * message + slots[slot, shift_rows, :]
        message = jnp.where(block > me, after, message)
    return message


def first_pass(seqs, tokens, channels, gates, bias, keep, upd, fgt, out, scale, shift, summary):
    def body(at, carried):
        given = list(carried)
        for seq in range(seqs):
            for half in range(STEP // SUB):
                rows = pl.ds(pl.multiple_of(seq * tokens + at * STEP + half * SUB, SUB), SUB)
                kept = keep[rows, :][:, 0:1]
                for number, lanes in enumerate(lane_blocks(channels)):
                    u = jnp.tanh(gates[0, rows, lanes] + bias[0:1, lanes])
                    f = sigmoid(gates[1, rows, lanes] + bias[1:2, lanes])
                    o = sigmoid(gates[2, rows, lanes] + bias[2:3, lanes])
                    upd[rows, lanes] = u
                    fgt[rows, lanes] = f
                    out[rows, lanes] = o
                    a, b = scan_down(f * kept, (1.0 - f) * u)
                    place = (seq * len(lane_blocks(channels)) + number) * 2
                    b = a * given[place + 1] + b
                    a = a * given[place]
                    scale[rows, lanes] = a
                    shift[rows, lanes] = b
                    given[place] = a[SUB - 1 : SUB]
                    given[place + 1] = b[SUB - 1 : SUB]
        return tuple(given)

    begin = []
    for seq in range(seqs):
        for lanes in lane_blocks(channels):
            width = lanes.stop - lanes.start
            begin += [jnp.ones((1, width), F32), jnp.zeros((1, width), F32)]
    end = lax.fori_loop(0, tokens // STEP, body, tuple(begin))
    place = 0
    for seq in range(seqs):
        for lanes in lane_blocks(channels):
            summary[seq : seq + 1, lanes] = end[place]
            summary[seqs + seq : seqs + seq + 1, lanes] = end[place + 1]
            place += 2


def back_pass(seqs, tokens, channels, upstream, keep, fgt, out, scale, shift, summary, row0):
    steps = tokens // STEP

    def body(index, carried):
        at = steps - 1 - index
        given = list(carried)
        for seq in range(seqs):
            whole = pl.ds(pl.multiple_of(seq * tokens + at * STEP, STEP), STEP)
            for number, lanes in enumerate(lane_blocks(channels)):
                ups = upstream[whole, lanes].astype(F32)
                place = (seq * len(lane_blocks(channels)) + number) * 2
                for half in reversed(range(STEP // SUB)):
                    rows = pl.ds(pl.multiple_of(seq * tokens + at * STEP + half * SUB, SUB), SUB)
                    kept = keep[rows, :][:, 0:1]
                    retain = fgt[rows, lanes] * kept
                    direct = ups[half * SUB : half * SUB + SUB] * out[rows, lanes]
                    a, b = scan_up(retain, retain * direct)
                    b = a * given[place + 1] + b
                    a = a * given[place]
                    scale[rows, lanes] = a
                    shift[rows, lanes] = b
                    given[place] = a[0:1]
                    given[place + 1] = b[0:1]
        return tuple(given)

    begin = []
    for seq in range(seqs):
        for lanes in lane_blocks(channels):
            width = lanes.stop - lanes.start
            begin += [jnp.ones((1, width), F32), jnp.zeros((1, width), F32)]
    end = lax.fori_loop(0, steps, body, tuple(begin))
    place = 0
    for seq in range(seqs):
        for lanes in lane_blocks(channels):
            summary[row0 + seq : row0 + seq + 1, lanes] = end[place]
            summary[row0 + seqs + seq : row0 + seqs + seq + 1, lanes] = end[place + 1]
            place += 2


def states_pass(seqs, tokens, channels, entering, out, scale, shift, state, pooled):
    def body(at, none):
        for seq in range(seqs):
            rows = pl.ds(pl.multiple_of(seq * tokens + at * STEP, STEP), STEP)
            for lanes in lane_blocks(channels):
                value = scale[rows, lanes] * entering[seq : seq + 1, lanes] + shift[rows, lanes]
                state[rows, lanes] = value
                pooled[rows, lanes] = (out[rows, lanes] * value).astype(BF16)
        return none

    lax.fori_loop(0, tokens // STEP, body, 0)


def grads_pass(seqs, tokens, channels, message, entering, upstream, keep, upd, fgt, out, state, scale, shift, grads, sums):
    steps = tokens // STEP
    sums[...] = jnp.zeros_like(sums)
    for seq in range(seqs):
        for lanes in lane_blocks(channels):
            width = lanes.stop - lanes.start

            def body(index, later, seq=seq, lanes=lanes, width=width):
                at = steps - 1 - index
                whole = pl.ds(pl.multiple_of(seq * tokens + at * STEP, STEP), STEP)
                row = lax.broadcasted_iota(jnp.int32, (STEP, width), 0)
                kept = keep[whole, :][:, 0:1]
                ups = upstream[whole, lanes].astype(F32)
                u, f, o = upd[whole, lanes], fgt[whole, lanes], out[whole, lanes]
                states = state[whole, lanes]
                arriving = scale[whole, lanes] * message[seq : seq + 1, lanes] + shift[whole, lanes]
                adjoint = ups * o + jnp.where(row == STEP - 1, later, pltpu.roll(arriving, STEP - 1, 0))
                tile = pl.ds(pl.multiple_of(seq * tokens + jnp.maximum(at * STEP - SUB, 0), SUB), SUB)
                last = state[tile, lanes][SUB - 1 : SUB]
                first = jnp.where(at == 0, entering[seq : seq + 1, lanes], last)
                before = jnp.where(row == 0, first, pltpu.roll(states, 1, 0))
                given = [
                    adjoint * (1.0 - f) * (1.0 - u * u),
                    adjoint * (before * kept - u) * f * (1.0 - f),
                    ups * states * o * (1.0 - o),
                ]
                for gate, value in enumerate(given):
                    value = value.astype(BF16)
                    grads[whole, gate * channels + lanes.start : gate * channels + lanes.stop] = value
                    value = value.astype(F32)
                    total = value[:SUB]
                    for half in range(1, STEP // SUB):
                        total = total + value[half * SUB : half * SUB + SUB]
                    sums[gate, :, lanes] += total
                return arriving[0:1]

            lax.fori_loop(0, steps, body, message[seq : seq + 1, lanes])


def forward_kernel(seqs, tokens, channels, gates, bias, keep, initial, hidden, upd, fgt, out, state, entering, scale, shift, summary, slots, send_sems, recv_sems):
    greet("seq")
    first_pass(seqs, tokens, channels, gates, bias, keep, upd, fgt, out, scale, shift, summary)
    copies = to_all(summary, slots, send_sems, recv_sems, "seq")
    for copy in copies:
        copy.wait()
    entering[...] = from_earlier(slots, initial[...], slice(0, seqs), slice(seqs, 2 * seqs), "seq")
    states_pass(seqs, tokens, channels, entering, out, scale, shift, state, hidden)


def top_kernel(seqs, tokens, channels, gates, bias, keep, initial, cotangent, pooled, grads, sums, upd, fgt, out, state, entering, message, scale, shift, back_scale, back_shift, summary, slots, send_sems, recv_sems):
    greet("seq")
    first_pass(seqs, tokens, channels, gates, bias, keep, upd, fgt, out, scale, shift, summary)
    back_pass(seqs, tokens, channels, cotangent, keep, fgt, out, back_scale, back_shift, summary, 2 * seqs)
    copies = to_all(summary, slots, send_sems, recv_sems, "seq")
    for copy in copies:
        copy.wait()
    entering[...] = from_earlier(slots, initial[...], slice(0, seqs), slice(seqs, 2 * seqs), "seq")
    message[...] = from_later(
        slots, (seqs, channels), slice(2 * seqs, 3 * seqs), slice(3 * seqs, 4 * seqs), "seq"
    )
    states_pass(seqs, tokens, channels, entering, out, scale, shift, state, pooled)
    grads_pass(seqs, tokens, channels, message, entering, cotangent, keep, upd, fgt, out, state, back_scale, back_shift, grads, sums)


def backward_kernel(seqs, tokens, channels, upstream, keep, upd, fgt, out, state, entering, grads, sums, message, scale, shift, summary, slots, send_sems, recv_sems):
    greet("seq")
    back_pass(seqs, tokens, channels, upstream, keep, fgt, out, scale, shift, summary, 0)
    copies = to_all(summary, slots, send_sems, recv_sems, "seq")
    for copy in copies:
        copy.wait()
    message[...] = from_later(slots, (seqs, channels), slice(0, seqs), slice(seqs, 2 * seqs), "seq")
    grads_pass(seqs, tokens, channels, message, entering, upstream, keep, upd, fgt, out, state, scale, shift, grads, sums)


def exchange_scratch(rows, channels):
    count = lax.axis_size("seq")
    return [
        pltpu.VMEM((rows, channels), F32),
        pltpu.VMEM((count - 1, rows, channels), F32),
        pltpu.SemaphoreType.DMA((count - 1,)),
        pltpu.SemaphoreType.DMA((count - 1,)),
    ]


def params(number):
    return pltpu.CompilerParams(collective_id=number, has_side_effects=True, vmem_limit_bytes=56 * 2**20)


def cost(elements, ops, moved):
    return pl.CostEstimate(flops=elements * ops, bytes_accessed=moved, transcendentals=elements * 3)


def pool_forward(seqs, tokens, gates, bias, keep, initial):
    channels = gates.shape[2]
    rows = seqs * tokens
    whole = jax.ShapeDtypeStruct((rows, channels), F32)
    return pl.pallas_call(
        functools.partial(forward_kernel, seqs, tokens, channels),
        out_shape=(
            jax.ShapeDtypeStruct((rows, channels), BF16),
            whole,
            whole,
            whole,
            whole,
            jax.ShapeDtypeStruct((seqs, channels), F32),
        ),
        in_specs=[VMEM] * 4,
        out_specs=[VMEM] * 6,
        scratch_shapes=[pltpu.VMEM((rows, channels), F32)] * 2 + exchange_scratch(2 * seqs, channels),
        compiler_params=params(1),
        cost_estimate=cost(rows * channels, 60, rows * channels * 30),
        name="pool_forward",
    )(gates, bias, keep, initial)


def pool_top(seqs, tokens, gates, bias, keep, initial, cotangent):
    channels = gates.shape[2]
    rows = seqs * tokens
    whole = pltpu.VMEM((rows, channels), F32)
    edge = pltpu.VMEM((seqs, channels), F32)
    return pl.pallas_call(
        functools.partial(top_kernel, seqs, tokens, channels),
        out_shape=(
            jax.ShapeDtypeStruct((rows, channels), BF16),
            jax.ShapeDtypeStruct((rows, 3 * channels), BF16),
            jax.ShapeDtypeStruct((3, SUB, channels), F32),
        ),
        in_specs=[VMEM] * 5,
        out_specs=[VMEM] * 3,
        scratch_shapes=[whole] * 4 + [edge] * 2 + [whole] * 4 + exchange_scratch(4 * seqs, channels),
        compiler_params=params(2),
        cost_estimate=cost(rows * channels, 120, rows * channels * 22),
        name="pool_top",
    )(gates, bias, keep, initial, cotangent)


def pool_backward(seqs, tokens, upstream, keep, upd, fgt, out, state, entering):
    rows, channels = upstream.shape
    whole = pltpu.VMEM((rows, channels), F32)
    return pl.pallas_call(
        functools.partial(backward_kernel, seqs, tokens, channels),
        out_shape=(
            jax.ShapeDtypeStruct((rows, 3 * channels), BF16),
            jax.ShapeDtypeStruct((3, SUB, channels), F32),
        ),
        in_specs=[VMEM] * 7,
        out_specs=[VMEM] * 2,
        scratch_shapes=[pltpu.VMEM((seqs, channels), F32)] + [whole] * 2 + exchange_scratch(2 * seqs, channels),
        compiler_params=params(3),
        cost_estimate=cost(rows * channels, 60, rows * channels * 26),
        name="pool_backward",
    )(upstream, keep, upd, fgt, out, state, entering)


def shifted(value, axis, steps):
    count = lax.axis_size(axis)
    initial, last = (max(0, -steps), min(count, count - steps))
    return lax.ppermute(value, axis, [(source, source + steps) for source in range(initial, last)])


def gather_channels(value):
    count = lax.axis_size("mp")
    if count != 2:
        return lax.all_gather(value, "mp", axis=value.ndim - 1, tiled=True)
    other = lax.ppermute(value, "mp", [(0, 1), (1, 0)])
    second = lax.axis_index("mp") == 1
    return jnp.concatenate([jnp.where(second, other, value), jnp.where(second, value, other)], value.ndim - 1)


def sum_channels(terms):
    count = lax.axis_size("mp")
    if count != 2:
        return lax.psum_scatter(terms, "mp", scatter_dimension=1, tiled=True)
    width = terms.shape[1] // 2
    second = lax.axis_index("mp") == 1
    low, high = terms[:, :width], terms[:, width:]
    other = lax.ppermute(jnp.where(second, low, high), "mp", [(0, 1), (1, 0)])
    return jnp.where(second, high, low) + other


def dot(lhs, rhs, dims):
    return lax.dot_general(lhs, rhs, (dims, ((), ())), preferred_element_type=F32)


def reduce_weights(partial):
    shard = lax.psum_scatter(partial.astype(BF16), ("dp", "seq"), scatter_dimension=0, tiled=True)
    return lax.all_gather(shard, ("dp", "seq"), axis=0, tiled=True).astype(F32)


def local(inputs, starts, init_state, weight_one, bias_one, weight_two, bias_two, cotangent):
    seqs, tokens, channels = inputs.shape
    rows = seqs * tokens
    width = weight_one.shape[1]
    keep = jnp.broadcast_to((1 - starts).astype(F32).reshape(rows, 1), (rows, 128))
    taps = weight_one.transpose(0, 2, 1, 3)
    mix = weight_two.transpose(1, 0, 2)

    edge = gather_channels(shifted(inputs[:, -1], "seq", 1))
    full = gather_channels(inputs)
    previous = jnp.concatenate([edge[:, None], full[:, :-1]], 1).reshape(rows, width)
    full = full.reshape(rows, width)
    both = jnp.concatenate([full, previous], 1)
    gates_one = jnp.einsum(
        "tkd,kgdc->gtc", both.reshape(rows, 2, width), taps, preferred_element_type=F32
    )
    hidden, upd, fgt, out, state, entering = pool_forward(seqs, tokens, gates_one, bias_one, keep, init_state[0])
    full_hidden = gather_channels(hidden)
    gates_two = jnp.einsum("td,gdc->gtc", full_hidden, mix, preferred_element_type=F32)
    pooled_two, grad_two, sums_two = pool_top(
        seqs, tokens, gates_two, bias_two, keep, init_state[1], cotangent.reshape(rows, channels)
    )
    hidden_terms = jnp.einsum(
        "tgc,gdc->td", grad_two.reshape(rows, 3, channels), mix, preferred_element_type=F32
    )
    hidden_grad = sum_channels(hidden_terms)
    grad_one, sums_one = pool_backward(seqs, tokens, hidden_grad, keep, upd, fgt, out, state, entering)
    weight_two_grad = dot(full_hidden, grad_two, ((0,), (0,)))
    weight_two_grad = reduce_weights(weight_two_grad)
    next_first = shifted(grad_one.reshape(seqs, tokens, -1)[:, 0], "seq", -1)
    following = jnp.concatenate([grad_one.reshape(seqs, tokens, -1)[:, 1:], next_first[:, None]], 1).reshape(rows, -1)
    weight_one_grad = jnp.stack(
        [
            reduce_weights(dot(full, grad_one, ((0,), (0,)))),
            reduce_weights(dot(previous, grad_one, ((0,), (0,)))),
        ]
    )
    input_terms = jnp.einsum(
        "tgc,gdc->td", grad_one.reshape(rows, 3, channels), taps[0], preferred_element_type=F32
    ) + jnp.einsum("tgc,gdc->td", following.reshape(rows, 3, channels), taps[1], preferred_element_type=F32)
    input_grad = sum_channels(input_terms)
    bias_one_grad, bias_two_grad = lax.psum((jnp.sum(sums_one, 1), jnp.sum(sums_two, 1)), ("dp", "seq"))
    return (
        pooled_two.reshape(seqs, tokens, channels),
        input_grad.reshape(seqs, tokens, channels),
        weight_one_grad.reshape(2, width, 3, channels),
        bias_one_grad,
        weight_two_grad.reshape(width, 3, channels),
        bias_two_grad,
    )


def solution(mesh):
    return jax.shard_map(
        local,
        mesh=mesh,
        in_specs=(
            P("dp", "seq", "mp"),
            P("dp", "seq"),
            P(None, "dp", "mp"),
            P(None, None, None, "mp"),
            P(None, "mp"),
            P(None, None, "mp"),
            P(None, "mp"),
            P("dp", "seq", "mp"),
        ),
        out_specs=(
            P("dp", "seq", "mp"),
            P("dp", "seq", "mp"),
            P(None, None, None, "mp"),
            P(None, "mp"),
            P(None, None, "mp"),
            P(None, "mp"),
        ),
        check_vma=False,
    )
```

```python
import functools

import jax
import jax.numpy as jnp
from jax import lax
from jax.experimental import pallas as pl
from jax.experimental.pallas import tpu as pltpu
from jax.sharding import PartitionSpec as P

F32 = jnp.float32
BF16 = jnp.bfloat16
SUB = 8
STEP = 16
EDGE = 16
PART = 64
LAG = 1
VMEM = pl.BlockSpec(memory_space=pltpu.VMEM)


def sigmoid(x):
    return 0.5 * jnp.tanh(0.5 * x) + 0.5


def lane_blocks(channels):
    width = 384 if channels % 384 == 0 else channels
    return [slice(at, at + width) for at in range(0, channels, width)]


def scan_down(scale, shift):
    row = lax.broadcasted_iota(jnp.int32, scale.shape, 0)
    for step in (1, 2, 4):
        earlier = row >= step
        scale_before = jnp.where(earlier, pltpu.roll(scale, step, 0), 1.0)
        shift_before = jnp.where(earlier, pltpu.roll(shift, step, 0), 0.0)
        shift = scale * shift_before + shift
        scale = scale * scale_before
    return scale, shift


def scan_up(scale, shift):
    row = lax.broadcasted_iota(jnp.int32, scale.shape, 0)
    for step in (1, 2, 4):
        later = row < SUB - step
        scale_after = jnp.where(later, pltpu.roll(scale, SUB - step, 0), 1.0)
        shift_after = jnp.where(later, pltpu.roll(shift, SUB - step, 0), 0.0)
        shift = scale * shift_after + shift
        scale = scale * scale_after
    return scale, shift


def greet(axis):
    count = lax.axis_size(axis)
    me = lax.axis_index(axis)
    barrier = pltpu.get_barrier_semaphore()
    for step in range(1, count):
        pl.semaphore_signal(
            barrier, inc=1, device_id={axis: lax.rem(me + step, count)}, device_id_type=pl.DeviceIdType.MESH
        )
    pl.semaphore_wait(barrier, count - 1)


def to_all(src, slots, send_sems, recv_sems, axis):
    count = lax.axis_size(axis)
    me = lax.axis_index(axis)
    copies = []
    for step in range(1, count):
        copies.append(
            pltpu.make_async_remote_copy(
                src_ref=src,
                dst_ref=slots.at[step - 1],
                send_sem=send_sems.at[step - 1],
                recv_sem=recv_sems.at[step - 1],
                device_id={axis: lax.rem(me + step, count)},
                device_id_type=pl.DeviceIdType.MESH,
            )
        )
    for copy in copies:
        copy.start()
    return copies


def from_earlier(slots, initial, scale_rows, shift_rows, axis):
    count = lax.axis_size(axis)
    me = lax.axis_index(axis)
    state = initial
    for block in range(count - 1):
        slot = jnp.maximum(me - block - 1, 0)
        after = slots[slot, scale_rows, :] * state + slots[slot, shift_rows, :]
        state = jnp.where(block < me, after, state)
    return state


def from_later(slots, shape, scale_rows, shift_rows, axis):
    count = lax.axis_size(axis)
    me = lax.axis_index(axis)
    message = jnp.zeros(shape, F32)
    for block in range(count - 1, 0, -1):
        slot = jnp.minimum(me + count - block - 1, count - 2)
        after = slots[slot, scale_rows, :] * message + slots[slot, shift_rows, :]
        message = jnp.where(block > me, after, message)
    return message


def first_pass(seqs, tokens, channels, gates, bias, keep, upd, fgt, out, scale, shift, summary):
    def body(at, carried):
        given = list(carried)
        for seq in range(seqs):
            for half in range(STEP // SUB):
                rows = pl.ds(pl.multiple_of(seq * tokens + at * STEP + half * SUB, SUB), SUB)
                kept = keep[rows, :][:, 0:1]
                for number, lanes in enumerate(lane_blocks(channels)):
                    u = jnp.tanh(gates[0, rows, lanes] + bias[0:1, lanes])
                    f = sigmoid(gates[1, rows, lanes] + bias[1:2, lanes])
                    o = sigmoid(gates[2, rows, lanes] + bias[2:3, lanes])
                    upd[rows, lanes] = u
                    fgt[rows, lanes] = f
                    out[rows, lanes] = o
                    a, b = scan_down(f * kept, (1.0 - f) * u)
                    place = (seq * len(lane_blocks(channels)) + number) * 2
                    b = a * given[place + 1] + b
                    a = a * given[place]
                    scale[rows, lanes] = a
                    shift[rows, lanes] = b
                    given[place] = a[SUB - 1 : SUB]
                    given[place + 1] = b[SUB - 1 : SUB]
        return tuple(given)

    begin = []
    for seq in range(seqs):
        for lanes in lane_blocks(channels):
            width = lanes.stop - lanes.start
            begin += [jnp.ones((1, width), F32), jnp.zeros((1, width), F32)]
    end = lax.fori_loop(0, tokens // STEP, body, tuple(begin))
    place = 0
    for seq in range(seqs):
        for lanes in lane_blocks(channels):
            summary[seq : seq + 1, lanes] = end[place]
            summary[seqs + seq : seqs + seq + 1, lanes] = end[place + 1]
            place += 2


def back_pass(seqs, tokens, channels, upstream, keep, fgt, out, scale, shift, summary, row0):
    steps = tokens // STEP

    def body(index, carried):
        at = steps - 1 - index
        given = list(carried)
        for seq in range(seqs):
            whole = pl.ds(pl.multiple_of(seq * tokens + at * STEP, STEP), STEP)
            for number, lanes in enumerate(lane_blocks(channels)):
                ups = upstream[whole, lanes].astype(F32)
                place = (seq * len(lane_blocks(channels)) + number) * 2
                for half in reversed(range(STEP // SUB)):
                    rows = pl.ds(pl.multiple_of(seq * tokens + at * STEP + half * SUB, SUB), SUB)
                    kept = keep[rows, :][:, 0:1]
                    retain = fgt[rows, lanes] * kept
                    direct = ups[half * SUB : half * SUB + SUB] * out[rows, lanes]
                    a, b = scan_up(retain, retain * direct)
                    b = a * given[place + 1] + b
                    a = a * given[place]
                    scale[rows, lanes] = a
                    shift[rows, lanes] = b
                    given[place] = a[0:1]
                    given[place + 1] = b[0:1]
        return tuple(given)

    begin = []
    for seq in range(seqs):
        for lanes in lane_blocks(channels):
            width = lanes.stop - lanes.start
            begin += [jnp.ones((1, width), F32), jnp.zeros((1, width), F32)]
    end = lax.fori_loop(0, steps, body, tuple(begin))
    place = 0
    for seq in range(seqs):
        for lanes in lane_blocks(channels):
            summary[row0 + seq : row0 + seq + 1, lanes] = end[place]
            summary[row0 + seqs + seq : row0 + seqs + seq + 1, lanes] = end[place + 1]
            place += 2


def states_pass(seqs, tokens, channels, entering, out, scale, shift, state, pooled):
    def body(at, none):
        for seq in range(seqs):
            rows = pl.ds(pl.multiple_of(seq * tokens + at * STEP, STEP), STEP)
            for lanes in lane_blocks(channels):
                value = scale[rows, lanes] * entering[seq : seq + 1, lanes] + shift[rows, lanes]
                state[rows, lanes] = value
                pooled[rows, lanes] = (out[rows, lanes] * value).astype(BF16)
        return none

    lax.fori_loop(0, tokens // STEP, body, 0)


def grads_pass(seqs, tokens, channels, message, entering, upstream, keep, upd, fgt, out, state, scale, shift, grads, sums):
    steps = tokens // STEP
    sums[...] = jnp.zeros_like(sums)
    if grads.shape[1] > 3 * channels:
        grads[:, 3 * channels :] = jnp.zeros((grads.shape[0], grads.shape[1] - 3 * channels), BF16)
    for seq in range(seqs):
        for lanes in lane_blocks(channels):
            width = lanes.stop - lanes.start

            def body(index, later, seq=seq, lanes=lanes, width=width):
                at = steps - 1 - index
                whole = pl.ds(pl.multiple_of(seq * tokens + at * STEP, STEP), STEP)
                row = lax.broadcasted_iota(jnp.int32, (STEP, width), 0)
                kept = keep[whole, :][:, 0:1]
                ups = upstream[whole, lanes].astype(F32)
                u, f, o = upd[whole, lanes], fgt[whole, lanes], out[whole, lanes]
                states = state[whole, lanes]
                arriving = scale[whole, lanes] * message[seq : seq + 1, lanes] + shift[whole, lanes]
                adjoint = ups * o + jnp.where(row == STEP - 1, later, pltpu.roll(arriving, STEP - 1, 0))
                tile = pl.ds(pl.multiple_of(seq * tokens + jnp.maximum(at * STEP - SUB, 0), SUB), SUB)
                last = state[tile, lanes][SUB - 1 : SUB]
                first = jnp.where(at == 0, entering[seq : seq + 1, lanes], last)
                before = jnp.where(row == 0, first, pltpu.roll(states, 1, 0))
                given = [
                    adjoint * (1.0 - f) * (1.0 - u * u),
                    adjoint * (before * kept - u) * f * (1.0 - f),
                    ups * states * o * (1.0 - o),
                ]
                for gate, value in enumerate(given):
                    value = value.astype(BF16)
                    grads[whole, gate * channels + lanes.start : gate * channels + lanes.stop] = value
                    value = value.astype(F32)
                    total = value[:SUB]
                    for half in range(1, STEP // SUB):
                        total = total + value[half * SUB : half * SUB + SUB]
                    sums[gate, :, lanes] += total
                return arriving[0:1]

            lax.fori_loop(0, steps, body, message[seq : seq + 1, lanes])


def forward_kernel(seqs, tokens, channels, gates, bias, keep, initial, hidden, upd, fgt, out, state, entering, scale, shift, summary, slots, send_sems, recv_sems):
    greet("seq")
    first_pass(seqs, tokens, channels, gates, bias, keep, upd, fgt, out, scale, shift, summary)
    copies = to_all(summary, slots, send_sems, recv_sems, "seq")
    for copy in copies:
        copy.wait()
    entering[...] = from_earlier(slots, initial[...], slice(0, seqs), slice(seqs, 2 * seqs), "seq")
    states_pass(seqs, tokens, channels, entering, out, scale, shift, state, hidden)


def top_kernel(seqs, tokens, channels, gates, bias, keep, initial, cotangent, pooled, grads, sums, upd, fgt, out, state, entering, message, scale, shift, back_scale, back_shift, summary, slots, send_sems, recv_sems):
    greet("seq")
    first_pass(seqs, tokens, channels, gates, bias, keep, upd, fgt, out, scale, shift, summary)
    back_pass(seqs, tokens, channels, cotangent, keep, fgt, out, back_scale, back_shift, summary, 2 * seqs)
    copies = to_all(summary, slots, send_sems, recv_sems, "seq")
    for copy in copies:
        copy.wait()
    entering[...] = from_earlier(slots, initial[...], slice(0, seqs), slice(seqs, 2 * seqs), "seq")
    message[...] = from_later(
        slots, (seqs, channels), slice(2 * seqs, 3 * seqs), slice(3 * seqs, 4 * seqs), "seq"
    )
    states_pass(seqs, tokens, channels, entering, out, scale, shift, state, pooled)
    grads_pass(seqs, tokens, channels, message, entering, cotangent, keep, upd, fgt, out, state, back_scale, back_shift, grads, sums)


def pass_edges(seqs, tokens, grads, edges, arrived, edge_sems):
    count = lax.axis_size("seq")
    me = lax.axis_index("seq")
    row = lax.broadcasted_iota(jnp.int32, edges.shape, 0)
    firsts = jnp.zeros(edges.shape, F32)
    for seq in range(seqs):
        tile = grads[seq * tokens : seq * tokens + EDGE, :].astype(F32)
        firsts = jnp.where(row == seq, pltpu.roll(tile, seq, 0) if seq else tile, firsts)
    edges[...] = firsts.astype(BF16)
    copy = pltpu.make_async_remote_copy(
        src_ref=edges,
        dst_ref=arrived,
        send_sem=edge_sems.at[0],
        recv_sem=edge_sems.at[1],
        device_id={"seq": lax.rem(me + count - 1, count)},
        device_id_type=pl.DeviceIdType.MESH,
    )
    rows = slice(seqs * tokens, seqs * tokens + EDGE)

    @pl.when(me > 0)
    def _():
        copy.start()

    @pl.when(me < count - 1)
    def _():
        copy.wait_recv()
        grads[rows, :] = arrived[...]

    @pl.when(me == count - 1)
    def _():
        grads[rows, :] = jnp.zeros(edges.shape, BF16)

    @pl.when(me > 0)
    def _():
        copy.wait_send()


def backward_kernel(seqs, tokens, channels, upstream, keep, upd, fgt, out, state, entering, grads, sums, message, scale, shift, summary, slots, send_sems, recv_sems, edges, arrived, edge_sems):
    greet("seq")
    back_pass(seqs, tokens, channels, upstream, keep, fgt, out, scale, shift, summary, 0)
    copies = to_all(summary, slots, send_sems, recv_sems, "seq")
    for copy in copies:
        copy.wait()
    message[...] = from_later(slots, (seqs, channels), slice(0, seqs), slice(seqs, 2 * seqs), "seq")
    grads_pass(seqs, tokens, channels, message, entering, upstream, keep, upd, fgt, out, state, scale, shift, grads, sums)
    pass_edges(seqs, tokens, grads, edges, arrived, edge_sems)


def exchange_scratch(rows, channels):
    count = lax.axis_size("seq")
    return [
        pltpu.VMEM((rows, channels), F32),
        pltpu.VMEM((count - 1, rows, channels), F32),
        pltpu.SemaphoreType.DMA((count - 1,)),
        pltpu.SemaphoreType.DMA((count - 1,)),
    ]


def params(number):
    return pltpu.CompilerParams(collective_id=number, has_side_effects=True, vmem_limit_bytes=56 * 2**20)


def cost(elements, ops, moved):
    return pl.CostEstimate(flops=elements * ops, bytes_accessed=moved, transcendentals=elements * 3)


def pool_forward(seqs, tokens, gates, bias, keep, initial):
    channels = gates.shape[2]
    rows = seqs * tokens
    whole = jax.ShapeDtypeStruct((rows, channels), F32)
    return pl.pallas_call(
        functools.partial(forward_kernel, seqs, tokens, channels),
        out_shape=(
            jax.ShapeDtypeStruct((rows, channels), BF16),
            whole,
            whole,
            whole,
            whole,
            jax.ShapeDtypeStruct((seqs, channels), F32),
        ),
        in_specs=[VMEM] * 4,
        out_specs=[VMEM] * 6,
        scratch_shapes=[pltpu.VMEM((rows, channels), F32)] * 2 + exchange_scratch(2 * seqs, channels),
        compiler_params=params(1),
        cost_estimate=cost(rows * channels, 60, rows * channels * 30),
        name="pool_forward",
    )(gates, bias, keep, initial)


def pool_top(seqs, tokens, lanes, gates, bias, keep, initial, cotangent):
    channels = gates.shape[2]
    rows = seqs * tokens
    whole = pltpu.VMEM((rows, channels), F32)
    edge = pltpu.VMEM((seqs, channels), F32)
    return pl.pallas_call(
        functools.partial(top_kernel, seqs, tokens, channels),
        out_shape=(
            jax.ShapeDtypeStruct((rows, channels), BF16),
            jax.ShapeDtypeStruct((rows, lanes), BF16),
            jax.ShapeDtypeStruct((3, SUB, channels), F32),
        ),
        in_specs=[VMEM] * 5,
        out_specs=[VMEM] * 3,
        scratch_shapes=[whole] * 4 + [edge] * 2 + [whole] * 4 + exchange_scratch(4 * seqs, channels),
        compiler_params=params(2),
        cost_estimate=cost(rows * channels, 120, rows * channels * 22),
        name="pool_top",
    )(gates, bias, keep, initial, cotangent)


def pool_backward(seqs, tokens, lanes, upstream, keep, upd, fgt, out, state, entering):
    rows, channels = upstream.shape
    whole = pltpu.VMEM((rows, channels), F32)
    return pl.pallas_call(
        functools.partial(backward_kernel, seqs, tokens, channels),
        out_shape=(
            jax.ShapeDtypeStruct((rows + EDGE, lanes), BF16),
            jax.ShapeDtypeStruct((3, SUB, channels), F32),
        ),
        in_specs=[VMEM] * 7,
        out_specs=[VMEM] * 2,
        scratch_shapes=[pltpu.VMEM((seqs, channels), F32)]
        + [whole] * 2
        + exchange_scratch(2 * seqs, channels)
        + [pltpu.VMEM((EDGE, lanes), BF16)] * 2
        + [pltpu.SemaphoreType.DMA((2,))],
        compiler_params=params(3),
        cost_estimate=cost(rows * channels, 60, rows * channels * 26),
        name="pool_backward",
    )(upstream, keep, upd, fgt, out, state, entering)


def spread_kernel(layers, parts, loads, sums, out, sums_out, own, ups, downs, acc, across, around, load_sems, up_sems, down_sems, line_send, line_recv, kept_sems, plane_send, plane_recv, sums_sems):
    line, plane = lax.axis_size("seq"), lax.axis_size("dp")
    at, here = lax.axis_index("seq"), lax.axis_index("dp")
    unit = line * parts
    depth = own.shape[0] // layers
    units = own.shape[0] // unit
    half = unit // 2
    beside = here + 1 - 2 * lax.rem(here, 2)
    below = lax.rem(here + 2, plane)
    across_from = lax.rem(beside + 2, plane)

    barrier = pltpu.get_barrier_semaphore()
    for axis, me, count in (("seq", at, line), ("dp", here, plane)):
        for step in range(1, count):
            pl.semaphore_signal(
                barrier, inc=1, device_id={axis: lax.rem(me + step, count)}, device_id_type=pl.DeviceIdType.MESH
            )
    pl.semaphore_wait(barrier, line + plane - 2)

    def remote(src, dst, send, recv, axis, target):
        return pltpu.make_async_remote_copy(
            src_ref=src,
            dst_ref=dst,
            send_sem=send,
            recv_sem=recv,
            device_id={axis: target},
            device_id_type=pl.DeviceIdType.MESH,
        )

    def load(layer):
        return pltpu.make_async_copy(loads[layer], own.at[pl.ds(layer * depth, depth)], load_sems.at[layer])

    def chunk(u, j):
        return pl.ds(pl.multiple_of(u * unit + j * parts, parts), parts)

    def up(src, u, j):
        number = u * (line - 1) + j - 1
        return remote(src, ups.at[u, j - 1], up_sems.at[0, number], up_sems.at[1, number], "seq", lax.rem(at + 1, line))

    def down(src, u, j):
        number = u * (line - 1) + j
        return remote(
            src, downs.at[u, j], down_sems.at[0, number], down_sems.at[1, number], "seq", lax.rem(at + line - 1, line)
        )

    def along(src, u, j, way, hop):
        return remote(
            src,
            out.at[here, chunk(u, j)],
            line_send.at[(u * 2 + way) * (line - 1) + hop],
            line_recv.at[u * line + j],
            "seq",
            lax.rem(at + (1 if way == 0 else line - 1), line),
        )

    def keep(u):
        return pltpu.make_async_copy(own.at[chunk(u, at)], out.at[here, chunk(u, at)], kept_sems.at[u])

    def rows(u, first, count):
        return pl.ds(pl.multiple_of(u * unit + first, half), count)

    def over(u, way):
        place = out.at[here, rows(u, 0, unit)]
        return remote(place, place, plane_send.at[u * 4 + way], plane_recv.at[u * 4 + way], "dp", (beside, below)[way])

    def onward(u, way):
        place = out.at[(beside, below)[way], rows(u, way * half, half)]
        return remote(
            place, place, plane_send.at[u * 4 + 2 + way], plane_recv.at[u * 4 + 2 + way], "dp", (below, beside)[way]
        )

    def corner(u, way):
        place = out.at[across_from, rows(u, way * half, half)]
        return remote(place, place, plane_send.at[u * 4 + 2 + way], plane_recv.at[u * 4 + 2 + way], "dp", (below, beside)[way])

    def sums_copy(slots, me, count, axis, number, step):
        return remote(
            slots.at[me],
            slots.at[me],
            sums_sems.at[number, 0, step - 1],
            sums_sems.at[number, 1, step - 1],
            axis,
            lax.rem(me + step, count),
        )

    def sums_arrival(slots, me, count, axis, number, step):
        place = slots.at[lax.rem(me + count - step, count)]
        return remote(place, place, sums_sems.at[number, 0, step - 1], sums_sems.at[number, 1, step - 1], axis, lax.rem(me + step, count))

    for layer in range(layers):
        load(layer).start()
    across[at] = sums[...]
    for step in range(1, line):
        sums_copy(across, at, line, "seq", 0, step).start()
    load(0).wait()

    def stage(index, none):
        @pl.when(index == 1)
        def _():
            for layer in range(1, layers):
                load(layer).wait()
            for step in range(1, line):
                sums_arrival(across, at, line, "seq", 0, step).wait_recv()
            total = across[0]
            for other in range(1, line):
                total = total + across[other]
            around[here] = total
            for step in range(1, plane):
                sums_copy(around, here, plane, "dp", 1, step).start()

        @pl.when(index == 3)
        def _():
            for step in range(1, plane):
                sums_arrival(around, here, plane, "dp", 1, step).wait_recv()
            total = around[0]
            for other in range(1, plane):
                total = total + around[other]
            sums_out[...] = total

        u = index - at

        @pl.when((u >= 0) & (u < units))
        def _():
            for j in range(1, line):

                @pl.when(at == 0)
                def _(j=j):
                    up(own.at[chunk(u, j)], u, j).start()

                @pl.when((at > 0) & (at <= j))
                def _(j=j):
                    up(ups.at[u, j - 1], u, j).wait_recv()

                @pl.when((at > 0) & (at < j))
                def _(j=j):
                    ups[u, j - 1] = (ups[u, j - 1].astype(F32) + own[chunk(u, j)].astype(F32)).astype(BF16)
                    up(ups.at[u, j - 1], u, j).start()

        v = index - (line - 1 - at)

        @pl.when((v >= 0) & (v < units))
        def _():
            for j in range(line - 1):

                @pl.when(at == line - 1)
                def _(j=j):
                    down(own.at[chunk(v, j)], v, j).start()

                @pl.when((at < line - 1) & (at >= j))
                def _(j=j):
                    down(downs.at[v, j], v, j).wait_recv()

                @pl.when((at < line - 1) & (at > j))
                def _(j=j):
                    downs[v, j] = (downs[v, j].astype(F32) + own[chunk(v, j)].astype(F32)).astype(BF16)
                    down(downs.at[v, j], v, j).start()

        w = index - (line - 1)

        @pl.when((w >= 0) & (w < units))
        def _():
            acc[...] = own[chunk(w, at)].astype(F32)

            @pl.when(at > 0)
            def _():
                acc[...] += ups[w, at - 1].astype(F32)

            @pl.when(at < line - 1)
            def _():
                acc[...] += downs[w, at].astype(F32)

            own[chunk(w, at)] = acc[...].astype(BF16)
            keep(w).start()

            @pl.when(at < line - 1)
            def _():
                along(own.at[chunk(w, at)], w, at, 0, 0).start()

            @pl.when(at > 0)
            def _():
                along(own.at[chunk(w, at)], w, at, 1, 0).start()

        for hop in range(1, line):
            x = index - (line - 1) - hop

            @pl.when((x >= 0) & (x < units))
            def _(x=x, hop=hop):
                @pl.when(at >= hop)
                def _():
                    src = out.at[here, chunk(x, at - hop)]
                    along(src, x, at - hop, 0, 0).wait_recv()
                    if hop < line - 1:

                        @pl.when(at < line - 1)
                        def _():
                            along(src, x, at - hop, 0, hop).start()

                @pl.when(at + hop < line)
                def _():
                    src = out.at[here, chunk(x, at + hop)]
                    along(src, x, at + hop, 1, 0).wait_recv()
                    if hop < line - 1:

                        @pl.when(at > 0)
                        def _():
                            along(src, x, at + hop, 1, hop).start()

        y = index - 2 * (line - 1)

        @pl.when((y >= 0) & (y < units))
        def _():
            keep(y).wait()
            over(y, 0).start()
            over(y, 1).start()

        z = y - LAG

        @pl.when((z >= 0) & (z < units))
        def _():
            for way in range(2):
                place = out.at[(beside, below)[way], rows(z, 0, unit)]
                remote(place, place, plane_send.at[z * 4 + way], plane_recv.at[z * 4 + way], "dp", (beside, below)[way]).wait_recv()
                onward(z, way).start()

        t = z - LAG

        @pl.when((t >= 0) & (t < units))
        def _():
            for way in range(2):
                corner(t, way).wait_recv()

        return none

    lax.fori_loop(0, units + 2 * (line - 1) + 2 * LAG, stage, 0)

    def settle(u, none):
        for j in range(1, line):

            @pl.when(at < j)
            def _(j=j):
                up(ups.at[u, j - 1], u, j).wait_send()

        for j in range(line - 1):

            @pl.when(at > j)
            def _(j=j):
                down(downs.at[u, j], u, j).wait_send()

        for hop in range(line - 1):

            @pl.when((at >= hop) & (at < line - 1))
            def _(hop=hop):
                along(out.at[here, chunk(u, at - hop)], u, at - hop, 0, hop).wait_send()

            @pl.when((at + hop < line) & (at > 0))
            def _(hop=hop):
                along(out.at[here, chunk(u, at + hop)], u, at + hop, 1, hop).wait_send()

        for way in range(2):
            over(u, way).wait_send()
            onward(u, way).wait_send()
        return none

    lax.fori_loop(0, units, settle, 0)
    for step in range(1, line):
        sums_copy(across, at, line, "seq", 0, step).wait_send()
    for step in range(1, plane):
        sums_copy(around, here, plane, "dp", 1, step).wait_send()


def spread(partials, sums):
    line, plane = lax.axis_size("seq"), lax.axis_size("dp")
    layers = len(partials)
    depth, width = partials[0].shape
    units = layers * depth // (line * PART)

    def kernel(*refs):
        spread_kernel(layers, PART, refs[:layers], *refs[layers:])

    dma = pltpu.SemaphoreType.DMA
    return pl.pallas_call(
        kernel,
        out_shape=(
            jax.ShapeDtypeStruct((plane, layers * depth, width), BF16),
            jax.ShapeDtypeStruct(sums.shape, F32),
        ),
        in_specs=[pl.BlockSpec(memory_space=pl.ANY)] * layers + [VMEM],
        out_specs=[pl.BlockSpec(memory_space=pl.ANY), VMEM],
        scratch_shapes=[
            pltpu.VMEM((layers * depth, width), BF16),
            pltpu.VMEM((units, line - 1, PART, width), BF16),
            pltpu.VMEM((units, line - 1, PART, width), BF16),
            pltpu.VMEM((PART, width), F32),
            pltpu.VMEM((line,) + sums.shape, F32),
            pltpu.VMEM((plane,) + sums.shape, F32),
            dma((layers,)),
            dma((2, units * (line - 1))),
            dma((2, units * (line - 1))),
            dma((units * 2 * (line - 1),)),
            dma((units * line,)),
            dma((units,)),
            dma((units * 4,)),
            dma((units * 4,)),
            dma((2, 2, max(line, plane) - 1)),
        ],
        compiler_params=params(4),
        cost_estimate=pl.CostEstimate(flops=0, bytes_accessed=layers * depth * width * 16, transcendentals=0),
        name="spread",
    )(*partials, sums)


def widen_kernel(tiles, blocks, given, out):
    per = given.shape[2] // 128
    for tile in range(tiles * blocks):
        source, place = divmod(tile, per)
        gate, column = divmod(tile, blocks)
        out[0, gate, :, column * 128 : column * 128 + 128] = given[
            source, :, place * 128 : place * 128 + 128
        ].astype(F32)


def widen(gathered, first, layers, depth, channels):
    plane, _, width = gathered.shape
    rows = 128
    steps = depth // rows
    return pl.pallas_call(
        functools.partial(widen_kernel, 3, channels // 128),
        grid=(layers, steps),
        out_shape=jax.ShapeDtypeStruct((layers, 3, depth, channels), F32),
        in_specs=[pl.BlockSpec((plane, rows, width), lambda layer, step: (0, (first + layer) * steps + step, 0))],
        out_specs=pl.BlockSpec((1, 3, rows, channels), lambda layer, step: (layer, 0, step, 0)),
        compiler_params=pltpu.CompilerParams(vmem_limit_bytes=32 * 2**20),
        name="widen",
    )(gathered)


def around_plane(value, steps):
    return lax.ppermute(value, "dp", [(at, at ^ steps) for at in range(4)])


def to_owners(grads, width):
    here = lax.axis_index("dp")
    blocks = []
    for steps, owner in enumerate((here, here + 1 - 2 * lax.rem(here, 2), lax.rem(here + 2, 4), 3 - here)):
        block = lax.dynamic_slice(grads, (0, owner * width), (grads.shape[0], width))
        blocks.append(around_plane(block, steps) if steps else block)
    return blocks


def shifted(value, axis, steps):
    count = lax.axis_size(axis)
    initial, last = (max(0, -steps), min(count, count - steps))
    return lax.ppermute(value, axis, [(source, source + steps) for source in range(initial, last)])


def gather_channels(value):
    count = lax.axis_size("mp")
    if count != 2:
        return lax.all_gather(value, "mp", axis=value.ndim - 1, tiled=True)
    other = lax.ppermute(value, "mp", [(0, 1), (1, 0)])
    second = lax.axis_index("mp") == 1
    return jnp.concatenate([jnp.where(second, other, value), jnp.where(second, value, other)], value.ndim - 1)


def sum_channels(terms):
    count = lax.axis_size("mp")
    if count != 2:
        return lax.psum_scatter(terms, "mp", scatter_dimension=1, tiled=True)
    width = terms.shape[1] // 2
    second = lax.axis_index("mp") == 1
    low, high = terms[:, :width], terms[:, width:]
    other = lax.ppermute(jnp.where(second, low, high), "mp", [(0, 1), (1, 0)])
    return jnp.where(second, high, low) + other


def dot(lhs, rhs, dims):
    return lax.dot_general(lhs, rhs, (dims, ((), ())), preferred_element_type=F32)


def reduce_weights(partial):
    shard = lax.psum_scatter(partial.astype(BF16), ("dp", "seq"), scatter_dimension=0, tiled=True)
    return lax.all_gather(shard, ("dp", "seq"), axis=0, tiled=True).astype(F32)


def local(inputs, starts, init_state, weight_one, bias_one, weight_two, bias_two, cotangent):
    seqs, tokens, channels = inputs.shape
    rows = seqs * tokens
    width = weight_one.shape[1]
    keep = jnp.broadcast_to((1 - starts).astype(F32).reshape(rows, 1), (rows, 128))
    taps = weight_one.transpose(0, 2, 1, 3)
    mix = weight_two.transpose(1, 0, 2)

    edge = gather_channels(shifted(inputs[:, -1], "seq", 1))
    full = gather_channels(inputs)
    previous = jnp.concatenate([edge[:, None], full[:, :-1]], 1).reshape(rows, width)
    full = full.reshape(rows, width)
    both = jnp.concatenate([full, previous], 1)
    gates_one = jnp.einsum(
        "tkd,kgdc->gtc", both.reshape(rows, 2, width), taps, preferred_element_type=F32
    )
    hidden, upd, fgt, out, state, entering = pool_forward(seqs, tokens, gates_one, bias_one, keep, init_state[0])
    full_hidden = gather_channels(hidden)
    gates_two = jnp.einsum("td,gdc->gtc", full_hidden, mix, preferred_element_type=F32)
    line, plane = lax.axis_size("seq"), lax.axis_size("dp")
    tiles = 3 * channels // 128
    spreads = plane == 4 and channels % 128 == 0 and width % (line * PART) == 0 and line > 1
    block = -(-tiles // plane) * 128
    lanes = plane * block if spreads else 3 * channels
    pooled_two, grad_two, sums_two = pool_top(
        seqs, tokens, lanes, gates_two, bias_two, keep, init_state[1], cotangent.reshape(rows, channels)
    )
    hidden_terms = jnp.einsum(
        "tgc,gdc->td", grad_two[:, : 3 * channels].reshape(rows, 3, channels), mix, preferred_element_type=F32
    )
    hidden_grad = sum_channels(hidden_terms)
    extended, sums_one = pool_backward(seqs, tokens, lanes, hidden_grad, keep, upd, fgt, out, state, entering)
    grad_one = extended[:rows, : 3 * channels]
    input_terms = jnp.einsum(
        "tgc,kgdc->ktd", grad_one.reshape(rows, 3, channels), taps, preferred_element_type=F32
    ).reshape(2, seqs, tokens, width)
    late = input_terms[1]
    late = jnp.concatenate([late[:, 1:], shifted(late[:, 0], "seq", -1)[:, None]], 1)
    input_grad = sum_channels((input_terms[0] + late).reshape(rows, width))
    sums = jnp.concatenate([jnp.sum(sums_one, 1), jnp.sum(sums_two, 1)])
    if spreads:
        every = [full] + [around_plane(full, steps) for steps in range(1, 4)]
        every_hidden = [full_hidden] + [around_plane(full_hidden, steps) for steps in range(1, 4)]
        blocks_two = to_owners(grad_two, block)
        blocks_one = to_owners(extended, block)
        partial_two = dot(jnp.concatenate(every_hidden), jnp.concatenate(blocks_two), ((0,), (0,))).astype(BF16)
        every = jnp.concatenate(every)
        partial_one = dot(every, jnp.concatenate([given[:rows] for given in blocks_one]), ((0,), (0,))).astype(BF16)
        following = []
        for given in blocks_one:
            for seq in range(seqs):
                following += [
                    given[seq * tokens + 1 : seq * tokens + tokens],
                    given[rows + seq : rows + seq + 1],
                ]
        partial_late = dot(every, jnp.concatenate(following), ((0,), (0,))).astype(BF16)
        gathered, sums = spread([partial_two, partial_one, partial_late], sums)
        weight_two_grad = widen(gathered, 0, 1, width, channels)[0].transpose(1, 0, 2)
        weight_one_grad = widen(gathered, 1, 2, width, channels).transpose(0, 2, 1, 3)
    else:
        sums = lax.psum(sums, ("dp", "seq"))
        weight_two_grad = reduce_weights(dot(full_hidden, grad_two, ((0,), (0,)))).reshape(width, 3, channels)
        weight_one_grad = jnp.stack(
            [
                reduce_weights(dot(full, grad_one, ((0,), (0,)))),
                reduce_weights(dot(previous, grad_one, ((0,), (0,)))),
            ]
        ).reshape(2, width, 3, channels)
    return (
        pooled_two.reshape(seqs, tokens, channels),
        input_grad.reshape(seqs, tokens, channels),
        weight_one_grad,
        sums[:3],
        weight_two_grad,
        sums[3:],
    )


def solution(mesh):
    return jax.shard_map(
        local,
        mesh=mesh,
        in_specs=(
            P("dp", "seq", "mp"),
            P("dp", "seq"),
            P(None, "dp", "mp"),
            P(None, None, None, "mp"),
            P(None, "mp"),
            P(None, None, "mp"),
            P(None, "mp"),
            P("dp", "seq", "mp"),
        ),
        out_specs=(
            P("dp", "seq", "mp"),
            P("dp", "seq", "mp"),
            P(None, None, None, "mp"),
            P(None, "mp"),
            P(None, None, "mp"),
            P(None, "mp"),
        ),
        check_vma=False,
    )
```

```python
import functools

import jax
import jax.numpy as jnp
from jax import lax
from jax.experimental import pallas as pl
from jax.experimental.pallas import tpu as pltpu
from jax.sharding import PartitionSpec as P

F32 = jnp.float32
BF16 = jnp.bfloat16
SUB = 8
STEP = 16
EDGE = 16
PART = 64
LAG = 1
VMEM = pl.BlockSpec(memory_space=pltpu.VMEM)


def sigmoid(x):
    return 0.5 * jnp.tanh(0.5 * x) + 0.5


def lane_blocks(channels):
    width = 384 if channels % 384 == 0 else channels
    return [slice(at, at + width) for at in range(0, channels, width)]


def scan_down(scale, shift):
    row = lax.broadcasted_iota(jnp.int32, scale.shape, 0)
    for step in (1, 2, 4):
        earlier = row >= step
        scale_before = jnp.where(earlier, pltpu.roll(scale, step, 0), 1.0)
        shift_before = jnp.where(earlier, pltpu.roll(shift, step, 0), 0.0)
        shift = scale * shift_before + shift
        scale = scale * scale_before
    return scale, shift


def scan_up(scale, shift):
    row = lax.broadcasted_iota(jnp.int32, scale.shape, 0)
    for step in (1, 2, 4):
        later = row < SUB - step
        scale_after = jnp.where(later, pltpu.roll(scale, SUB - step, 0), 1.0)
        shift_after = jnp.where(later, pltpu.roll(shift, SUB - step, 0), 0.0)
        shift = scale * shift_after + shift
        scale = scale * scale_after
    return scale, shift


def greet(axis):
    count = lax.axis_size(axis)
    me = lax.axis_index(axis)
    barrier = pltpu.get_barrier_semaphore()
    for step in range(1, count):
        pl.semaphore_signal(
            barrier, inc=1, device_id={axis: lax.rem(me + step, count)}, device_id_type=pl.DeviceIdType.MESH
        )
    pl.semaphore_wait(barrier, count - 1)


def to_all(src, slots, send_sems, recv_sems, axis):
    count = lax.axis_size(axis)
    me = lax.axis_index(axis)
    copies = []
    for step in range(1, count):
        copies.append(
            pltpu.make_async_remote_copy(
                src_ref=src,
                dst_ref=slots.at[step - 1],
                send_sem=send_sems.at[step - 1],
                recv_sem=recv_sems.at[step - 1],
                device_id={axis: lax.rem(me + step, count)},
                device_id_type=pl.DeviceIdType.MESH,
            )
        )
    for copy in copies:
        copy.start()
    return copies


def from_earlier(slots, initial, scale_rows, shift_rows, axis):
    count = lax.axis_size(axis)
    me = lax.axis_index(axis)
    state = initial
    for block in range(count - 1):
        slot = jnp.maximum(me - block - 1, 0)
        after = slots[slot, scale_rows, :] * state + slots[slot, shift_rows, :]
        state = jnp.where(block < me, after, state)
    return state


def from_later(slots, shape, scale_rows, shift_rows, axis):
    count = lax.axis_size(axis)
    me = lax.axis_index(axis)
    message = jnp.zeros(shape, F32)
    for block in range(count - 1, 0, -1):
        slot = jnp.minimum(me + count - block - 1, count - 2)
        after = slots[slot, scale_rows, :] * message + slots[slot, shift_rows, :]
        message = jnp.where(block > me, after, message)
    return message


def first_pass(seqs, tokens, channels, gates, bias, keep, upd, fgt, out, scale, shift, summary):
    def body(at, carried):
        given = list(carried)
        for seq in range(seqs):
            for half in range(STEP // SUB):
                rows = pl.ds(pl.multiple_of(seq * tokens + at * STEP + half * SUB, SUB), SUB)
                kept = keep[rows, :][:, 0:1]
                for number, lanes in enumerate(lane_blocks(channels)):
                    u = jnp.tanh(gates[0, rows, lanes] + bias[0:1, lanes])
                    f = sigmoid(gates[1, rows, lanes] + bias[1:2, lanes])
                    o = sigmoid(gates[2, rows, lanes] + bias[2:3, lanes])
                    upd[rows, lanes] = u
                    fgt[rows, lanes] = f
                    out[rows, lanes] = o
                    a, b = scan_down(f * kept, (1.0 - f) * u)
                    place = (seq * len(lane_blocks(channels)) + number) * 2
                    b = a * given[place + 1] + b
                    a = a * given[place]
                    scale[rows, lanes] = a
                    shift[rows, lanes] = b
                    given[place] = a[SUB - 1 : SUB]
                    given[place + 1] = b[SUB - 1 : SUB]
        return tuple(given)

    begin = []
    for seq in range(seqs):
        for lanes in lane_blocks(channels):
            width = lanes.stop - lanes.start
            begin += [jnp.ones((1, width), F32), jnp.zeros((1, width), F32)]
    end = lax.fori_loop(0, tokens // STEP, body, tuple(begin))
    place = 0
    for seq in range(seqs):
        for lanes in lane_blocks(channels):
            summary[seq : seq + 1, lanes] = end[place]
            summary[seqs + seq : seqs + seq + 1, lanes] = end[place + 1]
            place += 2


def back_pass(seqs, tokens, channels, upstream, keep, fgt, out, scale, shift, summary, row0):
    steps = tokens // STEP

    def body(index, carried):
        at = steps - 1 - index
        given = list(carried)
        for seq in range(seqs):
            whole = pl.ds(pl.multiple_of(seq * tokens + at * STEP, STEP), STEP)
            for number, lanes in enumerate(lane_blocks(channels)):
                ups = upstream[whole, lanes].astype(F32)
                place = (seq * len(lane_blocks(channels)) + number) * 2
                for half in reversed(range(STEP // SUB)):
                    rows = pl.ds(pl.multiple_of(seq * tokens + at * STEP + half * SUB, SUB), SUB)
                    kept = keep[rows, :][:, 0:1]
                    retain = fgt[rows, lanes] * kept
                    direct = ups[half * SUB : half * SUB + SUB] * out[rows, lanes]
                    a, b = scan_up(retain, retain * direct)
                    b = a * given[place + 1] + b
                    a = a * given[place]
                    scale[rows, lanes] = a
                    shift[rows, lanes] = b
                    given[place] = a[0:1]
                    given[place + 1] = b[0:1]
        return tuple(given)

    begin = []
    for seq in range(seqs):
        for lanes in lane_blocks(channels):
            width = lanes.stop - lanes.start
            begin += [jnp.ones((1, width), F32), jnp.zeros((1, width), F32)]
    end = lax.fori_loop(0, steps, body, tuple(begin))
    place = 0
    for seq in range(seqs):
        for lanes in lane_blocks(channels):
            summary[row0 + seq : row0 + seq + 1, lanes] = end[place]
            summary[row0 + seqs + seq : row0 + seqs + seq + 1, lanes] = end[place + 1]
            place += 2


def states_pass(seqs, tokens, channels, entering, out, scale, shift, state, pooled):
    def body(at, none):
        for seq in range(seqs):
            rows = pl.ds(pl.multiple_of(seq * tokens + at * STEP, STEP), STEP)
            for lanes in lane_blocks(channels):
                value = scale[rows, lanes] * entering[seq : seq + 1, lanes] + shift[rows, lanes]
                state[rows, lanes] = value
                pooled[rows, lanes] = (out[rows, lanes] * value).astype(BF16)
        return none

    lax.fori_loop(0, tokens // STEP, body, 0)


def grads_pass(seqs, tokens, channels, message, entering, upstream, keep, upd, fgt, out, state, scale, shift, grads, planes, sums):
    steps = tokens // STEP
    sums[...] = jnp.zeros_like(sums)
    if grads.shape[1] > 3 * channels:
        grads[:, 3 * channels :] = jnp.zeros((grads.shape[0], grads.shape[1] - 3 * channels), BF16)
    for seq in range(seqs):
        for lanes in lane_blocks(channels):
            width = lanes.stop - lanes.start

            def body(index, later, seq=seq, lanes=lanes, width=width):
                at = steps - 1 - index
                whole = pl.ds(pl.multiple_of(seq * tokens + at * STEP, STEP), STEP)
                row = lax.broadcasted_iota(jnp.int32, (STEP, width), 0)
                kept = keep[whole, :][:, 0:1]
                ups = upstream[whole, lanes].astype(F32)
                u, f, o = upd[whole, lanes], fgt[whole, lanes], out[whole, lanes]
                states = state[whole, lanes]
                arriving = scale[whole, lanes] * message[seq : seq + 1, lanes] + shift[whole, lanes]
                adjoint = ups * o + jnp.where(row == STEP - 1, later, pltpu.roll(arriving, STEP - 1, 0))
                tile = pl.ds(pl.multiple_of(seq * tokens + jnp.maximum(at * STEP - SUB, 0), SUB), SUB)
                last = state[tile, lanes][SUB - 1 : SUB]
                first = jnp.where(at == 0, entering[seq : seq + 1, lanes], last)
                before = jnp.where(row == 0, first, pltpu.roll(states, 1, 0))
                given = [
                    adjoint * (1.0 - f) * (1.0 - u * u),
                    adjoint * (before * kept - u) * f * (1.0 - f),
                    ups * states * o * (1.0 - o),
                ]
                for gate, value in enumerate(given):
                    value = value.astype(BF16)
                    grads[whole, gate * channels + lanes.start : gate * channels + lanes.stop] = value
                    planes[gate, whole, lanes] = value
                    value = value.astype(F32)
                    total = value[:SUB]
                    for half in range(1, STEP // SUB):
                        total = total + value[half * SUB : half * SUB + SUB]
                    sums[gate, :, lanes] += total
                return arriving[0:1]

            lax.fori_loop(0, steps, body, message[seq : seq + 1, lanes])


def forward_kernel(seqs, tokens, channels, gates, bias, keep, initial, hidden, upd, fgt, out, state, entering, scale, shift, summary, slots, send_sems, recv_sems):
    greet("seq")
    first_pass(seqs, tokens, channels, gates, bias, keep, upd, fgt, out, scale, shift, summary)
    copies = to_all(summary, slots, send_sems, recv_sems, "seq")
    for copy in copies:
        copy.wait()
    entering[...] = from_earlier(slots, initial[...], slice(0, seqs), slice(seqs, 2 * seqs), "seq")
    states_pass(seqs, tokens, channels, entering, out, scale, shift, state, hidden)


def top_kernel(seqs, tokens, channels, gates, bias, keep, initial, cotangent, pooled, grads, planes, sums, upd, fgt, out, state, entering, message, scale, shift, back_scale, back_shift, summary, slots, send_sems, recv_sems):
    greet("seq")
    first_pass(seqs, tokens, channels, gates, bias, keep, upd, fgt, out, scale, shift, summary)
    back_pass(seqs, tokens, channels, cotangent, keep, fgt, out, back_scale, back_shift, summary, 2 * seqs)
    copies = to_all(summary, slots, send_sems, recv_sems, "seq")
    for copy in copies:
        copy.wait()
    entering[...] = from_earlier(slots, initial[...], slice(0, seqs), slice(seqs, 2 * seqs), "seq")
    message[...] = from_later(
        slots, (seqs, channels), slice(2 * seqs, 3 * seqs), slice(3 * seqs, 4 * seqs), "seq"
    )
    states_pass(seqs, tokens, channels, entering, out, scale, shift, state, pooled)
    grads_pass(seqs, tokens, channels, message, entering, cotangent, keep, upd, fgt, out, state, back_scale, back_shift, grads, planes, sums)


def pass_edges(seqs, tokens, grads, edges, arrived, edge_sems):
    count = lax.axis_size("seq")
    me = lax.axis_index("seq")
    row = lax.broadcasted_iota(jnp.int32, edges.shape, 0)
    firsts = jnp.zeros(edges.shape, F32)
    for seq in range(seqs):
        tile = grads[seq * tokens : seq * tokens + EDGE, :].astype(F32)
        firsts = jnp.where(row == seq, pltpu.roll(tile, seq, 0) if seq else tile, firsts)
    edges[...] = firsts.astype(BF16)
    copy = pltpu.make_async_remote_copy(
        src_ref=edges,
        dst_ref=arrived,
        send_sem=edge_sems.at[0],
        recv_sem=edge_sems.at[1],
        device_id={"seq": lax.rem(me + count - 1, count)},
        device_id_type=pl.DeviceIdType.MESH,
    )
    rows = slice(seqs * tokens, seqs * tokens + EDGE)

    @pl.when(me > 0)
    def _():
        copy.start()

    @pl.when(me < count - 1)
    def _():
        copy.wait_recv()
        grads[rows, :] = arrived[...]

    @pl.when(me == count - 1)
    def _():
        grads[rows, :] = jnp.zeros(edges.shape, BF16)

    @pl.when(me > 0)
    def _():
        copy.wait_send()


def backward_kernel(seqs, tokens, channels, upstream, keep, upd, fgt, out, state, entering, grads, planes, sums, message, scale, shift, summary, slots, send_sems, recv_sems, edges, arrived, edge_sems):
    greet("seq")
    back_pass(seqs, tokens, channels, upstream, keep, fgt, out, scale, shift, summary, 0)
    copies = to_all(summary, slots, send_sems, recv_sems, "seq")
    for copy in copies:
        copy.wait()
    message[...] = from_later(slots, (seqs, channels), slice(0, seqs), slice(seqs, 2 * seqs), "seq")
    grads_pass(seqs, tokens, channels, message, entering, upstream, keep, upd, fgt, out, state, scale, shift, grads, planes, sums)
    pass_edges(seqs, tokens, grads, edges, arrived, edge_sems)


def exchange_scratch(rows, channels):
    count = lax.axis_size("seq")
    return [
        pltpu.VMEM((rows, channels), F32),
        pltpu.VMEM((count - 1, rows, channels), F32),
        pltpu.SemaphoreType.DMA((count - 1,)),
        pltpu.SemaphoreType.DMA((count - 1,)),
    ]


def params(number):
    return pltpu.CompilerParams(collective_id=number, has_side_effects=True, vmem_limit_bytes=56 * 2**20)


def cost(elements, ops, moved):
    return pl.CostEstimate(flops=elements * ops, bytes_accessed=moved, transcendentals=elements * 3)


def pool_forward(seqs, tokens, gates, bias, keep, initial):
    channels = gates.shape[2]
    rows = seqs * tokens
    whole = jax.ShapeDtypeStruct((rows, channels), F32)
    return pl.pallas_call(
        functools.partial(forward_kernel, seqs, tokens, channels),
        out_shape=(
            jax.ShapeDtypeStruct((rows, channels), BF16),
            whole,
            whole,
            whole,
            whole,
            jax.ShapeDtypeStruct((seqs, channels), F32),
        ),
        in_specs=[VMEM] * 4,
        out_specs=[VMEM] * 6,
        scratch_shapes=[pltpu.VMEM((rows, channels), F32)] * 2 + exchange_scratch(2 * seqs, channels),
        compiler_params=params(1),
        cost_estimate=cost(rows * channels, 60, rows * channels * 30),
        name="pool_forward",
    )(gates, bias, keep, initial)


def pool_top(seqs, tokens, lanes, gates, bias, keep, initial, cotangent):
    channels = gates.shape[2]
    rows = seqs * tokens
    whole = pltpu.VMEM((rows, channels), F32)
    edge = pltpu.VMEM((seqs, channels), F32)
    return pl.pallas_call(
        functools.partial(top_kernel, seqs, tokens, channels),
        out_shape=(
            jax.ShapeDtypeStruct((rows, channels), BF16),
            jax.ShapeDtypeStruct((rows, lanes), BF16),
            jax.ShapeDtypeStruct((3, rows, channels), BF16),
            jax.ShapeDtypeStruct((3, SUB, channels), F32),
        ),
        in_specs=[VMEM] * 5,
        out_specs=[VMEM] * 4,
        scratch_shapes=[whole] * 4 + [edge] * 2 + [whole] * 4 + exchange_scratch(4 * seqs, channels),
        compiler_params=params(2),
        cost_estimate=cost(rows * channels, 120, rows * channels * 22),
        name="pool_top",
    )(gates, bias, keep, initial, cotangent)


def pool_backward(seqs, tokens, lanes, upstream, keep, upd, fgt, out, state, entering):
    rows, channels = upstream.shape
    whole = pltpu.VMEM((rows, channels), F32)
    return pl.pallas_call(
        functools.partial(backward_kernel, seqs, tokens, channels),
        out_shape=(
            jax.ShapeDtypeStruct((rows + EDGE, lanes), BF16),
            jax.ShapeDtypeStruct((3, rows, channels), BF16),
            jax.ShapeDtypeStruct((3, SUB, channels), F32),
        ),
        in_specs=[VMEM] * 7,
        out_specs=[VMEM] * 3,
        scratch_shapes=[pltpu.VMEM((seqs, channels), F32)]
        + [whole] * 2
        + exchange_scratch(2 * seqs, channels)
        + [pltpu.VMEM((EDGE, lanes), BF16)] * 2
        + [pltpu.SemaphoreType.DMA((2,))],
        compiler_params=params(3),
        cost_estimate=cost(rows * channels, 60, rows * channels * 26),
        name="pool_backward",
    )(upstream, keep, upd, fgt, out, state, entering)


def shift_up(seqs, tokens, value, edges, result):
    width = value.shape[1]
    steps = tokens // STEP

    def body(index, none):
        sequence, at = index // steps, lax.rem(index, steps)
        row = lax.broadcasted_iota(jnp.int32, (STEP, width), 0)
        rows = pl.ds(pl.multiple_of(index * STEP, STEP), STEP)
        after = jnp.minimum(index + 1, value.shape[0] // STEP - 1)
        first = value[pl.ds(pl.multiple_of(after * STEP, STEP), STEP), :].astype(F32)[0:1]
        edge = edges[sequence // seqs].astype(F32)
        edge = jnp.where(lax.rem(sequence, seqs) == 0, edge[0:1], edge[1:2])
        moved = pltpu.roll(value[rows, :].astype(F32), STEP - 1, 0)
        moved = jnp.where(row == STEP - 1, jnp.where(at == steps - 1, edge, first), moved)
        result[rows, :] = moved.astype(BF16)
        return none

    lax.fori_loop(0, value.shape[0] // STEP, body, 0)


def spread_kernel(seqs, tokens, parts, hidden_own, hidden_other, full_own, full_other, *refs):
    blocks_two, (grads_one, sums, out, sums_out, rows_full, grads, grads_edge, moved, *rest) = refs[:4], refs[4:]
    _spread(seqs, tokens, parts, (hidden_own, hidden_other), (full_own, full_other), blocks_two, grads_one, sums, out, sums_out, rows_full, grads, grads_edge, moved, *rest)


def _spread(seqs, tokens, parts, hidden, full, blocks_two, grads_one, sums, out, sums_out, rows_full, grads, grads_edge, moved, own, ups, downs, acc, across, around, load_sems, swap_sems, up_sems, down_sems, line_send, line_recv, kept_sems, plane_send, plane_recv, sums_sems):
    line, plane = lax.axis_size("seq"), lax.axis_size("dp")
    at, here = lax.axis_index("seq"), lax.axis_index("dp")
    unit = line * parts
    units = own.shape[0] // unit
    blocks = units // 3
    width = own.shape[1]
    block_rows = seqs * tokens
    half = unit // 2
    beside = here + 1 - 2 * lax.rem(here, 2)
    below = lax.rem(here + 2, plane)
    across_from = lax.rem(beside + 2, plane)

    barrier = pltpu.get_barrier_semaphore()
    for axis, me, count in (("seq", at, line), ("dp", here, plane)):
        for step in range(1, count):
            pl.semaphore_signal(
                barrier, inc=1, device_id={axis: lax.rem(me + step, count)}, device_id_type=pl.DeviceIdType.MESH
            )
    pl.semaphore_wait(barrier, line + plane - 2)

    def remote(src, dst, send, recv, axis, target):
        return pltpu.make_async_remote_copy(
            src_ref=src,
            dst_ref=dst,
            send_sem=send,
            recv_sem=recv,
            device_id={axis: target},
            device_id_type=pl.DeviceIdType.MESH,
        )

    mine = lax.axis_index("mp")
    wide = rows_full.shape[1] // 2

    def load_rows(pair, number):
        return [
            pltpu.make_async_copy(
                pair[way],
                rows_full.at[:, pl.ds(pl.multiple_of((mine if way == 0 else 1 - mine) * wide, 128), wide)],
                load_sems.at[number + way],
            )
            for way in range(2)
        ]

    def plane_rows(owner):
        return pl.ds(pl.multiple_of(owner * block_rows, 16), block_rows)

    def peer(steps):
        return (here, beside, below, across_from)[steps]

    def load_two(steps):
        return pltpu.make_async_copy(blocks_two[steps], moved.at[plane_rows(peer(steps))], load_sems.at[4 + steps])

    def swap(steps, edge, arriving=False):
        columns = pl.ds(pl.multiple_of(peer(steps) * width, 128), width)
        source = peer(steps) if arriving else here
        if edge:
            src, dst = grads_one.at[block_rows : block_rows + EDGE, columns], grads_edge.at[source]
        else:
            src, dst = grads_one.at[0:block_rows, columns], grads.at[plane_rows(source)]
        number = steps * 2 + edge
        if steps == 0:
            return pltpu.make_async_copy(src, dst, swap_sems.at[0, number])
        return remote(src, dst, swap_sems.at[0, number], swap_sems.at[1, number], "dp", peer(steps))

    def product(block, right):
        columns = pl.ds(pl.multiple_of(block * unit, 128), unit)
        return lax.dot_general(
            rows_full[:, columns], right[...], (((0,), (0,)), ((), ())), preferred_element_type=F32
        ).astype(BF16)

    def whole(u):
        return pl.ds(pl.multiple_of(u * unit, unit), unit)

    def chunk(u, j):
        return pl.ds(pl.multiple_of(u * unit + j * parts, parts), parts)

    def up(src, u, j):
        number = u * (line - 1) + j - 1
        return remote(src, ups.at[u, j - 1], up_sems.at[0, number], up_sems.at[1, number], "seq", lax.rem(at + 1, line))

    def down(src, u, j):
        number = u * (line - 1) + j
        return remote(
            src, downs.at[u, j], down_sems.at[0, number], down_sems.at[1, number], "seq", lax.rem(at + line - 1, line)
        )

    def along(src, u, j, way, hop):
        return remote(
            src,
            out.at[here, chunk(u, j)],
            line_send.at[(u * 2 + way) * (line - 1) + hop],
            line_recv.at[u * line + j],
            "seq",
            lax.rem(at + (1 if way == 0 else line - 1), line),
        )

    def keep(u):
        return pltpu.make_async_copy(own.at[chunk(u, at)], out.at[here, chunk(u, at)], kept_sems.at[u])

    def rows(u, first, count):
        return pl.ds(pl.multiple_of(u * unit + first, half), count)

    def over(u, way):
        place = out.at[here, rows(u, 0, unit)]
        return remote(place, place, plane_send.at[u * 4 + way], plane_recv.at[u * 4 + way], "dp", (beside, below)[way])

    def onward(u, way):
        place = out.at[(beside, below)[way], rows(u, way * half, half)]
        return remote(
            place, place, plane_send.at[u * 4 + 2 + way], plane_recv.at[u * 4 + 2 + way], "dp", (below, beside)[way]
        )

    def corner(u, way):
        place = out.at[across_from, rows(u, way * half, half)]
        return remote(place, place, plane_send.at[u * 4 + 2 + way], plane_recv.at[u * 4 + 2 + way], "dp", (below, beside)[way])

    def sums_copy(slots, me, count, axis, number, step):
        return remote(
            slots.at[me],
            slots.at[me],
            sums_sems.at[number, 0, step - 1],
            sums_sems.at[number, 1, step - 1],
            axis,
            lax.rem(me + step, count),
        )

    def sums_arrival(slots, me, count, axis, number, step):
        place = slots.at[lax.rem(me + count - step, count)]
        return remote(place, place, sums_sems.at[number, 0, step - 1], sums_sems.at[number, 1, step - 1], axis, lax.rem(me + step, count))

    for steps in range(4):
        load_two(steps).start()
    for copy in load_rows(hidden, 0):
        copy.start()
    for steps in range(4):
        for edge in range(2):
            swap(steps, edge).start()
    across[at] = sums[...]
    for step in range(1, line):
        sums_copy(across, at, line, "seq", 0, step).start()
    for steps in range(4):
        load_two(steps).wait()
    for copy in load_rows(hidden, 0):
        copy.wait()

    def stage(index, none):
        @pl.when(index == 1)
        def _():
            for step in range(1, line):
                sums_arrival(across, at, line, "seq", 0, step).wait_recv()
            total = across[0]
            for other in range(1, line):
                total = total + across[other]
            around[here] = total
            for step in range(1, plane):
                sums_copy(around, here, plane, "dp", 1, step).start()

        @pl.when(index == 3)
        def _():
            for step in range(1, plane):
                sums_arrival(around, here, plane, "dp", 1, step).wait_recv()
            total = around[0]
            for other in range(1, plane):
                total = total + around[other]
            sums_out[...] = total

        @pl.when(index < blocks)
        def _():
            own[whole(index), :] = product(index, moved)

        @pl.when(index == blocks - 1)
        def _():
            for copy in load_rows(full, 2):
                copy.start()

        @pl.when(index == blocks)
        def _():
            for steps in range(4):
                for edge in range(2):
                    if steps:
                        swap(steps, edge, True).wait_recv()
                    else:
                        swap(steps, edge).wait()
            shift_up(seqs, tokens, grads, grads_edge, moved)
            for copy in load_rows(full, 2):
                copy.wait()

        @pl.when((index >= blocks) & (index < units) & (lax.rem(index - blocks, 2) == 0))
        def _():
            own[whole(index), :] = product((index - blocks) // 2, grads)

        @pl.when((index >= blocks) & (index < units) & (lax.rem(index - blocks, 2) == 1))
        def _():
            own[whole(index), :] = product((index - blocks) // 2, moved)

        u = index - at

        @pl.when((u >= 0) & (u < units))
        def _():
            for j in range(1, line):

                @pl.when(at == 0)
                def _(j=j):
                    up(own.at[chunk(u, j)], u, j).start()

                @pl.when((at > 0) & (at <= j))
                def _(j=j):
                    up(ups.at[u, j - 1], u, j).wait_recv()

                @pl.when((at > 0) & (at < j))
                def _(j=j):
                    ups[u, j - 1] = (ups[u, j - 1].astype(F32) + own[chunk(u, j)].astype(F32)).astype(BF16)
                    up(ups.at[u, j - 1], u, j).start()

        v = index - (line - 1 - at)

        @pl.when((v >= 0) & (v < units))
        def _():
            for j in range(line - 1):

                @pl.when(at == line - 1)
                def _(j=j):
                    down(own.at[chunk(v, j)], v, j).start()

                @pl.when((at < line - 1) & (at >= j))
                def _(j=j):
                    down(downs.at[v, j], v, j).wait_recv()

                @pl.when((at < line - 1) & (at > j))
                def _(j=j):
                    downs[v, j] = (downs[v, j].astype(F32) + own[chunk(v, j)].astype(F32)).astype(BF16)
                    down(downs.at[v, j], v, j).start()

        w = index - (line - 1)

        @pl.when((w >= 0) & (w < units))
        def _():
            acc[...] = own[chunk(w, at)].astype(F32)

            @pl.when(at > 0)
            def _():
                acc[...] += ups[w, at - 1].astype(F32)

            @pl.when(at < line - 1)
            def _():
                acc[...] += downs[w, at].astype(F32)

            own[chunk(w, at)] = acc[...].astype(BF16)
            keep(w).start()

            @pl.when(at < line - 1)
            def _():
                along(own.at[chunk(w, at)], w, at, 0, 0).start()

            @pl.when(at > 0)
            def _():
                along(own.at[chunk(w, at)], w, at, 1, 0).start()

        for hop in range(1, line):
            x = index - (line - 1) - hop

            @pl.when((x >= 0) & (x < units))
            def _(x=x, hop=hop):
                @pl.when(at >= hop)
                def _():
                    src = out.at[here, chunk(x, at - hop)]
                    along(src, x, at - hop, 0, 0).wait_recv()
                    if hop < line - 1:

                        @pl.when(at < line - 1)
                        def _():
                            along(src, x, at - hop, 0, hop).start()

                @pl.when(at + hop < line)
                def _():
                    src = out.at[here, chunk(x, at + hop)]
                    along(src, x, at + hop, 1, 0).wait_recv()
                    if hop < line - 1:

                        @pl.when(at > 0)
                        def _():
                            along(src, x, at + hop, 1, hop).start()

        y = index - 2 * (line - 1)

        @pl.when((y >= 0) & (y < units))
        def _():
            keep(y).wait()
            over(y, 0).start()
            over(y, 1).start()

        z = y - LAG

        @pl.when((z >= 0) & (z < units))
        def _():
            for way in range(2):
                place = out.at[(beside, below)[way], rows(z, 0, unit)]
                remote(place, place, plane_send.at[z * 4 + way], plane_recv.at[z * 4 + way], "dp", (beside, below)[way]).wait_recv()
                onward(z, way).start()

        t = z - LAG

        @pl.when((t >= 0) & (t < units))
        def _():
            for way in range(2):
                corner(t, way).wait_recv()

        return none

    lax.fori_loop(0, units + 2 * (line - 1) + 2 * LAG, stage, 0)

    def settle(u, none):
        for j in range(1, line):

            @pl.when(at < j)
            def _(j=j):
                up(ups.at[u, j - 1], u, j).wait_send()

        for j in range(line - 1):

            @pl.when(at > j)
            def _(j=j):
                down(downs.at[u, j], u, j).wait_send()

        for hop in range(line - 1):

            @pl.when((at >= hop) & (at < line - 1))
            def _(hop=hop):
                along(out.at[here, chunk(u, at - hop)], u, at - hop, 0, hop).wait_send()

            @pl.when((at + hop < line) & (at > 0))
            def _(hop=hop):
                along(out.at[here, chunk(u, at + hop)], u, at + hop, 1, hop).wait_send()

        for way in range(2):
            over(u, way).wait_send()
            onward(u, way).wait_send()
        return none

    lax.fori_loop(0, units, settle, 0)
    for steps in range(1, 4):
        for edge in range(2):
            swap(steps, edge).wait_send()
    for step in range(1, line):
        sums_copy(across, at, line, "seq", 0, step).wait_send()
    for step in range(1, plane):
        sums_copy(around, here, plane, "dp", 1, step).wait_send()


def spread(seqs, tokens, hidden, full, blocks_two, grads_one, sums):
    line, plane = lax.axis_size("seq"), lax.axis_size("dp")
    rows, width = blocks_two[0].shape
    depth = 2 * full[0].shape[1]
    units = 3 * depth // (line * PART)
    dma = pltpu.SemaphoreType.DMA
    hbm = pl.BlockSpec(memory_space=pl.ANY)
    return pl.pallas_call(
        functools.partial(spread_kernel, seqs, tokens, PART),
        out_shape=(
            jax.ShapeDtypeStruct((plane, 3 * depth, width), BF16),
            jax.ShapeDtypeStruct(sums.shape, F32),
        ),
        in_specs=[hbm] * 9 + [VMEM],
        out_specs=[hbm, VMEM],
        scratch_shapes=[
            pltpu.VMEM((plane * rows, depth), BF16),
            pltpu.VMEM((plane * rows, width), BF16),
            pltpu.VMEM((plane, EDGE, width), BF16),
            pltpu.VMEM((plane * rows, width), BF16),
            pltpu.VMEM((3 * depth, width), BF16),
            pltpu.VMEM((units, line - 1, PART, width), BF16),
            pltpu.VMEM((units, line - 1, PART, width), BF16),
            pltpu.VMEM((PART, width), F32),
            pltpu.VMEM((line,) + sums.shape, F32),
            pltpu.VMEM((plane,) + sums.shape, F32),
            dma((8,)),
            dma((2, 8)),
            dma((2, units * (line - 1))),
            dma((2, units * (line - 1))),
            dma((units * 2 * (line - 1),)),
            dma((units * line,)),
            dma((units,)),
            dma((units * 4,)),
            dma((units * 4,)),
            dma((2, 2, max(line, plane) - 1)),
        ],
        compiler_params=params(4),
        cost_estimate=pl.CostEstimate(
            flops=6 * plane * rows * depth * width, bytes_accessed=depth * width * 48, transcendentals=0
        ),
        name="spread",
    )(*hidden, *full, *blocks_two, grads_one, sums)


def widen_kernel(tiles, blocks, given, out):
    per = given.shape[2] // 128
    for tile in range(tiles * blocks):
        source, place = divmod(tile, per)
        gate, column = divmod(tile, blocks)
        out[0, gate, :, column * 128 : column * 128 + 128] = given[
            source, :, place * 128 : place * 128 + 128
        ].astype(F32)


def widen(gathered, layer_one, depth, channels, unit):
    plane, _, width = gathered.shape
    rows = 128
    steps, per = depth // rows, unit // rows
    taps = 2 if layer_one else 1

    def place(tap, step):
        if not layer_one:
            return (0, step, 0)
        return (0, steps + (step // per * 2 + tap) * per + lax.rem(step, per), 0)

    return pl.pallas_call(
        functools.partial(widen_kernel, 3, channels // 128),
        grid=(taps, steps),
        out_shape=jax.ShapeDtypeStruct((taps, 3, depth, channels), F32),
        in_specs=[pl.BlockSpec((plane, rows, width), place)],
        out_specs=pl.BlockSpec((1, 3, rows, channels), lambda tap, step: (tap, 0, step, 0)),
        compiler_params=pltpu.CompilerParams(vmem_limit_bytes=32 * 2**20),
        name="widen",
    )(gathered)


def plane_tokens(value):
    every = lax.all_gather(value, "dp", axis=0, tiled=True)
    return every, lax.ppermute(every, "mp", [(0, 1), (1, 0)])


def around_plane(value, steps):
    return lax.ppermute(value, "dp", [(at, at ^ steps) for at in range(4)])


def to_owners(grads, width):
    here = lax.axis_index("dp")
    blocks = []
    for steps, owner in enumerate((here, here + 1 - 2 * lax.rem(here, 2), lax.rem(here + 2, 4), 3 - here)):
        block = lax.dynamic_slice(grads, (0, owner * width), (grads.shape[0], width))
        blocks.append(around_plane(block, steps) if steps else block)
    return blocks


def shifted(value, axis, steps):
    count = lax.axis_size(axis)
    initial, last = (max(0, -steps), min(count, count - steps))
    return lax.ppermute(value, axis, [(source, source + steps) for source in range(initial, last)])


def gather_channels(value):
    count = lax.axis_size("mp")
    if count != 2:
        return lax.all_gather(value, "mp", axis=value.ndim - 1, tiled=True)
    other = lax.ppermute(value, "mp", [(0, 1), (1, 0)])
    second = lax.axis_index("mp") == 1
    return jnp.concatenate([jnp.where(second, other, value), jnp.where(second, value, other)], value.ndim - 1)


def sum_channels(terms):
    count = lax.axis_size("mp")
    if count != 2:
        return lax.psum_scatter(terms, "mp", scatter_dimension=1, tiled=True)
    width = terms.shape[1] // 2
    second = lax.axis_index("mp") == 1
    low, high = terms[:, :width], terms[:, width:]
    other = lax.ppermute(jnp.where(second, low, high), "mp", [(0, 1), (1, 0)])
    return jnp.where(second, high, low) + other


def dot(lhs, rhs, dims):
    return lax.dot_general(lhs, rhs, (dims, ((), ())), preferred_element_type=F32)


def reduce_weights(partial):
    shard = lax.psum_scatter(partial.astype(BF16), ("dp", "seq"), scatter_dimension=0, tiled=True)
    return lax.all_gather(shard, ("dp", "seq"), axis=0, tiled=True).astype(F32)


def local(inputs, starts, init_state, weight_one, bias_one, weight_two, bias_two, cotangent):
    seqs, tokens, channels = inputs.shape
    rows = seqs * tokens
    width = weight_one.shape[1]
    keep = jnp.broadcast_to((1 - starts).astype(F32).reshape(rows, 1), (rows, 128))
    taps = weight_one.transpose(0, 2, 1, 3)
    mix = weight_two.transpose(1, 0, 2)

    edge = gather_channels(shifted(inputs[:, -1], "seq", 1))
    full = gather_channels(inputs)
    previous = jnp.concatenate([edge[:, None], full[:, :-1]], 1).reshape(rows, width)
    full = full.reshape(rows, width)
    both = jnp.concatenate([full, previous], 1)
    gates_one = jnp.einsum(
        "tkd,kgdc->gtc", both.reshape(rows, 2, width), taps, preferred_element_type=F32
    )
    hidden, upd, fgt, out, state, entering = pool_forward(seqs, tokens, gates_one, bias_one, keep, init_state[0])
    full_hidden = gather_channels(hidden)
    gates_two = jnp.einsum("td,gdc->gtc", full_hidden, mix, preferred_element_type=F32)
    line, plane = lax.axis_size("seq"), lax.axis_size("dp")
    tiles = 3 * channels // 128
    spreads = plane == 4 and lax.axis_size("mp") == 2 and seqs == 2 and channels % 128 == 0 and width % (line * PART) == 0 and line > 1
    block = -(-tiles // plane) * 128
    lanes = plane * block if spreads else 3 * channels
    pooled_two, grad_two, planes_two, sums_two = pool_top(
        seqs, tokens, lanes, gates_two, bias_two, keep, init_state[1], cotangent.reshape(rows, channels)
    )
    hidden_terms = jnp.einsum(
        "gtc,gdc->td", planes_two, mix, preferred_element_type=F32
    )
    hidden_grad = sum_channels(hidden_terms)
    extended, planes_one, sums_one = pool_backward(seqs, tokens, lanes, hidden_grad, keep, upd, fgt, out, state, entering)
    grad_one = extended[:rows, : 3 * channels]
    input_terms = jnp.einsum(
        "gtc,kgdc->ktd", planes_one, taps, preferred_element_type=F32
    ).reshape(2, seqs, tokens, width)
    late = input_terms[1]
    late = jnp.concatenate([late[:, 1:], shifted(late[:, 0], "seq", -1)[:, None]], 1)
    input_grad = sum_channels((input_terms[0] + late).reshape(rows, width))
    sums = jnp.concatenate([jnp.sum(sums_one, 1), jnp.sum(sums_two, 1)])
    if spreads:
        gathered, sums = spread(
            seqs,
            tokens,
            plane_tokens(hidden),
            plane_tokens(inputs.reshape(rows, channels)),
            to_owners(grad_two, block),
            extended,
            sums,
        )
        weight_two_grad = widen(gathered, False, width, channels, line * PART)[0].transpose(1, 0, 2)
        weight_one_grad = widen(gathered, True, width, channels, line * PART).transpose(0, 2, 1, 3)
    else:
        sums = lax.psum(sums, ("dp", "seq"))
        weight_two_grad = reduce_weights(dot(full_hidden, grad_two, ((0,), (0,)))).reshape(width, 3, channels)
        weight_one_grad = jnp.stack(
            [
                reduce_weights(dot(full, grad_one, ((0,), (0,)))),
                reduce_weights(dot(previous, grad_one, ((0,), (0,)))),
            ]
        ).reshape(2, width, 3, channels)
    return (
        pooled_two.reshape(seqs, tokens, channels),
        input_grad.reshape(seqs, tokens, channels),
        weight_one_grad,
        sums[:3],
        weight_two_grad,
        sums[3:],
    )


def solution(mesh):
    return jax.shard_map(
        local,
        mesh=mesh,
        in_specs=(
            P("dp", "seq", "mp"),
            P("dp", "seq"),
            P(None, "dp", "mp"),
            P(None, None, None, "mp"),
            P(None, "mp"),
            P(None, None, "mp"),
            P(None, "mp"),
            P("dp", "seq", "mp"),
        ),
        out_specs=(
            P("dp", "seq", "mp"),
            P("dp", "seq", "mp"),
            P(None, None, None, "mp"),
            P(None, "mp"),
            P(None, None, "mp"),
            P(None, "mp"),
        ),
        check_vma=False,
    )
```

```python
import functools

import jax
import jax.numpy as jnp
from jax import lax
from jax.experimental import pallas as pl
from jax.experimental.pallas import tpu as pltpu
from jax.sharding import PartitionSpec as P

F32 = jnp.float32
BF16 = jnp.bfloat16
SUB = 8
STEP = 16
EDGE = 16
PART = 64
LAG = 2
TURN = 6
VMEM = pl.BlockSpec(memory_space=pltpu.VMEM)


def sigmoid(x):
    return 0.5 * jnp.tanh(0.5 * x) + 0.5


def lane_blocks(channels):
    width = 384 if channels % 384 == 0 else channels
    return [slice(at, at + width) for at in range(0, channels, width)]


def scan_down(scale, shift):
    row = lax.broadcasted_iota(jnp.int32, scale.shape, 0)
    for step in (1, 2, 4):
        earlier = row >= step
        scale_before = jnp.where(earlier, pltpu.roll(scale, step, 0), 1.0)
        shift_before = jnp.where(earlier, pltpu.roll(shift, step, 0), 0.0)
        shift = scale * shift_before + shift
        scale = scale * scale_before
    return scale, shift


def scan_up(scale, shift):
    row = lax.broadcasted_iota(jnp.int32, scale.shape, 0)
    for step in (1, 2, 4):
        later = row < SUB - step
        scale_after = jnp.where(later, pltpu.roll(scale, SUB - step, 0), 1.0)
        shift_after = jnp.where(later, pltpu.roll(shift, SUB - step, 0), 0.0)
        shift = scale * shift_after + shift
        scale = scale * scale_after
    return scale, shift


def greet(*axes):
    for axis in axes:
        count = lax.axis_size(axis)
        me = lax.axis_index(axis)
        for step in range(1, count):
            pl.semaphore_signal(
                pltpu.get_barrier_semaphore(),
                inc=1,
                device_id={axis: lax.rem(me + step, count)},
                device_id_type=pl.DeviceIdType.MESH,
            )


def met(*axes):
    pl.semaphore_wait(pltpu.get_barrier_semaphore(), sum(lax.axis_size(axis) - 1 for axis in axes))


def remote(src, dst, send, recv, axis, target):
    return pltpu.make_async_remote_copy(
        src_ref=src,
        dst_ref=dst,
        send_sem=send,
        recv_sem=recv,
        device_id={axis: target},
        device_id_type=pl.DeviceIdType.MESH,
    )


def to_all(src, slots, send_sems, recv_sems, axis):
    count = lax.axis_size(axis)
    me = lax.axis_index(axis)
    copies = []
    for step in range(1, count):
        copies.append(
            pltpu.make_async_remote_copy(
                src_ref=src,
                dst_ref=slots.at[step - 1],
                send_sem=send_sems.at[step - 1],
                recv_sem=recv_sems.at[step - 1],
                device_id={axis: lax.rem(me + step, count)},
                device_id_type=pl.DeviceIdType.MESH,
            )
        )
    for copy in copies:
        copy.start()
    return copies


def from_earlier(slots, initial, scale_rows, shift_rows, axis):
    count = lax.axis_size(axis)
    me = lax.axis_index(axis)
    state = initial
    for block in range(count - 1):
        slot = jnp.maximum(me - block - 1, 0)
        after = slots[slot, scale_rows, :] * state + slots[slot, shift_rows, :]
        state = jnp.where(block < me, after, state)
    return state


def from_later(slots, shape, scale_rows, shift_rows, axis):
    count = lax.axis_size(axis)
    me = lax.axis_index(axis)
    message = jnp.zeros(shape, F32)
    for block in range(count - 1, 0, -1):
        slot = jnp.minimum(me + count - block - 1, count - 2)
        after = slots[slot, scale_rows, :] * message + slots[slot, shift_rows, :]
        message = jnp.where(block > me, after, message)
    return message


def first_pass(seqs, tokens, channels, gates, bias, keep, upd, fgt, out, scale, shift, summary):
    def body(at, carried):
        given = list(carried)
        for seq in range(seqs):
            for half in range(STEP // SUB):
                rows = pl.ds(pl.multiple_of(seq * tokens + at * STEP + half * SUB, SUB), SUB)
                kept = keep[rows, :][:, 0:1]
                for number, lanes in enumerate(lane_blocks(channels)):
                    u = jnp.tanh(gates[0, rows, lanes] + bias[0:1, lanes])
                    f = sigmoid(gates[1, rows, lanes] + bias[1:2, lanes])
                    o = sigmoid(gates[2, rows, lanes] + bias[2:3, lanes])
                    upd[rows, lanes] = u
                    fgt[rows, lanes] = f
                    out[rows, lanes] = o
                    a, b = scan_down(f * kept, (1.0 - f) * u)
                    place = (seq * len(lane_blocks(channels)) + number) * 2
                    b = a * given[place + 1] + b
                    a = a * given[place]
                    scale[rows, lanes] = a
                    shift[rows, lanes] = b
                    given[place] = a[SUB - 1 : SUB]
                    given[place + 1] = b[SUB - 1 : SUB]
        return tuple(given)

    begin = []
    for seq in range(seqs):
        for lanes in lane_blocks(channels):
            width = lanes.stop - lanes.start
            begin += [jnp.ones((1, width), F32), jnp.zeros((1, width), F32)]
    end = lax.fori_loop(0, tokens // STEP, body, tuple(begin))
    place = 0
    for seq in range(seqs):
        for lanes in lane_blocks(channels):
            summary[seq : seq + 1, lanes] = end[place]
            summary[seqs + seq : seqs + seq + 1, lanes] = end[place + 1]
            place += 2


def back_pass(seqs, tokens, channels, upstream, keep, fgt, out, scale, shift, summary, row0):
    steps = tokens // STEP

    def body(index, carried):
        at = steps - 1 - index
        given = list(carried)
        for seq in range(seqs):
            whole = pl.ds(pl.multiple_of(seq * tokens + at * STEP, STEP), STEP)
            for number, lanes in enumerate(lane_blocks(channels)):
                ups = upstream[whole, lanes].astype(F32)
                place = (seq * len(lane_blocks(channels)) + number) * 2
                for half in reversed(range(STEP // SUB)):
                    rows = pl.ds(pl.multiple_of(seq * tokens + at * STEP + half * SUB, SUB), SUB)
                    kept = keep[rows, :][:, 0:1]
                    retain = fgt[rows, lanes] * kept
                    direct = ups[half * SUB : half * SUB + SUB] * out[rows, lanes]
                    a, b = scan_up(retain, retain * direct)
                    b = a * given[place + 1] + b
                    a = a * given[place]
                    scale[rows, lanes] = a
                    shift[rows, lanes] = b
                    given[place] = a[0:1]
                    given[place + 1] = b[0:1]
        return tuple(given)

    begin = []
    for seq in range(seqs):
        for lanes in lane_blocks(channels):
            width = lanes.stop - lanes.start
            begin += [jnp.ones((1, width), F32), jnp.zeros((1, width), F32)]
    end = lax.fori_loop(0, steps, body, tuple(begin))
    place = 0
    for seq in range(seqs):
        for lanes in lane_blocks(channels):
            summary[row0 + seq : row0 + seq + 1, lanes] = end[place]
            summary[row0 + seqs + seq : row0 + seqs + seq + 1, lanes] = end[place + 1]
            place += 2


def states_pass(seq, tokens, channels, entering, out, scale, shift, state, pooled):
    def body(at, none):
        rows = pl.ds(pl.multiple_of(seq * tokens + at * STEP, STEP), STEP)
        for lanes in lane_blocks(channels):
            value = scale[rows, lanes] * entering[seq : seq + 1, lanes] + shift[rows, lanes]
            state[rows, lanes] = value
            pooled[rows, lanes] = (out[rows, lanes] * value).astype(BF16)
        return none

    lax.fori_loop(0, tokens // STEP, body, 0)


def grads_pass(seqs, tokens, channels, message, entering, upstream, keep, upd, fgt, out, state, scale, shift, grads, planes, sums):
    steps = tokens // STEP
    sums[...] = jnp.zeros_like(sums)
    if grads.shape[1] > 3 * channels:
        grads[:, 3 * channels :] = jnp.zeros((grads.shape[0], grads.shape[1] - 3 * channels), BF16)
    for seq in range(seqs):
        for lanes in lane_blocks(channels):
            width = lanes.stop - lanes.start

            def body(index, later, seq=seq, lanes=lanes, width=width):
                at = steps - 1 - index
                whole = pl.ds(pl.multiple_of(seq * tokens + at * STEP, STEP), STEP)
                row = lax.broadcasted_iota(jnp.int32, (STEP, width), 0)
                kept = keep[whole, :][:, 0:1]
                ups = upstream[whole, lanes].astype(F32)
                u, f, o = upd[whole, lanes], fgt[whole, lanes], out[whole, lanes]
                states = state[whole, lanes]
                arriving = scale[whole, lanes] * message[seq : seq + 1, lanes] + shift[whole, lanes]
                adjoint = ups * o + jnp.where(row == STEP - 1, later, pltpu.roll(arriving, STEP - 1, 0))
                tile = pl.ds(pl.multiple_of(seq * tokens + jnp.maximum(at * STEP - SUB, 0), SUB), SUB)
                last = state[tile, lanes][SUB - 1 : SUB]
                first = jnp.where(at == 0, entering[seq : seq + 1, lanes], last)
                before = jnp.where(row == 0, first, pltpu.roll(states, 1, 0))
                given = [
                    adjoint * (1.0 - f) * (1.0 - u * u),
                    adjoint * (before * kept - u) * f * (1.0 - f),
                    ups * states * o * (1.0 - o),
                ]
                for gate, value in enumerate(given):
                    value = value.astype(BF16)
                    grads[whole, gate * channels + lanes.start : gate * channels + lanes.stop] = value
                    if planes is not None:
                        planes[gate, whole, lanes] = value
                    value = value.astype(F32)
                    total = value[:SUB]
                    for half in range(1, STEP // SUB):
                        total = total + value[half * SUB : half * SUB + SUB]
                    sums[gate, :, lanes] += total
                return arriving[0:1]

            lax.fori_loop(0, steps, body, message[seq : seq + 1, lanes])


def forward_kernel(seqs, tokens, channels, paired, gates, bias, keep, initial, *refs):
    given, refs = refs[: 7 if paired else 6], refs[7 if paired else 6 :]
    hidden_out, upd_out, fgt_out, out_out, state_out, entering = given[:6]
    hidden, upd, fgt, out, state, scale, shift, summary, slots, send_sems, recv_sems, save_sems, pair_sems = refs
    axes = ("seq", "mp") if paired else ("seq",)
    greet(*axes)
    first_pass(seqs, tokens, channels, gates, bias, keep, upd, fgt, out, scale, shift, summary)
    met(*axes)
    copies = to_all(summary, slots, send_sems, recv_sems, "seq")
    saves = [
        pltpu.make_async_copy(src, dst, save_sems.at[number])
        for number, (src, dst) in enumerate(((upd, upd_out), (fgt, fgt_out), (out, out_out), (state, state_out), (hidden, hidden_out)))
    ]
    for copy in saves[:3]:
        copy.start()
    for copy in copies:
        copy.wait()
    entering[...] = from_earlier(slots, initial[...], slice(0, seqs), slice(seqs, 2 * seqs), "seq")
    sent = []
    for seq in range(seqs):
        states_pass(seq, tokens, channels, entering, out, scale, shift, state, hidden)
        if paired:
            mine = lax.axis_index("mp")
            rows = pl.ds(seq * tokens, tokens)
            place = given[6].at[rows, pl.ds(pl.multiple_of(mine * channels, 128), channels)]
            sent.append(pltpu.make_async_copy(hidden.at[rows], place, pair_sems.at[2, seq]))
            sent.append(remote(hidden.at[rows], place, pair_sems.at[0, seq], pair_sems.at[1, seq], "mp", 1 - mine))
            for copy in sent[-2:]:
                copy.start()
    for copy in saves[3:]:
        copy.start()
    for copy in saves + sent:
        copy.wait()


def top_kernel(seqs, tokens, channels, gates, bias, keep, initial, cotangent, pooled, grads, planes, sums, upd, fgt, out, state, entering, message, scale, shift, back_scale, back_shift, summary, slots, send_sems, recv_sems):
    greet("seq")
    first_pass(seqs, tokens, channels, gates, bias, keep, upd, fgt, out, scale, shift, summary)
    back_pass(seqs, tokens, channels, cotangent, keep, fgt, out, back_scale, back_shift, summary, 2 * seqs)
    met("seq")
    copies = to_all(summary, slots, send_sems, recv_sems, "seq")
    for copy in copies:
        copy.wait()
    entering[...] = from_earlier(slots, initial[...], slice(0, seqs), slice(seqs, 2 * seqs), "seq")
    message[...] = from_later(
        slots, (seqs, channels), slice(2 * seqs, 3 * seqs), slice(3 * seqs, 4 * seqs), "seq"
    )
    for seq in range(seqs):
        states_pass(seq, tokens, channels, entering, out, scale, shift, state, pooled)
    grads_pass(seqs, tokens, channels, message, entering, cotangent, keep, upd, fgt, out, state, back_scale, back_shift, grads, planes, sums)


def pass_edges(seqs, tokens, grads, edges, arrived, edge_sems):
    count = lax.axis_size("seq")
    me = lax.axis_index("seq")
    row = lax.broadcasted_iota(jnp.int32, edges.shape, 0)
    firsts = jnp.zeros(edges.shape, F32)
    for seq in range(seqs):
        tile = grads[seq * tokens : seq * tokens + EDGE, :].astype(F32)
        firsts = jnp.where(row == seq, pltpu.roll(tile, seq, 0) if seq else tile, firsts)
    edges[...] = firsts.astype(BF16)
    copy = pltpu.make_async_remote_copy(
        src_ref=edges,
        dst_ref=arrived,
        send_sem=edge_sems.at[0],
        recv_sem=edge_sems.at[1],
        device_id={"seq": lax.rem(me + count - 1, count)},
        device_id_type=pl.DeviceIdType.MESH,
    )
    rows = slice(seqs * tokens, seqs * tokens + EDGE)

    @pl.when(me > 0)
    def _():
        copy.start()

    @pl.when(me < count - 1)
    def _():
        copy.wait_recv()
        grads[rows, :] = arrived[...]

    @pl.when(me == count - 1)
    def _():
        grads[rows, :] = jnp.zeros(edges.shape, BF16)

    @pl.when(me > 0)
    def _():
        copy.wait_send()


def backward_kernel(seqs, tokens, channels, upstream, keep, upd, fgt, out, state, entering, grads, sums, message, scale, shift, summary, slots, send_sems, recv_sems, edges, arrived, edge_sems):
    greet("seq")
    back_pass(seqs, tokens, channels, upstream, keep, fgt, out, scale, shift, summary, 0)
    met("seq")
    copies = to_all(summary, slots, send_sems, recv_sems, "seq")
    for copy in copies:
        copy.wait()
    message[...] = from_later(slots, (seqs, channels), slice(0, seqs), slice(seqs, 2 * seqs), "seq")
    grads_pass(seqs, tokens, channels, message, entering, upstream, keep, upd, fgt, out, state, scale, shift, grads, None, sums)
    pass_edges(seqs, tokens, grads, edges, arrived, edge_sems)


def neighbours():
    here = lax.axis_index("dp")
    beside = here + 1 - 2 * lax.rem(here, 2)
    return here, beside, lax.rem(here + 2, 4), lax.rem(beside + 2, 4)


def lower_kernel(seqs, tokens, channels, above, above_columns, mix, keep, upd_in, fgt_in, out_in, state_in, entering, grads, sums, swapped, weights, total, coming, upd, fgt, out, state, message, scale, shift, summary, slots, send_sems, recv_sems, edges, arrived, edge_sems, weight_sems, load_sems, pair_sems, swap_sems):
    greet("seq", "dp", "mp")
    mine = lax.axis_index("mp")
    width = swapped.shape[2]

    def load(step):
        side = jnp.where(step < 3, 1 - mine, mine)
        slot = lax.rem(step, 2)
        return pltpu.make_async_copy(
            mix.at[lax.rem(step, 3), pl.ds(pl.multiple_of(side * channels, 128), channels), :],
            weights.at[slot],
            weight_sems.at[slot],
        )

    load(0).start()
    loads = [
        pltpu.make_async_copy(src, dst, load_sems.at[number])
        for number, (src, dst) in enumerate(((upd_in, upd), (fgt_in, fgt), (out_in, out), (state_in, state)))
    ]
    for copy in loads:
        copy.start()
    met("seq", "dp", "mp")
    plane = neighbours()
    swaps = []
    for steps in (3, 1, 2, 0):
        src = above_columns.at[:, pl.ds(pl.multiple_of(plane[steps] * width, 128), width)]
        dst = swapped.at[plane[0]]
        if steps:
            swaps.append(remote(src, dst, swap_sems.at[0, steps], swap_sems.at[1, steps], "dp", plane[steps]))
        else:
            swaps.append(pltpu.make_async_copy(src, dst, swap_sems.at[0, steps]))
        swaps[-1].start()
    give = remote(total.at[0], coming, pair_sems.at[0], pair_sems.at[1], "mp", 1 - mine)

    def body(step, none):
        load(step).wait()

        @pl.when(step < 5)
        def _():
            load(step + 1).start()

        side, gate = step // 3, lax.rem(step, 3)
        rows = above.shape[1] // 2
        for half in range(2):
            place = pl.ds(half * rows, rows)
            term = lax.dot_general(
                above[gate, place, :], weights[lax.rem(step, 2)], (((1,), (1,)), ((), ())), preferred_element_type=F32
            )
            total[side, place, :] = jnp.where(gate == 0, term, total[side, place, :] + term)

        @pl.when(step == 2)
        def _():
            give.start()

        return none

    lax.fori_loop(0, 6, body, 0)
    give.wait_recv()
    total[1] += coming[...]
    for copy in loads:
        copy.wait()
    upstream = total.at[1]
    back_pass(seqs, tokens, channels, upstream, keep, fgt, out, scale, shift, summary, 0)
    copies = to_all(summary, slots, send_sems, recv_sems, "seq")
    for copy in copies:
        copy.wait()
    message[...] = from_later(slots, (seqs, channels), slice(0, seqs), slice(seqs, 2 * seqs), "seq")
    grads_pass(seqs, tokens, channels, message, entering, upstream, keep, upd, fgt, out, state, scale, shift, grads, None, sums)
    pass_edges(seqs, tokens, grads, edges, arrived, edge_sems)
    give.wait_send()
    for steps, copy in zip((3, 1, 2, 0), swaps):
        if steps:
            copy.wait_send()
            place = swapped.at[plane[steps]]
            remote(place, place, swap_sems.at[0, steps], swap_sems.at[1, steps], "dp", plane[steps]).wait_recv()
        else:
            copy.wait()


def exchange_scratch(rows, channels):
    count = lax.axis_size("seq")
    return [
        pltpu.VMEM((rows, channels), F32),
        pltpu.VMEM((count - 1, rows, channels), F32),
        pltpu.SemaphoreType.DMA((count - 1,)),
        pltpu.SemaphoreType.DMA((count - 1,)),
    ]


def params(number):
    return pltpu.CompilerParams(collective_id=number, has_side_effects=True, vmem_limit_bytes=56 * 2**20)


def cost(elements, ops, moved):
    return pl.CostEstimate(flops=elements * ops, bytes_accessed=moved, transcendentals=elements * 3)


def pool_forward(seqs, tokens, paired, gates, bias, keep, initial):
    channels = gates.shape[2]
    rows = seqs * tokens
    whole = jax.ShapeDtypeStruct((rows, channels), F32)
    shapes = [
        jax.ShapeDtypeStruct((rows, channels), BF16),
        whole,
        whole,
        whole,
        whole,
        jax.ShapeDtypeStruct((seqs, channels), F32),
    ]
    hbm = pl.BlockSpec(memory_space=pl.ANY)
    specs = [hbm] * 5 + [VMEM]
    if paired:
        shapes.append(jax.ShapeDtypeStruct((rows, 2 * channels), BF16))
        specs.append(hbm)
    return pl.pallas_call(
        functools.partial(forward_kernel, seqs, tokens, channels, paired),
        out_shape=shapes,
        in_specs=[VMEM] * 4,
        out_specs=specs,
        scratch_shapes=[pltpu.VMEM((rows, channels), BF16)]
        + [pltpu.VMEM((rows, channels), F32)] * 6
        + exchange_scratch(2 * seqs, channels)
        + [pltpu.SemaphoreType.DMA((5,)), pltpu.SemaphoreType.DMA((3, seqs))],
        compiler_params=params(1),
        cost_estimate=cost(rows * channels, 60, rows * channels * 30),
        name="pool_forward",
    )(gates, bias, keep, initial)


def pool_top(seqs, tokens, lanes, gates, bias, keep, initial, cotangent):
    channels = gates.shape[2]
    rows = seqs * tokens
    whole = pltpu.VMEM((rows, channels), F32)
    edge = pltpu.VMEM((seqs, channels), F32)
    return pl.pallas_call(
        functools.partial(top_kernel, seqs, tokens, channels),
        out_shape=(
            jax.ShapeDtypeStruct((rows, channels), BF16),
            jax.ShapeDtypeStruct((rows, lanes), BF16),
            jax.ShapeDtypeStruct((3, rows, channels), BF16),
            jax.ShapeDtypeStruct((3, SUB, channels), F32),
        ),
        in_specs=[VMEM] * 5,
        out_specs=[VMEM] * 4,
        scratch_shapes=[whole] * 4 + [edge] * 2 + [whole] * 4 + exchange_scratch(4 * seqs, channels),
        compiler_params=params(2),
        cost_estimate=cost(rows * channels, 120, rows * channels * 22),
        name="pool_top",
    )(gates, bias, keep, initial, cotangent)


def pool_backward(seqs, tokens, lanes, upstream, keep, upd, fgt, out, state, entering):
    rows, channels = upstream.shape
    whole = pltpu.VMEM((rows, channels), F32)
    return pl.pallas_call(
        functools.partial(backward_kernel, seqs, tokens, channels),
        out_shape=(
            jax.ShapeDtypeStruct((rows + EDGE, lanes), BF16),
            jax.ShapeDtypeStruct((3, SUB, channels), F32),
        ),
        in_specs=[VMEM] * 7,
        out_specs=[VMEM] * 2,
        scratch_shapes=[pltpu.VMEM((seqs, channels), F32)]
        + [whole] * 2
        + exchange_scratch(2 * seqs, channels)
        + [pltpu.VMEM((EDGE, lanes), BF16)] * 2
        + [pltpu.SemaphoreType.DMA((2,))],
        compiler_params=params(3),
        cost_estimate=cost(rows * channels, 60, rows * channels * 26),
        name="pool_backward",
    )(upstream, keep, upd, fgt, out, state, entering)


def pool_lower(seqs, tokens, above, above_columns, mix, keep, upd, fgt, out, state, entering):
    rows, channels = upd.shape
    lanes = above_columns.shape[1]
    whole = pltpu.VMEM((rows, channels), F32)
    hbm = pl.BlockSpec(memory_space=pl.ANY)
    dma = pltpu.SemaphoreType.DMA
    return pl.pallas_call(
        functools.partial(lower_kernel, seqs, tokens, channels),
        out_shape=(
            jax.ShapeDtypeStruct((rows + EDGE, lanes), BF16),
            jax.ShapeDtypeStruct((3, SUB, channels), F32),
            jax.ShapeDtypeStruct((4, rows, lanes // 4), BF16),
        ),
        in_specs=[VMEM, hbm, hbm, VMEM, hbm, hbm, hbm, hbm, VMEM],
        out_specs=[VMEM, VMEM, hbm],
        scratch_shapes=[
            pltpu.VMEM((2, channels, channels), BF16),
            pltpu.VMEM((2, rows, channels), F32),
            whole,
            whole,
            whole,
            whole,
            whole,
            pltpu.VMEM((seqs, channels), F32),
            whole,
            whole,
        ]
        + exchange_scratch(2 * seqs, channels)
        + [pltpu.VMEM((EDGE, lanes), BF16)] * 2
        + [dma((2,)), dma((2,)), dma((4,)), dma((2,)), dma((2, 4))],
        compiler_params=params(5),
        cost_estimate=pl.CostEstimate(
            flops=12 * rows * channels * channels, bytes_accessed=rows * channels * 40, transcendentals=0
        ),
        name="pool_lower",
    )(above, above_columns, mix, keep, upd, fgt, out, state, entering)


def shift_up(seqs, tokens, value, edges, result):
    width = value.shape[1]
    steps = tokens // STEP

    def body(index, none):
        sequence, at = index // steps, lax.rem(index, steps)
        row = lax.broadcasted_iota(jnp.int32, (STEP, width), 0)
        rows = pl.ds(pl.multiple_of(index * STEP, STEP), STEP)
        after = jnp.minimum(index + 1, value.shape[0] // STEP - 1)
        first = value[pl.ds(pl.multiple_of(after * STEP, STEP), STEP), :].astype(F32)[0:1]
        edge = edges[sequence // seqs].astype(F32)
        edge = jnp.where(lax.rem(sequence, seqs) == 0, edge[0:1], edge[1:2])
        moved = pltpu.roll(value[rows, :].astype(F32), STEP - 1, 0)
        moved = jnp.where(row == STEP - 1, jnp.where(at == steps - 1, edge, first), moved)
        result[rows, :] = moved.astype(BF16)
        return none

    lax.fori_loop(0, value.shape[0] // STEP, body, 0)


def spread_kernel(seqs, tokens, parts, turn, hidden, full, grads_two, grads_one, taps, sums, out, input_grad, sums_out, rows_full, grads, grads_edge, moved, own, ups, downs, acc, across, around, every, weights, leaving, coming, load_sems, swap_sems, up_sems, down_sems, line_send, line_recv, column_send, column_recv, kept_sems, plane_send, plane_recv, sums_sems, weight_sems, leaving_sems, coming_sems, result_sems, pair_sems, ready_sem):
    line, plane = lax.axis_size("seq"), lax.axis_size("dp")
    at, here = lax.axis_index("seq"), lax.axis_index("dp")
    unit = line * parts
    units = own.shape[0] // unit
    blocks = units // 3
    width = own.shape[1]
    block_rows = seqs * tokens
    half = unit // 2
    here, beside, below, across_from = neighbours()
    mine = lax.axis_index("mp")
    greet("seq", "dp", "mp")
    met("seq", "dp", "mp")

    def turned(u):
        return lax.rem(u, turn) == turn - 1

    def direct(u):
        return lax.rem(u, turn) != turn - 1

    wide = rows_full.shape[1] // 2

    def own_rows(value, number, way):
        place = rows_full.at[:, pl.ds(pl.multiple_of(mine * wide, 128), wide)]
        if way == 0:
            return pltpu.make_async_copy(value, place, load_sems.at[number])
        return remote(value, place, pair_sems.at[0, number], pair_sems.at[1, number], "mp", 1 - mine)

    def other_rows(number):
        place = rows_full.at[:, pl.ds(pl.multiple_of((1 - mine) * wide, 128), wide)]
        return remote(place, place, pair_sems.at[0, number], pair_sems.at[1, number], "mp", 1 - mine)

    def plane_rows(owner):
        return pl.ds(pl.multiple_of(owner * block_rows, 16), block_rows)

    def peer(steps):
        return (here, beside, below, across_from)[steps]

    def load_two():
        return pltpu.make_async_copy(grads_two, moved, load_sems.at[2])

    def swap(steps, edge, arriving=False):
        columns = pl.ds(pl.multiple_of(peer(steps) * width, 128), width)
        source = peer(steps) if arriving else here
        if edge:
            src, dst = grads_one.at[block_rows : block_rows + EDGE, columns], grads_edge.at[source]
        else:
            src, dst = grads_one.at[0:block_rows, columns], grads.at[plane_rows(source)]
        number = steps * 2 + edge
        if steps == 0:
            return pltpu.make_async_copy(src, dst, swap_sems.at[0, number])
        return remote(src, dst, swap_sems.at[0, number], swap_sems.at[1, number], "dp", peer(steps))

    def product(block, right):
        columns = pl.ds(pl.multiple_of(block * unit, 128), unit)
        return lax.dot_general(
            rows_full[:, columns], right[...], (((0,), (0,)), ((), ())), preferred_element_type=F32
        ).astype(BF16)

    narrow = leaving.shape[2]
    pieces = wide // narrow

    def load_weights(step):
        first = jnp.where(step < pieces, (1 - mine) * pieces + step, mine * pieces + step - pieces) * narrow
        slot = lax.rem(step, 2)
        return pltpu.make_async_copy(
            taps.at[:, :, pl.ds(pl.multiple_of(first, narrow), narrow), :], weights.at[slot], weight_sems.at[slot]
        )

    def load_every():
        return pltpu.make_async_copy(grads_one, every, load_sems.at[3])

    def leave(step):
        slot = lax.rem(step, 2)
        return remote(leaving.at[slot], coming.at[step], leaving_sems.at[slot], coming_sems.at[step], "mp", 1 - mine)

    def result(step):
        return pltpu.make_async_copy(
            coming.at[step],
            input_grad.at[:, pl.ds(pl.multiple_of(step * narrow, narrow), narrow)],
            result_sems.at[step],
        )

    def input_terms(slot):
        channels = taps.shape[3]
        now = jnp.zeros((block_rows, narrow), F32)
        late = jnp.zeros((block_rows + EDGE, narrow), F32)
        for gate in range(3):
            lanes = slice(gate * channels, gate * channels + channels)
            now += lax.dot_general(
                every[:block_rows, lanes], weights[slot, 0, gate], (((1,), (1,)), ((), ())), preferred_element_type=F32
            )
            late += lax.dot_general(
                every[:, lanes], weights[slot, 1, gate], (((1,), (1,)), ((), ())), preferred_element_type=F32
            )
        row = lax.broadcasted_iota(jnp.int32, now.shape, 0)
        after = pltpu.roll(late[:block_rows], block_rows - 1, 0)
        for seq in range(seqs):
            after = jnp.where(
                row == seq * tokens + tokens - 1, late[block_rows + seq : block_rows + seq + 1], after
            )
        return now + after

    def whole(u):
        return pl.ds(pl.multiple_of(u * unit, unit), unit)

    def chunk(u, j):
        return pl.ds(pl.multiple_of(u * unit + j * parts, parts), parts)

    def up(src, u, j):
        number = u * (line - 1) + j - 1
        return remote(src, ups.at[u, j - 1], up_sems.at[0, number], up_sems.at[1, number], "seq", lax.rem(at + 1, line))

    def down(src, u, j):
        number = u * (line - 1) + j
        return remote(
            src, downs.at[u, j], down_sems.at[0, number], down_sems.at[1, number], "seq", lax.rem(at + line - 1, line)
        )

    def along(src, u, j, way, hop):
        return remote(
            src,
            out.at[here, chunk(u, j)],
            line_send.at[(u * 2 + way) * (line - 1) + hop],
            line_recv.at[u * line + j],
            "seq",
            lax.rem(at + (1 if way == 0 else line - 1), line),
        )

    def column(src, steps, u, j, way, hop):
        number = u // turn * 4 + steps
        return remote(
            src,
            out.at[peer(steps), chunk(u, j)],
            column_send.at[(number * 2 + way) * (line - 1) + hop],
            column_recv.at[number * line + j],
            "seq",
            lax.rem(at + (1 if way == 0 else line - 1), line),
        )

    def over_part(src, u, way):
        return remote(
            src,
            out.at[here, chunk(u, at)],
            plane_send.at[u * 4 + way],
            plane_recv.at[u * 4 + way],
            "dp",
            (beside, below)[way],
        )

    def onward_part(owner, u, way):
        place = out.at[owner, pl.ds(pl.multiple_of(u * unit + at * parts + way * (parts // 2), 16), parts // 2)]
        return remote(
            place, place, plane_send.at[u * 4 + 2 + way], plane_recv.at[u * 4 + 2 + way], "dp", (below, beside)[way]
        )

    def keep(u):
        return pltpu.make_async_copy(own.at[chunk(u, at)], out.at[here, chunk(u, at)], kept_sems.at[u])

    def rows(u, first, count):
        return pl.ds(pl.multiple_of(u * unit + first, half), count)

    def over(u, way):
        place = out.at[here, rows(u, 0, unit)]
        return remote(place, place, plane_send.at[u * 4 + way], plane_recv.at[u * 4 + way], "dp", (beside, below)[way])

    def onward(u, way):
        place = out.at[(beside, below)[way], rows(u, way * half, half)]
        return remote(
            place, place, plane_send.at[u * 4 + 2 + way], plane_recv.at[u * 4 + 2 + way], "dp", (below, beside)[way]
        )

    def corner(u, way):
        place = out.at[across_from, rows(u, way * half, half)]
        return remote(place, place, plane_send.at[u * 4 + 2 + way], plane_recv.at[u * 4 + 2 + way], "dp", (below, beside)[way])

    def sums_copy(slots, me, count, axis, number, step):
        return remote(
            slots.at[me],
            slots.at[me],
            sums_sems.at[number, 0, step - 1],
            sums_sems.at[number, 1, step - 1],
            axis,
            lax.rem(me + step, count),
        )

    def sums_arrival(slots, me, count, axis, number, step):
        place = slots.at[lax.rem(me + count - step, count)]
        return remote(place, place, sums_sems.at[number, 0, step - 1], sums_sems.at[number, 1, step - 1], axis, lax.rem(me + step, count))

    for way in range(2):
        own_rows(hidden, 0, way).start()
    load_two().start()
    for steps in range(4):
        for edge in range(2):
            swap(steps, edge).start()
    load_every().start()
    load_weights(0).start()
    across[at] = sums[...]
    for step in range(1, line):
        sums_copy(across, at, line, "seq", 0, step).start()
    load_two().wait()
    own_rows(hidden, 0, 0).wait()
    other_rows(0).wait_recv()

    def stage(index, none):
        @pl.when(index == 1)
        def _():
            for step in range(1, line):
                sums_arrival(across, at, line, "seq", 0, step).wait_recv()
            total = across[0]
            for other in range(1, line):
                total = total + across[other]
            around[here] = total
            for step in range(1, plane):
                sums_copy(around, here, plane, "dp", 1, step).start()

        @pl.when(index == 3)
        def _():
            for step in range(1, plane):
                sums_arrival(around, here, plane, "dp", 1, step).wait_recv()
            total = around[0]
            for other in range(1, plane):
                total = total + around[other]
            sums_out[...] = total

        @pl.when(index < blocks)
        def _():
            own[whole(index), :] = product(index, moved)

        @pl.when(index == blocks - 1)
        def _():
            own_rows(hidden, 0, 1).wait_send()
            own_rows(full, 1, 0).start()
            pl.semaphore_signal(ready_sem, inc=1, device_id={"mp": 1 - mine}, device_id_type=pl.DeviceIdType.MESH)
            pl.semaphore_wait(ready_sem, 1)
            own_rows(full, 1, 1).start()

        @pl.when(index == blocks)
        def _():
            for steps in range(4):
                for edge in range(2):
                    if steps:
                        swap(steps, edge, True).wait_recv()
                    else:
                        swap(steps, edge).wait()
            shift_up(seqs, tokens, grads, grads_edge, moved)
            own_rows(full, 1, 0).wait()
            other_rows(1).wait_recv()
            load_every().wait()

        @pl.when((index >= blocks) & (index < units) & (lax.rem(index - blocks, 2) == 0))
        def _():
            own[whole(index), :] = product((index - blocks) // 2, grads)

        @pl.when((index >= blocks) & (index < units) & (lax.rem(index - blocks, 2) == 1))
        def _():
            own[whole(index), :] = product((index - blocks) // 2, moved)

        k = index - blocks

        @pl.when((k >= 0) & (k < 2 * pieces))
        def _():
            load_weights(k).wait()

            @pl.when(k + 1 < 2 * pieces)
            def _():
                load_weights(k + 1).start()

            terms = input_terms(lax.rem(k, 2))

            @pl.when(k < pieces)
            def _():
                @pl.when(k >= 2)
                def _():
                    leave(k - 2).wait_send()

                leaving[lax.rem(k, 2)] = terms
                leave(k).start()

            @pl.when(k >= pieces)
            def _():
                leave(k - pieces).wait_recv()
                coming[k - pieces] += terms
                result(k - pieces).start()

        u = index - at

        @pl.when((u >= 0) & (u < units))
        def _():
            for j in range(1, line):

                @pl.when(at == 0)
                def _(j=j):
                    up(own.at[chunk(u, j)], u, j).start()

                @pl.when((at > 0) & (at <= j))
                def _(j=j):
                    up(ups.at[u, j - 1], u, j).wait_recv()

                @pl.when((at > 0) & (at < j))
                def _(j=j):
                    ups[u, j - 1] = (ups[u, j - 1].astype(F32) + own[chunk(u, j)].astype(F32)).astype(BF16)
                    up(ups.at[u, j - 1], u, j).start()

        v = index - (line - 1 - at)

        @pl.when((v >= 0) & (v < units))
        def _():
            for j in range(line - 1):

                @pl.when(at == line - 1)
                def _(j=j):
                    down(own.at[chunk(v, j)], v, j).start()

                @pl.when((at < line - 1) & (at >= j))
                def _(j=j):
                    down(downs.at[v, j], v, j).wait_recv()

                @pl.when((at < line - 1) & (at > j))
                def _(j=j):
                    downs[v, j] = (downs[v, j].astype(F32) + own[chunk(v, j)].astype(F32)).astype(BF16)
                    down(downs.at[v, j], v, j).start()

        w = index - (line - 1)

        @pl.when((w >= 0) & (w < units))
        def _():
            acc[...] = own[chunk(w, at)].astype(F32)

            @pl.when(at > 0)
            def _():
                acc[...] += ups[w, at - 1].astype(F32)

            @pl.when(at < line - 1)
            def _():
                acc[...] += downs[w, at].astype(F32)

            own[chunk(w, at)] = acc[...].astype(BF16)
            keep(w).start()

            @pl.when(direct(w) & (at < line - 1))
            def _():
                along(own.at[chunk(w, at)], w, at, 0, 0).start()

            @pl.when(direct(w) & (at > 0))
            def _():
                along(own.at[chunk(w, at)], w, at, 1, 0).start()

            @pl.when(turned(w))
            def _():
                for way in range(2):
                    over_part(own.at[chunk(w, at)], w, way).start()

        c = index - line

        @pl.when((c >= 0) & (c < units) & turned(c))
        def _():
            keep(c).wait()
            for way in range(2):
                over_part(out.at[(beside, below)[way], chunk(c, at)], c, way).wait_recv()
                onward_part((beside, below)[way], c, way).start()

        d = index - line - 1

        @pl.when((d >= 0) & (d < units) & turned(d))
        def _():
            for way in range(2):
                onward_part(across_from, d, way).wait_recv()

        for steps in range(4):
            for hop in range(line):
                e = index - line - 1 - steps - hop

                @pl.when((e >= 0) & (e < units) & turned(e))
                def _(e=e, steps=steps, hop=hop):
                    @pl.when(at >= hop)
                    def _():
                        src = out.at[peer(steps), chunk(e, at - hop)]
                        if hop:
                            column(src, steps, e, at - hop, 0, 0).wait_recv()
                        if hop < line - 1:

                            @pl.when(at < line - 1)
                            def _():
                                column(src, steps, e, at - hop, 0, hop).start()

                    @pl.when(at + hop < line)
                    def _():
                        src = out.at[peer(steps), chunk(e, at + hop)]
                        if hop:
                            column(src, steps, e, at + hop, 1, 0).wait_recv()
                        if hop < line - 1:

                            @pl.when(at > 0)
                            def _():
                                column(src, steps, e, at + hop, 1, hop).start()

        for hop in range(1, line):
            x = index - (line - 1) - hop

            @pl.when((x >= 0) & (x < units) & direct(x))
            def _(x=x, hop=hop):
                @pl.when(at >= hop)
                def _():
                    src = out.at[here, chunk(x, at - hop)]
                    along(src, x, at - hop, 0, 0).wait_recv()
                    if hop < line - 1:

                        @pl.when(at < line - 1)
                        def _():
                            along(src, x, at - hop, 0, hop).start()

                @pl.when(at + hop < line)
                def _():
                    src = out.at[here, chunk(x, at + hop)]
                    along(src, x, at + hop, 1, 0).wait_recv()
                    if hop < line - 1:

                        @pl.when(at > 0)
                        def _():
                            along(src, x, at + hop, 1, hop).start()

        y = index - 2 * (line - 1)

        @pl.when((y >= 0) & (y < units) & direct(y))
        def _():
            keep(y).wait()
            over(y, 0).start()
            over(y, 1).start()

        z = y - LAG

        @pl.when((z >= 0) & (z < units) & direct(z))
        def _():
            for way in range(2):
                place = out.at[(beside, below)[way], rows(z, 0, unit)]
                remote(place, place, plane_send.at[z * 4 + way], plane_recv.at[z * 4 + way], "dp", (beside, below)[way]).wait_recv()
                onward(z, way).start()

        t = z - LAG

        @pl.when((t >= 0) & (t < units) & direct(t))
        def _():
            for way in range(2):
                corner(t, way).wait_recv()

        return none

    last_turned = units // turn * turn - 1
    lax.fori_loop(0, max(units + 2 * (line - 1) + 2 * LAG, last_turned + 2 * line + 4), stage, 0)

    def settle(u, none):
        for j in range(1, line):

            @pl.when(at < j)
            def _(j=j):
                up(ups.at[u, j - 1], u, j).wait_send()

        for j in range(line - 1):

            @pl.when(at > j)
            def _(j=j):
                down(downs.at[u, j], u, j).wait_send()

        for hop in range(line - 1):

            @pl.when(direct(u) & (at >= hop) & (at < line - 1))
            def _(hop=hop):
                along(out.at[here, chunk(u, at - hop)], u, at - hop, 0, hop).wait_send()

            @pl.when(direct(u) & (at + hop < line) & (at > 0))
            def _(hop=hop):
                along(out.at[here, chunk(u, at + hop)], u, at + hop, 1, hop).wait_send()

            @pl.when(turned(u) & (at >= hop) & (at < line - 1))
            def _(hop=hop):
                for steps in range(4):
                    column(out.at[here, chunk(u, at - hop)], steps, u, at - hop, 0, hop).wait_send()

            @pl.when(turned(u) & (at + hop < line) & (at > 0))
            def _(hop=hop):
                for steps in range(4):
                    column(out.at[here, chunk(u, at + hop)], steps, u, at + hop, 1, hop).wait_send()

        @pl.when(direct(u))
        def _():
            for way in range(2):
                over(u, way).wait_send()
                onward(u, way).wait_send()

        @pl.when(turned(u))
        def _():
            for way in range(2):
                over_part(out.at[here, chunk(u, at)], u, way).wait_send()
                onward_part(here, u, way).wait_send()

        return none

    lax.fori_loop(0, units, settle, 0)
    for steps in range(1, 4):
        for edge in range(2):
            swap(steps, edge).wait_send()
    own_rows(full, 1, 1).wait_send()
    for step in range(pieces - 2, pieces):
        leave(step).wait_send()
    for step in range(pieces):
        result(step).wait()
    for step in range(1, line):
        sums_copy(across, at, line, "seq", 0, step).wait_send()
    for step in range(1, plane):
        sums_copy(around, here, plane, "dp", 1, step).wait_send()


def spread(seqs, tokens, hidden, full, grads_two, grads_one, taps, sums):
    line, plane = lax.axis_size("seq"), lax.axis_size("dp")
    width = grads_two.shape[1]
    rows = grads_two.shape[0] // plane
    depth = 2 * full.shape[1]
    units = 3 * depth // (line * PART)
    channels = taps.shape[3]
    narrow = depth // (units - units // 3)
    pieces = channels // narrow
    turns = units // TURN
    dma = pltpu.SemaphoreType.DMA
    hbm = pl.BlockSpec(memory_space=pl.ANY)
    return pl.pallas_call(
        functools.partial(spread_kernel, seqs, tokens, PART, TURN),
        out_shape=(
            jax.ShapeDtypeStruct((plane, 3 * depth, width), BF16),
            jax.ShapeDtypeStruct((rows, channels), F32),
            jax.ShapeDtypeStruct(sums.shape, F32),
        ),
        in_specs=[hbm] * 5 + [VMEM],
        out_specs=[hbm, hbm, VMEM],
        scratch_shapes=[
            pltpu.VMEM((plane * rows, depth), BF16),
            pltpu.VMEM((plane * rows, width), BF16),
            pltpu.VMEM((plane, EDGE, width), BF16),
            pltpu.VMEM((plane * rows, width), BF16),
            pltpu.VMEM((3 * depth, width), BF16),
            pltpu.VMEM((units, line - 1, PART, width), BF16),
            pltpu.VMEM((units, line - 1, PART, width), BF16),
            pltpu.VMEM((PART, width), F32),
            pltpu.VMEM((line,) + sums.shape, F32),
            pltpu.VMEM((plane,) + sums.shape, F32),
            pltpu.VMEM(grads_one.shape, BF16),
            pltpu.VMEM((2, 2, 3, narrow, channels), BF16),
            pltpu.VMEM((2, rows, narrow), F32),
            pltpu.VMEM((pieces, rows, narrow), F32),
            dma((4,)),
            dma((2, 8)),
            dma((2, units * (line - 1))),
            dma((2, units * (line - 1))),
            dma((units * 2 * (line - 1),)),
            dma((units * line,)),
            dma((turns * 4 * 2 * (line - 1),)),
            dma((turns * 4 * line,)),
            dma((units,)),
            dma((units * 4,)),
            dma((units * 4,)),
            dma((2, 2, max(line, plane) - 1)),
            dma((2,)),
            dma((2,)),
            dma((pieces,)),
            dma((pieces,)),
            dma((2, 2)),
            pltpu.SemaphoreType.REGULAR,
        ],
        compiler_params=pltpu.CompilerParams(
            collective_id=4, has_side_effects=True, vmem_limit_bytes=62 * 2**20
        ),
        cost_estimate=pl.CostEstimate(
            flops=6 * plane * rows * depth * width, bytes_accessed=depth * width * 48, transcendentals=0
        ),
        name="spread",
    )(hidden, full, grads_two, grads_one, taps, sums)


def widen_kernel(tiles, blocks, given, out):
    per = given.shape[2] // 128
    for tile in range(tiles * blocks):
        source, place = divmod(tile, per)
        gate, column = divmod(tile, blocks)
        out[0, gate, :, column * 128 : column * 128 + 128] = given[
            source, :, place * 128 : place * 128 + 128
        ].astype(F32)


def widen(gathered, layer_one, depth, channels, unit):
    plane, _, width = gathered.shape
    rows = unit
    steps, per = depth // rows, unit // rows
    taps = 2 if layer_one else 1

    def place(tap, step):
        if not layer_one:
            return (0, step, 0)
        return (0, steps + (step // per * 2 + tap) * per + lax.rem(step, per), 0)

    return pl.pallas_call(
        functools.partial(widen_kernel, 3, channels // 128),
        grid=(taps, steps),
        out_shape=jax.ShapeDtypeStruct((taps, 3, depth, channels), F32),
        in_specs=[pl.BlockSpec((plane, rows, width), place)],
        out_specs=pl.BlockSpec((1, 3, rows, channels), lambda tap, step: (tap, 0, step, 0)),
        compiler_params=pltpu.CompilerParams(vmem_limit_bytes=32 * 2**20),
        name="widen",
    )(gathered)


def shifted(value, axis, steps):
    count = lax.axis_size(axis)
    initial, last = (max(0, -steps), min(count, count - steps))
    return lax.ppermute(value, axis, [(source, source + steps) for source in range(initial, last)])


def gather_channels(value):
    count = lax.axis_size("mp")
    if count != 2:
        return lax.all_gather(value, "mp", axis=value.ndim - 1, tiled=True)
    other = lax.ppermute(value, "mp", [(0, 1), (1, 0)])
    second = lax.axis_index("mp") == 1
    return jnp.concatenate([jnp.where(second, other, value), jnp.where(second, value, other)], value.ndim - 1)


def sum_channels(terms):
    count = lax.axis_size("mp")
    if count != 2:
        return lax.psum_scatter(terms, "mp", scatter_dimension=1, tiled=True)
    width = terms.shape[1] // 2
    second = lax.axis_index("mp") == 1
    low, high = terms[:, :width], terms[:, width:]
    other = lax.ppermute(jnp.where(second, low, high), "mp", [(0, 1), (1, 0)])
    return jnp.where(second, high, low) + other


def dot(lhs, rhs, dims):
    return lax.dot_general(lhs, rhs, (dims, ((), ())), preferred_element_type=F32)


def reduce_weights(partial):
    shard = lax.psum_scatter(partial.astype(BF16), ("dp", "seq"), scatter_dimension=0, tiled=True)
    return lax.all_gather(shard, ("dp", "seq"), axis=0, tiled=True).astype(F32)


def local(inputs, starts, init_state, weight_one, bias_one, weight_two, bias_two, cotangent):
    seqs, tokens, channels = inputs.shape
    rows = seqs * tokens
    width = weight_one.shape[1]
    keep = jnp.broadcast_to((1 - starts).astype(F32).reshape(rows, 1), (rows, 128))
    taps = weight_one.transpose(0, 2, 1, 3)
    mix = weight_two.transpose(1, 0, 2)

    edge = gather_channels(shifted(inputs[:, -1], "seq", 1))
    full = gather_channels(inputs)
    previous = jnp.concatenate([edge[:, None], full[:, :-1]], 1).reshape(rows, width)
    full = full.reshape(rows, width)
    both = jnp.concatenate([full, previous], 1)
    gates_one = jnp.einsum(
        "tkd,kgdc->gtc", both.reshape(rows, 2, width), taps, preferred_element_type=F32
    )
    line, plane = lax.axis_size("seq"), lax.axis_size("dp")
    tiles = 3 * channels // 128
    spreads = plane == 4 and lax.axis_size("mp") == 2 and seqs == 2 and channels % 128 == 0
    spreads = spreads and width % (line * PART) == 0 and line > 1
    block = -(-tiles // plane) * 128
    lanes = plane * block if spreads else 3 * channels
    hidden, upd, fgt, out, state, entering, *both_cores = pool_forward(
        seqs, tokens, spreads, gates_one, bias_one, keep, init_state[0]
    )
    full_hidden = both_cores[0] if spreads else gather_channels(hidden)
    gates_two = jnp.einsum("td,gdc->gtc", full_hidden, mix, preferred_element_type=F32)
    pooled_two, grad_two, planes_two, sums_two = pool_top(
        seqs, tokens, lanes, gates_two, bias_two, keep, init_state[1], cotangent.reshape(rows, channels)
    )
    if spreads:
        extended, sums_one, swapped = pool_lower(
            seqs, tokens, planes_two, grad_two, mix, keep, upd, fgt, out, state, entering
        )
        sums = jnp.concatenate([jnp.sum(sums_one, 1), jnp.sum(sums_two, 1)])
        gathered, input_grad, sums = spread(
            seqs,
            tokens,
            lax.all_gather(hidden, "dp", axis=0, tiled=True),
            lax.all_gather(inputs.reshape(rows, channels), "dp", axis=0, tiled=True),
            swapped.reshape(plane * rows, block),
            extended,
            taps,
            sums,
        )
        weight_two_grad = widen(gathered, False, width, channels, line * PART)[0].transpose(1, 0, 2)
        weight_one_grad = widen(gathered, True, width, channels, line * PART).transpose(0, 2, 1, 3)
    else:
        hidden_terms = jnp.einsum("gtc,gdc->td", planes_two, mix, preferred_element_type=F32)
        hidden_grad = sum_channels(hidden_terms)
        extended, sums_one = pool_backward(seqs, tokens, lanes, hidden_grad, keep, upd, fgt, out, state, entering)
        grad_one = extended[:rows]
        input_terms = jnp.einsum(
            "tgc,kgdc->ktd", grad_one.reshape(rows, 3, channels), taps, preferred_element_type=F32
        ).reshape(2, seqs, tokens, width)
        late = input_terms[1]
        late = jnp.concatenate([late[:, 1:], shifted(late[:, 0], "seq", -1)[:, None]], 1)
        input_grad = sum_channels((input_terms[0] + late).reshape(rows, width))
        sums = jnp.concatenate([jnp.sum(sums_one, 1), jnp.sum(sums_two, 1)])
        sums = lax.psum(sums, ("dp", "seq"))
        weight_two_grad = reduce_weights(dot(full_hidden, grad_two, ((0,), (0,)))).reshape(width, 3, channels)
        weight_one_grad = jnp.stack(
            [
                reduce_weights(dot(full, grad_one, ((0,), (0,)))),
                reduce_weights(dot(previous, grad_one, ((0,), (0,)))),
            ]
        ).reshape(2, width, 3, channels)
    return (
        pooled_two.reshape(seqs, tokens, channels),
        input_grad.reshape(seqs, tokens, channels),
        weight_one_grad,
        sums[:3],
        weight_two_grad,
        sums[3:],
    )


def solution(mesh):
    return jax.shard_map(
        local,
        mesh=mesh,
        in_specs=(
            P("dp", "seq", "mp"),
            P("dp", "seq"),
            P(None, "dp", "mp"),
            P(None, None, None, "mp"),
            P(None, "mp"),
            P(None, None, "mp"),
            P(None, "mp"),
            P("dp", "seq", "mp"),
        ),
        out_specs=(
            P("dp", "seq", "mp"),
            P("dp", "seq", "mp"),
            P(None, None, None, "mp"),
            P(None, "mp"),
            P(None, None, "mp"),
            P(None, "mp"),
        ),
        check_vma=False,
    )
```

```python
import functools

import jax
import jax.numpy as jnp
from jax import lax
from jax.experimental import pallas as pl
from jax.experimental.pallas import tpu as pltpu
from jax.sharding import PartitionSpec as P

F32 = jnp.float32
BF16 = jnp.bfloat16
SUB = 8
STEP = 16
EDGE = 16
PART = 64
LAG = 2
TURN = 6
TAIL = 2
VMEM = pl.BlockSpec(memory_space=pltpu.VMEM)


def sigmoid(x):
    return 0.5 * jnp.tanh(0.5 * x) + 0.5


def lane_blocks(channels):
    width = 384 if channels % 384 == 0 else channels
    return [slice(at, at + width) for at in range(0, channels, width)]


def scan_down(scale, shift):
    row = lax.broadcasted_iota(jnp.int32, scale.shape, 0)
    for step in (1, 2, 4):
        earlier = row >= step
        scale_before = jnp.where(earlier, pltpu.roll(scale, step, 0), 1.0)
        shift_before = jnp.where(earlier, pltpu.roll(shift, step, 0), 0.0)
        shift = scale * shift_before + shift
        scale = scale * scale_before
    return scale, shift


def scan_up(scale, shift):
    row = lax.broadcasted_iota(jnp.int32, scale.shape, 0)
    for step in (1, 2, 4):
        later = row < SUB - step
        scale_after = jnp.where(later, pltpu.roll(scale, SUB - step, 0), 1.0)
        shift_after = jnp.where(later, pltpu.roll(shift, SUB - step, 0), 0.0)
        shift = scale * shift_after + shift
        scale = scale * scale_after
    return scale, shift


def greet(*axes):
    for axis in axes:
        count = lax.axis_size(axis)
        me = lax.axis_index(axis)
        for step in range(1, count):
            pl.semaphore_signal(
                pltpu.get_barrier_semaphore(),
                inc=1,
                device_id={axis: lax.rem(me + step, count)},
                device_id_type=pl.DeviceIdType.MESH,
            )


def met(*axes):
    pl.semaphore_wait(pltpu.get_barrier_semaphore(), sum(lax.axis_size(axis) - 1 for axis in axes))


def remote(src, dst, send, recv, axis, target):
    return pltpu.make_async_remote_copy(
        src_ref=src,
        dst_ref=dst,
        send_sem=send,
        recv_sem=recv,
        device_id={axis: target},
        device_id_type=pl.DeviceIdType.MESH,
    )


def to_all(src, slots, send_sems, recv_sems, axis):
    count = lax.axis_size(axis)
    me = lax.axis_index(axis)
    copies = []
    for step in range(1, count):
        copies.append(
            pltpu.make_async_remote_copy(
                src_ref=src,
                dst_ref=slots.at[step - 1],
                send_sem=send_sems.at[step - 1],
                recv_sem=recv_sems.at[step - 1],
                device_id={axis: lax.rem(me + step, count)},
                device_id_type=pl.DeviceIdType.MESH,
            )
        )
    for copy in copies:
        copy.start()
    return copies


def from_earlier(slots, initial, scale_rows, shift_rows, axis):
    count = lax.axis_size(axis)
    me = lax.axis_index(axis)
    state = initial
    for block in range(count - 1):
        slot = jnp.maximum(me - block - 1, 0)
        after = slots[slot, scale_rows, :] * state + slots[slot, shift_rows, :]
        state = jnp.where(block < me, after, state)
    return state


def from_later(slots, shape, scale_rows, shift_rows, axis):
    count = lax.axis_size(axis)
    me = lax.axis_index(axis)
    message = jnp.zeros(shape, F32)
    for block in range(count - 1, 0, -1):
        slot = jnp.minimum(me + count - block - 1, count - 2)
        after = slots[slot, scale_rows, :] * message + slots[slot, shift_rows, :]
        message = jnp.where(block > me, after, message)
    return message


def first_pass(seqs, tokens, channels, gates, bias, keep, upd, fgt, out, scale, shift, summary):
    def body(at, carried):
        given = list(carried)
        for seq in range(seqs):
            for half in range(STEP // SUB):
                rows = pl.ds(pl.multiple_of(seq * tokens + at * STEP + half * SUB, SUB), SUB)
                kept = keep[rows, :][:, 0:1]
                for number, lanes in enumerate(lane_blocks(channels)):
                    u = jnp.tanh(gates[0, rows, lanes] + bias[0:1, lanes])
                    f = sigmoid(gates[1, rows, lanes] + bias[1:2, lanes])
                    o = sigmoid(gates[2, rows, lanes] + bias[2:3, lanes])
                    upd[rows, lanes] = u
                    fgt[rows, lanes] = f
                    out[rows, lanes] = o
                    a, b = scan_down(f * kept, (1.0 - f) * u)
                    place = (seq * len(lane_blocks(channels)) + number) * 2
                    b = a * given[place + 1] + b
                    a = a * given[place]
                    scale[rows, lanes] = a
                    shift[rows, lanes] = b
                    given[place] = a[SUB - 1 : SUB]
                    given[place + 1] = b[SUB - 1 : SUB]
        return tuple(given)

    begin = []
    for seq in range(seqs):
        for lanes in lane_blocks(channels):
            width = lanes.stop - lanes.start
            begin += [jnp.ones((1, width), F32), jnp.zeros((1, width), F32)]
    end = lax.fori_loop(0, tokens // STEP, body, tuple(begin))
    place = 0
    for seq in range(seqs):
        for lanes in lane_blocks(channels):
            summary[seq : seq + 1, lanes] = end[place]
            summary[seqs + seq : seqs + seq + 1, lanes] = end[place + 1]
            place += 2


def back_pass(seqs, tokens, channels, upstream, keep, fgt, out, scale, shift, summary, row0):
    steps = tokens // STEP

    def body(index, carried):
        at = steps - 1 - index
        given = list(carried)
        for seq in range(seqs):
            whole = pl.ds(pl.multiple_of(seq * tokens + at * STEP, STEP), STEP)
            for number, lanes in enumerate(lane_blocks(channels)):
                ups = upstream[whole, lanes].astype(F32)
                place = (seq * len(lane_blocks(channels)) + number) * 2
                for half in reversed(range(STEP // SUB)):
                    rows = pl.ds(pl.multiple_of(seq * tokens + at * STEP + half * SUB, SUB), SUB)
                    kept = keep[rows, :][:, 0:1]
                    retain = fgt[rows, lanes] * kept
                    direct = ups[half * SUB : half * SUB + SUB] * out[rows, lanes]
                    a, b = scan_up(retain, retain * direct)
                    b = a * given[place + 1] + b
                    a = a * given[place]
                    scale[rows, lanes] = a
                    shift[rows, lanes] = b
                    given[place] = a[0:1]
                    given[place + 1] = b[0:1]
        return tuple(given)

    begin = []
    for seq in range(seqs):
        for lanes in lane_blocks(channels):
            width = lanes.stop - lanes.start
            begin += [jnp.ones((1, width), F32), jnp.zeros((1, width), F32)]
    end = lax.fori_loop(0, steps, body, tuple(begin))
    place = 0
    for seq in range(seqs):
        for lanes in lane_blocks(channels):
            summary[row0 + seq : row0 + seq + 1, lanes] = end[place]
            summary[row0 + seqs + seq : row0 + seqs + seq + 1, lanes] = end[place + 1]
            place += 2


def states_pass(seq, tokens, channels, entering, out, scale, shift, state, pooled):
    def body(at, none):
        rows = pl.ds(pl.multiple_of(seq * tokens + at * STEP, STEP), STEP)
        for lanes in lane_blocks(channels):
            value = scale[rows, lanes] * entering[seq : seq + 1, lanes] + shift[rows, lanes]
            state[rows, lanes] = value
            pooled[rows, lanes] = (out[rows, lanes] * value).astype(BF16)
        return none

    lax.fori_loop(0, tokens // STEP, body, 0)


def grads_pass(seqs, tokens, channels, message, entering, upstream, keep, upd, fgt, out, state, scale, shift, grads, planes, sums):
    steps = tokens // STEP
    sums[...] = jnp.zeros_like(sums)
    if grads.shape[1] > 3 * channels:
        grads[:, 3 * channels :] = jnp.zeros((grads.shape[0], grads.shape[1] - 3 * channels), BF16)
    for seq in range(seqs):
        for lanes in lane_blocks(channels):
            width = lanes.stop - lanes.start

            def body(index, later, seq=seq, lanes=lanes, width=width):
                at = steps - 1 - index
                whole = pl.ds(pl.multiple_of(seq * tokens + at * STEP, STEP), STEP)
                row = lax.broadcasted_iota(jnp.int32, (STEP, width), 0)
                kept = keep[whole, :][:, 0:1]
                ups = upstream[whole, lanes].astype(F32)
                u, f, o = upd[whole, lanes], fgt[whole, lanes], out[whole, lanes]
                states = state[whole, lanes]
                arriving = scale[whole, lanes] * message[seq : seq + 1, lanes] + shift[whole, lanes]
                adjoint = ups * o + jnp.where(row == STEP - 1, later, pltpu.roll(arriving, STEP - 1, 0))
                tile = pl.ds(pl.multiple_of(seq * tokens + jnp.maximum(at * STEP - SUB, 0), SUB), SUB)
                last = state[tile, lanes][SUB - 1 : SUB]
                first = jnp.where(at == 0, entering[seq : seq + 1, lanes], last)
                before = jnp.where(row == 0, first, pltpu.roll(states, 1, 0))
                given = [
                    adjoint * (1.0 - f) * (1.0 - u * u),
                    adjoint * (before * kept - u) * f * (1.0 - f),
                    ups * states * o * (1.0 - o),
                ]
                for gate, value in enumerate(given):
                    value = value.astype(BF16)
                    grads[whole, gate * channels + lanes.start : gate * channels + lanes.stop] = value
                    if planes is not None:
                        planes[gate, whole, lanes] = value
                    value = value.astype(F32)
                    total = value[:SUB]
                    for half in range(1, STEP // SUB):
                        total = total + value[half * SUB : half * SUB + SUB]
                    sums[gate, :, lanes] += total
                return arriving[0:1]

            lax.fori_loop(0, steps, body, message[seq : seq + 1, lanes])


def forward_kernel(seqs, tokens, channels, paired, gates, bias, keep, initial, *refs):
    given, refs = refs[: 7 if paired else 6], refs[7 if paired else 6 :]
    hidden_out, upd_out, fgt_out, out_out, state_out, entering = given[:6]
    hidden, upd, fgt, out, state, scale, shift, summary, slots, send_sems, recv_sems, save_sems, pair_sems = refs
    axes = ("seq", "mp") if paired else ("seq",)
    greet(*axes)
    first_pass(seqs, tokens, channels, gates, bias, keep, upd, fgt, out, scale, shift, summary)
    met(*axes)
    copies = to_all(summary, slots, send_sems, recv_sems, "seq")
    saves = [
        pltpu.make_async_copy(src, dst, save_sems.at[number])
        for number, (src, dst) in enumerate(((upd, upd_out), (fgt, fgt_out), (out, out_out), (state, state_out), (hidden, hidden_out)))
    ]
    for copy in saves[:3]:
        copy.start()
    for copy in copies:
        copy.wait()
    entering[...] = from_earlier(slots, initial[...], slice(0, seqs), slice(seqs, 2 * seqs), "seq")
    sent = []
    for seq in range(seqs):
        states_pass(seq, tokens, channels, entering, out, scale, shift, state, hidden)
        if paired:
            mine = lax.axis_index("mp")
            rows = pl.ds(seq * tokens, tokens)
            place = given[6].at[rows, pl.ds(pl.multiple_of(mine * channels, 128), channels)]
            sent.append(pltpu.make_async_copy(hidden.at[rows], place, pair_sems.at[2, seq]))
            sent.append(remote(hidden.at[rows], place, pair_sems.at[0, seq], pair_sems.at[1, seq], "mp", 1 - mine))
            for copy in sent[-2:]:
                copy.start()
    for copy in saves[3:]:
        copy.start()
    for copy in saves + sent:
        copy.wait()


def top_kernel(seqs, tokens, channels, gates, bias, keep, initial, cotangent, pooled, grads, planes, sums, upd, fgt, out, state, entering, message, scale, shift, back_scale, back_shift, summary, slots, send_sems, recv_sems):
    greet("seq")
    first_pass(seqs, tokens, channels, gates, bias, keep, upd, fgt, out, scale, shift, summary)
    back_pass(seqs, tokens, channels, cotangent, keep, fgt, out, back_scale, back_shift, summary, 2 * seqs)
    met("seq")
    copies = to_all(summary, slots, send_sems, recv_sems, "seq")
    for copy in copies:
        copy.wait()
    entering[...] = from_earlier(slots, initial[...], slice(0, seqs), slice(seqs, 2 * seqs), "seq")
    message[...] = from_later(
        slots, (seqs, channels), slice(2 * seqs, 3 * seqs), slice(3 * seqs, 4 * seqs), "seq"
    )
    for seq in range(seqs):
        states_pass(seq, tokens, channels, entering, out, scale, shift, state, pooled)
    grads_pass(seqs, tokens, channels, message, entering, cotangent, keep, upd, fgt, out, state, back_scale, back_shift, grads, planes, sums)


def pass_edges(seqs, tokens, grads, edges, arrived, edge_sems):
    count = lax.axis_size("seq")
    me = lax.axis_index("seq")
    row = lax.broadcasted_iota(jnp.int32, edges.shape, 0)
    firsts = jnp.zeros(edges.shape, F32)
    for seq in range(seqs):
        tile = grads[seq * tokens : seq * tokens + EDGE, :].astype(F32)
        firsts = jnp.where(row == seq, pltpu.roll(tile, seq, 0) if seq else tile, firsts)
    edges[...] = firsts.astype(BF16)
    copy = pltpu.make_async_remote_copy(
        src_ref=edges,
        dst_ref=arrived,
        send_sem=edge_sems.at[0],
        recv_sem=edge_sems.at[1],
        device_id={"seq": lax.rem(me + count - 1, count)},
        device_id_type=pl.DeviceIdType.MESH,
    )
    rows = slice(seqs * tokens, seqs * tokens + EDGE)

    @pl.when(me > 0)
    def _():
        copy.start()

    @pl.when(me < count - 1)
    def _():
        copy.wait_recv()
        grads[rows, :] = arrived[...]

    @pl.when(me == count - 1)
    def _():
        grads[rows, :] = jnp.zeros(edges.shape, BF16)

    @pl.when(me > 0)
    def _():
        copy.wait_send()


def backward_kernel(seqs, tokens, channels, upstream, keep, upd, fgt, out, state, entering, grads, sums, message, scale, shift, summary, slots, send_sems, recv_sems, edges, arrived, edge_sems):
    greet("seq")
    back_pass(seqs, tokens, channels, upstream, keep, fgt, out, scale, shift, summary, 0)
    met("seq")
    copies = to_all(summary, slots, send_sems, recv_sems, "seq")
    for copy in copies:
        copy.wait()
    message[...] = from_later(slots, (seqs, channels), slice(0, seqs), slice(seqs, 2 * seqs), "seq")
    grads_pass(seqs, tokens, channels, message, entering, upstream, keep, upd, fgt, out, state, scale, shift, grads, None, sums)
    pass_edges(seqs, tokens, grads, edges, arrived, edge_sems)


def neighbours():
    here = lax.axis_index("dp")
    beside = here + 1 - 2 * lax.rem(here, 2)
    return here, beside, lax.rem(here + 2, 4), lax.rem(beside + 2, 4)


def upper_kernel(seqs, tokens, channels, full_hidden, hidden, mix, bias, keep, initial, cotangent, pooled, grads, planes, sums, every, weights, gates, state, entering, message, scale, shift, back_scale, back_shift, summary, slots, send_sems, recv_sems, weight_sems, plane_sems, kept_sem):
    greet("seq", "dp")
    here, beside, below, corner = neighbours()
    rows = seqs * tokens
    half = rows // 2

    def load(step):
        slot = lax.rem(step, 2)
        return pltpu.make_async_copy(
            mix.at[step // 2, pl.ds(pl.multiple_of(lax.rem(step, 2) * channels, 128), channels), :],
            weights.at[slot],
            weight_sems.at[slot],
        )

    def over(src, owner, way):
        place = every.at[owner]
        return remote(src, place, plane_sems.at[0, way], plane_sems.at[1, way], "dp", (beside, below)[way])

    def onward(owner, way):
        place = every.at[owner, pl.ds(way * half, half)]
        return remote(place, place, plane_sems.at[0, 2 + way], plane_sems.at[1, 2 + way], "dp", (below, beside)[way])

    load(0).start()
    kept = pltpu.make_async_copy(hidden, every.at[here], kept_sem)
    kept.start()
    met("seq", "dp")
    for way in range(2):
        over(hidden, here, way).start()

    def body(step, none):
        load(step).wait()

        @pl.when(step < 5)
        def _():
            load(step + 1).start()

        gate, part = step // 2, lax.rem(step, 2)
        columns = pl.ds(pl.multiple_of(part * channels, 128), channels)
        for side in range(2):
            place = pl.ds(side * half, half)
            term = jnp.dot(full_hidden[place, columns], weights[part], preferred_element_type=F32)
            gates[gate, place, :] = jnp.where(part == 0, term, gates[gate, place, :] + term)
        return none

    lax.fori_loop(0, 6, body, 0)
    upd, fgt, out = gates.at[0], gates.at[1], gates.at[2]
    first_pass(seqs, tokens, channels, gates, bias, keep, upd, fgt, out, scale, shift, summary)
    back_pass(seqs, tokens, channels, cotangent, keep, fgt, out, back_scale, back_shift, summary, 2 * seqs)
    copies = to_all(summary, slots, send_sems, recv_sems, "seq")
    for way in range(2):
        owner = (beside, below)[way]
        over(every.at[owner], owner, way).wait_recv()
        onward(owner, way).start()
    for copy in copies:
        copy.wait()
    entering[...] = from_earlier(slots, initial[...], slice(0, seqs), slice(seqs, 2 * seqs), "seq")
    message[...] = from_later(
        slots, (seqs, channels), slice(2 * seqs, 3 * seqs), slice(3 * seqs, 4 * seqs), "seq"
    )
    for seq in range(seqs):
        states_pass(seq, tokens, channels, entering, out, scale, shift, state, pooled)
    grads_pass(seqs, tokens, channels, message, entering, cotangent, keep, upd, fgt, out, state, back_scale, back_shift, grads, planes, sums)
    for way in range(2):
        over(hidden, here, way).wait_send()
        onward((beside, below)[way], way).wait_send()
        onward(corner, way).wait_recv()
    kept.wait()


def lower_kernel(seqs, tokens, channels, above, above_columns, mix, keep, upd_in, fgt_in, out_in, state_in, entering, grads, sums, swapped, weights, total, coming, upd, fgt, out, state, message, scale, shift, summary, slots, send_sems, recv_sems, edges, arrived, edge_sems, weight_sems, load_sems, pair_sems, swap_sems):
    greet("seq", "dp", "mp")
    mine = lax.axis_index("mp")
    width = swapped.shape[2]

    def load(step):
        side = jnp.where(step < 3, 1 - mine, mine)
        slot = lax.rem(step, 2)
        return pltpu.make_async_copy(
            mix.at[lax.rem(step, 3), pl.ds(pl.multiple_of(side * channels, 128), channels), :],
            weights.at[slot],
            weight_sems.at[slot],
        )

    load(0).start()
    loads = [
        pltpu.make_async_copy(src, dst, load_sems.at[number])
        for number, (src, dst) in enumerate(((upd_in, upd), (fgt_in, fgt), (out_in, out), (state_in, state)))
    ]
    for copy in loads:
        copy.start()
    met("seq", "dp", "mp")
    plane = neighbours()
    swaps = []
    for steps in (3, 1, 2, 0):
        src = above_columns.at[:, pl.ds(pl.multiple_of(plane[steps] * width, 128), width)]
        dst = swapped.at[plane[0]]
        if steps:
            swaps.append(remote(src, dst, swap_sems.at[0, steps], swap_sems.at[1, steps], "dp", plane[steps]))
        else:
            swaps.append(pltpu.make_async_copy(src, dst, swap_sems.at[0, steps]))
        swaps[-1].start()
    give = remote(total.at[0], coming, pair_sems.at[0], pair_sems.at[1], "mp", 1 - mine)

    def body(step, none):
        load(step).wait()

        @pl.when(step < 5)
        def _():
            load(step + 1).start()

        side, gate = step // 3, lax.rem(step, 3)
        rows = above.shape[1] // 2
        for half in range(2):
            place = pl.ds(half * rows, rows)
            term = lax.dot_general(
                above[gate, place, :], weights[lax.rem(step, 2)], (((1,), (1,)), ((), ())), preferred_element_type=F32
            )
            total[side, place, :] = jnp.where(gate == 0, term, total[side, place, :] + term)

        @pl.when(step == 2)
        def _():
            give.start()

        return none

    lax.fori_loop(0, 6, body, 0)
    give.wait_recv()
    total[1] += coming[...]
    for copy in loads:
        copy.wait()
    upstream = total.at[1]
    back_pass(seqs, tokens, channels, upstream, keep, fgt, out, scale, shift, summary, 0)
    copies = to_all(summary, slots, send_sems, recv_sems, "seq")
    for copy in copies:
        copy.wait()
    message[...] = from_later(slots, (seqs, channels), slice(0, seqs), slice(seqs, 2 * seqs), "seq")
    grads_pass(seqs, tokens, channels, message, entering, upstream, keep, upd, fgt, out, state, scale, shift, grads, None, sums)
    pass_edges(seqs, tokens, grads, edges, arrived, edge_sems)
    give.wait_send()
    for steps, copy in zip((3, 1, 2, 0), swaps):
        if steps:
            copy.wait_send()
            place = swapped.at[plane[steps]]
            remote(place, place, swap_sems.at[0, steps], swap_sems.at[1, steps], "dp", plane[steps]).wait_recv()
        else:
            copy.wait()


def exchange_scratch(rows, channels):
    count = lax.axis_size("seq")
    return [
        pltpu.VMEM((rows, channels), F32),
        pltpu.VMEM((count - 1, rows, channels), F32),
        pltpu.SemaphoreType.DMA((count - 1,)),
        pltpu.SemaphoreType.DMA((count - 1,)),
    ]


def params(number):
    return pltpu.CompilerParams(collective_id=number, has_side_effects=True, vmem_limit_bytes=56 * 2**20)


def cost(elements, ops, moved):
    return pl.CostEstimate(flops=elements * ops, bytes_accessed=moved, transcendentals=elements * 3)


def pool_forward(seqs, tokens, paired, gates, bias, keep, initial):
    channels = gates.shape[2]
    rows = seqs * tokens
    whole = jax.ShapeDtypeStruct((rows, channels), F32)
    shapes = [
        jax.ShapeDtypeStruct((rows, channels), BF16),
        whole,
        whole,
        whole,
        whole,
        jax.ShapeDtypeStruct((seqs, channels), F32),
    ]
    hbm = pl.BlockSpec(memory_space=pl.ANY)
    specs = [hbm] * 5 + [VMEM]
    if paired:
        shapes.append(jax.ShapeDtypeStruct((rows, 2 * channels), BF16))
        specs.append(hbm)
    return pl.pallas_call(
        functools.partial(forward_kernel, seqs, tokens, channels, paired),
        out_shape=shapes,
        in_specs=[VMEM] * 4,
        out_specs=specs,
        scratch_shapes=[pltpu.VMEM((rows, channels), BF16)]
        + [pltpu.VMEM((rows, channels), F32)] * 6
        + exchange_scratch(2 * seqs, channels)
        + [pltpu.SemaphoreType.DMA((5,)), pltpu.SemaphoreType.DMA((3, seqs))],
        compiler_params=params(1),
        cost_estimate=cost(rows * channels, 60, rows * channels * 30),
        name="pool_forward",
    )(gates, bias, keep, initial)


def pool_top(seqs, tokens, lanes, gates, bias, keep, initial, cotangent):
    channels = gates.shape[2]
    rows = seqs * tokens
    whole = pltpu.VMEM((rows, channels), F32)
    edge = pltpu.VMEM((seqs, channels), F32)
    return pl.pallas_call(
        functools.partial(top_kernel, seqs, tokens, channels),
        out_shape=(
            jax.ShapeDtypeStruct((rows, channels), BF16),
            jax.ShapeDtypeStruct((rows, lanes), BF16),
            jax.ShapeDtypeStruct((3, rows, channels), BF16),
            jax.ShapeDtypeStruct((3, SUB, channels), F32),
        ),
        in_specs=[VMEM] * 5,
        out_specs=[VMEM] * 4,
        scratch_shapes=[whole] * 4 + [edge] * 2 + [whole] * 4 + exchange_scratch(4 * seqs, channels),
        compiler_params=params(2),
        cost_estimate=cost(rows * channels, 120, rows * channels * 22),
        name="pool_top",
    )(gates, bias, keep, initial, cotangent)


def pool_upper(seqs, tokens, lanes, full_hidden, hidden, mix, bias, keep, initial, cotangent):
    rows, channels = hidden.shape
    whole = pltpu.VMEM((rows, channels), F32)
    edge = pltpu.VMEM((seqs, channels), F32)
    hbm = pl.BlockSpec(memory_space=pl.ANY)
    dma = pltpu.SemaphoreType.DMA
    return pl.pallas_call(
        functools.partial(upper_kernel, seqs, tokens, channels),
        out_shape=(
            jax.ShapeDtypeStruct((rows, channels), BF16),
            jax.ShapeDtypeStruct((rows, lanes), BF16),
            jax.ShapeDtypeStruct((3, rows, channels), BF16),
            jax.ShapeDtypeStruct((3, SUB, channels), F32),
            jax.ShapeDtypeStruct((4, rows, channels), BF16),
        ),
        in_specs=[VMEM, hbm, hbm, VMEM, VMEM, VMEM, VMEM],
        out_specs=[VMEM] * 4 + [hbm],
        scratch_shapes=[pltpu.VMEM((2, channels, channels), BF16), pltpu.VMEM((3, rows, channels), F32), whole, edge, edge]
        + [whole] * 4
        + exchange_scratch(4 * seqs, channels)
        + [dma((2,)), dma((2, 4)), dma],
        compiler_params=params(6),
        cost_estimate=pl.CostEstimate(
            flops=12 * rows * channels * channels, bytes_accessed=rows * channels * 40, transcendentals=0
        ),
        name="pool_upper",
    )(full_hidden, hidden, mix, bias, keep, initial, cotangent)


def pool_backward(seqs, tokens, lanes, upstream, keep, upd, fgt, out, state, entering):
    rows, channels = upstream.shape
    whole = pltpu.VMEM((rows, channels), F32)
    return pl.pallas_call(
        functools.partial(backward_kernel, seqs, tokens, channels),
        out_shape=(
            jax.ShapeDtypeStruct((rows + EDGE, lanes), BF16),
            jax.ShapeDtypeStruct((3, SUB, channels), F32),
        ),
        in_specs=[VMEM] * 7,
        out_specs=[VMEM] * 2,
        scratch_shapes=[pltpu.VMEM((seqs, channels), F32)]
        + [whole] * 2
        + exchange_scratch(2 * seqs, channels)
        + [pltpu.VMEM((EDGE, lanes), BF16)] * 2
        + [pltpu.SemaphoreType.DMA((2,))],
        compiler_params=params(3),
        cost_estimate=cost(rows * channels, 60, rows * channels * 26),
        name="pool_backward",
    )(upstream, keep, upd, fgt, out, state, entering)


def pool_lower(seqs, tokens, above, above_columns, mix, keep, upd, fgt, out, state, entering):
    rows, channels = upd.shape
    lanes = above_columns.shape[1]
    whole = pltpu.VMEM((rows, channels), F32)
    hbm = pl.BlockSpec(memory_space=pl.ANY)
    dma = pltpu.SemaphoreType.DMA
    return pl.pallas_call(
        functools.partial(lower_kernel, seqs, tokens, channels),
        out_shape=(
            jax.ShapeDtypeStruct((rows + EDGE, lanes), BF16),
            jax.ShapeDtypeStruct((3, SUB, channels), F32),
            jax.ShapeDtypeStruct((4, rows, lanes // 4), BF16),
        ),
        in_specs=[VMEM, hbm, hbm, VMEM, hbm, hbm, hbm, hbm, VMEM],
        out_specs=[VMEM, VMEM, hbm],
        scratch_shapes=[
            pltpu.VMEM((2, channels, channels), BF16),
            pltpu.VMEM((2, rows, channels), F32),
            whole,
            whole,
            whole,
            whole,
            whole,
            pltpu.VMEM((seqs, channels), F32),
            whole,
            whole,
        ]
        + exchange_scratch(2 * seqs, channels)
        + [pltpu.VMEM((EDGE, lanes), BF16)] * 2
        + [dma((2,)), dma((2,)), dma((4,)), dma((2,)), dma((2, 4))],
        compiler_params=params(5),
        cost_estimate=pl.CostEstimate(
            flops=12 * rows * channels * channels, bytes_accessed=rows * channels * 40, transcendentals=0
        ),
        name="pool_lower",
    )(above, above_columns, mix, keep, upd, fgt, out, state, entering)


def shift_up(seqs, tokens, value, edges, result):
    width = value.shape[1]
    steps = tokens // STEP

    def body(index, none):
        sequence, at = index // steps, lax.rem(index, steps)
        row = lax.broadcasted_iota(jnp.int32, (STEP, width), 0)
        rows = pl.ds(pl.multiple_of(index * STEP, STEP), STEP)
        after = jnp.minimum(index + 1, value.shape[0] // STEP - 1)
        first = value[pl.ds(pl.multiple_of(after * STEP, STEP), STEP), :].astype(F32)[0:1]
        edge = edges[sequence // seqs].astype(F32)
        edge = jnp.where(lax.rem(sequence, seqs) == 0, edge[0:1], edge[1:2])
        moved = pltpu.roll(value[rows, :].astype(F32), STEP - 1, 0)
        moved = jnp.where(row == STEP - 1, jnp.where(at == steps - 1, edge, first), moved)
        result[rows, :] = moved.astype(BF16)
        return none

    lax.fori_loop(0, value.shape[0] // STEP, body, 0)


def spread_kernel(seqs, tokens, parts, turn, tail, hidden, full, grads_two, grads_one, taps, sums, out, input_grad, sums_out, rows_full, grads, grads_edge, moved, own, ups, downs, acc, across, around, every, weights, leaving, coming, load_sems, swap_sems, up_sems, down_sems, line_send, line_recv, column_send, column_recv, kept_sems, plane_send, plane_recv, sums_sems, weight_sems, leaving_sems, coming_sems, result_sems, pair_sems, ready_sem):
    line, plane = lax.axis_size("seq"), lax.axis_size("dp")
    at, here = lax.axis_index("seq"), lax.axis_index("dp")
    unit = line * parts
    units = own.shape[0] // unit
    blocks = units // 3
    width = own.shape[1]
    block_rows = seqs * tokens
    half = unit // 2
    here, beside, below, across_from = neighbours()
    mine = lax.axis_index("mp")
    greet("seq", "dp", "mp")
    met("seq", "dp", "mp")

    def turned(u):
        return lax.rem(u, turn) == turn - 1

    def direct(u):
        return lax.rem(u, turn) != turn - 1

    wide = rows_full.shape[1] // 2

    def own_rows(value, number, way):
        place = rows_full.at[:, pl.ds(pl.multiple_of(mine * wide, 128), wide)]
        if way == 0:
            return pltpu.make_async_copy(value, place, load_sems.at[number])
        return remote(value, place, pair_sems.at[0, number], pair_sems.at[1, number], "mp", 1 - mine)

    def other_rows(number):
        place = rows_full.at[:, pl.ds(pl.multiple_of((1 - mine) * wide, 128), wide)]
        return remote(place, place, pair_sems.at[0, number], pair_sems.at[1, number], "mp", 1 - mine)

    def plane_rows(owner):
        return pl.ds(pl.multiple_of(owner * block_rows, 16), block_rows)

    def peer(steps):
        return (here, beside, below, across_from)[steps]

    def load_two():
        return pltpu.make_async_copy(grads_two, moved, load_sems.at[2])

    def swap(steps, edge, arriving=False):
        columns = pl.ds(pl.multiple_of(peer(steps) * width, 128), width)
        source = peer(steps) if arriving else here
        if edge:
            src, dst = grads_one.at[block_rows : block_rows + EDGE, columns], grads_edge.at[source]
        else:
            src, dst = grads_one.at[0:block_rows, columns], grads.at[plane_rows(source)]
        number = steps * 2 + edge
        if steps == 0:
            return pltpu.make_async_copy(src, dst, swap_sems.at[0, number])
        return remote(src, dst, swap_sems.at[0, number], swap_sems.at[1, number], "dp", peer(steps))

    def product(block, right):
        columns = pl.ds(pl.multiple_of(jnp.where(mine == 0, block, blocks - 1 - block) * unit, 128), unit)
        return lax.dot_general(
            rows_full[:, columns], right[...], (((0,), (0,)), ((), ())), preferred_element_type=F32
        ).astype(BF16)

    narrow = leaving.shape[2]
    pieces = wide // narrow

    def load_weights(step):
        first = jnp.where(step < pieces, (1 - mine) * pieces + step, mine * pieces + step - pieces) * narrow
        slot = lax.rem(step, 2)
        return pltpu.make_async_copy(
            taps.at[:, :, pl.ds(pl.multiple_of(first, narrow), narrow), :], weights.at[slot], weight_sems.at[slot]
        )

    def load_every():
        return pltpu.make_async_copy(grads_one, every, load_sems.at[3])

    def leave(step):
        slot = lax.rem(step, 2)
        return remote(leaving.at[slot], coming.at[step], leaving_sems.at[slot], coming_sems.at[step], "mp", 1 - mine)

    def result(step):
        return pltpu.make_async_copy(
            coming.at[step],
            input_grad.at[:, pl.ds(pl.multiple_of(step * narrow, narrow), narrow)],
            result_sems.at[step],
        )

    def input_terms(slot):
        channels = taps.shape[3]
        now = jnp.zeros((block_rows, narrow), F32)
        late = jnp.zeros((block_rows + EDGE, narrow), F32)
        for gate in range(3):
            lanes = slice(gate * channels, gate * channels + channels)
            now += lax.dot_general(
                every[:block_rows, lanes], weights[slot, 0, gate], (((1,), (1,)), ((), ())), preferred_element_type=F32
            )
            late += lax.dot_general(
                every[:, lanes], weights[slot, 1, gate], (((1,), (1,)), ((), ())), preferred_element_type=F32
            )
        row = lax.broadcasted_iota(jnp.int32, now.shape, 0)
        after = pltpu.roll(late[:block_rows], block_rows - 1, 0)
        for seq in range(seqs):
            after = jnp.where(
                row == seq * tokens + tokens - 1, late[block_rows + seq : block_rows + seq + 1], after
            )
        return now + after

    def whole(u):
        return pl.ds(pl.multiple_of(u * unit, unit), unit)

    def chunk(u, j):
        return pl.ds(pl.multiple_of(u * unit + j * parts, parts), parts)

    def up(src, u, j):
        number = u * (line - 1) + j - 1
        return remote(src, ups.at[u, j - 1], up_sems.at[0, number], up_sems.at[1, number], "seq", lax.rem(at + 1, line))

    def down(src, u, j):
        number = u * (line - 1) + j
        return remote(
            src, downs.at[u, j], down_sems.at[0, number], down_sems.at[1, number], "seq", lax.rem(at + line - 1, line)
        )

    def along(src, u, j, way, hop):
        return remote(
            src,
            out.at[here, chunk(u, j)],
            line_send.at[(u * 2 + way) * (line - 1) + hop],
            line_recv.at[u * line + j],
            "seq",
            lax.rem(at + (1 if way == 0 else line - 1), line),
        )

    def column(src, steps, u, j, way, hop):
        number = u // turn * 4 + steps
        return remote(
            src,
            out.at[peer(steps), chunk(u, j)],
            column_send.at[(number * 2 + way) * (line - 1) + hop],
            column_recv.at[number * line + j],
            "seq",
            lax.rem(at + (1 if way == 0 else line - 1), line),
        )

    def over_part(src, u, way):
        return remote(
            src,
            out.at[here, chunk(u, at)],
            plane_send.at[u * 4 + way],
            plane_recv.at[u * 4 + way],
            "dp",
            (beside, below)[way],
        )

    def onward_part(owner, u, way):
        place = out.at[owner, pl.ds(pl.multiple_of(u * unit + at * parts + way * (parts // 2), 16), parts // 2)]
        return remote(
            place, place, plane_send.at[u * 4 + 2 + way], plane_recv.at[u * 4 + 2 + way], "dp", (below, beside)[way]
        )

    def keep(u):
        return pltpu.make_async_copy(own.at[chunk(u, at)], out.at[here, chunk(u, at)], kept_sems.at[u])

    def rows(u, first, count):
        return pl.ds(pl.multiple_of(u * unit + first, half), count)

    def over(u, way):
        place = out.at[here, rows(u, 0, unit)]
        return remote(place, place, plane_send.at[u * 4 + way], plane_recv.at[u * 4 + way], "dp", (beside, below)[way])

    def onward(u, way):
        place = out.at[(beside, below)[way], rows(u, way * half, half)]
        return remote(
            place, place, plane_send.at[u * 4 + 2 + way], plane_recv.at[u * 4 + 2 + way], "dp", (below, beside)[way]
        )

    def corner(u, way):
        place = out.at[across_from, rows(u, way * half, half)]
        return remote(place, place, plane_send.at[u * 4 + 2 + way], plane_recv.at[u * 4 + 2 + way], "dp", (below, beside)[way])

    def sums_copy(slots, me, count, axis, number, step):
        return remote(
            slots.at[me],
            slots.at[me],
            sums_sems.at[number, 0, step - 1],
            sums_sems.at[number, 1, step - 1],
            axis,
            lax.rem(me + step, count),
        )

    def sums_arrival(slots, me, count, axis, number, step):
        place = slots.at[lax.rem(me + count - step, count)]
        return remote(place, place, sums_sems.at[number, 0, step - 1], sums_sems.at[number, 1, step - 1], axis, lax.rem(me + step, count))

    for way in range(2):
        own_rows(hidden, 0, way).start()
    load_two().start()
    for steps in range(4):
        for edge in range(2):
            swap(steps, edge).start()
    load_every().start()
    load_weights(0).start()
    across[at] = sums[...]
    for step in range(1, line):
        sums_copy(across, at, line, "seq", 0, step).start()
    load_two().wait()
    own_rows(hidden, 0, 0).wait()

    def stage(index, none):
        @pl.when(index == 1)
        def _():
            for step in range(1, line):
                sums_arrival(across, at, line, "seq", 0, step).wait_recv()
            total = across[0]
            for other in range(1, line):
                total = total + across[other]
            around[here] = total
            for step in range(1, plane):
                sums_copy(around, here, plane, "dp", 1, step).start()

        @pl.when(index == 3)
        def _():
            for step in range(1, plane):
                sums_arrival(around, here, plane, "dp", 1, step).wait_recv()
            total = around[0]
            for other in range(1, plane):
                total = total + around[other]
            sums_out[...] = total

        @pl.when(index == wide // unit)
        def _():
            other_rows(0).wait_recv()

        @pl.when(index == blocks + 2 * (wide // unit))
        def _():
            other_rows(1).wait_recv()

        @pl.when(index < blocks)
        def _():
            own[whole(index), :] = product(index, moved)

        @pl.when(index == blocks - 1)
        def _():
            own_rows(hidden, 0, 1).wait_send()
            own_rows(full, 1, 0).start()
            pl.semaphore_signal(ready_sem, inc=1, device_id={"mp": 1 - mine}, device_id_type=pl.DeviceIdType.MESH)
            pl.semaphore_wait(ready_sem, 1)
            own_rows(full, 1, 1).start()

        @pl.when(index == blocks)
        def _():
            for steps in range(4):
                for edge in range(2):
                    if steps:
                        swap(steps, edge, True).wait_recv()
                    else:
                        swap(steps, edge).wait()
            shift_up(seqs, tokens, grads, grads_edge, moved)
            own_rows(full, 1, 0).wait()
            load_every().wait()

        @pl.when((index >= blocks) & (index < units) & (lax.rem(index - blocks, 2) == 0))
        def _():
            own[whole(index), :] = product((index - blocks) // 2, grads)

        @pl.when((index >= blocks) & (index < units) & (lax.rem(index - blocks, 2) == 1))
        def _():
            own[whole(index), :] = product((index - blocks) // 2, moved)

        k = index - blocks

        @pl.when((k >= 0) & (k < 2 * pieces))
        def _():
            load_weights(k).wait()

            @pl.when(k + 1 < 2 * pieces)
            def _():
                load_weights(k + 1).start()

            terms = input_terms(lax.rem(k, 2))

            @pl.when(k < pieces)
            def _():
                @pl.when(k >= 2)
                def _():
                    leave(k - 2).wait_send()

                leaving[lax.rem(k, 2)] = terms
                leave(k).start()

            @pl.when(k >= pieces)
            def _():
                leave(k - pieces).wait_recv()
                coming[k - pieces] += terms
                result(k - pieces).start()

        u = index - at

        @pl.when((u >= 0) & (u < units))
        def _():
            for j in range(line - 1, 0, -1):

                @pl.when(at == 0)
                def _(j=j):
                    up(own.at[chunk(u, j)], u, j).start()

                @pl.when((at > 0) & (at <= j))
                def _(j=j):
                    up(ups.at[u, j - 1], u, j).wait_recv()

                @pl.when((at > 0) & (at < j))
                def _(j=j):
                    ups[u, j - 1] = (ups[u, j - 1].astype(F32) + own[chunk(u, j)].astype(F32)).astype(BF16)
                    up(ups.at[u, j - 1], u, j).start()

        v = index - (line - 1 - at)

        @pl.when((v >= 0) & (v < units))
        def _():
            for j in range(line - 1):

                @pl.when(at == line - 1)
                def _(j=j):
                    down(own.at[chunk(v, j)], v, j).start()

                @pl.when((at < line - 1) & (at >= j))
                def _(j=j):
                    down(downs.at[v, j], v, j).wait_recv()

                @pl.when((at < line - 1) & (at > j))
                def _(j=j):
                    downs[v, j] = (downs[v, j].astype(F32) + own[chunk(v, j)].astype(F32)).astype(BF16)
                    down(downs.at[v, j], v, j).start()

        w = index - (line - 1)

        @pl.when((w >= 0) & (w < units))
        def _():
            acc[...] = own[chunk(w, at)].astype(F32)

            @pl.when(at > 0)
            def _():
                acc[...] += ups[w, at - 1].astype(F32)

            @pl.when(at < line - 1)
            def _():
                acc[...] += downs[w, at].astype(F32)

            own[chunk(w, at)] = acc[...].astype(BF16)
            keep(w).start()

            @pl.when(direct(w) & (at < line - 1))
            def _():
                along(own.at[chunk(w, at)], w, at, 0, 0).start()

            @pl.when(direct(w) & (at > 0))
            def _():
                along(own.at[chunk(w, at)], w, at, 1, 0).start()

            @pl.when(turned(w))
            def _():
                for way in range(2):
                    over_part(own.at[chunk(w, at)], w, way).start()

        c = index - line

        @pl.when((c >= 0) & (c < units) & turned(c))
        def _():
            keep(c).wait()
            for way in range(2):
                over_part(out.at[(beside, below)[way], chunk(c, at)], c, way).wait_recv()
                onward_part((beside, below)[way], c, way).start()

        d = index - line - 1

        @pl.when((d >= 0) & (d < units) & turned(d))
        def _():
            for way in range(2):
                onward_part(across_from, d, way).wait_recv()

        for steps in range(4):
            for hop in range(line):
                e = index - line - 1 - steps - hop

                @pl.when((e >= 0) & (e < units) & turned(e))
                def _(e=e, steps=steps, hop=hop):
                    @pl.when(at >= hop)
                    def _():
                        src = out.at[peer(steps), chunk(e, at - hop)]
                        if hop:
                            column(src, steps, e, at - hop, 0, 0).wait_recv()
                        if hop < line - 1:

                            @pl.when(at < line - 1)
                            def _():
                                column(src, steps, e, at - hop, 0, hop).start()

                    @pl.when(at + hop < line)
                    def _():
                        src = out.at[peer(steps), chunk(e, at + hop)]
                        if hop:
                            column(src, steps, e, at + hop, 1, 0).wait_recv()
                        if hop < line - 1:

                            @pl.when(at > 0)
                            def _():
                                column(src, steps, e, at + hop, 1, hop).start()

        for hop in range(1, line):
            x = index - (line - 1) - hop

            @pl.when((x >= 0) & (x < units) & direct(x))
            def _(x=x, hop=hop):
                @pl.when(at >= hop)
                def _():
                    src = out.at[here, chunk(x, at - hop)]
                    along(src, x, at - hop, 0, 0).wait_recv()
                    if hop < line - 1:

                        @pl.when(at < line - 1)
                        def _():
                            along(src, x, at - hop, 0, hop).start()

                @pl.when(at + hop < line)
                def _():
                    src = out.at[here, chunk(x, at + hop)]
                    along(src, x, at + hop, 1, 0).wait_recv()
                    if hop < line - 1:

                        @pl.when(at > 0)
                        def _():
                            along(src, x, at + hop, 1, hop).start()

        y = index - 2 * (line - 1)

        @pl.when((y >= 0) & (y < units) & direct(y))
        def _():
            keep(y).wait()

        @pl.when((y >= 0) & (y < units - tail) & direct(y))
        def _():
            over(y, 0).start()
            over(y, 1).start()

        z = y - LAG

        @pl.when((z >= 0) & (z < units - tail) & direct(z))
        def _():
            for way in range(2):
                place = out.at[(beside, below)[way], rows(z, 0, unit)]
                remote(place, place, plane_send.at[z * 4 + way], plane_recv.at[z * 4 + way], "dp", (beside, below)[way]).wait_recv()
                onward(z, way).start()

        t = z - LAG

        @pl.when((t >= 0) & (t < units - tail) & direct(t))
        def _():
            for way in range(2):
                corner(t, way).wait_recv()

        return none

    last_turned = units // turn * turn - 1
    lax.fori_loop(
        0, max(units + 2 * (line - 1), units - tail + 2 * (line - 1) + 2 * LAG, last_turned + 2 * line + 4), stage, 0
    )

    def settle(u, none):
        for j in range(1, line):

            @pl.when(at < j)
            def _(j=j):
                up(ups.at[u, j - 1], u, j).wait_send()

        for j in range(line - 1):

            @pl.when(at > j)
            def _(j=j):
                down(downs.at[u, j], u, j).wait_send()

        for hop in range(line - 1):

            @pl.when(direct(u) & (at >= hop) & (at < line - 1))
            def _(hop=hop):
                along(out.at[here, chunk(u, at - hop)], u, at - hop, 0, hop).wait_send()

            @pl.when(direct(u) & (at + hop < line) & (at > 0))
            def _(hop=hop):
                along(out.at[here, chunk(u, at + hop)], u, at + hop, 1, hop).wait_send()

            @pl.when(turned(u) & (at >= hop) & (at < line - 1))
            def _(hop=hop):
                for steps in range(4):
                    column(out.at[here, chunk(u, at - hop)], steps, u, at - hop, 0, hop).wait_send()

            @pl.when(turned(u) & (at + hop < line) & (at > 0))
            def _(hop=hop):
                for steps in range(4):
                    column(out.at[here, chunk(u, at + hop)], steps, u, at + hop, 1, hop).wait_send()

        @pl.when(direct(u) & (u < units - tail))
        def _():
            for way in range(2):
                over(u, way).wait_send()
                onward(u, way).wait_send()

        @pl.when(turned(u))
        def _():
            for way in range(2):
                over_part(out.at[here, chunk(u, at)], u, way).wait_send()
                onward_part(here, u, way).wait_send()

        return none

    lax.fori_loop(0, units, settle, 0)
    for steps in range(1, 4):
        for edge in range(2):
            swap(steps, edge).wait_send()
    own_rows(full, 1, 1).wait_send()
    for step in range(pieces - 2, pieces):
        leave(step).wait_send()
    for step in range(pieces):
        result(step).wait()
    for step in range(1, line):
        sums_copy(across, at, line, "seq", 0, step).wait_send()
    for step in range(1, plane):
        sums_copy(around, here, plane, "dp", 1, step).wait_send()


def spread(seqs, tokens, hidden, full, grads_two, grads_one, taps, sums):
    line, plane = lax.axis_size("seq"), lax.axis_size("dp")
    width = grads_two.shape[1]
    rows = grads_two.shape[0] // plane
    depth = 2 * full.shape[1]
    units = 3 * depth // (line * PART)
    channels = taps.shape[3]
    narrow = depth // (units - units // 3)
    pieces = channels // narrow
    turns = units // TURN
    dma = pltpu.SemaphoreType.DMA
    hbm = pl.BlockSpec(memory_space=pl.ANY)
    return pl.pallas_call(
        functools.partial(spread_kernel, seqs, tokens, PART, TURN, TAIL),
        out_shape=(
            jax.ShapeDtypeStruct((plane, 3 * depth, width), BF16),
            jax.ShapeDtypeStruct((rows, channels), F32),
            jax.ShapeDtypeStruct(sums.shape, F32),
        ),
        in_specs=[hbm] * 5 + [VMEM],
        out_specs=[hbm, hbm, VMEM],
        scratch_shapes=[
            pltpu.VMEM((plane * rows, depth), BF16),
            pltpu.VMEM((plane * rows, width), BF16),
            pltpu.VMEM((plane, EDGE, width), BF16),
            pltpu.VMEM((plane * rows, width), BF16),
            pltpu.VMEM((3 * depth, width), BF16),
            pltpu.VMEM((units, line - 1, PART, width), BF16),
            pltpu.VMEM((units, line - 1, PART, width), BF16),
            pltpu.VMEM((PART, width), F32),
            pltpu.VMEM((line,) + sums.shape, F32),
            pltpu.VMEM((plane,) + sums.shape, F32),
            pltpu.VMEM(grads_one.shape, BF16),
            pltpu.VMEM((2, 2, 3, narrow, channels), BF16),
            pltpu.VMEM((2, rows, narrow), F32),
            pltpu.VMEM((pieces, rows, narrow), F32),
            dma((4,)),
            dma((2, 8)),
            dma((2, units * (line - 1))),
            dma((2, units * (line - 1))),
            dma((units * 2 * (line - 1),)),
            dma((units * line,)),
            dma((turns * 4 * 2 * (line - 1),)),
            dma((turns * 4 * line,)),
            dma((units,)),
            dma((units * 4,)),
            dma((units * 4,)),
            dma((2, 2, max(line, plane) - 1)),
            dma((2,)),
            dma((2,)),
            dma((pieces,)),
            dma((pieces,)),
            dma((2, 2)),
            pltpu.SemaphoreType.REGULAR,
        ],
        compiler_params=pltpu.CompilerParams(
            collective_id=4, has_side_effects=True, vmem_limit_bytes=62 * 2**20
        ),
        cost_estimate=pl.CostEstimate(
            flops=6 * plane * rows * depth * width, bytes_accessed=depth * width * 48, transcendentals=0
        ),
        name="spread",
    )(hidden, full, grads_two, grads_one, taps, sums)


def widen_kernel(blocks, core, given, *refs):
    out = refs[-1]
    per = given.shape[2] // 128
    for tile in range(3 * blocks):
        source, place = divmod(tile, per)
        gate, column = divmod(tile, blocks)
        out[0, gate, :, column * 128 : column * 128 + 128] = given[
            source, :, place * 128 : place * 128 + 128
        ].astype(F32)


def widen(gathered, first, taps, start, count, depth, channels, unit, core, into=None):
    plane, _, width = gathered.shape
    last = depth // unit - 1

    def source(tap, step, core):
        return (0, first + step * taps + tap, 0)

    def target(tap, step, core):
        block = start + step
        return (tap, 0, jnp.where(core[0] == 0, block, last - block), 0)

    given = (core, gathered) if into is None else (core, gathered, into)
    return pl.pallas_call(
        functools.partial(widen_kernel, channels // 128),
        grid_spec=pltpu.PrefetchScalarGridSpec(
            num_scalar_prefetch=1,
            grid=(taps, count),
            in_specs=[pl.BlockSpec((plane, unit, width), source)] + [pl.BlockSpec(memory_space=pl.ANY)] * (len(given) - 2),
            out_specs=pl.BlockSpec((1, 3, unit, channels), target),
        ),
        out_shape=jax.ShapeDtypeStruct((taps, 3, depth, channels), F32),
        input_output_aliases={} if into is None else {2: 0},
        compiler_params=pltpu.CompilerParams(vmem_limit_bytes=40 * 2**20),
        cost_estimate=pl.CostEstimate(
            flops=0, bytes_accessed=taps * count * unit * (plane * width * 2 + channels * 12), transcendentals=0
        ),
        name="widen",
    )(*given)


def shifted(value, axis, steps):
    count = lax.axis_size(axis)
    initial, last = (max(0, -steps), min(count, count - steps))
    return lax.ppermute(value, axis, [(source, source + steps) for source in range(initial, last)])


def gather_channels(value):
    count = lax.axis_size("mp")
    if count != 2:
        return lax.all_gather(value, "mp", axis=value.ndim - 1, tiled=True)
    other = lax.ppermute(value, "mp", [(0, 1), (1, 0)])
    second = lax.axis_index("mp") == 1
    return jnp.concatenate([jnp.where(second, other, value), jnp.where(second, value, other)], value.ndim - 1)


def sum_channels(terms):
    count = lax.axis_size("mp")
    if count != 2:
        return lax.psum_scatter(terms, "mp", scatter_dimension=1, tiled=True)
    width = terms.shape[1] // 2
    second = lax.axis_index("mp") == 1
    low, high = terms[:, :width], terms[:, width:]
    other = lax.ppermute(jnp.where(second, low, high), "mp", [(0, 1), (1, 0)])
    return jnp.where(second, high, low) + other


def dot(lhs, rhs, dims):
    return lax.dot_general(lhs, rhs, (dims, ((), ())), preferred_element_type=F32)


def reduce_weights(partial):
    shard = lax.psum_scatter(partial.astype(BF16), ("dp", "seq"), scatter_dimension=0, tiled=True)
    return lax.all_gather(shard, ("dp", "seq"), axis=0, tiled=True).astype(F32)


def local(inputs, starts, init_state, weight_one, bias_one, weight_two, bias_two, cotangent):
    seqs, tokens, channels = inputs.shape
    rows = seqs * tokens
    width = weight_one.shape[1]
    keep = jnp.broadcast_to((1 - starts).astype(F32).reshape(rows, 1), (rows, 128))
    taps = weight_one.transpose(0, 2, 1, 3)
    mix = weight_two.transpose(1, 0, 2)

    edge = gather_channels(shifted(inputs[:, -1], "seq", 1))
    full = gather_channels(inputs)
    previous = jnp.concatenate([edge[:, None], full[:, :-1]], 1).reshape(rows, width)
    full = full.reshape(rows, width)
    both = jnp.concatenate([full, previous], 1)
    gates_one = jnp.einsum(
        "tkd,kgdc->gtc", both.reshape(rows, 2, width), taps, preferred_element_type=F32
    )
    line, plane = lax.axis_size("seq"), lax.axis_size("dp")
    tiles = 3 * channels // 128
    spreads = plane == 4 and lax.axis_size("mp") == 2 and seqs == 2 and channels % 128 == 0
    spreads = spreads and width % (line * PART) == 0 and line > 1
    block = -(-tiles // plane) * 128
    lanes = plane * block if spreads else 3 * channels
    hidden, upd, fgt, out, state, entering, *both_cores = pool_forward(
        seqs, tokens, spreads, gates_one, bias_one, keep, init_state[0]
    )
    full_hidden = both_cores[0] if spreads else gather_channels(hidden)
    upstream = cotangent.reshape(rows, channels)
    if spreads:
        pooled_two, grad_two, planes_two, sums_two, every_hidden = pool_upper(
            seqs, tokens, lanes, full_hidden, hidden, mix, bias_two, keep, init_state[1], upstream
        )
        extended, sums_one, swapped = pool_lower(
            seqs, tokens, planes_two, grad_two, mix, keep, upd, fgt, out, state, entering
        )
        sums = jnp.concatenate([jnp.sum(sums_one, 1), jnp.sum(sums_two, 1)])
        gathered, input_grad, sums = spread(
            seqs,
            tokens,
            every_hidden.reshape(plane * rows, channels),
            lax.all_gather(inputs.reshape(rows, channels), "dp", axis=0, tiled=True),
            swapped.reshape(plane * rows, block),
            extended,
            taps,
            sums,
        )
        unit = line * PART
        blocks = width // unit
        core = lax.axis_index("mp").reshape(1)
        behind = TAIL // 2
        kept = lax.dynamic_slice(
            gathered, (lax.axis_index("dp"), (3 * blocks - TAIL) * unit, 0), (1, TAIL * unit, block)
        )
        tail = lax.all_gather(kept, "dp", axis=0, tiled=True)
        weight_two_grad = widen(gathered, 0, 1, 0, blocks, width, channels, unit, core)
        weight_one_grad = widen(gathered, blocks, 2, 0, blocks - behind, width, channels, unit, core)
        weight_one_grad = widen(
            tail, 0, 2, blocks - behind, behind, width, channels, unit, core, weight_one_grad
        )
        weight_two_grad = weight_two_grad[0].transpose(1, 0, 2)
        weight_one_grad = weight_one_grad.transpose(0, 2, 1, 3)
    else:
        gates_two = jnp.einsum("td,gdc->gtc", full_hidden, mix, preferred_element_type=F32)
        pooled_two, grad_two, planes_two, sums_two = pool_top(
            seqs, tokens, lanes, gates_two, bias_two, keep, init_state[1], upstream
        )
        hidden_terms = jnp.einsum("gtc,gdc->td", planes_two, mix, preferred_element_type=F32)
        hidden_grad = sum_channels(hidden_terms)
        extended, sums_one = pool_backward(seqs, tokens, lanes, hidden_grad, keep, upd, fgt, out, state, entering)
        grad_one = extended[:rows]
        input_terms = jnp.einsum(
            "tgc,kgdc->ktd", grad_one.reshape(rows, 3, channels), taps, preferred_element_type=F32
        ).reshape(2, seqs, tokens, width)
        late = input_terms[1]
        late = jnp.concatenate([late[:, 1:], shifted(late[:, 0], "seq", -1)[:, None]], 1)
        input_grad = sum_channels((input_terms[0] + late).reshape(rows, width))
        sums = jnp.concatenate([jnp.sum(sums_one, 1), jnp.sum(sums_two, 1)])
        sums = lax.psum(sums, ("dp", "seq"))
        weight_two_grad = reduce_weights(dot(full_hidden, grad_two, ((0,), (0,)))).reshape(width, 3, channels)
        weight_one_grad = jnp.stack(
            [
                reduce_weights(dot(full, grad_one, ((0,), (0,)))),
                reduce_weights(dot(previous, grad_one, ((0,), (0,)))),
            ]
        ).reshape(2, width, 3, channels)
    return (
        pooled_two.reshape(seqs, tokens, channels),
        input_grad.reshape(seqs, tokens, channels),
        weight_one_grad,
        sums[:3],
        weight_two_grad,
        sums[3:],
    )


def solution(mesh):
    return jax.shard_map(
        local,
        mesh=mesh,
        in_specs=(
            P("dp", "seq", "mp"),
            P("dp", "seq"),
            P(None, "dp", "mp"),
            P(None, None, None, "mp"),
            P(None, "mp"),
            P(None, None, "mp"),
            P(None, "mp"),
            P("dp", "seq", "mp"),
        ),
        out_specs=(
            P("dp", "seq", "mp"),
            P("dp", "seq", "mp"),
            P(None, None, None, "mp"),
            P(None, "mp"),
            P(None, None, "mp"),
            P(None, "mp"),
        ),
        check_vma=False,
    )
```

```python
import functools

import jax
import jax.numpy as jnp
from jax import lax
from jax.experimental import pallas as pl
from jax.experimental.pallas import tpu as pltpu
from jax.sharding import PartitionSpec as P

F32 = jnp.float32
BF16 = jnp.bfloat16
SUB = 8
STEP = 16
EDGE = 16
PART = 64
LAG = 2
TURN = 6
TAIL = 2
VMEM = pl.BlockSpec(memory_space=pltpu.VMEM)


def sigmoid(x):
    return 0.5 * jnp.tanh(0.5 * x) + 0.5


def lane_blocks(channels):
    width = 384 if channels % 384 == 0 else channels
    return [slice(at, at + width) for at in range(0, channels, width)]


def scan_down(scale, shift):
    row = lax.broadcasted_iota(jnp.int32, scale.shape, 0)
    for step in (1, 2, 4):
        earlier = row >= step
        scale_before = jnp.where(earlier, pltpu.roll(scale, step, 0), 1.0)
        shift_before = jnp.where(earlier, pltpu.roll(shift, step, 0), 0.0)
        shift = scale * shift_before + shift
        scale = scale * scale_before
    return scale, shift


def scan_up(scale, shift):
    row = lax.broadcasted_iota(jnp.int32, scale.shape, 0)
    for step in (1, 2, 4):
        later = row < SUB - step
        scale_after = jnp.where(later, pltpu.roll(scale, SUB - step, 0), 1.0)
        shift_after = jnp.where(later, pltpu.roll(shift, SUB - step, 0), 0.0)
        shift = scale * shift_after + shift
        scale = scale * scale_after
    return scale, shift


def greet(*axes):
    for axis in axes:
        count = lax.axis_size(axis)
        me = lax.axis_index(axis)
        for step in range(1, count):
            pl.semaphore_signal(
                pltpu.get_barrier_semaphore(),
                inc=1,
                device_id={axis: lax.rem(me + step, count)},
                device_id_type=pl.DeviceIdType.MESH,
            )


def met(*axes):
    pl.semaphore_wait(pltpu.get_barrier_semaphore(), sum(lax.axis_size(axis) - 1 for axis in axes))


def remote(src, dst, send, recv, axis, target):
    return pltpu.make_async_remote_copy(
        src_ref=src,
        dst_ref=dst,
        send_sem=send,
        recv_sem=recv,
        device_id={axis: target},
        device_id_type=pl.DeviceIdType.MESH,
    )


def to_all(src, slots, send_sems, recv_sems, axis):
    count = lax.axis_size(axis)
    me = lax.axis_index(axis)
    copies = []
    for step in range(1, count):
        copies.append(
            pltpu.make_async_remote_copy(
                src_ref=src,
                dst_ref=slots.at[step - 1],
                send_sem=send_sems.at[step - 1],
                recv_sem=recv_sems.at[step - 1],
                device_id={axis: lax.rem(me + step, count)},
                device_id_type=pl.DeviceIdType.MESH,
            )
        )
    for copy in copies:
        copy.start()
    return copies


def from_earlier(slots, initial, scale_rows, shift_rows, axis):
    count = lax.axis_size(axis)
    me = lax.axis_index(axis)
    state = initial
    for block in range(count - 1):
        slot = jnp.maximum(me - block - 1, 0)
        after = slots[slot, scale_rows, :] * state + slots[slot, shift_rows, :]
        state = jnp.where(block < me, after, state)
    return state


def from_later(slots, shape, scale_rows, shift_rows, axis):
    count = lax.axis_size(axis)
    me = lax.axis_index(axis)
    message = jnp.zeros(shape, F32)
    for block in range(count - 1, 0, -1):
        slot = jnp.minimum(me + count - block - 1, count - 2)
        after = slots[slot, scale_rows, :] * message + slots[slot, shift_rows, :]
        message = jnp.where(block > me, after, message)
    return message


def first_pass(seqs, tokens, channels, gates, bias, keep, upd, fgt, out, scale, shift, summary):
    def body(at, carried):
        given = list(carried)
        for seq in range(seqs):
            for half in range(STEP // SUB):
                rows = pl.ds(pl.multiple_of(seq * tokens + at * STEP + half * SUB, SUB), SUB)
                kept = keep[rows, :][:, 0:1]
                for number, lanes in enumerate(lane_blocks(channels)):
                    u = jnp.tanh(gates[0, rows, lanes] + bias[0:1, lanes])
                    f = sigmoid(gates[1, rows, lanes] + bias[1:2, lanes])
                    o = sigmoid(gates[2, rows, lanes] + bias[2:3, lanes])
                    upd[rows, lanes] = u
                    fgt[rows, lanes] = f
                    out[rows, lanes] = o
                    a, b = scan_down(f * kept, (1.0 - f) * u)
                    place = (seq * len(lane_blocks(channels)) + number) * 2
                    b = a * given[place + 1] + b
                    a = a * given[place]
                    scale[rows, lanes] = a
                    shift[rows, lanes] = b
                    given[place] = a[SUB - 1 : SUB]
                    given[place + 1] = b[SUB - 1 : SUB]
        return tuple(given)

    begin = []
    for seq in range(seqs):
        for lanes in lane_blocks(channels):
            width = lanes.stop - lanes.start
            begin += [jnp.ones((1, width), F32), jnp.zeros((1, width), F32)]
    end = lax.fori_loop(0, tokens // STEP, body, tuple(begin))
    place = 0
    for seq in range(seqs):
        for lanes in lane_blocks(channels):
            summary[seq : seq + 1, lanes] = end[place]
            summary[seqs + seq : seqs + seq + 1, lanes] = end[place + 1]
            place += 2


def back_pass(seqs, tokens, channels, upstream, keep, fgt, out, scale, shift, summary, row0):
    steps = tokens // STEP

    def body(index, carried):
        at = steps - 1 - index
        given = list(carried)
        for seq in range(seqs):
            whole = pl.ds(pl.multiple_of(seq * tokens + at * STEP, STEP), STEP)
            for number, lanes in enumerate(lane_blocks(channels)):
                ups = upstream[whole, lanes].astype(F32)
                place = (seq * len(lane_blocks(channels)) + number) * 2
                for half in reversed(range(STEP // SUB)):
                    rows = pl.ds(pl.multiple_of(seq * tokens + at * STEP + half * SUB, SUB), SUB)
                    kept = keep[rows, :][:, 0:1]
                    retain = fgt[rows, lanes] * kept
                    direct = ups[half * SUB : half * SUB + SUB] * out[rows, lanes]
                    a, b = scan_up(retain, retain * direct)
                    b = a * given[place + 1] + b
                    a = a * given[place]
                    scale[rows, lanes] = a
                    shift[rows, lanes] = b
                    given[place] = a[0:1]
                    given[place + 1] = b[0:1]
        return tuple(given)

    begin = []
    for seq in range(seqs):
        for lanes in lane_blocks(channels):
            width = lanes.stop - lanes.start
            begin += [jnp.ones((1, width), F32), jnp.zeros((1, width), F32)]
    end = lax.fori_loop(0, steps, body, tuple(begin))
    place = 0
    for seq in range(seqs):
        for lanes in lane_blocks(channels):
            summary[row0 + seq : row0 + seq + 1, lanes] = end[place]
            summary[row0 + seqs + seq : row0 + seqs + seq + 1, lanes] = end[place + 1]
            place += 2


def states_pass(seq, tokens, channels, entering, out, scale, shift, state, pooled):
    def body(at, none):
        rows = pl.ds(pl.multiple_of(seq * tokens + at * STEP, STEP), STEP)
        for lanes in lane_blocks(channels):
            value = scale[rows, lanes] * entering[seq : seq + 1, lanes] + shift[rows, lanes]
            state[rows, lanes] = value
            pooled[rows, lanes] = (out[rows, lanes] * value).astype(BF16)
        return none

    lax.fori_loop(0, tokens // STEP, body, 0)


def grads_pass(seqs, tokens, channels, message, entering, upstream, keep, upd, fgt, out, state, scale, shift, grads, planes, sums):
    steps = tokens // STEP
    sums[...] = jnp.zeros_like(sums)
    if grads.shape[1] > 3 * channels:
        grads[:, 3 * channels :] = jnp.zeros((grads.shape[0], grads.shape[1] - 3 * channels), BF16)
    for seq in range(seqs):
        for lanes in lane_blocks(channels):
            width = lanes.stop - lanes.start

            def body(index, later, seq=seq, lanes=lanes, width=width):
                at = steps - 1 - index
                whole = pl.ds(pl.multiple_of(seq * tokens + at * STEP, STEP), STEP)
                row = lax.broadcasted_iota(jnp.int32, (STEP, width), 0)
                kept = keep[whole, :][:, 0:1]
                ups = upstream[whole, lanes].astype(F32)
                u, f, o = upd[whole, lanes], fgt[whole, lanes], out[whole, lanes]
                states = state[whole, lanes]
                arriving = scale[whole, lanes] * message[seq : seq + 1, lanes] + shift[whole, lanes]
                adjoint = ups * o + jnp.where(row == STEP - 1, later, pltpu.roll(arriving, STEP - 1, 0))
                tile = pl.ds(pl.multiple_of(seq * tokens + jnp.maximum(at * STEP - SUB, 0), SUB), SUB)
                last = state[tile, lanes][SUB - 1 : SUB]
                first = jnp.where(at == 0, entering[seq : seq + 1, lanes], last)
                before = jnp.where(row == 0, first, pltpu.roll(states, 1, 0))
                given = [
                    adjoint * (1.0 - f) * (1.0 - u * u),
                    adjoint * (before * kept - u) * f * (1.0 - f),
                    ups * states * o * (1.0 - o),
                ]
                for gate, value in enumerate(given):
                    value = value.astype(BF16)
                    grads[whole, gate * channels + lanes.start : gate * channels + lanes.stop] = value
                    if planes is not None:
                        planes[gate, whole, lanes] = value
                    value = value.astype(F32)
                    total = value[:SUB]
                    for half in range(1, STEP // SUB):
                        total = total + value[half * SUB : half * SUB + SUB]
                    sums[gate, :, lanes] += total
                return arriving[0:1]

            lax.fori_loop(0, steps, body, message[seq : seq + 1, lanes])


def forward_kernel(seqs, tokens, channels, gates, bias, keep, initial, hidden, upd, fgt, out, state, entering, scale, shift, summary, slots, send_sems, recv_sems):
    greet("seq")
    first_pass(seqs, tokens, channels, gates, bias, keep, upd, fgt, out, scale, shift, summary)
    met("seq")
    copies = to_all(summary, slots, send_sems, recv_sems, "seq")
    for copy in copies:
        copy.wait()
    entering[...] = from_earlier(slots, initial[...], slice(0, seqs), slice(seqs, 2 * seqs), "seq")
    for seq in range(seqs):
        states_pass(seq, tokens, channels, entering, out, scale, shift, state, hidden)


def top_kernel(seqs, tokens, channels, gates, bias, keep, initial, cotangent, pooled, grads, planes, sums, upd, fgt, out, state, entering, message, scale, shift, back_scale, back_shift, summary, slots, send_sems, recv_sems):
    greet("seq")
    first_pass(seqs, tokens, channels, gates, bias, keep, upd, fgt, out, scale, shift, summary)
    back_pass(seqs, tokens, channels, cotangent, keep, fgt, out, back_scale, back_shift, summary, 2 * seqs)
    met("seq")
    copies = to_all(summary, slots, send_sems, recv_sems, "seq")
    for copy in copies:
        copy.wait()
    entering[...] = from_earlier(slots, initial[...], slice(0, seqs), slice(seqs, 2 * seqs), "seq")
    message[...] = from_later(
        slots, (seqs, channels), slice(2 * seqs, 3 * seqs), slice(3 * seqs, 4 * seqs), "seq"
    )
    for seq in range(seqs):
        states_pass(seq, tokens, channels, entering, out, scale, shift, state, pooled)
    grads_pass(seqs, tokens, channels, message, entering, cotangent, keep, upd, fgt, out, state, back_scale, back_shift, grads, planes, sums)


def pass_edges(seqs, tokens, grads, edges, arrived, edge_sems):
    count = lax.axis_size("seq")
    me = lax.axis_index("seq")
    row = lax.broadcasted_iota(jnp.int32, edges.shape, 0)
    firsts = jnp.zeros(edges.shape, F32)
    for seq in range(seqs):
        tile = grads[seq * tokens : seq * tokens + EDGE, :].astype(F32)
        firsts = jnp.where(row == seq, pltpu.roll(tile, seq, 0) if seq else tile, firsts)
    edges[...] = firsts.astype(BF16)
    copy = pltpu.make_async_remote_copy(
        src_ref=edges,
        dst_ref=arrived,
        send_sem=edge_sems.at[0],
        recv_sem=edge_sems.at[1],
        device_id={"seq": lax.rem(me + count - 1, count)},
        device_id_type=pl.DeviceIdType.MESH,
    )
    rows = slice(seqs * tokens, seqs * tokens + EDGE)

    @pl.when(me > 0)
    def _():
        copy.start()

    @pl.when(me < count - 1)
    def _():
        copy.wait_recv()
        grads[rows, :] = arrived[...]

    @pl.when(me == count - 1)
    def _():
        grads[rows, :] = jnp.zeros(edges.shape, BF16)

    @pl.when(me > 0)
    def _():
        copy.wait_send()


def backward_kernel(seqs, tokens, channels, upstream, keep, upd, fgt, out, state, entering, grads, sums, message, scale, shift, summary, slots, send_sems, recv_sems, edges, arrived, edge_sems):
    greet("seq")
    back_pass(seqs, tokens, channels, upstream, keep, fgt, out, scale, shift, summary, 0)
    met("seq")
    copies = to_all(summary, slots, send_sems, recv_sems, "seq")
    for copy in copies:
        copy.wait()
    message[...] = from_later(slots, (seqs, channels), slice(0, seqs), slice(seqs, 2 * seqs), "seq")
    grads_pass(seqs, tokens, channels, message, entering, upstream, keep, upd, fgt, out, state, scale, shift, grads, None, sums)
    pass_edges(seqs, tokens, grads, edges, arrived, edge_sems)


def neighbours():
    here = lax.axis_index("dp")
    beside = here + 1 - 2 * lax.rem(here, 2)
    return here, beside, lax.rem(here + 2, 4), lax.rem(beside + 2, 4)


def relay(value, every, plane_sems, kept_sem):
    here, beside, below, corner = neighbours()
    near = (beside, below)
    half = value.shape[0] // 2

    def over(src, owner, way):
        place = every.at[owner]
        return remote(src, place, plane_sems.at[0, way], plane_sems.at[1, way], "dp", near[way])

    def onward(owner, way):
        place = every.at[owner, pl.ds(way * half, half)]
        return remote(place, place, plane_sems.at[0, 2 + way], plane_sems.at[1, 2 + way], "dp", near[1 - way])

    def keep():
        return pltpu.make_async_copy(value, every.at[here], kept_sem)

    def start():
        for way in range(2):
            over(value, here, way).start()
        keep().start()

    def forward():
        for way in range(2):
            over(every.at[near[way]], near[way], way).wait_recv()
            onward(near[way], way).start()

    def finish():
        for way in range(2):
            over(value, here, way).wait_send()
            onward(near[way], way).wait_send()
            onward(corner, way).wait_recv()
        keep().wait()

    return start, forward, finish


def first_kernel(seqs, tokens, channels, inputs, taps, bias, keep, initial, hidden_out, upd_out, fgt_out, out_out, state_out, entering, both_out, every, both, edges, weights, gates, hidden, state, scale, shift, summary, slots, send_sems, recv_sems, weight_sems, plane_sems, kept_sem, pair_sems, edge_sems, save_sems):
    axes = ("seq", "dp", "mp")
    line, at, mine = lax.axis_size("seq"), lax.axis_index("seq"), lax.axis_index("mp")
    after, before = lax.rem(at + 1, line), lax.rem(at + line - 1, line)
    greet(*axes)
    pl.semaphore_signal(
        pltpu.get_barrier_semaphore(),
        inc=1,
        device_id={"seq": before, "mp": 1 - mine},
        device_id_type=pl.DeviceIdType.MESH,
    )
    rows = seqs * tokens
    half = rows // 2
    gather_start, gather_forward, gather_finish = relay(inputs, every, plane_sems, kept_sem)

    def load(step):
        slot = lax.rem(step, 2)
        side = jnp.where(lax.rem(step // 3, 2) == 0, mine, 1 - mine)
        return pltpu.make_async_copy(
            taps.at[step // 6, lax.rem(step, 3), pl.ds(pl.multiple_of(side * channels, 128), channels), :],
            weights.at[slot],
            weight_sems.at[slot],
        )

    def lanes_of(core):
        return pl.ds(pl.multiple_of(core * channels, 128), channels)

    own = pltpu.make_async_copy(inputs, both.at[0, :, lanes_of(mine)], pair_sems.at[0])
    give = remote(inputs, both.at[0, :, lanes_of(mine)], pair_sems.at[1], pair_sems.at[2], "mp", 1 - mine)
    take = remote(inputs, both.at[0, :, lanes_of(1 - mine)], pair_sems.at[1], pair_sems.at[2], "mp", 1 - mine)

    def edge(seq, other, arriving=False):
        core = jnp.where(other, 1 - mine, mine)
        return pltpu.make_async_remote_copy(
            src_ref=inputs.at[seq * tokens + tokens - EDGE : seq * tokens + tokens],
            dst_ref=edges.at[core if arriving else mine, seq],
            send_sem=edge_sems.at[0, other, seq],
            recv_sem=edge_sems.at[1, other, seq],
            device_id={"seq": after, "mp": core},
            device_id_type=pl.DeviceIdType.MESH,
        )

    load(0).start()
    own.start()
    pl.semaphore_wait(pltpu.get_barrier_semaphore(), sum(lax.axis_size(axis) - 1 for axis in axes) + 1)
    give.start()

    @pl.when(at < line - 1)
    def _():
        for seq in range(seqs):
            for other in range(2):
                edge(seq, other).start()

    @pl.when(at == 0)
    def _():
        edges[...] = jnp.zeros(edges.shape, BF16)

    gather_start()
    own.wait()

    def shift_down():
        width = 2 * channels
        steps = tokens // STEP

        def body(index, none):
            seq, tile = index // steps, lax.rem(index, steps)
            row = lax.broadcasted_iota(jnp.int32, (STEP, width), 0)
            place = pl.ds(pl.multiple_of(index * STEP, STEP), STEP)
            ahead = pl.ds(pl.multiple_of(jnp.maximum(index - 1, 0) * STEP, STEP), STEP)
            last = both[0, ahead, :].astype(F32)[STEP - 1 : STEP]
            outer = jnp.concatenate([edges[0, seq], edges[1, seq]], 1).astype(F32)[EDGE - 1 : EDGE]
            moved = pltpu.roll(both[0, place, :].astype(F32), 1, 0)
            both[1, place, :] = jnp.where(row == 0, jnp.where(tile == 0, outer, last), moved).astype(BF16)
            return none

        lax.fori_loop(0, rows // STEP, body, 0)

    def body(step, none):
        @pl.when(step == 3)
        def _():
            take.wait_recv()

        @pl.when(step == 6)
        def _():
            @pl.when(at > 0)
            def _():
                for seq in range(seqs):
                    for other in range(2):
                        edge(seq, other, True).wait_recv()

            shift_down()

        load(step).wait()

        @pl.when(step < 11)
        def _():
            load(step + 1).start()

        gate, part = lax.rem(step, 3), lax.rem(step // 3, 2)
        columns = lanes_of(jnp.where(part == 0, mine, 1 - mine))
        for side in range(2):
            place = pl.ds(side * half, half)
            term = jnp.dot(
                both[step // 6, place, columns], weights[lax.rem(step, 2)], preferred_element_type=F32
            )
            gates[gate, place, :] = jnp.where(step < 3, term, gates[gate, place, :] + term)
        return none

    lax.fori_loop(0, 12, body, 0)
    upd, fgt, out = gates.at[0], gates.at[1], gates.at[2]
    first_pass(seqs, tokens, channels, gates, bias, keep, upd, fgt, out, scale, shift, summary)
    copies = to_all(summary, slots, send_sems, recv_sems, "seq")
    gather_forward()
    saves = [
        pltpu.make_async_copy(src, dst, save_sems.at[number])
        for number, (src, dst) in enumerate(((upd, upd_out), (fgt, fgt_out), (out, out_out), (state, state_out), (hidden, hidden_out)))
    ]
    for copy in saves[:3]:
        copy.start()
    for copy in copies:
        copy.wait()
    entering[...] = from_earlier(slots, initial[...], slice(0, seqs), slice(seqs, 2 * seqs), "seq")
    sent = []
    for seq in range(seqs):
        states_pass(seq, tokens, channels, entering, out, scale, shift, state, hidden)
        part = pl.ds(seq * tokens, tokens)
        place = both_out.at[part, lanes_of(mine)]
        sent.append(pltpu.make_async_copy(hidden.at[part], place, pair_sems.at[3 + 3 * seq]))
        sent.append(remote(hidden.at[part], place, pair_sems.at[4 + 3 * seq], pair_sems.at[5 + 3 * seq], "mp", 1 - mine))
        for copy in sent[-2:]:
            copy.start()
    for copy in saves[3:]:
        copy.start()
    for copy in saves + sent:
        copy.wait()
    give.wait_send()

    @pl.when(at < line - 1)
    def _():
        for seq in range(seqs):
            for other in range(2):
                edge(seq, other).wait_send()

    gather_finish()


def upper_kernel(seqs, tokens, channels, full_hidden, hidden, mix, bias, keep, initial, cotangent, pooled, grads, planes, sums, every, weights, gates, state, entering, message, scale, shift, back_scale, back_shift, summary, slots, send_sems, recv_sems, weight_sems, plane_sems, kept_sem):
    greet("seq", "dp")
    half = seqs * tokens // 2
    gather_start, gather_forward, gather_finish = relay(hidden, every, plane_sems, kept_sem)

    def load(step):
        slot = lax.rem(step, 2)
        return pltpu.make_async_copy(
            mix.at[step // 2, pl.ds(pl.multiple_of(lax.rem(step, 2) * channels, 128), channels), :],
            weights.at[slot],
            weight_sems.at[slot],
        )

    load(0).start()
    met("seq", "dp")
    gather_start()

    def body(step, none):
        load(step).wait()

        @pl.when(step < 5)
        def _():
            load(step + 1).start()

        gate, part = step // 2, lax.rem(step, 2)
        columns = pl.ds(pl.multiple_of(part * channels, 128), channels)
        for side in range(2):
            place = pl.ds(side * half, half)
            term = jnp.dot(full_hidden[place, columns], weights[part], preferred_element_type=F32)
            gates[gate, place, :] = jnp.where(part == 0, term, gates[gate, place, :] + term)
        return none

    lax.fori_loop(0, 6, body, 0)
    upd, fgt, out = gates.at[0], gates.at[1], gates.at[2]
    first_pass(seqs, tokens, channels, gates, bias, keep, upd, fgt, out, scale, shift, summary)
    back_pass(seqs, tokens, channels, cotangent, keep, fgt, out, back_scale, back_shift, summary, 2 * seqs)
    copies = to_all(summary, slots, send_sems, recv_sems, "seq")
    gather_forward()
    for copy in copies:
        copy.wait()
    entering[...] = from_earlier(slots, initial[...], slice(0, seqs), slice(seqs, 2 * seqs), "seq")
    message[...] = from_later(
        slots, (seqs, channels), slice(2 * seqs, 3 * seqs), slice(3 * seqs, 4 * seqs), "seq"
    )
    for seq in range(seqs):
        states_pass(seq, tokens, channels, entering, out, scale, shift, state, pooled)
    grads_pass(seqs, tokens, channels, message, entering, cotangent, keep, upd, fgt, out, state, back_scale, back_shift, grads, planes, sums)
    gather_finish()


def lower_kernel(seqs, tokens, channels, above, above_columns, mix, keep, upd_in, fgt_in, out_in, state_in, entering, grads, sums, swapped, weights, total, coming, upd, fgt, out, state, message, scale, shift, summary, slots, send_sems, recv_sems, edges, arrived, edge_sems, weight_sems, load_sems, pair_sems, swap_sems):
    greet("seq", "dp", "mp")
    mine = lax.axis_index("mp")
    width = swapped.shape[2]

    def load(step):
        side = jnp.where(step < 3, 1 - mine, mine)
        slot = lax.rem(step, 2)
        return pltpu.make_async_copy(
            mix.at[lax.rem(step, 3), pl.ds(pl.multiple_of(side * channels, 128), channels), :],
            weights.at[slot],
            weight_sems.at[slot],
        )

    load(0).start()
    loads = [
        pltpu.make_async_copy(src, dst, load_sems.at[number])
        for number, (src, dst) in enumerate(((upd_in, upd), (fgt_in, fgt), (out_in, out), (state_in, state)))
    ]
    for copy in loads:
        copy.start()
    met("seq", "dp", "mp")
    plane = neighbours()
    swaps = []
    for steps in (3, 1, 2, 0):
        src = above_columns.at[:, pl.ds(pl.multiple_of(plane[steps] * width, 128), width)]
        dst = swapped.at[plane[0]]
        if steps:
            swaps.append(remote(src, dst, swap_sems.at[0, steps], swap_sems.at[1, steps], "dp", plane[steps]))
        else:
            swaps.append(pltpu.make_async_copy(src, dst, swap_sems.at[0, steps]))
        swaps[-1].start()
    give = remote(total.at[0], coming, pair_sems.at[0], pair_sems.at[1], "mp", 1 - mine)

    def body(step, none):
        load(step).wait()

        @pl.when(step < 5)
        def _():
            load(step + 1).start()

        side, gate = step // 3, lax.rem(step, 3)
        rows = above.shape[1] // 2
        for half in range(2):
            place = pl.ds(half * rows, rows)
            term = lax.dot_general(
                above[gate, place, :], weights[lax.rem(step, 2)], (((1,), (1,)), ((), ())), preferred_element_type=F32
            )
            total[side, place, :] = jnp.where(gate == 0, term, total[side, place, :] + term)

        @pl.when(step == 2)
        def _():
            give.start()

        return none

    lax.fori_loop(0, 6, body, 0)
    give.wait_recv()
    total[1] += coming[...]
    for copy in loads:
        copy.wait()
    upstream = total.at[1]
    back_pass(seqs, tokens, channels, upstream, keep, fgt, out, scale, shift, summary, 0)
    copies = to_all(summary, slots, send_sems, recv_sems, "seq")
    for copy in copies:
        copy.wait()
    message[...] = from_later(slots, (seqs, channels), slice(0, seqs), slice(seqs, 2 * seqs), "seq")
    grads_pass(seqs, tokens, channels, message, entering, upstream, keep, upd, fgt, out, state, scale, shift, grads, None, sums)
    pass_edges(seqs, tokens, grads, edges, arrived, edge_sems)
    give.wait_send()
    for steps, copy in zip((3, 1, 2, 0), swaps):
        if steps:
            copy.wait_send()
            place = swapped.at[plane[steps]]
            remote(place, place, swap_sems.at[0, steps], swap_sems.at[1, steps], "dp", plane[steps]).wait_recv()
        else:
            copy.wait()


def exchange_scratch(rows, channels):
    count = lax.axis_size("seq")
    return [
        pltpu.VMEM((rows, channels), F32),
        pltpu.VMEM((count - 1, rows, channels), F32),
        pltpu.SemaphoreType.DMA((count - 1,)),
        pltpu.SemaphoreType.DMA((count - 1,)),
    ]


def params(number):
    return pltpu.CompilerParams(collective_id=number, has_side_effects=True, vmem_limit_bytes=56 * 2**20)


def cost(elements, ops, moved):
    return pl.CostEstimate(flops=elements * ops, bytes_accessed=moved, transcendentals=elements * 3)


def pool_forward(seqs, tokens, gates, bias, keep, initial):
    channels = gates.shape[2]
    rows = seqs * tokens
    whole = jax.ShapeDtypeStruct((rows, channels), F32)
    return pl.pallas_call(
        functools.partial(forward_kernel, seqs, tokens, channels),
        out_shape=(
            jax.ShapeDtypeStruct((rows, channels), BF16),
            whole,
            whole,
            whole,
            whole,
            jax.ShapeDtypeStruct((seqs, channels), F32),
        ),
        in_specs=[VMEM] * 4,
        out_specs=[VMEM] * 6,
        scratch_shapes=[pltpu.VMEM((rows, channels), F32)] * 2 + exchange_scratch(2 * seqs, channels),
        compiler_params=params(1),
        cost_estimate=cost(rows * channels, 60, rows * channels * 30),
        name="pool_forward",
    )(gates, bias, keep, initial)


def pool_top(seqs, tokens, lanes, gates, bias, keep, initial, cotangent):
    channels = gates.shape[2]
    rows = seqs * tokens
    whole = pltpu.VMEM((rows, channels), F32)
    edge = pltpu.VMEM((seqs, channels), F32)
    return pl.pallas_call(
        functools.partial(top_kernel, seqs, tokens, channels),
        out_shape=(
            jax.ShapeDtypeStruct((rows, channels), BF16),
            jax.ShapeDtypeStruct((rows, lanes), BF16),
            jax.ShapeDtypeStruct((3, rows, channels), BF16),
            jax.ShapeDtypeStruct((3, SUB, channels), F32),
        ),
        in_specs=[VMEM] * 5,
        out_specs=[VMEM] * 4,
        scratch_shapes=[whole] * 4 + [edge] * 2 + [whole] * 4 + exchange_scratch(4 * seqs, channels),
        compiler_params=params(2),
        cost_estimate=cost(rows * channels, 120, rows * channels * 22),
        name="pool_top",
    )(gates, bias, keep, initial, cotangent)


def pool_first(seqs, tokens, inputs, taps, bias, keep, initial):
    rows, channels = inputs.shape
    whole = jax.ShapeDtypeStruct((rows, channels), F32)
    hbm = pl.BlockSpec(memory_space=pl.ANY)
    dma = pltpu.SemaphoreType.DMA
    return pl.pallas_call(
        functools.partial(first_kernel, seqs, tokens, channels),
        out_shape=(
            jax.ShapeDtypeStruct((rows, channels), BF16),
            whole,
            whole,
            whole,
            whole,
            jax.ShapeDtypeStruct((seqs, channels), F32),
            jax.ShapeDtypeStruct((rows, 2 * channels), BF16),
            jax.ShapeDtypeStruct((4, rows, channels), BF16),
        ),
        in_specs=[hbm, hbm, VMEM, VMEM, VMEM],
        out_specs=[hbm] * 5 + [VMEM, hbm, hbm],
        scratch_shapes=[
            pltpu.VMEM((2, rows, 2 * channels), BF16),
            pltpu.VMEM((2, seqs, EDGE, channels), BF16),
            pltpu.VMEM((2, channels, channels), BF16),
            pltpu.VMEM((3, rows, channels), F32),
            pltpu.VMEM((rows, channels), BF16),
        ]
        + [pltpu.VMEM((rows, channels), F32)] * 3
        + exchange_scratch(2 * seqs, channels)
        + [dma((2,)), dma((2, 4)), dma, dma((3 + 3 * seqs,)), dma((2, 2, seqs)), dma((5,))],
        compiler_params=params(7),
        cost_estimate=pl.CostEstimate(
            flops=24 * rows * channels * channels, bytes_accessed=rows * channels * 80, transcendentals=0
        ),
        name="pool_first",
    )(inputs, taps, bias, keep, initial)


def pool_upper(seqs, tokens, lanes, full_hidden, hidden, mix, bias, keep, initial, cotangent):
    rows, channels = hidden.shape
    whole = pltpu.VMEM((rows, channels), F32)
    edge = pltpu.VMEM((seqs, channels), F32)
    hbm = pl.BlockSpec(memory_space=pl.ANY)
    dma = pltpu.SemaphoreType.DMA
    return pl.pallas_call(
        functools.partial(upper_kernel, seqs, tokens, channels),
        out_shape=(
            jax.ShapeDtypeStruct((rows, channels), BF16),
            jax.ShapeDtypeStruct((rows, lanes), BF16),
            jax.ShapeDtypeStruct((3, rows, channels), BF16),
            jax.ShapeDtypeStruct((3, SUB, channels), F32),
            jax.ShapeDtypeStruct((4, rows, channels), BF16),
        ),
        in_specs=[VMEM, hbm, hbm, VMEM, VMEM, VMEM, VMEM],
        out_specs=[VMEM] * 4 + [hbm],
        scratch_shapes=[pltpu.VMEM((2, channels, channels), BF16), pltpu.VMEM((3, rows, channels), F32), whole, edge, edge]
        + [whole] * 4
        + exchange_scratch(4 * seqs, channels)
        + [dma((2,)), dma((2, 4)), dma],
        compiler_params=params(6),
        cost_estimate=pl.CostEstimate(
            flops=12 * rows * channels * channels, bytes_accessed=rows * channels * 40, transcendentals=0
        ),
        name="pool_upper",
    )(full_hidden, hidden, mix, bias, keep, initial, cotangent)


def pool_backward(seqs, tokens, lanes, upstream, keep, upd, fgt, out, state, entering):
    rows, channels = upstream.shape
    whole = pltpu.VMEM((rows, channels), F32)
    return pl.pallas_call(
        functools.partial(backward_kernel, seqs, tokens, channels),
        out_shape=(
            jax.ShapeDtypeStruct((rows + EDGE, lanes), BF16),
            jax.ShapeDtypeStruct((3, SUB, channels), F32),
        ),
        in_specs=[VMEM] * 7,
        out_specs=[VMEM] * 2,
        scratch_shapes=[pltpu.VMEM((seqs, channels), F32)]
        + [whole] * 2
        + exchange_scratch(2 * seqs, channels)
        + [pltpu.VMEM((EDGE, lanes), BF16)] * 2
        + [pltpu.SemaphoreType.DMA((2,))],
        compiler_params=params(3),
        cost_estimate=cost(rows * channels, 60, rows * channels * 26),
        name="pool_backward",
    )(upstream, keep, upd, fgt, out, state, entering)


def pool_lower(seqs, tokens, above, above_columns, mix, keep, upd, fgt, out, state, entering):
    rows, channels = upd.shape
    lanes = above_columns.shape[1]
    whole = pltpu.VMEM((rows, channels), F32)
    hbm = pl.BlockSpec(memory_space=pl.ANY)
    dma = pltpu.SemaphoreType.DMA
    return pl.pallas_call(
        functools.partial(lower_kernel, seqs, tokens, channels),
        out_shape=(
            jax.ShapeDtypeStruct((rows + EDGE, lanes), BF16),
            jax.ShapeDtypeStruct((3, SUB, channels), F32),
            jax.ShapeDtypeStruct((4, rows, lanes // 4), BF16),
        ),
        in_specs=[VMEM, hbm, hbm, VMEM, hbm, hbm, hbm, hbm, VMEM],
        out_specs=[VMEM, VMEM, hbm],
        scratch_shapes=[
            pltpu.VMEM((2, channels, channels), BF16),
            pltpu.VMEM((2, rows, channels), F32),
            whole,
            whole,
            whole,
            whole,
            whole,
            pltpu.VMEM((seqs, channels), F32),
            whole,
            whole,
        ]
        + exchange_scratch(2 * seqs, channels)
        + [pltpu.VMEM((EDGE, lanes), BF16)] * 2
        + [dma((2,)), dma((2,)), dma((4,)), dma((2,)), dma((2, 4))],
        compiler_params=params(5),
        cost_estimate=pl.CostEstimate(
            flops=12 * rows * channels * channels, bytes_accessed=rows * channels * 40, transcendentals=0
        ),
        name="pool_lower",
    )(above, above_columns, mix, keep, upd, fgt, out, state, entering)


def shift_up(seqs, tokens, value, edges, result):
    width = value.shape[1]
    steps = tokens // STEP

    def body(index, none):
        sequence, at = index // steps, lax.rem(index, steps)
        row = lax.broadcasted_iota(jnp.int32, (STEP, width), 0)
        rows = pl.ds(pl.multiple_of(index * STEP, STEP), STEP)
        after = jnp.minimum(index + 1, value.shape[0] // STEP - 1)
        first = value[pl.ds(pl.multiple_of(after * STEP, STEP), STEP), :].astype(F32)[0:1]
        edge = edges[sequence // seqs].astype(F32)
        edge = jnp.where(lax.rem(sequence, seqs) == 0, edge[0:1], edge[1:2])
        moved = pltpu.roll(value[rows, :].astype(F32), STEP - 1, 0)
        moved = jnp.where(row == STEP - 1, jnp.where(at == steps - 1, edge, first), moved)
        result[rows, :] = moved.astype(BF16)
        return none

    lax.fori_loop(0, value.shape[0] // STEP, body, 0)


def spread_kernel(seqs, tokens, parts, turn, tail, hidden, full, grads_two, grads_one, taps, sums, out, input_grad, sums_out, rows_full, grads, grads_edge, moved, own, ups, downs, acc, across, around, every, weights, leaving, coming, load_sems, swap_sems, up_sems, down_sems, line_send, line_recv, column_send, column_recv, kept_sems, plane_send, plane_recv, sums_sems, weight_sems, leaving_sems, coming_sems, result_sems, pair_sems, ready_sem):
    line, plane = lax.axis_size("seq"), lax.axis_size("dp")
    at, here = lax.axis_index("seq"), lax.axis_index("dp")
    unit = line * parts
    units = own.shape[0] // unit
    blocks = units // 3
    width = own.shape[1]
    block_rows = seqs * tokens
    half = unit // 2
    here, beside, below, across_from = neighbours()
    mine = lax.axis_index("mp")
    greet("seq", "dp", "mp")
    met("seq", "dp", "mp")

    def turned(u):
        return lax.rem(u, turn) == turn - 1

    def direct(u):
        return lax.rem(u, turn) != turn - 1

    wide = rows_full.shape[1] // 2

    def own_rows(value, number, way):
        place = rows_full.at[:, pl.ds(pl.multiple_of(mine * wide, 128), wide)]
        if way == 0:
            return pltpu.make_async_copy(value, place, load_sems.at[number])
        return remote(value, place, pair_sems.at[0, number], pair_sems.at[1, number], "mp", 1 - mine)

    def other_rows(number):
        place = rows_full.at[:, pl.ds(pl.multiple_of((1 - mine) * wide, 128), wide)]
        return remote(place, place, pair_sems.at[0, number], pair_sems.at[1, number], "mp", 1 - mine)

    def plane_rows(owner):
        return pl.ds(pl.multiple_of(owner * block_rows, 16), block_rows)

    def peer(steps):
        return (here, beside, below, across_from)[steps]

    def load_two():
        return pltpu.make_async_copy(grads_two, moved, load_sems.at[2])

    def swap(steps, edge, arriving=False):
        columns = pl.ds(pl.multiple_of(peer(steps) * width, 128), width)
        source = peer(steps) if arriving else here
        if edge:
            src, dst = grads_one.at[block_rows : block_rows + EDGE, columns], grads_edge.at[source]
        else:
            src, dst = grads_one.at[0:block_rows, columns], grads.at[plane_rows(source)]
        number = steps * 2 + edge
        if steps == 0:
            return pltpu.make_async_copy(src, dst, swap_sems.at[0, number])
        return remote(src, dst, swap_sems.at[0, number], swap_sems.at[1, number], "dp", peer(steps))

    def product(block, right):
        columns = pl.ds(pl.multiple_of(jnp.where(mine == 0, block, blocks - 1 - block) * unit, 128), unit)
        return lax.dot_general(
            rows_full[:, columns], right[...], (((0,), (0,)), ((), ())), preferred_element_type=F32
        ).astype(BF16)

    narrow = leaving.shape[2]
    pieces = wide // narrow

    def load_weights(step):
        first = jnp.where(step < pieces, (1 - mine) * pieces + step, mine * pieces + step - pieces) * narrow
        slot = lax.rem(step, 2)
        return pltpu.make_async_copy(
            taps.at[:, :, pl.ds(pl.multiple_of(first, narrow), narrow), :], weights.at[slot], weight_sems.at[slot]
        )

    def load_every():
        return pltpu.make_async_copy(grads_one, every, load_sems.at[3])

    def leave(step):
        slot = lax.rem(step, 2)
        return remote(leaving.at[slot], coming.at[step], leaving_sems.at[slot], coming_sems.at[step], "mp", 1 - mine)

    def result(step):
        return pltpu.make_async_copy(
            coming.at[step],
            input_grad.at[:, pl.ds(pl.multiple_of(step * narrow, narrow), narrow)],
            result_sems.at[step],
        )

    def input_terms(slot):
        channels = taps.shape[3]
        now = jnp.zeros((block_rows, narrow), F32)
        late = jnp.zeros((block_rows + EDGE, narrow), F32)
        for gate in range(3):
            lanes = slice(gate * channels, gate * channels + channels)
            now += lax.dot_general(
                every[:block_rows, lanes], weights[slot, 0, gate], (((1,), (1,)), ((), ())), preferred_element_type=F32
            )
            late += lax.dot_general(
                every[:, lanes], weights[slot, 1, gate], (((1,), (1,)), ((), ())), preferred_element_type=F32
            )
        row = lax.broadcasted_iota(jnp.int32, now.shape, 0)
        after = pltpu.roll(late[:block_rows], block_rows - 1, 0)
        for seq in range(seqs):
            after = jnp.where(
                row == seq * tokens + tokens - 1, late[block_rows + seq : block_rows + seq + 1], after
            )
        return now + after

    def whole(u):
        return pl.ds(pl.multiple_of(u * unit, unit), unit)

    def chunk(u, j):
        return pl.ds(pl.multiple_of(u * unit + j * parts, parts), parts)

    def up(src, u, j):
        number = u * (line - 1) + j - 1
        return remote(src, ups.at[u, j - 1], up_sems.at[0, number], up_sems.at[1, number], "seq", lax.rem(at + 1, line))

    def down(src, u, j):
        number = u * (line - 1) + j
        return remote(
            src, downs.at[u, j], down_sems.at[0, number], down_sems.at[1, number], "seq", lax.rem(at + line - 1, line)
        )

    def along(src, u, j, way, hop):
        return remote(
            src,
            out.at[here, chunk(u, j)],
            line_send.at[(u * 2 + way) * (line - 1) + hop],
            line_recv.at[u * line + j],
            "seq",
            lax.rem(at + (1 if way == 0 else line - 1), line),
        )

    def column(src, steps, u, j, way, hop):
        number = u // turn * 4 + steps
        return remote(
            src,
            out.at[peer(steps), chunk(u, j)],
            column_send.at[(number * 2 + way) * (line - 1) + hop],
            column_recv.at[number * line + j],
            "seq",
            lax.rem(at + (1 if way == 0 else line - 1), line),
        )

    def over_part(src, u, way):
        return remote(
            src,
            out.at[here, chunk(u, at)],
            plane_send.at[u * 4 + way],
            plane_recv.at[u * 4 + way],
            "dp",
            (beside, below)[way],
        )

    def onward_part(owner, u, way):
        place = out.at[owner, pl.ds(pl.multiple_of(u * unit + at * parts + way * (parts // 2), 16), parts // 2)]
        return remote(
            place, place, plane_send.at[u * 4 + 2 + way], plane_recv.at[u * 4 + 2 + way], "dp", (below, beside)[way]
        )

    def keep(u):
        return pltpu.make_async_copy(own.at[chunk(u, at)], out.at[here, chunk(u, at)], kept_sems.at[u])

    def rows(u, first, count):
        return pl.ds(pl.multiple_of(u * unit + first, half), count)

    def over(u, way):
        place = out.at[here, rows(u, 0, unit)]
        return remote(place, place, plane_send.at[u * 4 + way], plane_recv.at[u * 4 + way], "dp", (beside, below)[way])

    def onward(u, way):
        place = out.at[(beside, below)[way], rows(u, way * half, half)]
        return remote(
            place, place, plane_send.at[u * 4 + 2 + way], plane_recv.at[u * 4 + 2 + way], "dp", (below, beside)[way]
        )

    def corner(u, way):
        place = out.at[across_from, rows(u, way * half, half)]
        return remote(place, place, plane_send.at[u * 4 + 2 + way], plane_recv.at[u * 4 + 2 + way], "dp", (below, beside)[way])

    def sums_copy(slots, me, count, axis, number, step):
        return remote(
            slots.at[me],
            slots.at[me],
            sums_sems.at[number, 0, step - 1],
            sums_sems.at[number, 1, step - 1],
            axis,
            lax.rem(me + step, count),
        )

    def sums_arrival(slots, me, count, axis, number, step):
        place = slots.at[lax.rem(me + count - step, count)]
        return remote(place, place, sums_sems.at[number, 0, step - 1], sums_sems.at[number, 1, step - 1], axis, lax.rem(me + step, count))

    for way in range(2):
        own_rows(hidden, 0, way).start()
    load_two().start()
    for steps in range(4):
        for edge in range(2):
            swap(steps, edge).start()
    load_every().start()
    load_weights(0).start()
    across[at] = sums[...]
    for step in range(1, line):
        sums_copy(across, at, line, "seq", 0, step).start()
    load_two().wait()
    own_rows(hidden, 0, 0).wait()

    def stage(index, none):
        @pl.when(index == 1)
        def _():
            for step in range(1, line):
                sums_arrival(across, at, line, "seq", 0, step).wait_recv()
            total = across[0]
            for other in range(1, line):
                total = total + across[other]
            around[here] = total
            for step in range(1, plane):
                sums_copy(around, here, plane, "dp", 1, step).start()

        @pl.when(index == 3)
        def _():
            for step in range(1, plane):
                sums_arrival(around, here, plane, "dp", 1, step).wait_recv()
            total = around[0]
            for other in range(1, plane):
                total = total + around[other]
            sums_out[...] = total

        @pl.when(index == wide // unit)
        def _():
            other_rows(0).wait_recv()

        @pl.when(index == blocks + 2 * (wide // unit))
        def _():
            other_rows(1).wait_recv()

        @pl.when(index < blocks)
        def _():
            own[whole(index), :] = product(index, moved)

        @pl.when(index == blocks - 1)
        def _():
            own_rows(hidden, 0, 1).wait_send()
            own_rows(full, 1, 0).start()
            pl.semaphore_signal(ready_sem, inc=1, device_id={"mp": 1 - mine}, device_id_type=pl.DeviceIdType.MESH)
            pl.semaphore_wait(ready_sem, 1)
            own_rows(full, 1, 1).start()

        @pl.when(index == blocks)
        def _():
            for steps in range(4):
                for edge in range(2):
                    if steps:
                        swap(steps, edge, True).wait_recv()
                    else:
                        swap(steps, edge).wait()
            shift_up(seqs, tokens, grads, grads_edge, moved)
            own_rows(full, 1, 0).wait()
            load_every().wait()

        @pl.when((index >= blocks) & (index < units) & (lax.rem(index - blocks, 2) == 0))
        def _():
            own[whole(index), :] = product((index - blocks) // 2, grads)

        @pl.when((index >= blocks) & (index < units) & (lax.rem(index - blocks, 2) == 1))
        def _():
            own[whole(index), :] = product((index - blocks) // 2, moved)

        k = index - blocks

        @pl.when((k >= 0) & (k < 2 * pieces))
        def _():
            load_weights(k).wait()

            @pl.when(k + 1 < 2 * pieces)
            def _():
                load_weights(k + 1).start()

            terms = input_terms(lax.rem(k, 2))

            @pl.when(k < pieces)
            def _():
                @pl.when(k >= 2)
                def _():
                    leave(k - 2).wait_send()

                leaving[lax.rem(k, 2)] = terms
                leave(k).start()

            @pl.when(k >= pieces)
            def _():
                leave(k - pieces).wait_recv()
                coming[k - pieces] += terms
                result(k - pieces).start()

        u = index - at

        @pl.when((u >= 0) & (u < units))
        def _():
            for j in range(line - 1, 0, -1):

                @pl.when(at == 0)
                def _(j=j):
                    up(own.at[chunk(u, j)], u, j).start()

                @pl.when((at > 0) & (at <= j))
                def _(j=j):
                    up(ups.at[u, j - 1], u, j).wait_recv()

                @pl.when((at > 0) & (at < j))
                def _(j=j):
                    ups[u, j - 1] = (ups[u, j - 1].astype(F32) + own[chunk(u, j)].astype(F32)).astype(BF16)
                    up(ups.at[u, j - 1], u, j).start()

        v = index - (line - 1 - at)

        @pl.when((v >= 0) & (v < units))
        def _():
            for j in range(line - 1):

                @pl.when(at == line - 1)
                def _(j=j):
                    down(own.at[chunk(v, j)], v, j).start()

                @pl.when((at < line - 1) & (at >= j))
                def _(j=j):
                    down(downs.at[v, j], v, j).wait_recv()

                @pl.when((at < line - 1) & (at > j))
                def _(j=j):
                    downs[v, j] = (downs[v, j].astype(F32) + own[chunk(v, j)].astype(F32)).astype(BF16)
                    down(downs.at[v, j], v, j).start()

        w = index - (line - 1)

        @pl.when((w >= 0) & (w < units))
        def _():
            acc[...] = own[chunk(w, at)].astype(F32)

            @pl.when(at > 0)
            def _():
                acc[...] += ups[w, at - 1].astype(F32)

            @pl.when(at < line - 1)
            def _():
                acc[...] += downs[w, at].astype(F32)

            own[chunk(w, at)] = acc[...].astype(BF16)
            keep(w).start()

            @pl.when(direct(w) & (at < line - 1))
            def _():
                along(own.at[chunk(w, at)], w, at, 0, 0).start()

            @pl.when(direct(w) & (at > 0))
            def _():
                along(own.at[chunk(w, at)], w, at, 1, 0).start()

            @pl.when(turned(w))
            def _():
                for way in range(2):
                    over_part(own.at[chunk(w, at)], w, way).start()

        c = index - line

        @pl.when((c >= 0) & (c < units) & turned(c))
        def _():
            keep(c).wait()
            for way in range(2):
                over_part(out.at[(beside, below)[way], chunk(c, at)], c, way).wait_recv()
                onward_part((beside, below)[way], c, way).start()

        d = index - line - 1

        @pl.when((d >= 0) & (d < units) & turned(d))
        def _():
            for way in range(2):
                onward_part(across_from, d, way).wait_recv()

        for steps in range(4):
            for hop in range(line):
                e = index - line - 1 - steps - hop

                @pl.when((e >= 0) & (e < units) & turned(e))
                def _(e=e, steps=steps, hop=hop):
                    @pl.when(at >= hop)
                    def _():
                        src = out.at[peer(steps), chunk(e, at - hop)]
                        if hop:
                            column(src, steps, e, at - hop, 0, 0).wait_recv()
                        if hop < line - 1:

                            @pl.when(at < line - 1)
                            def _():
                                column(src, steps, e, at - hop, 0, hop).start()

                    @pl.when(at + hop < line)
                    def _():
                        src = out.at[peer(steps), chunk(e, at + hop)]
                        if hop:
                            column(src, steps, e, at + hop, 1, 0).wait_recv()
                        if hop < line - 1:

                            @pl.when(at > 0)
                            def _():
                                column(src, steps, e, at + hop, 1, hop).start()

        for hop in range(1, line):
            x = index - (line - 1) - hop

            @pl.when((x >= 0) & (x < units) & direct(x))
            def _(x=x, hop=hop):
                @pl.when(at >= hop)
                def _():
                    src = out.at[here, chunk(x, at - hop)]
                    along(src, x, at - hop, 0, 0).wait_recv()
                    if hop < line - 1:

                        @pl.when(at < line - 1)
                        def _():
                            along(src, x, at - hop, 0, hop).start()

                @pl.when(at + hop < line)
                def _():
                    src = out.at[here, chunk(x, at + hop)]
                    along(src, x, at + hop, 1, 0).wait_recv()
                    if hop < line - 1:

                        @pl.when(at > 0)
                        def _():
                            along(src, x, at + hop, 1, hop).start()

        y = index - 2 * (line - 1)

        @pl.when((y >= 0) & (y < units) & direct(y))
        def _():
            keep(y).wait()

        @pl.when((y >= 0) & (y < units - tail) & direct(y))
        def _():
            over(y, 0).start()
            over(y, 1).start()

        z = y - LAG

        @pl.when((z >= 0) & (z < units - tail) & direct(z))
        def _():
            for way in range(2):
                place = out.at[(beside, below)[way], rows(z, 0, unit)]
                remote(place, place, plane_send.at[z * 4 + way], plane_recv.at[z * 4 + way], "dp", (beside, below)[way]).wait_recv()
                onward(z, way).start()

        t = z - LAG

        @pl.when((t >= 0) & (t < units - tail) & direct(t))
        def _():
            for way in range(2):
                corner(t, way).wait_recv()

        return none

    last_turned = units // turn * turn - 1
    lax.fori_loop(
        0, max(units + 2 * (line - 1), units - tail + 2 * (line - 1) + 2 * LAG, last_turned + 2 * line + 4), stage, 0
    )

    def settle(u, none):
        for j in range(1, line):

            @pl.when(at < j)
            def _(j=j):
                up(ups.at[u, j - 1], u, j).wait_send()

        for j in range(line - 1):

            @pl.when(at > j)
            def _(j=j):
                down(downs.at[u, j], u, j).wait_send()

        for hop in range(line - 1):

            @pl.when(direct(u) & (at >= hop) & (at < line - 1))
            def _(hop=hop):
                along(out.at[here, chunk(u, at - hop)], u, at - hop, 0, hop).wait_send()

            @pl.when(direct(u) & (at + hop < line) & (at > 0))
            def _(hop=hop):
                along(out.at[here, chunk(u, at + hop)], u, at + hop, 1, hop).wait_send()

            @pl.when(turned(u) & (at >= hop) & (at < line - 1))
            def _(hop=hop):
                for steps in range(4):
                    column(out.at[here, chunk(u, at - hop)], steps, u, at - hop, 0, hop).wait_send()

            @pl.when(turned(u) & (at + hop < line) & (at > 0))
            def _(hop=hop):
                for steps in range(4):
                    column(out.at[here, chunk(u, at + hop)], steps, u, at + hop, 1, hop).wait_send()

        @pl.when(direct(u) & (u < units - tail))
        def _():
            for way in range(2):
                over(u, way).wait_send()
                onward(u, way).wait_send()

        @pl.when(turned(u))
        def _():
            for way in range(2):
                over_part(out.at[here, chunk(u, at)], u, way).wait_send()
                onward_part(here, u, way).wait_send()

        return none

    lax.fori_loop(0, units, settle, 0)
    for steps in range(1, 4):
        for edge in range(2):
            swap(steps, edge).wait_send()
    own_rows(full, 1, 1).wait_send()
    for step in range(pieces - 2, pieces):
        leave(step).wait_send()
    for step in range(pieces):
        result(step).wait()
    for step in range(1, line):
        sums_copy(across, at, line, "seq", 0, step).wait_send()
    for step in range(1, plane):
        sums_copy(around, here, plane, "dp", 1, step).wait_send()


def spread(seqs, tokens, hidden, full, grads_two, grads_one, taps, sums):
    line, plane = lax.axis_size("seq"), lax.axis_size("dp")
    width = grads_two.shape[1]
    rows = grads_two.shape[0] // plane
    depth = 2 * full.shape[1]
    units = 3 * depth // (line * PART)
    channels = taps.shape[3]
    narrow = depth // (units - units // 3)
    pieces = channels // narrow
    turns = units // TURN
    dma = pltpu.SemaphoreType.DMA
    hbm = pl.BlockSpec(memory_space=pl.ANY)
    return pl.pallas_call(
        functools.partial(spread_kernel, seqs, tokens, PART, TURN, TAIL),
        out_shape=(
            jax.ShapeDtypeStruct((plane, 3 * depth, width), BF16),
            jax.ShapeDtypeStruct((rows, channels), F32),
            jax.ShapeDtypeStruct(sums.shape, F32),
        ),
        in_specs=[hbm] * 5 + [VMEM],
        out_specs=[hbm, hbm, VMEM],
        scratch_shapes=[
            pltpu.VMEM((plane * rows, depth), BF16),
            pltpu.VMEM((plane * rows, width), BF16),
            pltpu.VMEM((plane, EDGE, width), BF16),
            pltpu.VMEM((plane * rows, width), BF16),
            pltpu.VMEM((3 * depth, width), BF16),
            pltpu.VMEM((units, line - 1, PART, width), BF16),
            pltpu.VMEM((units, line - 1, PART, width), BF16),
            pltpu.VMEM((PART, width), F32),
            pltpu.VMEM((line,) + sums.shape, F32),
            pltpu.VMEM((plane,) + sums.shape, F32),
            pltpu.VMEM(grads_one.shape, BF16),
            pltpu.VMEM((2, 2, 3, narrow, channels), BF16),
            pltpu.VMEM((2, rows, narrow), F32),
            pltpu.VMEM((pieces, rows, narrow), F32),
            dma((4,)),
            dma((2, 8)),
            dma((2, units * (line - 1))),
            dma((2, units * (line - 1))),
            dma((units * 2 * (line - 1),)),
            dma((units * line,)),
            dma((turns * 4 * 2 * (line - 1),)),
            dma((turns * 4 * line,)),
            dma((units,)),
            dma((units * 4,)),
            dma((units * 4,)),
            dma((2, 2, max(line, plane) - 1)),
            dma((2,)),
            dma((2,)),
            dma((pieces,)),
            dma((pieces,)),
            dma((2, 2)),
            pltpu.SemaphoreType.REGULAR,
        ],
        compiler_params=pltpu.CompilerParams(
            collective_id=4, has_side_effects=True, vmem_limit_bytes=62 * 2**20
        ),
        cost_estimate=pl.CostEstimate(
            flops=6 * plane * rows * depth * width, bytes_accessed=depth * width * 48, transcendentals=0
        ),
        name="spread",
    )(hidden, full, grads_two, grads_one, taps, sums)


def widen_kernel(blocks, core, given, *refs):
    out = refs[-1]
    per = given.shape[2] // 128
    for tile in range(3 * blocks):
        source, place = divmod(tile, per)
        gate, column = divmod(tile, blocks)
        out[0, gate, :, column * 128 : column * 128 + 128] = given[
            source, :, place * 128 : place * 128 + 128
        ].astype(F32)


def widen(gathered, first, taps, start, count, depth, channels, unit, core, into=None):
    plane, _, width = gathered.shape
    last = depth // unit - 1

    def source(tap, step, core):
        return (0, first + step * taps + tap, 0)

    def target(tap, step, core):
        block = start + step
        return (tap, 0, jnp.where(core[0] == 0, block, last - block), 0)

    given = (core, gathered) if into is None else (core, gathered, into)
    return pl.pallas_call(
        functools.partial(widen_kernel, channels // 128),
        grid_spec=pltpu.PrefetchScalarGridSpec(
            num_scalar_prefetch=1,
            grid=(taps, count),
            in_specs=[pl.BlockSpec((plane, unit, width), source)] + [pl.BlockSpec(memory_space=pl.ANY)] * (len(given) - 2),
            out_specs=pl.BlockSpec((1, 3, unit, channels), target),
        ),
        out_shape=jax.ShapeDtypeStruct((taps, 3, depth, channels), F32),
        input_output_aliases={} if into is None else {2: 0},
        compiler_params=pltpu.CompilerParams(vmem_limit_bytes=40 * 2**20),
        cost_estimate=pl.CostEstimate(
            flops=0, bytes_accessed=taps * count * unit * (plane * width * 2 + channels * 12), transcendentals=0
        ),
        name="widen",
    )(*given)


def shifted(value, axis, steps):
    count = lax.axis_size(axis)
    initial, last = (max(0, -steps), min(count, count - steps))
    return lax.ppermute(value, axis, [(source, source + steps) for source in range(initial, last)])


def gather_channels(value):
    count = lax.axis_size("mp")
    if count != 2:
        return lax.all_gather(value, "mp", axis=value.ndim - 1, tiled=True)
    other = lax.ppermute(value, "mp", [(0, 1), (1, 0)])
    second = lax.axis_index("mp") == 1
    return jnp.concatenate([jnp.where(second, other, value), jnp.where(second, value, other)], value.ndim - 1)


def sum_channels(terms):
    count = lax.axis_size("mp")
    if count != 2:
        return lax.psum_scatter(terms, "mp", scatter_dimension=1, tiled=True)
    width = terms.shape[1] // 2
    second = lax.axis_index("mp") == 1
    low, high = terms[:, :width], terms[:, width:]
    other = lax.ppermute(jnp.where(second, low, high), "mp", [(0, 1), (1, 0)])
    return jnp.where(second, high, low) + other


def dot(lhs, rhs, dims):
    return lax.dot_general(lhs, rhs, (dims, ((), ())), preferred_element_type=F32)


def reduce_weights(partial):
    shard = lax.psum_scatter(partial.astype(BF16), ("dp", "seq"), scatter_dimension=0, tiled=True)
    return lax.all_gather(shard, ("dp", "seq"), axis=0, tiled=True).astype(F32)


def local(inputs, starts, init_state, weight_one, bias_one, weight_two, bias_two, cotangent):
    seqs, tokens, channels = inputs.shape
    rows = seqs * tokens
    width = weight_one.shape[1]
    keep = jnp.broadcast_to((1 - starts).astype(F32).reshape(rows, 1), (rows, 128))
    taps = weight_one.transpose(0, 2, 1, 3)
    mix = weight_two.transpose(1, 0, 2)

    line, plane = lax.axis_size("seq"), lax.axis_size("dp")
    tiles = 3 * channels // 128
    spreads = plane == 4 and lax.axis_size("mp") == 2 and seqs == 2 and channels % 128 == 0
    spreads = spreads and width % (line * PART) == 0 and line > 1
    block = -(-tiles // plane) * 128
    lanes = plane * block if spreads else 3 * channels
    upstream = cotangent.reshape(rows, channels)
    if spreads:
        hidden, upd, fgt, out, state, entering, full_hidden, every = pool_first(
            seqs, tokens, inputs.reshape(rows, channels), taps, bias_one, keep, init_state[0]
        )
        pooled_two, grad_two, planes_two, sums_two, every_hidden = pool_upper(
            seqs, tokens, lanes, full_hidden, hidden, mix, bias_two, keep, init_state[1], upstream
        )
        extended, sums_one, swapped = pool_lower(
            seqs, tokens, planes_two, grad_two, mix, keep, upd, fgt, out, state, entering
        )
        sums = jnp.concatenate([jnp.sum(sums_one, 1), jnp.sum(sums_two, 1)])
        gathered, input_grad, sums = spread(
            seqs,
            tokens,
            every_hidden.reshape(plane * rows, channels),
            every.reshape(plane * rows, channels),
            swapped.reshape(plane * rows, block),
            extended,
            taps,
            sums,
        )
        unit = line * PART
        blocks = width // unit
        core = lax.axis_index("mp").reshape(1)
        behind = TAIL // 2
        kept = lax.dynamic_slice(
            gathered, (lax.axis_index("dp"), (3 * blocks - TAIL) * unit, 0), (1, TAIL * unit, block)
        )
        tail = lax.all_gather(kept, "dp", axis=0, tiled=True)
        weight_two_grad = widen(gathered, 0, 1, 0, blocks, width, channels, unit, core)
        weight_one_grad = widen(gathered, blocks, 2, 0, blocks - behind, width, channels, unit, core)
        weight_one_grad = widen(
            tail, 0, 2, blocks - behind, behind, width, channels, unit, core, weight_one_grad
        )
        weight_two_grad = weight_two_grad[0].transpose(1, 0, 2)
        weight_one_grad = weight_one_grad.transpose(0, 2, 1, 3)
    else:
        edge = gather_channels(shifted(inputs[:, -1], "seq", 1))
        full = gather_channels(inputs)
        previous = jnp.concatenate([edge[:, None], full[:, :-1]], 1).reshape(rows, width)
        full = full.reshape(rows, width)
        both = jnp.concatenate([full, previous], 1)
        gates_one = jnp.einsum(
            "tkd,kgdc->gtc", both.reshape(rows, 2, width), taps, preferred_element_type=F32
        )
        hidden, upd, fgt, out, state, entering = pool_forward(seqs, tokens, gates_one, bias_one, keep, init_state[0])
        full_hidden = gather_channels(hidden)
        gates_two = jnp.einsum("td,gdc->gtc", full_hidden, mix, preferred_element_type=F32)
        pooled_two, grad_two, planes_two, sums_two = pool_top(
            seqs, tokens, lanes, gates_two, bias_two, keep, init_state[1], upstream
        )
        hidden_terms = jnp.einsum("gtc,gdc->td", planes_two, mix, preferred_element_type=F32)
        hidden_grad = sum_channels(hidden_terms)
        extended, sums_one = pool_backward(seqs, tokens, lanes, hidden_grad, keep, upd, fgt, out, state, entering)
        grad_one = extended[:rows]
        input_terms = jnp.einsum(
            "tgc,kgdc->ktd", grad_one.reshape(rows, 3, channels), taps, preferred_element_type=F32
        ).reshape(2, seqs, tokens, width)
        late = input_terms[1]
        late = jnp.concatenate([late[:, 1:], shifted(late[:, 0], "seq", -1)[:, None]], 1)
        input_grad = sum_channels((input_terms[0] + late).reshape(rows, width))
        sums = jnp.concatenate([jnp.sum(sums_one, 1), jnp.sum(sums_two, 1)])
        sums = lax.psum(sums, ("dp", "seq"))
        weight_two_grad = reduce_weights(dot(full_hidden, grad_two, ((0,), (0,)))).reshape(width, 3, channels)
        weight_one_grad = jnp.stack(
            [
                reduce_weights(dot(full, grad_one, ((0,), (0,)))),
                reduce_weights(dot(previous, grad_one, ((0,), (0,)))),
            ]
        ).reshape(2, width, 3, channels)
    return (
        pooled_two.reshape(seqs, tokens, channels),
        input_grad.reshape(seqs, tokens, channels),
        weight_one_grad,
        sums[:3],
        weight_two_grad,
        sums[3:],
    )


def solution(mesh):
    return jax.shard_map(
        local,
        mesh=mesh,
        in_specs=(
            P("dp", "seq", "mp"),
            P("dp", "seq"),
            P(None, "dp", "mp"),
            P(None, None, None, "mp"),
            P(None, "mp"),
            P(None, None, "mp"),
            P(None, "mp"),
            P("dp", "seq", "mp"),
        ),
        out_specs=(
            P("dp", "seq", "mp"),
            P("dp", "seq", "mp"),
            P(None, None, None, "mp"),
            P(None, "mp"),
            P(None, None, "mp"),
            P(None, "mp"),
        ),
        check_vma=False,
    )
```

```python
import functools

import jax
import jax.numpy as jnp
from jax import lax
from jax.experimental import pallas as pl
from jax.experimental.pallas import tpu as pltpu
from jax.sharding import PartitionSpec as P

F32 = jnp.float32
BF16 = jnp.bfloat16
SUB = 8
STEP = 16
EDGE = 16
PART = 64
LAG = 2
TURN = 4
TAIL = 2
VMEM = pl.BlockSpec(memory_space=pltpu.VMEM)


def sigmoid(x):
    return 0.5 * jnp.tanh(0.5 * x) + 0.5


def lane_blocks(channels):
    width = 384 if channels % 384 == 0 else channels
    return [slice(at, at + width) for at in range(0, channels, width)]


def scan_down(scale, shift):
    row = lax.broadcasted_iota(jnp.int32, scale.shape, 0)
    for step in (1, 2, 4):
        earlier = row >= step
        scale_before = jnp.where(earlier, pltpu.roll(scale, step, 0), 1.0)
        shift_before = jnp.where(earlier, pltpu.roll(shift, step, 0), 0.0)
        shift = scale * shift_before + shift
        scale = scale * scale_before
    return scale, shift


def scan_up(scale, shift):
    row = lax.broadcasted_iota(jnp.int32, scale.shape, 0)
    for step in (1, 2, 4):
        later = row < SUB - step
        scale_after = jnp.where(later, pltpu.roll(scale, SUB - step, 0), 1.0)
        shift_after = jnp.where(later, pltpu.roll(shift, SUB - step, 0), 0.0)
        shift = scale * shift_after + shift
        scale = scale * scale_after
    return scale, shift


def greet(*axes):
    for axis in axes:
        count = lax.axis_size(axis)
        me = lax.axis_index(axis)
        for step in range(1, count):
            pl.semaphore_signal(
                pltpu.get_barrier_semaphore(),
                inc=1,
                device_id={axis: lax.rem(me + step, count)},
                device_id_type=pl.DeviceIdType.MESH,
            )


def met(*axes):
    pl.semaphore_wait(pltpu.get_barrier_semaphore(), sum(lax.axis_size(axis) - 1 for axis in axes))


def remote(src, dst, send, recv, axis, target):
    return pltpu.make_async_remote_copy(
        src_ref=src,
        dst_ref=dst,
        send_sem=send,
        recv_sem=recv,
        device_id={axis: target},
        device_id_type=pl.DeviceIdType.MESH,
    )


def to_all(src, slots, send_sems, recv_sems, axis):
    count = lax.axis_size(axis)
    me = lax.axis_index(axis)
    copies = []
    for step in range(1, count):
        copies.append(
            pltpu.make_async_remote_copy(
                src_ref=src,
                dst_ref=slots.at[step - 1],
                send_sem=send_sems.at[step - 1],
                recv_sem=recv_sems.at[step - 1],
                device_id={axis: lax.rem(me + step, count)},
                device_id_type=pl.DeviceIdType.MESH,
            )
        )
    for copy in copies:
        copy.start()
    return copies


def from_earlier(slots, initial, scale_rows, shift_rows, axis):
    count = lax.axis_size(axis)
    me = lax.axis_index(axis)
    state = initial
    for block in range(count - 1):
        slot = jnp.maximum(me - block - 1, 0)
        after = slots[slot, scale_rows, :] * state + slots[slot, shift_rows, :]
        state = jnp.where(block < me, after, state)
    return state


def from_later(slots, shape, scale_rows, shift_rows, axis):
    count = lax.axis_size(axis)
    me = lax.axis_index(axis)
    message = jnp.zeros(shape, F32)
    for block in range(count - 1, 0, -1):
        slot = jnp.minimum(me + count - block - 1, count - 2)
        after = slots[slot, scale_rows, :] * message + slots[slot, shift_rows, :]
        message = jnp.where(block > me, after, message)
    return message


def first_pass(seqs, tokens, channels, gates, bias, keep, upd, fgt, out, scale, shift, summary):
    def body(at, carried):
        given = list(carried)
        for seq in range(seqs):
            for half in range(STEP // SUB):
                rows = pl.ds(pl.multiple_of(seq * tokens + at * STEP + half * SUB, SUB), SUB)
                kept = keep[rows, :][:, 0:1]
                for number, lanes in enumerate(lane_blocks(channels)):
                    u = jnp.tanh(gates[0, rows, lanes] + bias[0:1, lanes])
                    f = sigmoid(gates[1, rows, lanes] + bias[1:2, lanes])
                    o = sigmoid(gates[2, rows, lanes] + bias[2:3, lanes])
                    upd[rows, lanes] = u
                    fgt[rows, lanes] = f
                    out[rows, lanes] = o
                    a, b = scan_down(f * kept, (1.0 - f) * u)
                    place = (seq * len(lane_blocks(channels)) + number) * 2
                    b = a * given[place + 1] + b
                    a = a * given[place]
                    scale[rows, lanes] = a
                    shift[rows, lanes] = b
                    given[place] = a[SUB - 1 : SUB]
                    given[place + 1] = b[SUB - 1 : SUB]
        return tuple(given)

    begin = []
    for seq in range(seqs):
        for lanes in lane_blocks(channels):
            width = lanes.stop - lanes.start
            begin += [jnp.ones((1, width), F32), jnp.zeros((1, width), F32)]
    end = lax.fori_loop(0, tokens // STEP, body, tuple(begin))
    place = 0
    for seq in range(seqs):
        for lanes in lane_blocks(channels):
            summary[seq : seq + 1, lanes] = end[place]
            summary[seqs + seq : seqs + seq + 1, lanes] = end[place + 1]
            place += 2


def back_pass(seqs, tokens, channels, upstream, keep, fgt, out, scale, shift, summary, row0):
    steps = tokens // STEP

    def body(index, carried):
        at = steps - 1 - index
        given = list(carried)
        for seq in range(seqs):
            whole = pl.ds(pl.multiple_of(seq * tokens + at * STEP, STEP), STEP)
            for number, lanes in enumerate(lane_blocks(channels)):
                ups = upstream[whole, lanes].astype(F32)
                place = (seq * len(lane_blocks(channels)) + number) * 2
                for half in reversed(range(STEP // SUB)):
                    rows = pl.ds(pl.multiple_of(seq * tokens + at * STEP + half * SUB, SUB), SUB)
                    kept = keep[rows, :][:, 0:1]
                    retain = fgt[rows, lanes] * kept
                    direct = ups[half * SUB : half * SUB + SUB] * out[rows, lanes]
                    a, b = scan_up(retain, retain * direct)
                    b = a * given[place + 1] + b
                    a = a * given[place]
                    scale[rows, lanes] = a
                    shift[rows, lanes] = b
                    given[place] = a[0:1]
                    given[place + 1] = b[0:1]
        return tuple(given)

    begin = []
    for seq in range(seqs):
        for lanes in lane_blocks(channels):
            width = lanes.stop - lanes.start
            begin += [jnp.ones((1, width), F32), jnp.zeros((1, width), F32)]
    end = lax.fori_loop(0, steps, body, tuple(begin))
    place = 0
    for seq in range(seqs):
        for lanes in lane_blocks(channels):
            summary[row0 + seq : row0 + seq + 1, lanes] = end[place]
            summary[row0 + seqs + seq : row0 + seqs + seq + 1, lanes] = end[place + 1]
            place += 2


def states_pass(seq, tokens, channels, entering, out, scale, shift, state, pooled):
    def body(at, none):
        rows = pl.ds(pl.multiple_of(seq * tokens + at * STEP, STEP), STEP)
        for lanes in lane_blocks(channels):
            value = scale[rows, lanes] * entering[seq : seq + 1, lanes] + shift[rows, lanes]
            state[rows, lanes] = value
            pooled[rows, lanes] = (out[rows, lanes] * value).astype(BF16)
        return none

    lax.fori_loop(0, tokens // STEP, body, 0)


def grads_pass(seqs, tokens, channels, message, entering, upstream, keep, upd, fgt, out, state, scale, shift, grads, planes, sums):
    steps = tokens // STEP
    sums[...] = jnp.zeros_like(sums)
    if grads.shape[1] > 3 * channels:
        grads[:, 3 * channels :] = jnp.zeros((grads.shape[0], grads.shape[1] - 3 * channels), BF16)
    for seq in range(seqs):
        for lanes in lane_blocks(channels):
            width = lanes.stop - lanes.start

            def body(index, later, seq=seq, lanes=lanes, width=width):
                at = steps - 1 - index
                whole = pl.ds(pl.multiple_of(seq * tokens + at * STEP, STEP), STEP)
                row = lax.broadcasted_iota(jnp.int32, (STEP, width), 0)
                kept = keep[whole, :][:, 0:1]
                ups = upstream[whole, lanes].astype(F32)
                u, f, o = upd[whole, lanes], fgt[whole, lanes], out[whole, lanes]
                states = state[whole, lanes]
                arriving = scale[whole, lanes] * message[seq : seq + 1, lanes] + shift[whole, lanes]
                adjoint = ups * o + jnp.where(row == STEP - 1, later, pltpu.roll(arriving, STEP - 1, 0))
                tile = pl.ds(pl.multiple_of(seq * tokens + jnp.maximum(at * STEP - SUB, 0), SUB), SUB)
                last = state[tile, lanes][SUB - 1 : SUB]
                first = jnp.where(at == 0, entering[seq : seq + 1, lanes], last)
                before = jnp.where(row == 0, first, pltpu.roll(states, 1, 0))
                given = [
                    adjoint * (1.0 - f) * (1.0 - u * u),
                    adjoint * (before * kept - u) * f * (1.0 - f),
                    ups * states * o * (1.0 - o),
                ]
                for gate, value in enumerate(given):
                    value = value.astype(BF16)
                    grads[whole, gate * channels + lanes.start : gate * channels + lanes.stop] = value
                    if planes is not None:
                        planes[gate, whole, lanes] = value
                    value = value.astype(F32)
                    total = value[:SUB]
                    for half in range(1, STEP // SUB):
                        total = total + value[half * SUB : half * SUB + SUB]
                    sums[gate, :, lanes] += total
                return arriving[0:1]

            lax.fori_loop(0, steps, body, message[seq : seq + 1, lanes])


def forward_kernel(seqs, tokens, channels, gates, bias, keep, initial, hidden, upd, fgt, out, state, entering, scale, shift, summary, slots, send_sems, recv_sems):
    greet("seq")
    first_pass(seqs, tokens, channels, gates, bias, keep, upd, fgt, out, scale, shift, summary)
    met("seq")
    copies = to_all(summary, slots, send_sems, recv_sems, "seq")
    for copy in copies:
        copy.wait()
    entering[...] = from_earlier(slots, initial[...], slice(0, seqs), slice(seqs, 2 * seqs), "seq")
    for seq in range(seqs):
        states_pass(seq, tokens, channels, entering, out, scale, shift, state, hidden)


def top_kernel(seqs, tokens, channels, gates, bias, keep, initial, cotangent, pooled, grads, planes, sums, upd, fgt, out, state, entering, message, scale, shift, back_scale, back_shift, summary, slots, send_sems, recv_sems):
    greet("seq")
    first_pass(seqs, tokens, channels, gates, bias, keep, upd, fgt, out, scale, shift, summary)
    back_pass(seqs, tokens, channels, cotangent, keep, fgt, out, back_scale, back_shift, summary, 2 * seqs)
    met("seq")
    copies = to_all(summary, slots, send_sems, recv_sems, "seq")
    for copy in copies:
        copy.wait()
    entering[...] = from_earlier(slots, initial[...], slice(0, seqs), slice(seqs, 2 * seqs), "seq")
    message[...] = from_later(
        slots, (seqs, channels), slice(2 * seqs, 3 * seqs), slice(3 * seqs, 4 * seqs), "seq"
    )
    for seq in range(seqs):
        states_pass(seq, tokens, channels, entering, out, scale, shift, state, pooled)
    grads_pass(seqs, tokens, channels, message, entering, cotangent, keep, upd, fgt, out, state, back_scale, back_shift, grads, planes, sums)


def pass_edges(seqs, tokens, grads, edges, arrived, edge_sems):
    count = lax.axis_size("seq")
    me = lax.axis_index("seq")
    row = lax.broadcasted_iota(jnp.int32, edges.shape, 0)
    firsts = jnp.zeros(edges.shape, F32)
    for seq in range(seqs):
        tile = grads[seq * tokens : seq * tokens + EDGE, :].astype(F32)
        firsts = jnp.where(row == seq, pltpu.roll(tile, seq, 0) if seq else tile, firsts)
    edges[...] = firsts.astype(BF16)
    copy = pltpu.make_async_remote_copy(
        src_ref=edges,
        dst_ref=arrived,
        send_sem=edge_sems.at[0],
        recv_sem=edge_sems.at[1],
        device_id={"seq": lax.rem(me + count - 1, count)},
        device_id_type=pl.DeviceIdType.MESH,
    )
    rows = slice(seqs * tokens, seqs * tokens + EDGE)

    @pl.when(me > 0)
    def _():
        copy.start()

    @pl.when(me < count - 1)
    def _():
        copy.wait_recv()
        grads[rows, :] = arrived[...]

    @pl.when(me == count - 1)
    def _():
        grads[rows, :] = jnp.zeros(edges.shape, BF16)

    @pl.when(me > 0)
    def _():
        copy.wait_send()


def backward_kernel(seqs, tokens, channels, upstream, keep, upd, fgt, out, state, entering, grads, sums, message, scale, shift, summary, slots, send_sems, recv_sems, edges, arrived, edge_sems):
    greet("seq")
    back_pass(seqs, tokens, channels, upstream, keep, fgt, out, scale, shift, summary, 0)
    met("seq")
    copies = to_all(summary, slots, send_sems, recv_sems, "seq")
    for copy in copies:
        copy.wait()
    message[...] = from_later(slots, (seqs, channels), slice(0, seqs), slice(seqs, 2 * seqs), "seq")
    grads_pass(seqs, tokens, channels, message, entering, upstream, keep, upd, fgt, out, state, scale, shift, grads, None, sums)
    pass_edges(seqs, tokens, grads, edges, arrived, edge_sems)


def neighbours():
    here = lax.axis_index("dp")
    beside = here + 1 - 2 * lax.rem(here, 2)
    return here, beside, lax.rem(here + 2, 4), lax.rem(beside + 2, 4)


def relay(value, every, plane_sems, kept_sem):
    here, beside, below, corner = neighbours()
    near = (beside, below)
    half = value.shape[0] // 2

    def over(src, owner, way):
        place = every.at[owner]
        return remote(src, place, plane_sems.at[0, way], plane_sems.at[1, way], "dp", near[way])

    def onward(owner, way):
        place = every.at[owner, pl.ds(way * half, half)]
        return remote(place, place, plane_sems.at[0, 2 + way], plane_sems.at[1, 2 + way], "dp", near[1 - way])

    def keep():
        return pltpu.make_async_copy(value, every.at[here], kept_sem)

    def start():
        for way in range(2):
            over(value, here, way).start()
        keep().start()

    def forward():
        for way in range(2):
            over(every.at[near[way]], near[way], way).wait_recv()
            onward(near[way], way).start()

    def finish():
        for way in range(2):
            over(value, here, way).wait_send()
            onward(near[way], way).wait_send()
            onward(corner, way).wait_recv()
        keep().wait()

    return start, forward, finish


def first_kernel(seqs, tokens, channels, inputs, taps, bias, keep, initial, hidden_out, upd_out, fgt_out, out_out, state_out, entering, both_out, every, both, edges, weights, gates, hidden, state, scale, shift, summary, slots, send_sems, recv_sems, weight_sems, plane_sems, kept_sem, pair_sems, edge_sems, save_sems):
    axes = ("seq", "dp", "mp")
    line, at, mine = lax.axis_size("seq"), lax.axis_index("seq"), lax.axis_index("mp")
    after, before = lax.rem(at + 1, line), lax.rem(at + line - 1, line)
    greet(*axes)
    pl.semaphore_signal(
        pltpu.get_barrier_semaphore(),
        inc=1,
        device_id={"seq": before, "mp": 1 - mine},
        device_id_type=pl.DeviceIdType.MESH,
    )
    rows = seqs * tokens
    half = rows // 2
    gather_start, gather_forward, gather_finish = relay(inputs, every, plane_sems, kept_sem)

    def load(step):
        slot = lax.rem(step, 2)
        side = jnp.where(lax.rem(step // 3, 2) == 0, mine, 1 - mine)
        return pltpu.make_async_copy(
            taps.at[step // 6, lax.rem(step, 3), pl.ds(pl.multiple_of(side * channels, 128), channels), :],
            weights.at[slot],
            weight_sems.at[slot],
        )

    def lanes_of(core):
        return pl.ds(pl.multiple_of(core * channels, 128), channels)

    own = pltpu.make_async_copy(inputs, both.at[0, :, lanes_of(mine)], pair_sems.at[0])
    give = remote(inputs, both.at[0, :, lanes_of(mine)], pair_sems.at[1], pair_sems.at[2], "mp", 1 - mine)
    take = remote(inputs, both.at[0, :, lanes_of(1 - mine)], pair_sems.at[1], pair_sems.at[2], "mp", 1 - mine)

    def edge(seq, other, arriving=False):
        core = jnp.where(other, 1 - mine, mine)
        return pltpu.make_async_remote_copy(
            src_ref=inputs.at[seq * tokens + tokens - EDGE : seq * tokens + tokens],
            dst_ref=edges.at[core if arriving else mine, seq],
            send_sem=edge_sems.at[0, other, seq],
            recv_sem=edge_sems.at[1, other, seq],
            device_id={"seq": after, "mp": core},
            device_id_type=pl.DeviceIdType.MESH,
        )

    load(0).start()
    own.start()
    pl.semaphore_wait(pltpu.get_barrier_semaphore(), sum(lax.axis_size(axis) - 1 for axis in axes) + 1)
    give.start()

    @pl.when(at < line - 1)
    def _():
        for seq in range(seqs):
            for other in range(2):
                edge(seq, other).start()

    @pl.when(at == 0)
    def _():
        edges[...] = jnp.zeros(edges.shape, BF16)

    gather_start()
    own.wait()

    def shift_down():
        width = 2 * channels
        steps = tokens // STEP

        def body(index, none):
            seq, tile = index // steps, lax.rem(index, steps)
            row = lax.broadcasted_iota(jnp.int32, (STEP, width), 0)
            place = pl.ds(pl.multiple_of(index * STEP, STEP), STEP)
            ahead = pl.ds(pl.multiple_of(jnp.maximum(index - 1, 0) * STEP, STEP), STEP)
            last = both[0, ahead, :].astype(F32)[STEP - 1 : STEP]
            outer = jnp.concatenate([edges[0, seq], edges[1, seq]], 1).astype(F32)[EDGE - 1 : EDGE]
            moved = pltpu.roll(both[0, place, :].astype(F32), 1, 0)
            both[1, place, :] = jnp.where(row == 0, jnp.where(tile == 0, outer, last), moved).astype(BF16)
            return none

        lax.fori_loop(0, rows // STEP, body, 0)

    def body(step, none):
        @pl.when(step == 3)
        def _():
            take.wait_recv()

        @pl.when(step == 6)
        def _():
            @pl.when(at > 0)
            def _():
                for seq in range(seqs):
                    for other in range(2):
                        edge(seq, other, True).wait_recv()

            shift_down()

        load(step).wait()

        @pl.when(step < 11)
        def _():
            load(step + 1).start()

        gate, part = lax.rem(step, 3), lax.rem(step // 3, 2)
        columns = lanes_of(jnp.where(part == 0, mine, 1 - mine))
        for side in range(2):
            place = pl.ds(side * half, half)
            term = jnp.dot(
                both[step // 6, place, columns], weights[lax.rem(step, 2)], preferred_element_type=F32
            )
            gates[gate, place, :] = jnp.where(step < 3, term, gates[gate, place, :] + term)
        return none

    lax.fori_loop(0, 12, body, 0)
    upd, fgt, out = gates.at[0], gates.at[1], gates.at[2]
    first_pass(seqs, tokens, channels, gates, bias, keep, upd, fgt, out, scale, shift, summary)
    copies = to_all(summary, slots, send_sems, recv_sems, "seq")
    gather_forward()
    saves = [
        pltpu.make_async_copy(src, dst, save_sems.at[number])
        for number, (src, dst) in enumerate(((upd, upd_out), (fgt, fgt_out), (out, out_out), (state, state_out), (hidden, hidden_out)))
    ]
    for copy in saves[:3]:
        copy.start()
    for copy in copies:
        copy.wait()
    entering[...] = from_earlier(slots, initial[...], slice(0, seqs), slice(seqs, 2 * seqs), "seq")
    sent = []
    for seq in range(seqs):
        states_pass(seq, tokens, channels, entering, out, scale, shift, state, hidden)
        part = pl.ds(seq * tokens, tokens)
        place = both_out.at[part, lanes_of(mine)]
        sent.append(pltpu.make_async_copy(hidden.at[part], place, pair_sems.at[3 + 3 * seq]))
        sent.append(remote(hidden.at[part], place, pair_sems.at[4 + 3 * seq], pair_sems.at[5 + 3 * seq], "mp", 1 - mine))
        for copy in sent[-2:]:
            copy.start()
    for copy in saves[3:]:
        copy.start()
    for copy in saves + sent:
        copy.wait()
    give.wait_send()

    @pl.when(at < line - 1)
    def _():
        for seq in range(seqs):
            for other in range(2):
                edge(seq, other).wait_send()

    gather_finish()


def upper_kernel(seqs, tokens, channels, full_hidden, hidden, mix, bias, keep, initial, cotangent, pooled, grads, planes, sums, every, weights, gates, state, entering, message, scale, shift, back_scale, back_shift, summary, slots, send_sems, recv_sems, weight_sems, plane_sems, kept_sem):
    greet("seq", "dp")
    half = seqs * tokens // 2
    gather_start, gather_forward, gather_finish = relay(hidden, every, plane_sems, kept_sem)

    def load(step):
        slot = lax.rem(step, 2)
        return pltpu.make_async_copy(
            mix.at[step // 2, pl.ds(pl.multiple_of(lax.rem(step, 2) * channels, 128), channels), :],
            weights.at[slot],
            weight_sems.at[slot],
        )

    load(0).start()
    met("seq", "dp")
    gather_start()

    def body(step, none):
        load(step).wait()

        @pl.when(step < 5)
        def _():
            load(step + 1).start()

        gate, part = step // 2, lax.rem(step, 2)
        columns = pl.ds(pl.multiple_of(part * channels, 128), channels)
        for side in range(2):
            place = pl.ds(side * half, half)
            term = jnp.dot(full_hidden[place, columns], weights[part], preferred_element_type=F32)
            gates[gate, place, :] = jnp.where(part == 0, term, gates[gate, place, :] + term)
        return none

    lax.fori_loop(0, 6, body, 0)
    upd, fgt, out = gates.at[0], gates.at[1], gates.at[2]
    first_pass(seqs, tokens, channels, gates, bias, keep, upd, fgt, out, scale, shift, summary)
    back_pass(seqs, tokens, channels, cotangent, keep, fgt, out, back_scale, back_shift, summary, 2 * seqs)
    copies = to_all(summary, slots, send_sems, recv_sems, "seq")
    gather_forward()
    for copy in copies:
        copy.wait()
    entering[...] = from_earlier(slots, initial[...], slice(0, seqs), slice(seqs, 2 * seqs), "seq")
    message[...] = from_later(
        slots, (seqs, channels), slice(2 * seqs, 3 * seqs), slice(3 * seqs, 4 * seqs), "seq"
    )
    for seq in range(seqs):
        states_pass(seq, tokens, channels, entering, out, scale, shift, state, pooled)
    grads_pass(seqs, tokens, channels, message, entering, cotangent, keep, upd, fgt, out, state, back_scale, back_shift, grads, planes, sums)
    gather_finish()


def lower_kernel(seqs, tokens, channels, above, above_columns, mix, keep, upd_in, fgt_in, out_in, state_in, entering, grads, sums, swapped, weights, total, coming, upd, fgt, out, state, message, scale, shift, summary, slots, send_sems, recv_sems, edges, arrived, edge_sems, weight_sems, load_sems, pair_sems, swap_sems):
    greet("seq", "dp", "mp")
    mine = lax.axis_index("mp")
    width = swapped.shape[2]

    def load(step):
        side = jnp.where(step < 3, 1 - mine, mine)
        slot = lax.rem(step, 2)
        return pltpu.make_async_copy(
            mix.at[lax.rem(step, 3), pl.ds(pl.multiple_of(side * channels, 128), channels), :],
            weights.at[slot],
            weight_sems.at[slot],
        )

    load(0).start()
    loads = [
        pltpu.make_async_copy(src, dst, load_sems.at[number])
        for number, (src, dst) in enumerate(((upd_in, upd), (fgt_in, fgt), (out_in, out), (state_in, state)))
    ]
    for copy in loads:
        copy.start()
    met("seq", "dp", "mp")
    plane = neighbours()
    swaps = []
    for steps in (3, 1, 2, 0):
        src = above_columns.at[:, pl.ds(pl.multiple_of(plane[steps] * width, 128), width)]
        dst = swapped.at[plane[0]]
        if steps:
            swaps.append(remote(src, dst, swap_sems.at[0, steps], swap_sems.at[1, steps], "dp", plane[steps]))
        else:
            swaps.append(pltpu.make_async_copy(src, dst, swap_sems.at[0, steps]))
        swaps[-1].start()
    give = remote(total.at[0], coming, pair_sems.at[0], pair_sems.at[1], "mp", 1 - mine)

    def body(step, none):
        load(step).wait()

        @pl.when(step < 5)
        def _():
            load(step + 1).start()

        side, gate = step // 3, lax.rem(step, 3)
        rows = above.shape[1] // 2
        for half in range(2):
            place = pl.ds(half * rows, rows)
            term = lax.dot_general(
                above[gate, place, :], weights[lax.rem(step, 2)], (((1,), (1,)), ((), ())), preferred_element_type=F32
            )
            total[side, place, :] = jnp.where(gate == 0, term, total[side, place, :] + term)

        @pl.when(step == 2)
        def _():
            give.start()

        return none

    lax.fori_loop(0, 6, body, 0)
    give.wait_recv()
    total[1] += coming[...]
    for copy in loads:
        copy.wait()
    upstream = total.at[1]
    back_pass(seqs, tokens, channels, upstream, keep, fgt, out, scale, shift, summary, 0)
    copies = to_all(summary, slots, send_sems, recv_sems, "seq")
    for copy in copies:
        copy.wait()
    message[...] = from_later(slots, (seqs, channels), slice(0, seqs), slice(seqs, 2 * seqs), "seq")
    grads_pass(seqs, tokens, channels, message, entering, upstream, keep, upd, fgt, out, state, scale, shift, grads, None, sums)
    pass_edges(seqs, tokens, grads, edges, arrived, edge_sems)
    give.wait_send()
    for steps, copy in zip((3, 1, 2, 0), swaps):
        if steps:
            copy.wait_send()
            place = swapped.at[plane[steps]]
            remote(place, place, swap_sems.at[0, steps], swap_sems.at[1, steps], "dp", plane[steps]).wait_recv()
        else:
            copy.wait()


def exchange_scratch(rows, channels):
    count = lax.axis_size("seq")
    return [
        pltpu.VMEM((rows, channels), F32),
        pltpu.VMEM((count - 1, rows, channels), F32),
        pltpu.SemaphoreType.DMA((count - 1,)),
        pltpu.SemaphoreType.DMA((count - 1,)),
    ]


def params(number):
    return pltpu.CompilerParams(collective_id=number, has_side_effects=True, vmem_limit_bytes=56 * 2**20)


def cost(elements, ops, moved):
    return pl.CostEstimate(flops=elements * ops, bytes_accessed=moved, transcendentals=elements * 3)


def pool_forward(seqs, tokens, gates, bias, keep, initial):
    channels = gates.shape[2]
    rows = seqs * tokens
    whole = jax.ShapeDtypeStruct((rows, channels), F32)
    return pl.pallas_call(
        functools.partial(forward_kernel, seqs, tokens, channels),
        out_shape=(
            jax.ShapeDtypeStruct((rows, channels), BF16),
            whole,
            whole,
            whole,
            whole,
            jax.ShapeDtypeStruct((seqs, channels), F32),
        ),
        in_specs=[VMEM] * 4,
        out_specs=[VMEM] * 6,
        scratch_shapes=[pltpu.VMEM((rows, channels), F32)] * 2 + exchange_scratch(2 * seqs, channels),
        compiler_params=params(1),
        cost_estimate=cost(rows * channels, 60, rows * channels * 30),
        name="pool_forward",
    )(gates, bias, keep, initial)


def pool_top(seqs, tokens, lanes, gates, bias, keep, initial, cotangent):
    channels = gates.shape[2]
    rows = seqs * tokens
    whole = pltpu.VMEM((rows, channels), F32)
    edge = pltpu.VMEM((seqs, channels), F32)
    return pl.pallas_call(
        functools.partial(top_kernel, seqs, tokens, channels),
        out_shape=(
            jax.ShapeDtypeStruct((rows, channels), BF16),
            jax.ShapeDtypeStruct((rows, lanes), BF16),
            jax.ShapeDtypeStruct((3, rows, channels), BF16),
            jax.ShapeDtypeStruct((3, SUB, channels), F32),
        ),
        in_specs=[VMEM] * 5,
        out_specs=[VMEM] * 4,
        scratch_shapes=[whole] * 4 + [edge] * 2 + [whole] * 4 + exchange_scratch(4 * seqs, channels),
        compiler_params=params(2),
        cost_estimate=cost(rows * channels, 120, rows * channels * 22),
        name="pool_top",
    )(gates, bias, keep, initial, cotangent)


def pool_first(seqs, tokens, inputs, taps, bias, keep, initial):
    rows, channels = inputs.shape
    whole = jax.ShapeDtypeStruct((rows, channels), F32)
    hbm = pl.BlockSpec(memory_space=pl.ANY)
    dma = pltpu.SemaphoreType.DMA
    return pl.pallas_call(
        functools.partial(first_kernel, seqs, tokens, channels),
        out_shape=(
            jax.ShapeDtypeStruct((rows, channels), BF16),
            whole,
            whole,
            whole,
            whole,
            jax.ShapeDtypeStruct((seqs, channels), F32),
            jax.ShapeDtypeStruct((rows, 2 * channels), BF16),
            jax.ShapeDtypeStruct((4, rows, channels), BF16),
        ),
        in_specs=[hbm, hbm, VMEM, VMEM, VMEM],
        out_specs=[hbm] * 5 + [VMEM, hbm, hbm],
        scratch_shapes=[
            pltpu.VMEM((2, rows, 2 * channels), BF16),
            pltpu.VMEM((2, seqs, EDGE, channels), BF16),
            pltpu.VMEM((2, channels, channels), BF16),
            pltpu.VMEM((3, rows, channels), F32),
            pltpu.VMEM((rows, channels), BF16),
        ]
        + [pltpu.VMEM((rows, channels), F32)] * 3
        + exchange_scratch(2 * seqs, channels)
        + [dma((2,)), dma((2, 4)), dma, dma((3 + 3 * seqs,)), dma((2, 2, seqs)), dma((5,))],
        compiler_params=params(7),
        cost_estimate=pl.CostEstimate(
            flops=24 * rows * channels * channels, bytes_accessed=rows * channels * 80, transcendentals=0
        ),
        name="pool_first",
    )(inputs, taps, bias, keep, initial)


def pool_upper(seqs, tokens, lanes, full_hidden, hidden, mix, bias, keep, initial, cotangent):
    rows, channels = hidden.shape
    whole = pltpu.VMEM((rows, channels), F32)
    edge = pltpu.VMEM((seqs, channels), F32)
    hbm = pl.BlockSpec(memory_space=pl.ANY)
    dma = pltpu.SemaphoreType.DMA
    return pl.pallas_call(
        functools.partial(upper_kernel, seqs, tokens, channels),
        out_shape=(
            jax.ShapeDtypeStruct((rows, channels), BF16),
            jax.ShapeDtypeStruct((rows, lanes), BF16),
            jax.ShapeDtypeStruct((3, rows, channels), BF16),
            jax.ShapeDtypeStruct((3, SUB, channels), F32),
            jax.ShapeDtypeStruct((4, rows, channels), BF16),
        ),
        in_specs=[VMEM, hbm, hbm, VMEM, VMEM, VMEM, VMEM],
        out_specs=[VMEM] * 4 + [hbm],
        scratch_shapes=[pltpu.VMEM((2, channels, channels), BF16), pltpu.VMEM((3, rows, channels), F32), whole, edge, edge]
        + [whole] * 4
        + exchange_scratch(4 * seqs, channels)
        + [dma((2,)), dma((2, 4)), dma],
        compiler_params=params(6),
        cost_estimate=pl.CostEstimate(
            flops=12 * rows * channels * channels, bytes_accessed=rows * channels * 40, transcendentals=0
        ),
        name="pool_upper",
    )(full_hidden, hidden, mix, bias, keep, initial, cotangent)


def pool_backward(seqs, tokens, lanes, upstream, keep, upd, fgt, out, state, entering):
    rows, channels = upstream.shape
    whole = pltpu.VMEM((rows, channels), F32)
    return pl.pallas_call(
        functools.partial(backward_kernel, seqs, tokens, channels),
        out_shape=(
            jax.ShapeDtypeStruct((rows + EDGE, lanes), BF16),
            jax.ShapeDtypeStruct((3, SUB, channels), F32),
        ),
        in_specs=[VMEM] * 7,
        out_specs=[VMEM] * 2,
        scratch_shapes=[pltpu.VMEM((seqs, channels), F32)]
        + [whole] * 2
        + exchange_scratch(2 * seqs, channels)
        + [pltpu.VMEM((EDGE, lanes), BF16)] * 2
        + [pltpu.SemaphoreType.DMA((2,))],
        compiler_params=params(3),
        cost_estimate=cost(rows * channels, 60, rows * channels * 26),
        name="pool_backward",
    )(upstream, keep, upd, fgt, out, state, entering)


def pool_lower(seqs, tokens, above, above_columns, mix, keep, upd, fgt, out, state, entering):
    rows, channels = upd.shape
    lanes = above_columns.shape[1]
    whole = pltpu.VMEM((rows, channels), F32)
    hbm = pl.BlockSpec(memory_space=pl.ANY)
    dma = pltpu.SemaphoreType.DMA
    return pl.pallas_call(
        functools.partial(lower_kernel, seqs, tokens, channels),
        out_shape=(
            jax.ShapeDtypeStruct((rows + EDGE, lanes), BF16),
            jax.ShapeDtypeStruct((3, SUB, channels), F32),
            jax.ShapeDtypeStruct((4, rows, lanes // 4), BF16),
        ),
        in_specs=[VMEM, hbm, hbm, VMEM, hbm, hbm, hbm, hbm, VMEM],
        out_specs=[VMEM, VMEM, hbm],
        scratch_shapes=[
            pltpu.VMEM((2, channels, channels), BF16),
            pltpu.VMEM((2, rows, channels), F32),
            whole,
            whole,
            whole,
            whole,
            whole,
            pltpu.VMEM((seqs, channels), F32),
            whole,
            whole,
        ]
        + exchange_scratch(2 * seqs, channels)
        + [pltpu.VMEM((EDGE, lanes), BF16)] * 2
        + [dma((2,)), dma((2,)), dma((4,)), dma((2,)), dma((2, 4))],
        compiler_params=params(5),
        cost_estimate=pl.CostEstimate(
            flops=12 * rows * channels * channels, bytes_accessed=rows * channels * 40, transcendentals=0
        ),
        name="pool_lower",
    )(above, above_columns, mix, keep, upd, fgt, out, state, entering)


def shift_up(seqs, tokens, value, edges, result):
    width = value.shape[1]
    steps = tokens // STEP

    def body(index, none):
        sequence, at = index // steps, lax.rem(index, steps)
        row = lax.broadcasted_iota(jnp.int32, (STEP, width), 0)
        rows = pl.ds(pl.multiple_of(index * STEP, STEP), STEP)
        after = jnp.minimum(index + 1, value.shape[0] // STEP - 1)
        first = value[pl.ds(pl.multiple_of(after * STEP, STEP), STEP), :].astype(F32)[0:1]
        edge = edges[sequence // seqs].astype(F32)
        edge = jnp.where(lax.rem(sequence, seqs) == 0, edge[0:1], edge[1:2])
        moved = pltpu.roll(value[rows, :].astype(F32), STEP - 1, 0)
        moved = jnp.where(row == STEP - 1, jnp.where(at == steps - 1, edge, first), moved)
        result[rows, :] = moved.astype(BF16)
        return none

    lax.fori_loop(0, value.shape[0] // STEP, body, 0)


def spread_kernel(seqs, tokens, parts, turn, tail, hidden, full, grads_two, grads_one, taps, sums, out, input_grad, sums_out, rows_full, grads, grads_edge, moved, own, ups, downs, acc, across, around, every, weights, leaving, coming, load_sems, swap_sems, up_sems, down_sems, line_send, line_recv, column_send, column_recv, kept_sems, plane_send, plane_recv, sums_sems, weight_sems, leaving_sems, coming_sems, result_sems, pair_sems, ready_sem):
    line, plane = lax.axis_size("seq"), lax.axis_size("dp")
    at, here = lax.axis_index("seq"), lax.axis_index("dp")
    unit = line * parts
    units = own.shape[0] // unit
    blocks = units // 3
    width = own.shape[1]
    block_rows = seqs * tokens
    half = unit // 2
    here, beside, below, across_from = neighbours()
    mine = lax.axis_index("mp")
    greet("seq", "dp", "mp")
    met("seq", "dp", "mp")

    def turned(u):
        return lax.rem(u, turn) == turn - 1

    def direct(u):
        return lax.rem(u, turn) != turn - 1

    wide = rows_full.shape[1] // 2

    def own_rows(value, number, way):
        place = rows_full.at[:, pl.ds(pl.multiple_of(mine * wide, 128), wide)]
        if way == 0:
            return pltpu.make_async_copy(value, place, load_sems.at[number])
        return remote(value, place, pair_sems.at[0, number], pair_sems.at[1, number], "mp", 1 - mine)

    def other_rows(number):
        place = rows_full.at[:, pl.ds(pl.multiple_of((1 - mine) * wide, 128), wide)]
        return remote(place, place, pair_sems.at[0, number], pair_sems.at[1, number], "mp", 1 - mine)

    def plane_rows(owner):
        return pl.ds(pl.multiple_of(owner * block_rows, 16), block_rows)

    def peer(steps):
        return (here, beside, below, across_from)[steps]

    def load_two():
        return pltpu.make_async_copy(grads_two, moved, load_sems.at[2])

    def swap(steps, edge, arriving=False):
        columns = pl.ds(pl.multiple_of(peer(steps) * width, 128), width)
        source = peer(steps) if arriving else here
        if edge:
            src, dst = grads_one.at[block_rows : block_rows + EDGE, columns], grads_edge.at[source]
        else:
            src, dst = grads_one.at[0:block_rows, columns], grads.at[plane_rows(source)]
        number = steps * 2 + edge
        if steps == 0:
            return pltpu.make_async_copy(src, dst, swap_sems.at[0, number])
        return remote(src, dst, swap_sems.at[0, number], swap_sems.at[1, number], "dp", peer(steps))

    def product(block, right):
        columns = pl.ds(pl.multiple_of(jnp.where(mine == 0, block, blocks - 1 - block) * unit, 128), unit)
        return lax.dot_general(
            rows_full[:, columns], right[...], (((0,), (0,)), ((), ())), preferred_element_type=F32
        ).astype(BF16)

    narrow = leaving.shape[2]
    pieces = wide // narrow

    def load_weights(step):
        first = jnp.where(step < pieces, (1 - mine) * pieces + step, mine * pieces + step - pieces) * narrow
        slot = lax.rem(step, 2)
        return pltpu.make_async_copy(
            taps.at[:, :, pl.ds(pl.multiple_of(first, narrow), narrow), :], weights.at[slot], weight_sems.at[slot]
        )

    def load_every():
        return pltpu.make_async_copy(grads_one, every, load_sems.at[3])

    def leave(step):
        slot = lax.rem(step, 2)
        return remote(leaving.at[slot], coming.at[step], leaving_sems.at[slot], coming_sems.at[step], "mp", 1 - mine)

    def result(step):
        return pltpu.make_async_copy(
            coming.at[step],
            input_grad.at[:, pl.ds(pl.multiple_of(step * narrow, narrow), narrow)],
            result_sems.at[step],
        )

    def input_terms(slot):
        channels = taps.shape[3]
        now = jnp.zeros((block_rows, narrow), F32)
        late = jnp.zeros((block_rows + EDGE, narrow), F32)
        for gate in range(3):
            lanes = slice(gate * channels, gate * channels + channels)
            now += lax.dot_general(
                every[:block_rows, lanes], weights[slot, 0, gate], (((1,), (1,)), ((), ())), preferred_element_type=F32
            )
            late += lax.dot_general(
                every[:, lanes], weights[slot, 1, gate], (((1,), (1,)), ((), ())), preferred_element_type=F32
            )
        row = lax.broadcasted_iota(jnp.int32, now.shape, 0)
        after = pltpu.roll(late[:block_rows], block_rows - 1, 0)
        for seq in range(seqs):
            after = jnp.where(
                row == seq * tokens + tokens - 1, late[block_rows + seq : block_rows + seq + 1], after
            )
        return now + after

    def whole(u):
        return pl.ds(pl.multiple_of(u * unit, unit), unit)

    def chunk(u, j):
        return pl.ds(pl.multiple_of(u * unit + j * parts, parts), parts)

    def up(src, u, j):
        number = u * (line - 1) + j - 1
        return remote(src, ups.at[u, j - 1], up_sems.at[0, number], up_sems.at[1, number], "seq", lax.rem(at + 1, line))

    def down(src, u, j):
        number = u * (line - 1) + j
        return remote(
            src, downs.at[u, j], down_sems.at[0, number], down_sems.at[1, number], "seq", lax.rem(at + line - 1, line)
        )

    def along(src, u, j, way, hop):
        return remote(
            src,
            out.at[here, chunk(u, j)],
            line_send.at[(u * 2 + way) * (line - 1) + hop],
            line_recv.at[u * line + j],
            "seq",
            lax.rem(at + (1 if way == 0 else line - 1), line),
        )

    at_end = (at == 0) | (at == line - 1)
    share = line // 2 * parts
    begin = jnp.where(at == 0, 0, line // 2) * parts

    def owner_of(u, j):
        return jnp.where(turned(u), (line - 1) * (j >= line // 2), j)

    def column(steps, u, way):
        number = (u // turn * 4 + steps) * 2 + way
        place = out.at[peer(steps), rows(u, way * share, share)]
        return remote(
            place,
            place,
            column_send.at[number],
            column_recv.at[number],
            "seq",
            lax.rem(at + (1 if way == 0 else line - 1), line),
        )

    def end_rows(u):
        return pl.ds(pl.multiple_of(u * unit + begin, parts), share)

    def keep_part(u):
        return pltpu.make_async_copy(own.at[end_rows(u)], out.at[here, end_rows(u)], kept_sems.at[u])

    def over_part(src, u, way):
        return remote(
            src,
            out.at[here, end_rows(u)],
            plane_send.at[u * 4 + way],
            plane_recv.at[u * 4 + way],
            "dp",
            (beside, below)[way],
        )

    def onward_part(owner, u, way):
        place = out.at[owner, pl.ds(pl.multiple_of(u * unit + begin + way * (share // 2), 16), share // 2)]
        return remote(
            place, place, plane_send.at[u * 4 + 2 + way], plane_recv.at[u * 4 + 2 + way], "dp", (below, beside)[way]
        )

    def keep(u):
        return pltpu.make_async_copy(own.at[chunk(u, at)], out.at[here, chunk(u, at)], kept_sems.at[u])

    def rows(u, first, count):
        return pl.ds(pl.multiple_of(u * unit + first, half), count)

    def over(u, way):
        place = out.at[here, rows(u, 0, unit)]
        return remote(place, place, plane_send.at[u * 4 + way], plane_recv.at[u * 4 + way], "dp", (beside, below)[way])

    def onward(u, way):
        place = out.at[(beside, below)[way], rows(u, way * half, half)]
        return remote(
            place, place, plane_send.at[u * 4 + 2 + way], plane_recv.at[u * 4 + 2 + way], "dp", (below, beside)[way]
        )

    def corner(u, way):
        place = out.at[across_from, rows(u, way * half, half)]
        return remote(place, place, plane_send.at[u * 4 + 2 + way], plane_recv.at[u * 4 + 2 + way], "dp", (below, beside)[way])

    def sums_copy(slots, me, count, axis, number, step):
        return remote(
            slots.at[me],
            slots.at[me],
            sums_sems.at[number, 0, step - 1],
            sums_sems.at[number, 1, step - 1],
            axis,
            lax.rem(me + step, count),
        )

    def sums_arrival(slots, me, count, axis, number, step):
        place = slots.at[lax.rem(me + count - step, count)]
        return remote(place, place, sums_sems.at[number, 0, step - 1], sums_sems.at[number, 1, step - 1], axis, lax.rem(me + step, count))

    for way in range(2):
        own_rows(hidden, 0, way).start()
    load_two().start()
    for steps in range(4):
        for edge in range(2):
            swap(steps, edge).start()
    load_every().start()
    load_weights(0).start()
    across[at] = sums[...]
    for step in range(1, line):
        sums_copy(across, at, line, "seq", 0, step).start()
    load_two().wait()
    own_rows(hidden, 0, 0).wait()

    def stage(index, none):
        @pl.when(index == 1)
        def _():
            for step in range(1, line):
                sums_arrival(across, at, line, "seq", 0, step).wait_recv()
            total = across[0]
            for other in range(1, line):
                total = total + across[other]
            around[here] = total
            for step in range(1, plane):
                sums_copy(around, here, plane, "dp", 1, step).start()

        @pl.when(index == 3)
        def _():
            for step in range(1, plane):
                sums_arrival(around, here, plane, "dp", 1, step).wait_recv()
            total = around[0]
            for other in range(1, plane):
                total = total + around[other]
            sums_out[...] = total

        @pl.when(index == wide // unit)
        def _():
            other_rows(0).wait_recv()

        @pl.when(index == blocks + 2 * (wide // unit))
        def _():
            other_rows(1).wait_recv()

        @pl.when(index < blocks)
        def _():
            own[whole(index), :] = product(index, moved)

        @pl.when(index == blocks - 1)
        def _():
            own_rows(hidden, 0, 1).wait_send()
            own_rows(full, 1, 0).start()
            pl.semaphore_signal(ready_sem, inc=1, device_id={"mp": 1 - mine}, device_id_type=pl.DeviceIdType.MESH)
            pl.semaphore_wait(ready_sem, 1)
            own_rows(full, 1, 1).start()

        @pl.when(index == blocks)
        def _():
            for steps in range(4):
                for edge in range(2):
                    if steps:
                        swap(steps, edge, True).wait_recv()
                    else:
                        swap(steps, edge).wait()
            shift_up(seqs, tokens, grads, grads_edge, moved)
            own_rows(full, 1, 0).wait()
            load_every().wait()

        @pl.when((index >= blocks) & (index < units) & (lax.rem(index - blocks, 2) == 0))
        def _():
            own[whole(index), :] = product((index - blocks) // 2, grads)

        @pl.when((index >= blocks) & (index < units) & (lax.rem(index - blocks, 2) == 1))
        def _():
            own[whole(index), :] = product((index - blocks) // 2, moved)

        k = index - blocks

        @pl.when((k >= 0) & (k < 2 * pieces))
        def _():
            load_weights(k).wait()

            @pl.when(k + 1 < 2 * pieces)
            def _():
                load_weights(k + 1).start()

            terms = input_terms(lax.rem(k, 2))

            @pl.when(k < pieces)
            def _():
                @pl.when(k >= 2)
                def _():
                    leave(k - 2).wait_send()

                leaving[lax.rem(k, 2)] = terms
                leave(k).start()

            @pl.when(k >= pieces)
            def _():
                leave(k - pieces).wait_recv()
                coming[k - pieces] += terms
                result(k - pieces).start()

        u = index - at

        @pl.when((u >= 0) & (u < units))
        def _():
            for j in range(line - 1, 0, -1):

                owner = owner_of(u, j)

                @pl.when((at == 0) & (at < owner))
                def _(j=j):
                    up(own.at[chunk(u, j)], u, j).start()

                @pl.when((at > 0) & (at <= owner))
                def _(j=j):
                    up(ups.at[u, j - 1], u, j).wait_recv()

                @pl.when((at > 0) & (at < owner))
                def _(j=j):
                    ups[u, j - 1] = (ups[u, j - 1].astype(F32) + own[chunk(u, j)].astype(F32)).astype(BF16)
                    up(ups.at[u, j - 1], u, j).start()

        v = index - (line - 1 - at)

        @pl.when((v >= 0) & (v < units))
        def _():
            for j in range(line - 1):

                owner = owner_of(v, j)

                @pl.when((at == line - 1) & (at > owner))
                def _(j=j):
                    down(own.at[chunk(v, j)], v, j).start()

                @pl.when((at < line - 1) & (at >= owner))
                def _(j=j):
                    down(downs.at[v, j], v, j).wait_recv()

                @pl.when((at < line - 1) & (at > owner))
                def _(j=j):
                    downs[v, j] = (downs[v, j].astype(F32) + own[chunk(v, j)].astype(F32)).astype(BF16)
                    down(downs.at[v, j], v, j).start()

        w = index - (line - 1)

        @pl.when((w >= 0) & (w < units) & direct(w))
        def _():
            acc[...] = own[chunk(w, at)].astype(F32)

            @pl.when(at > 0)
            def _():
                acc[...] += ups[w, at - 1].astype(F32)

            @pl.when(at < line - 1)
            def _():
                acc[...] += downs[w, at].astype(F32)

            own[chunk(w, at)] = acc[...].astype(BF16)
            keep(w).start()

            @pl.when(at < line - 1)
            def _():
                along(own.at[chunk(w, at)], w, at, 0, 0).start()

            @pl.when(at > 0)
            def _():
                along(own.at[chunk(w, at)], w, at, 1, 0).start()

        @pl.when((w >= 0) & (w < units) & turned(w))
        def _():
            @pl.when(at == 0)
            def _():
                for j in range(line // 2):
                    own[chunk(w, j)] = (own[chunk(w, j)].astype(F32) + downs[w, j].astype(F32)).astype(BF16)

            @pl.when(at == line - 1)
            def _():
                for j in range(line // 2, line):
                    own[chunk(w, j)] = (own[chunk(w, j)].astype(F32) + ups[w, j - 1].astype(F32)).astype(BF16)

            @pl.when(at_end)
            def _():
                keep_part(w).start()
                for way in range(2):
                    over_part(own.at[end_rows(w)], w, way).start()

        c = index - line

        @pl.when((c >= 0) & (c < units) & turned(c) & at_end)
        def _():
            keep_part(c).wait()
            for way in range(2):
                over_part(out.at[(beside, below)[way], end_rows(c)], c, way).wait_recv()
                onward_part((beside, below)[way], c, way).start()

        d = index - line - 1

        @pl.when((d >= 0) & (d < units) & turned(d) & at_end)
        def _():
            for way in range(2):
                onward_part(across_from, d, way).wait_recv()

        for steps in range(4):
            for way in range(2):
                hops = at if way == 0 else line - 1 - at
                e = d - steps - hops

                @pl.when((e >= 0) & (e < units) & turned(e))
                def _(e=e, steps=steps, way=way, hops=hops):
                    @pl.when(hops > 0)
                    def _():
                        column(steps, e, way).wait_recv()

                    @pl.when(hops < line - 1)
                    def _():
                        column(steps, e, way).start()

        for hop in range(1, line):
            x = index - (line - 1) - hop

            @pl.when((x >= 0) & (x < units) & direct(x))
            def _(x=x, hop=hop):
                @pl.when(at >= hop)
                def _():
                    src = out.at[here, chunk(x, at - hop)]
                    along(src, x, at - hop, 0, 0).wait_recv()
                    if hop < line - 1:

                        @pl.when(at < line - 1)
                        def _():
                            along(src, x, at - hop, 0, hop).start()

                @pl.when(at + hop < line)
                def _():
                    src = out.at[here, chunk(x, at + hop)]
                    along(src, x, at + hop, 1, 0).wait_recv()
                    if hop < line - 1:

                        @pl.when(at > 0)
                        def _():
                            along(src, x, at + hop, 1, hop).start()

        y = index - 2 * (line - 1)

        @pl.when((y >= 0) & (y < units) & direct(y))
        def _():
            keep(y).wait()

        @pl.when((y >= 0) & (y < units - tail) & direct(y))
        def _():
            over(y, 0).start()
            over(y, 1).start()

        z = y - LAG

        @pl.when((z >= 0) & (z < units - tail) & direct(z))
        def _():
            for way in range(2):
                place = out.at[(beside, below)[way], rows(z, 0, unit)]
                remote(place, place, plane_send.at[z * 4 + way], plane_recv.at[z * 4 + way], "dp", (beside, below)[way]).wait_recv()
                onward(z, way).start()

        t = z - LAG

        @pl.when((t >= 0) & (t < units - tail) & direct(t))
        def _():
            for way in range(2):
                corner(t, way).wait_recv()

        return none

    last_turned = units // turn * turn - 1
    lax.fori_loop(
        0, max(units + 2 * (line - 1), units - tail + 2 * (line - 1) + 2 * LAG, last_turned + 2 * line + 4), stage, 0
    )

    def settle(u, none):
        for j in range(1, line):

            @pl.when(at < owner_of(u, j))
            def _(j=j):
                up(ups.at[u, j - 1], u, j).wait_send()

        for j in range(line - 1):

            @pl.when(at > owner_of(u, j))
            def _(j=j):
                down(downs.at[u, j], u, j).wait_send()

        for hop in range(line - 1):

            @pl.when(direct(u) & (at >= hop) & (at < line - 1))
            def _(hop=hop):
                along(out.at[here, chunk(u, at - hop)], u, at - hop, 0, hop).wait_send()

            @pl.when(direct(u) & (at + hop < line) & (at > 0))
            def _(hop=hop):
                along(out.at[here, chunk(u, at + hop)], u, at + hop, 1, hop).wait_send()

        @pl.when(turned(u))
        def _():
            for steps in range(4):

                @pl.when(at < line - 1)
                def _(steps=steps):
                    column(steps, u, 0).wait_send()

                @pl.when(at > 0)
                def _(steps=steps):
                    column(steps, u, 1).wait_send()

        @pl.when(direct(u) & (u < units - tail))
        def _():
            for way in range(2):
                over(u, way).wait_send()
                onward(u, way).wait_send()

        @pl.when(turned(u) & at_end)
        def _():
            for way in range(2):
                over_part(out.at[here, end_rows(u)], u, way).wait_send()
                onward_part(here, u, way).wait_send()

        return none

    lax.fori_loop(0, units, settle, 0)
    for steps in range(1, 4):
        for edge in range(2):
            swap(steps, edge).wait_send()
    own_rows(full, 1, 1).wait_send()
    for step in range(pieces - 2, pieces):
        leave(step).wait_send()
    for step in range(pieces):
        result(step).wait()
    for step in range(1, line):
        sums_copy(across, at, line, "seq", 0, step).wait_send()
    for step in range(1, plane):
        sums_copy(around, here, plane, "dp", 1, step).wait_send()


def spread(seqs, tokens, hidden, full, grads_two, grads_one, taps, sums):
    line, plane = lax.axis_size("seq"), lax.axis_size("dp")
    width = grads_two.shape[1]
    rows = grads_two.shape[0] // plane
    depth = 2 * full.shape[1]
    units = 3 * depth // (line * PART)
    channels = taps.shape[3]
    narrow = depth // (units - units // 3)
    pieces = channels // narrow
    turns = units // TURN
    dma = pltpu.SemaphoreType.DMA
    hbm = pl.BlockSpec(memory_space=pl.ANY)
    return pl.pallas_call(
        functools.partial(spread_kernel, seqs, tokens, PART, TURN, TAIL),
        out_shape=(
            jax.ShapeDtypeStruct((plane, 3 * depth, width), BF16),
            jax.ShapeDtypeStruct((rows, channels), F32),
            jax.ShapeDtypeStruct(sums.shape, F32),
        ),
        in_specs=[hbm] * 5 + [VMEM],
        out_specs=[hbm, hbm, VMEM],
        scratch_shapes=[
            pltpu.VMEM((plane * rows, depth), BF16),
            pltpu.VMEM((plane * rows, width), BF16),
            pltpu.VMEM((plane, EDGE, width), BF16),
            pltpu.VMEM((plane * rows, width), BF16),
            pltpu.VMEM((3 * depth, width), BF16),
            pltpu.VMEM((units, line - 1, PART, width), BF16),
            pltpu.VMEM((units, line - 1, PART, width), BF16),
            pltpu.VMEM((PART, width), F32),
            pltpu.VMEM((line,) + sums.shape, F32),
            pltpu.VMEM((plane,) + sums.shape, F32),
            pltpu.VMEM(grads_one.shape, BF16),
            pltpu.VMEM((2, 2, 3, narrow, channels), BF16),
            pltpu.VMEM((2, rows, narrow), F32),
            pltpu.VMEM((pieces, rows, narrow), F32),
            dma((4,)),
            dma((2, 8)),
            dma((2, units * (line - 1))),
            dma((2, units * (line - 1))),
            dma((units * 2 * (line - 1),)),
            dma((units * line,)),
            dma((turns * 8,)),
            dma((turns * 8,)),
            dma((units,)),
            dma((units * 4,)),
            dma((units * 4,)),
            dma((2, 2, max(line, plane) - 1)),
            dma((2,)),
            dma((2,)),
            dma((pieces,)),
            dma((pieces,)),
            dma((2, 2)),
            pltpu.SemaphoreType.REGULAR,
        ],
        compiler_params=pltpu.CompilerParams(
            collective_id=4, has_side_effects=True, vmem_limit_bytes=62 * 2**20
        ),
        cost_estimate=pl.CostEstimate(
            flops=6 * plane * rows * depth * width, bytes_accessed=depth * width * 48, transcendentals=0
        ),
        name="spread",
    )(hidden, full, grads_two, grads_one, taps, sums)


def widen_kernel(blocks, core, given, *refs):
    out = refs[-1]
    per = given.shape[2] // 128
    for tile in range(3 * blocks):
        source, place = divmod(tile, per)
        gate, column = divmod(tile, blocks)
        out[0, gate, :, column * 128 : column * 128 + 128] = given[
            source, :, place * 128 : place * 128 + 128
        ].astype(F32)


def widen(gathered, first, taps, start, count, depth, channels, unit, core, into=None):
    plane, _, width = gathered.shape
    last = depth // unit - 1

    def source(tap, step, core):
        return (0, first + step * taps + tap, 0)

    def target(tap, step, core):
        block = start + step
        return (tap, 0, jnp.where(core[0] == 0, block, last - block), 0)

    given = (core, gathered) if into is None else (core, gathered, into)
    return pl.pallas_call(
        functools.partial(widen_kernel, channels // 128),
        grid_spec=pltpu.PrefetchScalarGridSpec(
            num_scalar_prefetch=1,
            grid=(taps, count),
            in_specs=[pl.BlockSpec((plane, unit, width), source)] + [pl.BlockSpec(memory_space=pl.ANY)] * (len(given) - 2),
            out_specs=pl.BlockSpec((1, 3, unit, channels), target),
        ),
        out_shape=jax.ShapeDtypeStruct((taps, 3, depth, channels), F32),
        input_output_aliases={} if into is None else {2: 0},
        compiler_params=pltpu.CompilerParams(vmem_limit_bytes=40 * 2**20),
        cost_estimate=pl.CostEstimate(
            flops=0, bytes_accessed=taps * count * unit * (plane * width * 2 + channels * 12), transcendentals=0
        ),
        name="widen",
    )(*given)


def shifted(value, axis, steps):
    count = lax.axis_size(axis)
    initial, last = (max(0, -steps), min(count, count - steps))
    return lax.ppermute(value, axis, [(source, source + steps) for source in range(initial, last)])


def gather_channels(value):
    count = lax.axis_size("mp")
    if count != 2:
        return lax.all_gather(value, "mp", axis=value.ndim - 1, tiled=True)
    other = lax.ppermute(value, "mp", [(0, 1), (1, 0)])
    second = lax.axis_index("mp") == 1
    return jnp.concatenate([jnp.where(second, other, value), jnp.where(second, value, other)], value.ndim - 1)


def sum_channels(terms):
    count = lax.axis_size("mp")
    if count != 2:
        return lax.psum_scatter(terms, "mp", scatter_dimension=1, tiled=True)
    width = terms.shape[1] // 2
    second = lax.axis_index("mp") == 1
    low, high = terms[:, :width], terms[:, width:]
    other = lax.ppermute(jnp.where(second, low, high), "mp", [(0, 1), (1, 0)])
    return jnp.where(second, high, low) + other


def dot(lhs, rhs, dims):
    return lax.dot_general(lhs, rhs, (dims, ((), ())), preferred_element_type=F32)


def reduce_weights(partial):
    shard = lax.psum_scatter(partial.astype(BF16), ("dp", "seq"), scatter_dimension=0, tiled=True)
    return lax.all_gather(shard, ("dp", "seq"), axis=0, tiled=True).astype(F32)


def local(inputs, starts, init_state, weight_one, bias_one, weight_two, bias_two, cotangent):
    seqs, tokens, channels = inputs.shape
    rows = seqs * tokens
    width = weight_one.shape[1]
    keep = jnp.broadcast_to((1 - starts).astype(F32).reshape(rows, 1), (rows, 128))
    taps = weight_one.transpose(0, 2, 1, 3)
    mix = weight_two.transpose(1, 0, 2)

    line, plane = lax.axis_size("seq"), lax.axis_size("dp")
    tiles = 3 * channels // 128
    spreads = plane == 4 and lax.axis_size("mp") == 2 and seqs == 2 and line % 2 == 0 and channels % 128 == 0
    spreads = spreads and width % (line * PART) == 0 and line > 1
    block = -(-tiles // plane) * 128
    lanes = plane * block if spreads else 3 * channels
    upstream = cotangent.reshape(rows, channels)
    if spreads:
        hidden, upd, fgt, out, state, entering, full_hidden, every = pool_first(
            seqs, tokens, inputs.reshape(rows, channels), taps, bias_one, keep, init_state[0]
        )
        pooled_two, grad_two, planes_two, sums_two, every_hidden = pool_upper(
            seqs, tokens, lanes, full_hidden, hidden, mix, bias_two, keep, init_state[1], upstream
        )
        extended, sums_one, swapped = pool_lower(
            seqs, tokens, planes_two, grad_two, mix, keep, upd, fgt, out, state, entering
        )
        sums = jnp.concatenate([jnp.sum(sums_one, 1), jnp.sum(sums_two, 1)])
        gathered, input_grad, sums = spread(
            seqs,
            tokens,
            every_hidden.reshape(plane * rows, channels),
            every.reshape(plane * rows, channels),
            swapped.reshape(plane * rows, block),
            extended,
            taps,
            sums,
        )
        unit = line * PART
        blocks = width // unit
        core = lax.axis_index("mp").reshape(1)
        behind = TAIL // 2
        kept = lax.dynamic_slice(
            gathered, (lax.axis_index("dp"), (3 * blocks - TAIL) * unit, 0), (1, TAIL * unit, block)
        )
        tail = lax.all_gather(kept, "dp", axis=0, tiled=True)
        weight_two_grad = widen(gathered, 0, 1, 0, blocks, width, channels, unit, core)
        weight_one_grad = widen(gathered, blocks, 2, 0, blocks - behind, width, channels, unit, core)
        weight_one_grad = widen(
            tail, 0, 2, blocks - behind, behind, width, channels, unit, core, weight_one_grad
        )
        weight_two_grad = weight_two_grad[0].transpose(1, 0, 2)
        weight_one_grad = weight_one_grad.transpose(0, 2, 1, 3)
    else:
        edge = gather_channels(shifted(inputs[:, -1], "seq", 1))
        full = gather_channels(inputs)
        previous = jnp.concatenate([edge[:, None], full[:, :-1]], 1).reshape(rows, width)
        full = full.reshape(rows, width)
        both = jnp.concatenate([full, previous], 1)
        gates_one = jnp.einsum(
            "tkd,kgdc->gtc", both.reshape(rows, 2, width), taps, preferred_element_type=F32
        )
        hidden, upd, fgt, out, state, entering = pool_forward(seqs, tokens, gates_one, bias_one, keep, init_state[0])
        full_hidden = gather_channels(hidden)
        gates_two = jnp.einsum("td,gdc->gtc", full_hidden, mix, preferred_element_type=F32)
        pooled_two, grad_two, planes_two, sums_two = pool_top(
            seqs, tokens, lanes, gates_two, bias_two, keep, init_state[1], upstream
        )
        hidden_terms = jnp.einsum("gtc,gdc->td", planes_two, mix, preferred_element_type=F32)
        hidden_grad = sum_channels(hidden_terms)
        extended, sums_one = pool_backward(seqs, tokens, lanes, hidden_grad, keep, upd, fgt, out, state, entering)
        grad_one = extended[:rows]
        input_terms = jnp.einsum(
            "tgc,kgdc->ktd", grad_one.reshape(rows, 3, channels), taps, preferred_element_type=F32
        ).reshape(2, seqs, tokens, width)
        late = input_terms[1]
        late = jnp.concatenate([late[:, 1:], shifted(late[:, 0], "seq", -1)[:, None]], 1)
        input_grad = sum_channels((input_terms[0] + late).reshape(rows, width))
        sums = jnp.concatenate([jnp.sum(sums_one, 1), jnp.sum(sums_two, 1)])
        sums = lax.psum(sums, ("dp", "seq"))
        weight_two_grad = reduce_weights(dot(full_hidden, grad_two, ((0,), (0,)))).reshape(width, 3, channels)
        weight_one_grad = jnp.stack(
            [
                reduce_weights(dot(full, grad_one, ((0,), (0,)))),
                reduce_weights(dot(previous, grad_one, ((0,), (0,)))),
            ]
        ).reshape(2, width, 3, channels)
    return (
        pooled_two.reshape(seqs, tokens, channels),
        input_grad.reshape(seqs, tokens, channels),
        weight_one_grad,
        sums[:3],
        weight_two_grad,
        sums[3:],
    )


def solution(mesh):
    return jax.shard_map(
        local,
        mesh=mesh,
        in_specs=(
            P("dp", "seq", "mp"),
            P("dp", "seq"),
            P(None, "dp", "mp"),
            P(None, None, None, "mp"),
            P(None, "mp"),
            P(None, None, "mp"),
            P(None, "mp"),
            P("dp", "seq", "mp"),
        ),
        out_specs=(
            P("dp", "seq", "mp"),
            P("dp", "seq", "mp"),
            P(None, None, None, "mp"),
            P(None, "mp"),
            P(None, None, "mp"),
            P(None, "mp"),
        ),
        check_vma=False,
    )
```

```python
import functools

import jax
import jax.numpy as jnp
from jax import lax
from jax.experimental import pallas as pl
from jax.experimental.pallas import tpu as pltpu
from jax.sharding import PartitionSpec as P

F32 = jnp.float32
BF16 = jnp.bfloat16
SUB = 8
STEP = 16
EDGE = 16
PART = 64
LAG = 2
TURN = 4
TAIL = 2
VMEM = pl.BlockSpec(memory_space=pltpu.VMEM)


def sigmoid(x):
    return 0.5 * jnp.tanh(0.5 * x) + 0.5


def lane_blocks(channels):
    width = 384 if channels % 384 == 0 else channels
    return [slice(at, at + width) for at in range(0, channels, width)]


def scan_down(scale, shift):
    row = lax.broadcasted_iota(jnp.int32, scale.shape, 0)
    for step in (1, 2, 4):
        earlier = row >= step
        scale_before = jnp.where(earlier, pltpu.roll(scale, step, 0), 1.0)
        shift_before = jnp.where(earlier, pltpu.roll(shift, step, 0), 0.0)
        shift = scale * shift_before + shift
        scale = scale * scale_before
    return scale, shift


def scan_up(scale, shift):
    row = lax.broadcasted_iota(jnp.int32, scale.shape, 0)
    for step in (1, 2, 4):
        later = row < SUB - step
        scale_after = jnp.where(later, pltpu.roll(scale, SUB - step, 0), 1.0)
        shift_after = jnp.where(later, pltpu.roll(shift, SUB - step, 0), 0.0)
        shift = scale * shift_after + shift
        scale = scale * scale_after
    return scale, shift


def greet(*axes):
    for axis in axes:
        count = lax.axis_size(axis)
        me = lax.axis_index(axis)
        for step in range(1, count):
            pl.semaphore_signal(
                pltpu.get_barrier_semaphore(),
                inc=1,
                device_id={axis: lax.rem(me + step, count)},
                device_id_type=pl.DeviceIdType.MESH,
            )


def met(*axes):
    pl.semaphore_wait(pltpu.get_barrier_semaphore(), sum(lax.axis_size(axis) - 1 for axis in axes))


def remote(src, dst, send, recv, axis, target):
    return pltpu.make_async_remote_copy(
        src_ref=src,
        dst_ref=dst,
        send_sem=send,
        recv_sem=recv,
        device_id={axis: target},
        device_id_type=pl.DeviceIdType.MESH,
    )


def to_all(src, slots, send_sems, recv_sems, axis):
    count = lax.axis_size(axis)
    me = lax.axis_index(axis)
    copies = []
    for step in range(1, count):
        copies.append(
            pltpu.make_async_remote_copy(
                src_ref=src,
                dst_ref=slots.at[step - 1],
                send_sem=send_sems.at[step - 1],
                recv_sem=recv_sems.at[step - 1],
                device_id={axis: lax.rem(me + step, count)},
                device_id_type=pl.DeviceIdType.MESH,
            )
        )
    for copy in copies:
        copy.start()
    return copies


def from_earlier(slots, initial, scale_rows, shift_rows, axis):
    count = lax.axis_size(axis)
    me = lax.axis_index(axis)
    state = initial
    for block in range(count - 1):
        slot = jnp.maximum(me - block - 1, 0)
        after = slots[slot, scale_rows, :] * state + slots[slot, shift_rows, :]
        state = jnp.where(block < me, after, state)
    return state


def from_later(slots, shape, scale_rows, shift_rows, axis):
    count = lax.axis_size(axis)
    me = lax.axis_index(axis)
    message = jnp.zeros(shape, F32)
    for block in range(count - 1, 0, -1):
        slot = jnp.minimum(me + count - block - 1, count - 2)
        after = slots[slot, scale_rows, :] * message + slots[slot, shift_rows, :]
        message = jnp.where(block > me, after, message)
    return message


def first_pass(seqs, tokens, channels, gates, bias, keep, upd, fgt, out, scale, shift, summary):
    def body(at, carried):
        given = list(carried)
        for seq in range(seqs):
            for half in range(STEP // SUB):
                rows = pl.ds(pl.multiple_of(seq * tokens + at * STEP + half * SUB, SUB), SUB)
                kept = keep[rows, :][:, 0:1]
                for number, lanes in enumerate(lane_blocks(channels)):
                    u = jnp.tanh(gates[0, rows, lanes] + bias[0:1, lanes])
                    f = sigmoid(gates[1, rows, lanes] + bias[1:2, lanes])
                    o = sigmoid(gates[2, rows, lanes] + bias[2:3, lanes])
                    upd[rows, lanes] = u
                    fgt[rows, lanes] = f
                    out[rows, lanes] = o
                    a, b = scan_down(f * kept, (1.0 - f) * u)
                    place = (seq * len(lane_blocks(channels)) + number) * 2
                    b = a * given[place + 1] + b
                    a = a * given[place]
                    scale[rows, lanes] = a
                    shift[rows, lanes] = b
                    given[place] = a[SUB - 1 : SUB]
                    given[place + 1] = b[SUB - 1 : SUB]
        return tuple(given)

    begin = []
    for seq in range(seqs):
        for lanes in lane_blocks(channels):
            width = lanes.stop - lanes.start
            begin += [jnp.ones((1, width), F32), jnp.zeros((1, width), F32)]
    end = lax.fori_loop(0, tokens // STEP, body, tuple(begin))
    place = 0
    for seq in range(seqs):
        for lanes in lane_blocks(channels):
            summary[seq : seq + 1, lanes] = end[place]
            summary[seqs + seq : seqs + seq + 1, lanes] = end[place + 1]
            place += 2


def back_pass(seqs, tokens, channels, upstream, keep, fgt, out, scale, shift, summary, row0):
    steps = tokens // STEP

    def body(index, carried):
        at = steps - 1 - index
        given = list(carried)
        for seq in range(seqs):
            whole = pl.ds(pl.multiple_of(seq * tokens + at * STEP, STEP), STEP)
            for number, lanes in enumerate(lane_blocks(channels)):
                ups = upstream[whole, lanes].astype(F32)
                place = (seq * len(lane_blocks(channels)) + number) * 2
                for half in reversed(range(STEP // SUB)):
                    rows = pl.ds(pl.multiple_of(seq * tokens + at * STEP + half * SUB, SUB), SUB)
                    kept = keep[rows, :][:, 0:1]
                    retain = fgt[rows, lanes] * kept
                    direct = ups[half * SUB : half * SUB + SUB] * out[rows, lanes]
                    a, b = scan_up(retain, retain * direct)
                    b = a * given[place + 1] + b
                    a = a * given[place]
                    scale[rows, lanes] = a
                    shift[rows, lanes] = b
                    given[place] = a[0:1]
                    given[place + 1] = b[0:1]
        return tuple(given)

    begin = []
    for seq in range(seqs):
        for lanes in lane_blocks(channels):
            width = lanes.stop - lanes.start
            begin += [jnp.ones((1, width), F32), jnp.zeros((1, width), F32)]
    end = lax.fori_loop(0, steps, body, tuple(begin))
    place = 0
    for seq in range(seqs):
        for lanes in lane_blocks(channels):
            summary[row0 + seq : row0 + seq + 1, lanes] = end[place]
            summary[row0 + seqs + seq : row0 + seqs + seq + 1, lanes] = end[place + 1]
            place += 2


def states_pass(seq, tokens, channels, entering, out, scale, shift, state, pooled):
    def body(at, none):
        rows = pl.ds(pl.multiple_of(seq * tokens + at * STEP, STEP), STEP)
        for lanes in lane_blocks(channels):
            value = scale[rows, lanes] * entering[seq : seq + 1, lanes] + shift[rows, lanes]
            state[rows, lanes] = value
            pooled[rows, lanes] = (out[rows, lanes] * value).astype(BF16)
        return none

    lax.fori_loop(0, tokens // STEP, body, 0)


def grads_pass(seqs, tokens, channels, message, entering, upstream, keep, upd, fgt, out, state, scale, shift, grads, planes, sums):
    steps = tokens // STEP
    sums[...] = jnp.zeros_like(sums)
    if grads.shape[1] > 3 * channels:
        grads[:, 3 * channels :] = jnp.zeros((grads.shape[0], grads.shape[1] - 3 * channels), BF16)
    for seq in range(seqs):
        for lanes in lane_blocks(channels):
            width = lanes.stop - lanes.start

            def body(index, later, seq=seq, lanes=lanes, width=width):
                at = steps - 1 - index
                whole = pl.ds(pl.multiple_of(seq * tokens + at * STEP, STEP), STEP)
                row = lax.broadcasted_iota(jnp.int32, (STEP, width), 0)
                kept = keep[whole, :][:, 0:1]
                ups = upstream[whole, lanes].astype(F32)
                u, f, o = upd[whole, lanes], fgt[whole, lanes], out[whole, lanes]
                states = state[whole, lanes]
                arriving = scale[whole, lanes] * message[seq : seq + 1, lanes] + shift[whole, lanes]
                adjoint = ups * o + jnp.where(row == STEP - 1, later, pltpu.roll(arriving, STEP - 1, 0))
                tile = pl.ds(pl.multiple_of(seq * tokens + jnp.maximum(at * STEP - SUB, 0), SUB), SUB)
                last = state[tile, lanes][SUB - 1 : SUB]
                first = jnp.where(at == 0, entering[seq : seq + 1, lanes], last)
                before = jnp.where(row == 0, first, pltpu.roll(states, 1, 0))
                given = [
                    adjoint * (1.0 - f) * (1.0 - u * u),
                    adjoint * (before * kept - u) * f * (1.0 - f),
                    ups * states * o * (1.0 - o),
                ]
                for gate, value in enumerate(given):
                    value = value.astype(BF16)
                    grads[whole, gate * channels + lanes.start : gate * channels + lanes.stop] = value
                    if planes is not None:
                        planes[gate, whole, lanes] = value
                    value = value.astype(F32)
                    total = value[:SUB]
                    for half in range(1, STEP // SUB):
                        total = total + value[half * SUB : half * SUB + SUB]
                    sums[gate, :, lanes] += total
                return arriving[0:1]

            lax.fori_loop(0, steps, body, message[seq : seq + 1, lanes])


def forward_kernel(seqs, tokens, channels, gates, bias, keep, initial, hidden, upd, fgt, out, state, entering, scale, shift, summary, slots, send_sems, recv_sems):
    greet("seq")
    first_pass(seqs, tokens, channels, gates, bias, keep, upd, fgt, out, scale, shift, summary)
    met("seq")
    copies = to_all(summary, slots, send_sems, recv_sems, "seq")
    for copy in copies:
        copy.wait()
    entering[...] = from_earlier(slots, initial[...], slice(0, seqs), slice(seqs, 2 * seqs), "seq")
    for seq in range(seqs):
        states_pass(seq, tokens, channels, entering, out, scale, shift, state, hidden)


def top_kernel(seqs, tokens, channels, gates, bias, keep, initial, cotangent, pooled, grads, planes, sums, upd, fgt, out, state, entering, message, scale, shift, back_scale, back_shift, summary, slots, send_sems, recv_sems):
    greet("seq")
    first_pass(seqs, tokens, channels, gates, bias, keep, upd, fgt, out, scale, shift, summary)
    back_pass(seqs, tokens, channels, cotangent, keep, fgt, out, back_scale, back_shift, summary, 2 * seqs)
    met("seq")
    copies = to_all(summary, slots, send_sems, recv_sems, "seq")
    for copy in copies:
        copy.wait()
    entering[...] = from_earlier(slots, initial[...], slice(0, seqs), slice(seqs, 2 * seqs), "seq")
    message[...] = from_later(
        slots, (seqs, channels), slice(2 * seqs, 3 * seqs), slice(3 * seqs, 4 * seqs), "seq"
    )
    for seq in range(seqs):
        states_pass(seq, tokens, channels, entering, out, scale, shift, state, pooled)
    grads_pass(seqs, tokens, channels, message, entering, cotangent, keep, upd, fgt, out, state, back_scale, back_shift, grads, planes, sums)


def pass_edges(seqs, tokens, grads, edges, arrived, edge_sems):
    count = lax.axis_size("seq")
    me = lax.axis_index("seq")
    row = lax.broadcasted_iota(jnp.int32, edges.shape, 0)
    firsts = jnp.zeros(edges.shape, F32)
    for seq in range(seqs):
        tile = grads[seq * tokens : seq * tokens + EDGE, :].astype(F32)
        firsts = jnp.where(row == seq, pltpu.roll(tile, seq, 0) if seq else tile, firsts)
    edges[...] = firsts.astype(BF16)
    copy = pltpu.make_async_remote_copy(
        src_ref=edges,
        dst_ref=arrived,
        send_sem=edge_sems.at[0],
        recv_sem=edge_sems.at[1],
        device_id={"seq": lax.rem(me + count - 1, count)},
        device_id_type=pl.DeviceIdType.MESH,
    )
    rows = slice(seqs * tokens, seqs * tokens + EDGE)

    @pl.when(me > 0)
    def _():
        copy.start()

    @pl.when(me < count - 1)
    def _():
        copy.wait_recv()
        grads[rows, :] = arrived[...]

    @pl.when(me == count - 1)
    def _():
        grads[rows, :] = jnp.zeros(edges.shape, BF16)

    @pl.when(me > 0)
    def _():
        copy.wait_send()


def backward_kernel(seqs, tokens, channels, upstream, keep, upd, fgt, out, state, entering, grads, sums, message, scale, shift, summary, slots, send_sems, recv_sems, edges, arrived, edge_sems):
    greet("seq")
    back_pass(seqs, tokens, channels, upstream, keep, fgt, out, scale, shift, summary, 0)
    met("seq")
    copies = to_all(summary, slots, send_sems, recv_sems, "seq")
    for copy in copies:
        copy.wait()
    message[...] = from_later(slots, (seqs, channels), slice(0, seqs), slice(seqs, 2 * seqs), "seq")
    grads_pass(seqs, tokens, channels, message, entering, upstream, keep, upd, fgt, out, state, scale, shift, grads, None, sums)
    pass_edges(seqs, tokens, grads, edges, arrived, edge_sems)


def neighbours():
    here = lax.axis_index("dp")
    beside = here + 1 - 2 * lax.rem(here, 2)
    return here, beside, lax.rem(here + 2, 4), lax.rem(beside + 2, 4)


def relay(value, every, plane_sems, kept_sem):
    here, beside, below, corner = neighbours()
    near = (beside, below)
    half = value.shape[0] // 2

    def over(src, owner, way):
        place = every.at[owner]
        return remote(src, place, plane_sems.at[0, way], plane_sems.at[1, way], "dp", near[way])

    def onward(owner, way):
        place = every.at[owner, pl.ds(way * half, half)]
        return remote(place, place, plane_sems.at[0, 2 + way], plane_sems.at[1, 2 + way], "dp", near[1 - way])

    def keep():
        return pltpu.make_async_copy(value, every.at[here], kept_sem)

    def start():
        for way in range(2):
            over(value, here, way).start()
        keep().start()

    def forward():
        for way in range(2):
            over(every.at[near[way]], near[way], way).wait_recv()
            onward(near[way], way).start()

    def finish():
        for way in range(2):
            over(value, here, way).wait_send()
            onward(near[way], way).wait_send()
            onward(corner, way).wait_recv()
        keep().wait()

    return start, forward, finish


def first_stage(seqs, tokens, channels, inputs, taps, bias, keep, initial, full_hidden, every, both, edges, weights, gates, hidden, state, entering, scale, shift, summary, slots, send_sems, recv_sems, weight_sems, plane_sems, kept_sem, pair_sems, edge_sems):
    axes = ("seq", "dp", "mp")
    line, at, mine = lax.axis_size("seq"), lax.axis_index("seq"), lax.axis_index("mp")
    after, before = lax.rem(at + 1, line), lax.rem(at + line - 1, line)
    greet(*axes)
    pl.semaphore_signal(
        pltpu.get_barrier_semaphore(),
        inc=1,
        device_id={"seq": before, "mp": 1 - mine},
        device_id_type=pl.DeviceIdType.MESH,
    )
    rows = seqs * tokens
    half = rows // 2
    gather_start, gather_forward, gather_finish = relay(inputs, every, plane_sems, kept_sem)

    def load(step):
        slot = lax.rem(step, 2)
        side = jnp.where(lax.rem(step // 3, 2) == 0, mine, 1 - mine)
        return pltpu.make_async_copy(
            taps.at[step // 6, lax.rem(step, 3), pl.ds(pl.multiple_of(side * channels, 128), channels), :],
            weights.at[slot],
            weight_sems.at[slot],
        )

    def lanes_of(core):
        return pl.ds(pl.multiple_of(core * channels, 128), channels)

    own = pltpu.make_async_copy(inputs, both.at[0, :, lanes_of(mine)], pair_sems.at[0])
    give = remote(inputs, both.at[0, :, lanes_of(mine)], pair_sems.at[1], pair_sems.at[2], "mp", 1 - mine)
    take = remote(inputs, both.at[0, :, lanes_of(1 - mine)], pair_sems.at[1], pair_sems.at[2], "mp", 1 - mine)

    def edge(seq, other, arriving=False):
        core = jnp.where(other, 1 - mine, mine)
        return pltpu.make_async_remote_copy(
            src_ref=inputs.at[seq * tokens + tokens - EDGE : seq * tokens + tokens],
            dst_ref=edges.at[core if arriving else mine, seq],
            send_sem=edge_sems.at[0, other, seq],
            recv_sem=edge_sems.at[1, other, seq],
            device_id={"seq": after, "mp": core},
            device_id_type=pl.DeviceIdType.MESH,
        )

    load(0).start()
    own.start()
    pl.semaphore_wait(pltpu.get_barrier_semaphore(), sum(lax.axis_size(axis) - 1 for axis in axes) + 1)
    give.start()

    @pl.when(at < line - 1)
    def _():
        for seq in range(seqs):
            for other in range(2):
                edge(seq, other).start()

    @pl.when(at == 0)
    def _():
        edges[...] = jnp.zeros(edges.shape, BF16)

    gather_start()
    own.wait()

    def shift_down():
        width = 2 * channels
        steps = tokens // STEP

        def body(index, none):
            seq, tile = index // steps, lax.rem(index, steps)
            row = lax.broadcasted_iota(jnp.int32, (STEP, width), 0)
            place = pl.ds(pl.multiple_of(index * STEP, STEP), STEP)
            ahead = pl.ds(pl.multiple_of(jnp.maximum(index - 1, 0) * STEP, STEP), STEP)
            last = both[0, ahead, :].astype(F32)[STEP - 1 : STEP]
            outer = jnp.concatenate([edges[0, seq], edges[1, seq]], 1).astype(F32)[EDGE - 1 : EDGE]
            moved = pltpu.roll(both[0, place, :].astype(F32), 1, 0)
            both[1, place, :] = jnp.where(row == 0, jnp.where(tile == 0, outer, last), moved).astype(BF16)
            return none

        lax.fori_loop(0, rows // STEP, body, 0)

    def body(step, none):
        @pl.when(step == 3)
        def _():
            take.wait_recv()

        @pl.when(step == 6)
        def _():
            @pl.when(at > 0)
            def _():
                for seq in range(seqs):
                    for other in range(2):
                        edge(seq, other, True).wait_recv()

            shift_down()

        load(step).wait()

        @pl.when(step < 11)
        def _():
            load(step + 1).start()

        gate, part = lax.rem(step, 3), lax.rem(step // 3, 2)
        columns = lanes_of(jnp.where(part == 0, mine, 1 - mine))
        for side in range(2):
            place = pl.ds(side * half, half)
            term = jnp.dot(
                both[step // 6, place, columns], weights[lax.rem(step, 2)], preferred_element_type=F32
            )
            gates[gate, place, :] = jnp.where(step < 3, term, gates[gate, place, :] + term)
        return none

    lax.fori_loop(0, 12, body, 0)
    upd, fgt, out = gates.at[0], gates.at[1], gates.at[2]
    first_pass(seqs, tokens, channels, gates, bias, keep, upd, fgt, out, scale, shift, summary)
    copies = to_all(summary, slots, send_sems, recv_sems, "seq")
    gather_forward()
    for copy in copies:
        copy.wait()
    entering[...] = from_earlier(slots, initial[...], slice(0, seqs), slice(seqs, 2 * seqs), "seq")
    sent = []
    for seq in range(seqs):
        states_pass(seq, tokens, channels, entering, out, scale, shift, state, hidden)
        part = pl.ds(seq * tokens, tokens)
        place = full_hidden.at[part, lanes_of(mine)]
        sent.append(pltpu.make_async_copy(hidden.at[part], place, pair_sems.at[3 + 3 * seq]))
        sent.append(remote(hidden.at[part], place, pair_sems.at[4 + 3 * seq], pair_sems.at[5 + 3 * seq], "mp", 1 - mine))
        for copy in sent[-2:]:
            copy.start()

    def finish():
        give.wait_send()

        @pl.when(at < line - 1)
        def _():
            for seq in range(seqs):
                for other in range(2):
                    edge(seq, other).wait_send()

        gather_finish()

    def hidden_here():
        for copy in sent:
            copy.wait()

    return hidden_here, finish


def upper_stage(seqs, tokens, channels, full_hidden, hidden_here, hidden, mix, bias, keep, initial, cotangent, pooled, grads, planes, sums, every, weights, gates, state, entering, message, scale, shift, back_scale, back_shift, summary, slots, send_sems, recv_sems, weight_sems, plane_sems, kept_sem):
    half = seqs * tokens // 2
    gather_start, gather_forward, gather_finish = relay(hidden, every, plane_sems, kept_sem)

    def load(step):
        slot = lax.rem(step, 2)
        return pltpu.make_async_copy(
            mix.at[step // 2, pl.ds(pl.multiple_of(lax.rem(step, 2) * channels, 128), channels), :],
            weights.at[slot],
            weight_sems.at[slot],
        )

    load(0).start()
    gather_start()
    hidden_here()

    def body(step, none):
        load(step).wait()

        @pl.when(step < 5)
        def _():
            load(step + 1).start()

        gate, part = step // 2, lax.rem(step, 2)
        columns = pl.ds(pl.multiple_of(part * channels, 128), channels)
        for side in range(2):
            place = pl.ds(side * half, half)
            term = jnp.dot(full_hidden[place, columns], weights[part], preferred_element_type=F32)
            gates[gate, place, :] = jnp.where(part == 0, term, gates[gate, place, :] + term)
        return none

    lax.fori_loop(0, 6, body, 0)
    upd, fgt, out = gates.at[0], gates.at[1], gates.at[2]
    first_pass(seqs, tokens, channels, gates, bias, keep, upd, fgt, out, scale, shift, summary)
    back_pass(seqs, tokens, channels, cotangent, keep, fgt, out, back_scale, back_shift, summary, 2 * seqs)
    copies = to_all(summary, slots, send_sems, recv_sems, "seq")
    gather_forward()
    for copy in copies:
        copy.wait()
    entering[...] = from_earlier(slots, initial[...], slice(0, seqs), slice(seqs, 2 * seqs), "seq")
    message[...] = from_later(
        slots, (seqs, channels), slice(2 * seqs, 3 * seqs), slice(3 * seqs, 4 * seqs), "seq"
    )
    for seq in range(seqs):
        states_pass(seq, tokens, channels, entering, out, scale, shift, state, pooled)
    grads_pass(seqs, tokens, channels, message, entering, cotangent, keep, upd, fgt, out, state, back_scale, back_shift, grads, planes, sums)
    return gather_finish


def lower_stage(seqs, tokens, channels, above, above_columns, mix, keep, upd, fgt, out, state, entering, grads, sums, swapped, weights, total, coming, message, scale, shift, summary, slots, send_sems, recv_sems, edges, arrived, edge_sems, weight_sems, pair_sems, swap_sems):
    mine = lax.axis_index("mp")
    width = swapped.shape[2]

    def load(step):
        side = jnp.where(step < 3, 1 - mine, mine)
        slot = lax.rem(step, 2)
        return pltpu.make_async_copy(
            mix.at[lax.rem(step, 3), pl.ds(pl.multiple_of(side * channels, 128), channels), :],
            weights.at[slot],
            weight_sems.at[slot],
        )

    load(0).start()
    plane = neighbours()
    swaps = []
    for steps in (3, 1, 2, 0):
        src = above_columns.at[:, pl.ds(pl.multiple_of(plane[steps] * width, 128), width)]
        dst = swapped.at[plane[0]]
        if steps:
            swaps.append(remote(src, dst, swap_sems.at[0, steps], swap_sems.at[1, steps], "dp", plane[steps]))
        else:
            swaps.append(pltpu.make_async_copy(src, dst, swap_sems.at[0, steps]))
        swaps[-1].start()
    give = remote(total.at[0], coming, pair_sems.at[0], pair_sems.at[1], "mp", 1 - mine)

    def body(step, none):
        load(step).wait()

        @pl.when(step < 5)
        def _():
            load(step + 1).start()

        side, gate = step // 3, lax.rem(step, 3)
        rows = above.shape[1] // 2
        for half in range(2):
            place = pl.ds(half * rows, rows)
            term = lax.dot_general(
                above[gate, place, :], weights[lax.rem(step, 2)], (((1,), (1,)), ((), ())), preferred_element_type=F32
            )
            total[side, place, :] = jnp.where(gate == 0, term, total[side, place, :] + term)

        @pl.when(step == 2)
        def _():
            give.start()

        return none

    lax.fori_loop(0, 6, body, 0)
    give.wait_recv()
    total[1] += coming[...]
    upstream = total.at[1]
    back_pass(seqs, tokens, channels, upstream, keep, fgt, out, scale, shift, summary, 0)
    copies = to_all(summary, slots, send_sems, recv_sems, "seq")
    for copy in copies:
        copy.wait()
    message[...] = from_later(slots, (seqs, channels), slice(0, seqs), slice(seqs, 2 * seqs), "seq")
    grads_pass(seqs, tokens, channels, message, entering, upstream, keep, upd, fgt, out, state, scale, shift, grads, None, sums)
    pass_edges(seqs, tokens, grads, edges, arrived, edge_sems)
    give.wait_send()
    for steps, copy in zip((3, 1, 2, 0), swaps):
        if steps:
            copy.wait_send()
            place = swapped.at[plane[steps]]
            remote(place, place, swap_sems.at[0, steps], swap_sems.at[1, steps], "dp", plane[steps]).wait_recv()
        else:
            copy.wait()


def front_kernel(seqs, tokens, channels, inputs, taps, mix, bias_one, bias_two, keep, initial_one, initial_two, cotangent, pooled, sums_one, sums_two, extended, every, every_hidden, swapped, both, edges, weights, gates_one, gates_two, hidden, full_hidden, planes, grads_two, coming, state_one, state_two, scale, shift, back_scale, back_shift, entering_one, entering_two, message, edge_out, edge_in, *refs):
    one, two, three = refs[:4], refs[4:8], refs[8:12]
    weight_sems, inputs_sems, inputs_kept, pair_sems, edge_sems, hidden_sems, hidden_kept, first_sems, give_sems, swap_sems = refs[12:]
    hidden_here, inputs_end = first_stage(
        seqs, tokens, channels, inputs, taps, bias_one, keep, initial_one, full_hidden, every, both, edges, weights,
        gates_one, hidden, state_one, entering_one, scale, shift, *one, weight_sems, inputs_sems, inputs_kept, pair_sems,
        edge_sems,
    )
    hidden_end = upper_stage(
        seqs, tokens, channels, full_hidden, hidden_here, hidden, mix, bias_two, keep, initial_two, cotangent, pooled,
        grads_two, planes, sums_two, every_hidden, weights, gates_two, state_two, entering_two, message, scale, shift,
        back_scale, back_shift, *two, weight_sems, hidden_sems, hidden_kept,
    )
    lower_stage(
        seqs, tokens, channels, planes, grads_two, mix, keep, gates_one.at[0], gates_one.at[1], gates_one.at[2],
        state_one, entering_one, extended, sums_one, swapped, weights, gates_two, coming, message, scale, shift, *three,
        edge_out, edge_in, first_sems, weight_sems, give_sems, swap_sems,
    )
    inputs_end()
    hidden_end()


def exchange_scratch(rows, channels):
    count = lax.axis_size("seq")
    return [
        pltpu.VMEM((rows, channels), F32),
        pltpu.VMEM((count - 1, rows, channels), F32),
        pltpu.SemaphoreType.DMA((count - 1,)),
        pltpu.SemaphoreType.DMA((count - 1,)),
    ]


def params(number):
    return pltpu.CompilerParams(collective_id=number, has_side_effects=True, vmem_limit_bytes=56 * 2**20)


def cost(elements, ops, moved):
    return pl.CostEstimate(flops=elements * ops, bytes_accessed=moved, transcendentals=elements * 3)


def pool_forward(seqs, tokens, gates, bias, keep, initial):
    channels = gates.shape[2]
    rows = seqs * tokens
    whole = jax.ShapeDtypeStruct((rows, channels), F32)
    return pl.pallas_call(
        functools.partial(forward_kernel, seqs, tokens, channels),
        out_shape=(
            jax.ShapeDtypeStruct((rows, channels), BF16),
            whole,
            whole,
            whole,
            whole,
            jax.ShapeDtypeStruct((seqs, channels), F32),
        ),
        in_specs=[VMEM] * 4,
        out_specs=[VMEM] * 6,
        scratch_shapes=[pltpu.VMEM((rows, channels), F32)] * 2 + exchange_scratch(2 * seqs, channels),
        compiler_params=params(1),
        cost_estimate=cost(rows * channels, 60, rows * channels * 30),
        name="pool_forward",
    )(gates, bias, keep, initial)


def pool_top(seqs, tokens, lanes, gates, bias, keep, initial, cotangent):
    channels = gates.shape[2]
    rows = seqs * tokens
    whole = pltpu.VMEM((rows, channels), F32)
    edge = pltpu.VMEM((seqs, channels), F32)
    return pl.pallas_call(
        functools.partial(top_kernel, seqs, tokens, channels),
        out_shape=(
            jax.ShapeDtypeStruct((rows, channels), BF16),
            jax.ShapeDtypeStruct((rows, lanes), BF16),
            jax.ShapeDtypeStruct((3, rows, channels), BF16),
            jax.ShapeDtypeStruct((3, SUB, channels), F32),
        ),
        in_specs=[VMEM] * 5,
        out_specs=[VMEM] * 4,
        scratch_shapes=[whole] * 4 + [edge] * 2 + [whole] * 4 + exchange_scratch(4 * seqs, channels),
        compiler_params=params(2),
        cost_estimate=cost(rows * channels, 120, rows * channels * 22),
        name="pool_top",
    )(gates, bias, keep, initial, cotangent)


def front(seqs, tokens, lanes, inputs, taps, mix, bias_one, bias_two, keep, initial_one, initial_two, cotangent):
    rows, channels = inputs.shape
    hbm = pl.BlockSpec(memory_space=pl.ANY)
    dma = pltpu.SemaphoreType.DMA
    whole = pltpu.VMEM((rows, channels), F32)
    few = pltpu.VMEM((seqs, channels), F32)
    return pl.pallas_call(
        functools.partial(front_kernel, seqs, tokens, channels),
        out_shape=(
            jax.ShapeDtypeStruct((rows, channels), BF16),
            jax.ShapeDtypeStruct((3, SUB, channels), F32),
            jax.ShapeDtypeStruct((3, SUB, channels), F32),
            jax.ShapeDtypeStruct((rows + EDGE, lanes), BF16),
            jax.ShapeDtypeStruct((4, rows, channels), BF16),
            jax.ShapeDtypeStruct((4, rows, channels), BF16),
            jax.ShapeDtypeStruct((4, rows, lanes // 4), BF16),
        ),
        in_specs=[hbm] * 3 + [VMEM] * 6,
        out_specs=[VMEM] * 4 + [hbm] * 3,
        scratch_shapes=[
            pltpu.VMEM((2, rows, 2 * channels), BF16),
            pltpu.VMEM((2, seqs, EDGE, channels), BF16),
            pltpu.VMEM((2, channels, channels), BF16),
            pltpu.VMEM((3, rows, channels), F32),
            pltpu.VMEM((3, rows, channels), F32),
            pltpu.VMEM((rows, channels), BF16),
            pltpu.VMEM((rows, 2 * channels), BF16),
            pltpu.VMEM((3, rows, channels), BF16),
            pltpu.VMEM((rows, lanes), BF16),
        ]
        + [whole] * 7
        + [few] * 3
        + [pltpu.VMEM((EDGE, lanes), BF16)] * 2
        + exchange_scratch(2 * seqs, channels)
        + exchange_scratch(4 * seqs, channels)
        + exchange_scratch(2 * seqs, channels)
        + [dma((2,)), dma((2, 4)), dma, dma((3 + 3 * seqs,)), dma((2, 2, seqs))]
        + [dma((2, 4)), dma, dma((2,)), dma((2,)), dma((2, 4))],
        compiler_params=pltpu.CompilerParams(
            collective_id=7, has_side_effects=True, vmem_limit_bytes=62 * 2**20
        ),
        cost_estimate=pl.CostEstimate(
            flops=48 * rows * channels * channels, bytes_accessed=rows * channels * 160, transcendentals=0
        ),
        name="front",
    )(inputs, taps, mix, bias_one, bias_two, keep, initial_one, initial_two, cotangent)


def pool_backward(seqs, tokens, lanes, upstream, keep, upd, fgt, out, state, entering):
    rows, channels = upstream.shape
    whole = pltpu.VMEM((rows, channels), F32)
    return pl.pallas_call(
        functools.partial(backward_kernel, seqs, tokens, channels),
        out_shape=(
            jax.ShapeDtypeStruct((rows + EDGE, lanes), BF16),
            jax.ShapeDtypeStruct((3, SUB, channels), F32),
        ),
        in_specs=[VMEM] * 7,
        out_specs=[VMEM] * 2,
        scratch_shapes=[pltpu.VMEM((seqs, channels), F32)]
        + [whole] * 2
        + exchange_scratch(2 * seqs, channels)
        + [pltpu.VMEM((EDGE, lanes), BF16)] * 2
        + [pltpu.SemaphoreType.DMA((2,))],
        compiler_params=params(3),
        cost_estimate=cost(rows * channels, 60, rows * channels * 26),
        name="pool_backward",
    )(upstream, keep, upd, fgt, out, state, entering)


def shift_up(seqs, tokens, value, edges, result):
    width = value.shape[1]
    steps = tokens // STEP

    def body(index, none):
        sequence, at = index // steps, lax.rem(index, steps)
        row = lax.broadcasted_iota(jnp.int32, (STEP, width), 0)
        rows = pl.ds(pl.multiple_of(index * STEP, STEP), STEP)
        after = jnp.minimum(index + 1, value.shape[0] // STEP - 1)
        first = value[pl.ds(pl.multiple_of(after * STEP, STEP), STEP), :].astype(F32)[0:1]
        edge = edges[sequence // seqs].astype(F32)
        edge = jnp.where(lax.rem(sequence, seqs) == 0, edge[0:1], edge[1:2])
        moved = pltpu.roll(value[rows, :].astype(F32), STEP - 1, 0)
        moved = jnp.where(row == STEP - 1, jnp.where(at == steps - 1, edge, first), moved)
        result[rows, :] = moved.astype(BF16)
        return none

    lax.fori_loop(0, value.shape[0] // STEP, body, 0)


def spread_kernel(seqs, tokens, parts, turn, tail, hidden, full, grads_two, grads_one, taps, sums, out, input_grad, sums_out, rows_full, grads, grads_edge, moved, own, ups, downs, acc, across, around, every, weights, leaving, coming, load_sems, swap_sems, up_sems, down_sems, line_send, line_recv, column_send, column_recv, kept_sems, plane_send, plane_recv, sums_sems, weight_sems, leaving_sems, coming_sems, result_sems, pair_sems, ready_sem):
    line, plane = lax.axis_size("seq"), lax.axis_size("dp")
    at, here = lax.axis_index("seq"), lax.axis_index("dp")
    unit = line * parts
    units = own.shape[0] // unit
    blocks = units // 3
    width = own.shape[1]
    block_rows = seqs * tokens
    half = unit // 2
    here, beside, below, across_from = neighbours()
    mine = lax.axis_index("mp")
    greet("seq", "dp", "mp")
    met("seq", "dp", "mp")

    def turned(u):
        return lax.rem(u, turn) == turn - 1

    def direct(u):
        return lax.rem(u, turn) != turn - 1

    wide = rows_full.shape[1] // 2

    def own_rows(value, number, way):
        place = rows_full.at[:, pl.ds(pl.multiple_of(mine * wide, 128), wide)]
        if way == 0:
            return pltpu.make_async_copy(value, place, load_sems.at[number])
        return remote(value, place, pair_sems.at[0, number], pair_sems.at[1, number], "mp", 1 - mine)

    def other_rows(number):
        place = rows_full.at[:, pl.ds(pl.multiple_of((1 - mine) * wide, 128), wide)]
        return remote(place, place, pair_sems.at[0, number], pair_sems.at[1, number], "mp", 1 - mine)

    def plane_rows(owner):
        return pl.ds(pl.multiple_of(owner * block_rows, 16), block_rows)

    def peer(steps):
        return (here, beside, below, across_from)[steps]

    def load_two():
        return pltpu.make_async_copy(grads_two, moved, load_sems.at[2])

    def swap(steps, edge, arriving=False):
        columns = pl.ds(pl.multiple_of(peer(steps) * width, 128), width)
        source = peer(steps) if arriving else here
        if edge:
            src, dst = grads_one.at[block_rows : block_rows + EDGE, columns], grads_edge.at[source]
        else:
            src, dst = grads_one.at[0:block_rows, columns], grads.at[plane_rows(source)]
        number = steps * 2 + edge
        if steps == 0:
            return pltpu.make_async_copy(src, dst, swap_sems.at[0, number])
        return remote(src, dst, swap_sems.at[0, number], swap_sems.at[1, number], "dp", peer(steps))

    def product(block, right):
        columns = pl.ds(pl.multiple_of(jnp.where(mine == 0, block, blocks - 1 - block) * unit, 128), unit)
        return lax.dot_general(
            rows_full[:, columns], right[...], (((0,), (0,)), ((), ())), preferred_element_type=F32
        ).astype(BF16)

    narrow = leaving.shape[2]
    pieces = wide // narrow

    def load_weights(step):
        first = jnp.where(step < pieces, (1 - mine) * pieces + step, mine * pieces + step - pieces) * narrow
        slot = lax.rem(step, 2)
        return pltpu.make_async_copy(
            taps.at[:, :, pl.ds(pl.multiple_of(first, narrow), narrow), :], weights.at[slot], weight_sems.at[slot]
        )

    def load_every():
        return pltpu.make_async_copy(grads_one, every, load_sems.at[3])

    def leave(step):
        slot = lax.rem(step, 2)
        return remote(leaving.at[slot], coming.at[step], leaving_sems.at[slot], coming_sems.at[step], "mp", 1 - mine)

    def result(step):
        return pltpu.make_async_copy(
            coming.at[step],
            input_grad.at[:, pl.ds(pl.multiple_of(step * narrow, narrow), narrow)],
            result_sems.at[step],
        )

    def input_terms(slot):
        channels = taps.shape[3]
        now = jnp.zeros((block_rows, narrow), F32)
        late = jnp.zeros((block_rows + EDGE, narrow), F32)
        for gate in range(3):
            lanes = slice(gate * channels, gate * channels + channels)
            now += lax.dot_general(
                every[:block_rows, lanes], weights[slot, 0, gate], (((1,), (1,)), ((), ())), preferred_element_type=F32
            )
            late += lax.dot_general(
                every[:, lanes], weights[slot, 1, gate], (((1,), (1,)), ((), ())), preferred_element_type=F32
            )
        row = lax.broadcasted_iota(jnp.int32, now.shape, 0)
        after = pltpu.roll(late[:block_rows], block_rows - 1, 0)
        for seq in range(seqs):
            after = jnp.where(
                row == seq * tokens + tokens - 1, late[block_rows + seq : block_rows + seq + 1], after
            )
        return now + after

    def whole(u):
        return pl.ds(pl.multiple_of(u * unit, unit), unit)

    def chunk(u, j):
        return pl.ds(pl.multiple_of(u * unit + j * parts, parts), parts)

    def up(src, u, j):
        number = u * (line - 1) + j - 1
        return remote(src, ups.at[u, j - 1], up_sems.at[0, number], up_sems.at[1, number], "seq", lax.rem(at + 1, line))

    def down(src, u, j):
        number = u * (line - 1) + j
        return remote(
            src, downs.at[u, j], down_sems.at[0, number], down_sems.at[1, number], "seq", lax.rem(at + line - 1, line)
        )

    def along(src, u, j, way, hop):
        return remote(
            src,
            out.at[here, chunk(u, j)],
            line_send.at[(u * 2 + way) * (line - 1) + hop],
            line_recv.at[u * line + j],
            "seq",
            lax.rem(at + (1 if way == 0 else line - 1), line),
        )

    at_end = (at == 0) | (at == line - 1)
    share = line // 2 * parts
    begin = jnp.where(at == 0, 0, line // 2) * parts

    def owner_of(u, j):
        return jnp.where(turned(u), (line - 1) * (j >= line // 2), j)

    def column(steps, u, way):
        number = (u // turn * 4 + steps) * 2 + way
        place = out.at[peer(steps), rows(u, way * share, share)]
        return remote(
            place,
            place,
            column_send.at[number],
            column_recv.at[number],
            "seq",
            lax.rem(at + (1 if way == 0 else line - 1), line),
        )

    def end_rows(u):
        return pl.ds(pl.multiple_of(u * unit + begin, parts), share)

    def keep_part(u):
        return pltpu.make_async_copy(own.at[end_rows(u)], out.at[here, end_rows(u)], kept_sems.at[u])

    def over_part(src, u, way):
        return remote(
            src,
            out.at[here, end_rows(u)],
            plane_send.at[u * 4 + way],
            plane_recv.at[u * 4 + way],
            "dp",
            (beside, below)[way],
        )

    def onward_part(owner, u, way):
        place = out.at[owner, pl.ds(pl.multiple_of(u * unit + begin + way * (share // 2), 16), share // 2)]
        return remote(
            place, place, plane_send.at[u * 4 + 2 + way], plane_recv.at[u * 4 + 2 + way], "dp", (below, beside)[way]
        )

    def keep(u):
        return pltpu.make_async_copy(own.at[chunk(u, at)], out.at[here, chunk(u, at)], kept_sems.at[u])

    def rows(u, first, count):
        return pl.ds(pl.multiple_of(u * unit + first, half), count)

    def over(u, way):
        place = out.at[here, rows(u, 0, unit)]
        return remote(place, place, plane_send.at[u * 4 + way], plane_recv.at[u * 4 + way], "dp", (beside, below)[way])

    def onward(u, way):
        place = out.at[(beside, below)[way], rows(u, way * half, half)]
        return remote(
            place, place, plane_send.at[u * 4 + 2 + way], plane_recv.at[u * 4 + 2 + way], "dp", (below, beside)[way]
        )

    def corner(u, way):
        place = out.at[across_from, rows(u, way * half, half)]
        return remote(place, place, plane_send.at[u * 4 + 2 + way], plane_recv.at[u * 4 + 2 + way], "dp", (below, beside)[way])

    def sums_copy(slots, me, count, axis, number, step):
        return remote(
            slots.at[me],
            slots.at[me],
            sums_sems.at[number, 0, step - 1],
            sums_sems.at[number, 1, step - 1],
            axis,
            lax.rem(me + step, count),
        )

    def sums_arrival(slots, me, count, axis, number, step):
        place = slots.at[lax.rem(me + count - step, count)]
        return remote(place, place, sums_sems.at[number, 0, step - 1], sums_sems.at[number, 1, step - 1], axis, lax.rem(me + step, count))

    for way in range(2):
        own_rows(hidden, 0, way).start()
    load_two().start()
    for steps in range(4):
        for edge in range(2):
            swap(steps, edge).start()
    load_every().start()
    load_weights(0).start()
    across[at] = sums[...]
    for step in range(1, line):
        sums_copy(across, at, line, "seq", 0, step).start()
    load_two().wait()
    own_rows(hidden, 0, 0).wait()

    def stage(index, none):
        @pl.when(index == 1)
        def _():
            for step in range(1, line):
                sums_arrival(across, at, line, "seq", 0, step).wait_recv()
            total = across[0]
            for other in range(1, line):
                total = total + across[other]
            around[here] = total
            for step in range(1, plane):
                sums_copy(around, here, plane, "dp", 1, step).start()

        @pl.when(index == 3)
        def _():
            for step in range(1, plane):
                sums_arrival(around, here, plane, "dp", 1, step).wait_recv()
            total = around[0]
            for other in range(1, plane):
                total = total + around[other]
            sums_out[...] = total

        @pl.when(index == wide // unit)
        def _():
            other_rows(0).wait_recv()

        @pl.when(index == blocks + 2 * (wide // unit))
        def _():
            other_rows(1).wait_recv()

        @pl.when(index < blocks)
        def _():
            own[whole(index), :] = product(index, moved)

        @pl.when(index == blocks - 1)
        def _():
            own_rows(hidden, 0, 1).wait_send()
            own_rows(full, 1, 0).start()
            pl.semaphore_signal(ready_sem, inc=1, device_id={"mp": 1 - mine}, device_id_type=pl.DeviceIdType.MESH)
            pl.semaphore_wait(ready_sem, 1)
            own_rows(full, 1, 1).start()

        @pl.when(index == blocks)
        def _():
            for steps in range(4):
                for edge in range(2):
                    if steps:
                        swap(steps, edge, True).wait_recv()
                    else:
                        swap(steps, edge).wait()
            shift_up(seqs, tokens, grads, grads_edge, moved)
            own_rows(full, 1, 0).wait()
            load_every().wait()

        @pl.when((index >= blocks) & (index < units) & (lax.rem(index - blocks, 2) == 0))
        def _():
            own[whole(index), :] = product((index - blocks) // 2, grads)

        @pl.when((index >= blocks) & (index < units) & (lax.rem(index - blocks, 2) == 1))
        def _():
            own[whole(index), :] = product((index - blocks) // 2, moved)

        k = index - blocks

        @pl.when((k >= 0) & (k < 2 * pieces))
        def _():
            load_weights(k).wait()

            @pl.when(k + 1 < 2 * pieces)
            def _():
                load_weights(k + 1).start()

            terms = input_terms(lax.rem(k, 2))

            @pl.when(k < pieces)
            def _():
                @pl.when(k >= 2)
                def _():
                    leave(k - 2).wait_send()

                leaving[lax.rem(k, 2)] = terms
                leave(k).start()

            @pl.when(k >= pieces)
            def _():
                leave(k - pieces).wait_recv()
                coming[k - pieces] += terms
                result(k - pieces).start()

        u = index - at

        @pl.when((u >= 0) & (u < units))
        def _():
            for j in range(line - 1, 0, -1):

                owner = owner_of(u, j)

                @pl.when((at == 0) & (at < owner))
                def _(j=j):
                    up(own.at[chunk(u, j)], u, j).start()

                @pl.when((at > 0) & (at <= owner))
                def _(j=j):
                    up(ups.at[u, j - 1], u, j).wait_recv()

                @pl.when((at > 0) & (at < owner))
                def _(j=j):
                    ups[u, j - 1] = (ups[u, j - 1].astype(F32) + own[chunk(u, j)].astype(F32)).astype(BF16)
                    up(ups.at[u, j - 1], u, j).start()

        v = index - (line - 1 - at)

        @pl.when((v >= 0) & (v < units))
        def _():
            for j in range(line - 1):

                owner = owner_of(v, j)

                @pl.when((at == line - 1) & (at > owner))
                def _(j=j):
                    down(own.at[chunk(v, j)], v, j).start()

                @pl.when((at < line - 1) & (at >= owner))
                def _(j=j):
                    down(downs.at[v, j], v, j).wait_recv()

                @pl.when((at < line - 1) & (at > owner))
                def _(j=j):
                    downs[v, j] = (downs[v, j].astype(F32) + own[chunk(v, j)].astype(F32)).astype(BF16)
                    down(downs.at[v, j], v, j).start()

        w = index - (line - 1)

        @pl.when((w >= 0) & (w < units) & direct(w))
        def _():
            acc[...] = own[chunk(w, at)].astype(F32)

            @pl.when(at > 0)
            def _():
                acc[...] += ups[w, at - 1].astype(F32)

            @pl.when(at < line - 1)
            def _():
                acc[...] += downs[w, at].astype(F32)

            own[chunk(w, at)] = acc[...].astype(BF16)
            keep(w).start()

            @pl.when(at < line - 1)
            def _():
                along(own.at[chunk(w, at)], w, at, 0, 0).start()

            @pl.when(at > 0)
            def _():
                along(own.at[chunk(w, at)], w, at, 1, 0).start()

        @pl.when((w >= 0) & (w < units) & turned(w))
        def _():
            @pl.when(at == 0)
            def _():
                for j in range(line // 2):
                    own[chunk(w, j)] = (own[chunk(w, j)].astype(F32) + downs[w, j].astype(F32)).astype(BF16)

            @pl.when(at == line - 1)
            def _():
                for j in range(line // 2, line):
                    own[chunk(w, j)] = (own[chunk(w, j)].astype(F32) + ups[w, j - 1].astype(F32)).astype(BF16)

            @pl.when(at_end)
            def _():
                keep_part(w).start()
                for way in range(2):
                    over_part(own.at[end_rows(w)], w, way).start()

        c = index - line

        @pl.when((c >= 0) & (c < units) & turned(c) & at_end)
        def _():
            keep_part(c).wait()
            for way in range(2):
                over_part(out.at[(beside, below)[way], end_rows(c)], c, way).wait_recv()
                onward_part((beside, below)[way], c, way).start()

        d = index - line - 1

        @pl.when((d >= 0) & (d < units) & turned(d) & at_end)
        def _():
            for way in range(2):
                onward_part(across_from, d, way).wait_recv()

        for steps in range(4):
            for way in range(2):
                hops = at if way == 0 else line - 1 - at
                e = d - steps - hops

                @pl.when((e >= 0) & (e < units) & turned(e))
                def _(e=e, steps=steps, way=way, hops=hops):
                    @pl.when(hops > 0)
                    def _():
                        column(steps, e, way).wait_recv()

                    @pl.when(hops < line - 1)
                    def _():
                        column(steps, e, way).start()

        for hop in range(1, line):
            x = index - (line - 1) - hop

            @pl.when((x >= 0) & (x < units) & direct(x))
            def _(x=x, hop=hop):
                @pl.when(at >= hop)
                def _():
                    src = out.at[here, chunk(x, at - hop)]
                    along(src, x, at - hop, 0, 0).wait_recv()
                    if hop < line - 1:

                        @pl.when(at < line - 1)
                        def _():
                            along(src, x, at - hop, 0, hop).start()

                @pl.when(at + hop < line)
                def _():
                    src = out.at[here, chunk(x, at + hop)]
                    along(src, x, at + hop, 1, 0).wait_recv()
                    if hop < line - 1:

                        @pl.when(at > 0)
                        def _():
                            along(src, x, at + hop, 1, hop).start()

        y = index - 2 * (line - 1)

        @pl.when((y >= 0) & (y < units) & direct(y))
        def _():
            keep(y).wait()

        @pl.when((y >= 0) & (y < units - tail) & direct(y))
        def _():
            over(y, 0).start()
            over(y, 1).start()

        z = y - LAG

        @pl.when((z >= 0) & (z < units - tail) & direct(z))
        def _():
            for way in range(2):
                place = out.at[(beside, below)[way], rows(z, 0, unit)]
                remote(place, place, plane_send.at[z * 4 + way], plane_recv.at[z * 4 + way], "dp", (beside, below)[way]).wait_recv()
                onward(z, way).start()

        t = z - LAG

        @pl.when((t >= 0) & (t < units - tail) & direct(t))
        def _():
            for way in range(2):
                corner(t, way).wait_recv()

        return none

    last_turned = units // turn * turn - 1
    lax.fori_loop(
        0, max(units + 2 * (line - 1), units - tail + 2 * (line - 1) + 2 * LAG, last_turned + 2 * line + 4), stage, 0
    )

    def settle(u, none):
        for j in range(1, line):

            @pl.when(at < owner_of(u, j))
            def _(j=j):
                up(ups.at[u, j - 1], u, j).wait_send()

        for j in range(line - 1):

            @pl.when(at > owner_of(u, j))
            def _(j=j):
                down(downs.at[u, j], u, j).wait_send()

        for hop in range(line - 1):

            @pl.when(direct(u) & (at >= hop) & (at < line - 1))
            def _(hop=hop):
                along(out.at[here, chunk(u, at - hop)], u, at - hop, 0, hop).wait_send()

            @pl.when(direct(u) & (at + hop < line) & (at > 0))
            def _(hop=hop):
                along(out.at[here, chunk(u, at + hop)], u, at + hop, 1, hop).wait_send()

        @pl.when(turned(u))
        def _():
            for steps in range(4):

                @pl.when(at < line - 1)
                def _(steps=steps):
                    column(steps, u, 0).wait_send()

                @pl.when(at > 0)
                def _(steps=steps):
                    column(steps, u, 1).wait_send()

        @pl.when(direct(u) & (u < units - tail))
        def _():
            for way in range(2):
                over(u, way).wait_send()
                onward(u, way).wait_send()

        @pl.when(turned(u) & at_end)
        def _():
            for way in range(2):
                over_part(out.at[here, end_rows(u)], u, way).wait_send()
                onward_part(here, u, way).wait_send()

        return none

    lax.fori_loop(0, units, settle, 0)
    for steps in range(1, 4):
        for edge in range(2):
            swap(steps, edge).wait_send()
    own_rows(full, 1, 1).wait_send()
    for step in range(pieces - 2, pieces):
        leave(step).wait_send()
    for step in range(pieces):
        result(step).wait()
    for step in range(1, line):
        sums_copy(across, at, line, "seq", 0, step).wait_send()
    for step in range(1, plane):
        sums_copy(around, here, plane, "dp", 1, step).wait_send()


def spread(seqs, tokens, hidden, full, grads_two, grads_one, taps, sums):
    line, plane = lax.axis_size("seq"), lax.axis_size("dp")
    width = grads_two.shape[1]
    rows = grads_two.shape[0] // plane
    depth = 2 * full.shape[1]
    units = 3 * depth // (line * PART)
    channels = taps.shape[3]
    narrow = depth // (units - units // 3)
    pieces = channels // narrow
    turns = units // TURN
    dma = pltpu.SemaphoreType.DMA
    hbm = pl.BlockSpec(memory_space=pl.ANY)
    return pl.pallas_call(
        functools.partial(spread_kernel, seqs, tokens, PART, TURN, TAIL),
        out_shape=(
            jax.ShapeDtypeStruct((plane, 3 * depth, width), BF16),
            jax.ShapeDtypeStruct((rows, channels), F32),
            jax.ShapeDtypeStruct(sums.shape, F32),
        ),
        in_specs=[hbm] * 5 + [VMEM],
        out_specs=[hbm, hbm, VMEM],
        scratch_shapes=[
            pltpu.VMEM((plane * rows, depth), BF16),
            pltpu.VMEM((plane * rows, width), BF16),
            pltpu.VMEM((plane, EDGE, width), BF16),
            pltpu.VMEM((plane * rows, width), BF16),
            pltpu.VMEM((3 * depth, width), BF16),
            pltpu.VMEM((units, line - 1, PART, width), BF16),
            pltpu.VMEM((units, line - 1, PART, width), BF16),
            pltpu.VMEM((PART, width), F32),
            pltpu.VMEM((line,) + sums.shape, F32),
            pltpu.VMEM((plane,) + sums.shape, F32),
            pltpu.VMEM(grads_one.shape, BF16),
            pltpu.VMEM((2, 2, 3, narrow, channels), BF16),
            pltpu.VMEM((2, rows, narrow), F32),
            pltpu.VMEM((pieces, rows, narrow), F32),
            dma((4,)),
            dma((2, 8)),
            dma((2, units * (line - 1))),
            dma((2, units * (line - 1))),
            dma((units * 2 * (line - 1),)),
            dma((units * line,)),
            dma((turns * 8,)),
            dma((turns * 8,)),
            dma((units,)),
            dma((units * 4,)),
            dma((units * 4,)),
            dma((2, 2, max(line, plane) - 1)),
            dma((2,)),
            dma((2,)),
            dma((pieces,)),
            dma((pieces,)),
            dma((2, 2)),
            pltpu.SemaphoreType.REGULAR,
        ],
        compiler_params=pltpu.CompilerParams(
            collective_id=4, has_side_effects=True, vmem_limit_bytes=62 * 2**20
        ),
        cost_estimate=pl.CostEstimate(
            flops=6 * plane * rows * depth * width, bytes_accessed=depth * width * 48, transcendentals=0
        ),
        name="spread",
    )(hidden, full, grads_two, grads_one, taps, sums)


def widen_kernel(blocks, core, given, *refs):
    out = refs[-1]
    per = given.shape[2] // 128
    for tile in range(3 * blocks):
        source, place = divmod(tile, per)
        gate, column = divmod(tile, blocks)
        out[0, gate, :, column * 128 : column * 128 + 128] = given[
            source, :, place * 128 : place * 128 + 128
        ].astype(F32)


def widen(gathered, first, taps, start, count, depth, channels, unit, core, into=None):
    plane, _, width = gathered.shape
    last = depth // unit - 1

    def source(tap, step, core):
        return (0, first + step * taps + tap, 0)

    def target(tap, step, core):
        block = start + step
        return (tap, 0, jnp.where(core[0] == 0, block, last - block), 0)

    given = (core, gathered) if into is None else (core, gathered, into)
    return pl.pallas_call(
        functools.partial(widen_kernel, channels // 128),
        grid_spec=pltpu.PrefetchScalarGridSpec(
            num_scalar_prefetch=1,
            grid=(taps, count),
            in_specs=[pl.BlockSpec((plane, unit, width), source)] + [pl.BlockSpec(memory_space=pl.ANY)] * (len(given) - 2),
            out_specs=pl.BlockSpec((1, 3, unit, channels), target),
        ),
        out_shape=jax.ShapeDtypeStruct((taps, 3, depth, channels), F32),
        input_output_aliases={} if into is None else {2: 0},
        compiler_params=pltpu.CompilerParams(vmem_limit_bytes=40 * 2**20),
        cost_estimate=pl.CostEstimate(
            flops=0, bytes_accessed=taps * count * unit * (plane * width * 2 + channels * 12), transcendentals=0
        ),
        name="widen",
    )(*given)


def shifted(value, axis, steps):
    count = lax.axis_size(axis)
    initial, last = (max(0, -steps), min(count, count - steps))
    return lax.ppermute(value, axis, [(source, source + steps) for source in range(initial, last)])


def gather_channels(value):
    count = lax.axis_size("mp")
    if count != 2:
        return lax.all_gather(value, "mp", axis=value.ndim - 1, tiled=True)
    other = lax.ppermute(value, "mp", [(0, 1), (1, 0)])
    second = lax.axis_index("mp") == 1
    return jnp.concatenate([jnp.where(second, other, value), jnp.where(second, value, other)], value.ndim - 1)


def sum_channels(terms):
    count = lax.axis_size("mp")
    if count != 2:
        return lax.psum_scatter(terms, "mp", scatter_dimension=1, tiled=True)
    width = terms.shape[1] // 2
    second = lax.axis_index("mp") == 1
    low, high = terms[:, :width], terms[:, width:]
    other = lax.ppermute(jnp.where(second, low, high), "mp", [(0, 1), (1, 0)])
    return jnp.where(second, high, low) + other


def dot(lhs, rhs, dims):
    return lax.dot_general(lhs, rhs, (dims, ((), ())), preferred_element_type=F32)


def reduce_weights(partial):
    shard = lax.psum_scatter(partial.astype(BF16), ("dp", "seq"), scatter_dimension=0, tiled=True)
    return lax.all_gather(shard, ("dp", "seq"), axis=0, tiled=True).astype(F32)


def local(inputs, starts, init_state, weight_one, bias_one, weight_two, bias_two, cotangent):
    seqs, tokens, channels = inputs.shape
    rows = seqs * tokens
    width = weight_one.shape[1]
    keep = jnp.broadcast_to((1 - starts).astype(F32).reshape(rows, 1), (rows, 128))
    taps = weight_one.transpose(0, 2, 1, 3)
    mix = weight_two.transpose(1, 0, 2)

    line, plane = lax.axis_size("seq"), lax.axis_size("dp")
    tiles = 3 * channels // 128
    spreads = plane == 4 and lax.axis_size("mp") == 2 and seqs == 2 and line % 2 == 0 and channels % 128 == 0
    spreads = spreads and width % (line * PART) == 0 and line > 1
    block = -(-tiles // plane) * 128
    lanes = plane * block if spreads else 3 * channels
    upstream = cotangent.reshape(rows, channels)
    if spreads:
        pooled_two, sums_one, sums_two, extended, every, every_hidden, swapped = front(
            seqs,
            tokens,
            lanes,
            inputs.reshape(rows, channels),
            taps,
            mix,
            bias_one,
            bias_two,
            keep,
            init_state[0],
            init_state[1],
            upstream,
        )
        sums = jnp.concatenate([jnp.sum(sums_one, 1), jnp.sum(sums_two, 1)])
        gathered, input_grad, sums = spread(
            seqs,
            tokens,
            every_hidden.reshape(plane * rows, channels),
            every.reshape(plane * rows, channels),
            swapped.reshape(plane * rows, block),
            extended,
            taps,
            sums,
        )
        unit = line * PART
        blocks = width // unit
        core = lax.axis_index("mp").reshape(1)
        behind = TAIL // 2
        kept = lax.dynamic_slice(
            gathered, (lax.axis_index("dp"), (3 * blocks - TAIL) * unit, 0), (1, TAIL * unit, block)
        )
        tail = lax.all_gather(kept, "dp", axis=0, tiled=True)
        weight_two_grad = widen(gathered, 0, 1, 0, blocks, width, channels, unit, core)
        weight_one_grad = widen(gathered, blocks, 2, 0, blocks - behind, width, channels, unit, core)
        weight_one_grad = widen(
            tail, 0, 2, blocks - behind, behind, width, channels, unit, core, weight_one_grad
        )
        weight_two_grad = weight_two_grad[0].transpose(1, 0, 2)
        weight_one_grad = weight_one_grad.transpose(0, 2, 1, 3)
    else:
        edge = gather_channels(shifted(inputs[:, -1], "seq", 1))
        full = gather_channels(inputs)
        previous = jnp.concatenate([edge[:, None], full[:, :-1]], 1).reshape(rows, width)
        full = full.reshape(rows, width)
        both = jnp.concatenate([full, previous], 1)
        gates_one = jnp.einsum(
            "tkd,kgdc->gtc", both.reshape(rows, 2, width), taps, preferred_element_type=F32
        )
        hidden, upd, fgt, out, state, entering = pool_forward(seqs, tokens, gates_one, bias_one, keep, init_state[0])
        full_hidden = gather_channels(hidden)
        gates_two = jnp.einsum("td,gdc->gtc", full_hidden, mix, preferred_element_type=F32)
        pooled_two, grad_two, planes_two, sums_two = pool_top(
            seqs, tokens, lanes, gates_two, bias_two, keep, init_state[1], upstream
        )
        hidden_terms = jnp.einsum("gtc,gdc->td", planes_two, mix, preferred_element_type=F32)
        hidden_grad = sum_channels(hidden_terms)
        extended, sums_one = pool_backward(seqs, tokens, lanes, hidden_grad, keep, upd, fgt, out, state, entering)
        grad_one = extended[:rows]
        input_terms = jnp.einsum(
            "tgc,kgdc->ktd", grad_one.reshape(rows, 3, channels), taps, preferred_element_type=F32
        ).reshape(2, seqs, tokens, width)
        late = input_terms[1]
        late = jnp.concatenate([late[:, 1:], shifted(late[:, 0], "seq", -1)[:, None]], 1)
        input_grad = sum_channels((input_terms[0] + late).reshape(rows, width))
        sums = jnp.concatenate([jnp.sum(sums_one, 1), jnp.sum(sums_two, 1)])
        sums = lax.psum(sums, ("dp", "seq"))
        weight_two_grad = reduce_weights(dot(full_hidden, grad_two, ((0,), (0,)))).reshape(width, 3, channels)
        weight_one_grad = jnp.stack(
            [
                reduce_weights(dot(full, grad_one, ((0,), (0,)))),
                reduce_weights(dot(previous, grad_one, ((0,), (0,)))),
            ]
        ).reshape(2, width, 3, channels)
    return (
        pooled_two.reshape(seqs, tokens, channels),
        input_grad.reshape(seqs, tokens, channels),
        weight_one_grad,
        sums[:3],
        weight_two_grad,
        sums[3:],
    )


def solution(mesh):
    return jax.shard_map(
        local,
        mesh=mesh,
        in_specs=(
            P("dp", "seq", "mp"),
            P("dp", "seq"),
            P(None, "dp", "mp"),
            P(None, None, None, "mp"),
            P(None, "mp"),
            P(None, None, "mp"),
            P(None, "mp"),
            P("dp", "seq", "mp"),
        ),
        out_specs=(
            P("dp", "seq", "mp"),
            P("dp", "seq", "mp"),
            P(None, None, None, "mp"),
            P(None, "mp"),
            P(None, None, "mp"),
            P(None, "mp"),
        ),
        check_vma=False,
    )
```

```python
import functools

import jax
import jax.numpy as jnp
from jax import lax
from jax.experimental import pallas as pl
from jax.experimental.pallas import tpu as pltpu
from jax.sharding import PartitionSpec as P

F32 = jnp.float32
BF16 = jnp.bfloat16
SUB = 8
STEP = 16
EDGE = 16
PART = 64
LAG = 2
TURN = 4
TAIL = 2
VMEM = pl.BlockSpec(memory_space=pltpu.VMEM)


def sigmoid(x):
    small = jnp.exp(-jnp.abs(x))
    return jnp.where(x >= 0.0, 1.0, small) / (1.0 + small)


def lane_blocks(channels):
    width = 384 if channels % 384 == 0 else channels
    return [slice(at, at + width) for at in range(0, channels, width)]


def scan_down(scale, shift):
    row = lax.broadcasted_iota(jnp.int32, scale.shape, 0)
    for step in (1, 2, 4):
        earlier = row >= step
        scale_before = jnp.where(earlier, pltpu.roll(scale, step, 0), 1.0)
        shift_before = jnp.where(earlier, pltpu.roll(shift, step, 0), 0.0)
        shift = scale * shift_before + shift
        scale = scale * scale_before
    return scale, shift


def scan_up(scale, shift):
    row = lax.broadcasted_iota(jnp.int32, scale.shape, 0)
    for step in (1, 2, 4):
        later = row < SUB - step
        scale_after = jnp.where(later, pltpu.roll(scale, SUB - step, 0), 1.0)
        shift_after = jnp.where(later, pltpu.roll(shift, SUB - step, 0), 0.0)
        shift = scale * shift_after + shift
        scale = scale * scale_after
    return scale, shift


def greet(*axes):
    for axis in axes:
        count = lax.axis_size(axis)
        me = lax.axis_index(axis)
        for step in range(1, count):
            pl.semaphore_signal(
                pltpu.get_barrier_semaphore(),
                inc=1,
                device_id={axis: lax.rem(me + step, count)},
                device_id_type=pl.DeviceIdType.MESH,
            )


def met(*axes):
    pl.semaphore_wait(pltpu.get_barrier_semaphore(), sum(lax.axis_size(axis) - 1 for axis in axes))


def remote(src, dst, send, recv, axis, target):
    return pltpu.make_async_remote_copy(
        src_ref=src,
        dst_ref=dst,
        send_sem=send,
        recv_sem=recv,
        device_id={axis: target},
        device_id_type=pl.DeviceIdType.MESH,
    )


def to_all(src, slots, send_sems, recv_sems, axis):
    count = lax.axis_size(axis)
    me = lax.axis_index(axis)
    copies = []
    for step in range(1, count):
        copies.append(
            pltpu.make_async_remote_copy(
                src_ref=src,
                dst_ref=slots.at[step - 1],
                send_sem=send_sems.at[step - 1],
                recv_sem=recv_sems.at[step - 1],
                device_id={axis: lax.rem(me + step, count)},
                device_id_type=pl.DeviceIdType.MESH,
            )
        )
    for copy in copies:
        copy.start()
    return copies


def from_earlier(slots, initial, scale_rows, shift_rows, axis):
    count = lax.axis_size(axis)
    me = lax.axis_index(axis)
    state = initial
    for block in range(count - 1):
        slot = jnp.maximum(me - block - 1, 0)
        after = slots[slot, scale_rows, :] * state + slots[slot, shift_rows, :]
        state = jnp.where(block < me, after, state)
    return state


def from_later(slots, shape, scale_rows, shift_rows, axis):
    count = lax.axis_size(axis)
    me = lax.axis_index(axis)
    message = jnp.zeros(shape, F32)
    for block in range(count - 1, 0, -1):
        slot = jnp.minimum(me + count - block - 1, count - 2)
        after = slots[slot, scale_rows, :] * message + slots[slot, shift_rows, :]
        message = jnp.where(block > me, after, message)
    return message


def first_pass(seqs, tokens, channels, gates, bias, keep, upd, fgt, out, scale, shift, summary):
    def body(at, carried):
        given = list(carried)
        for seq in range(seqs):
            for half in range(STEP // SUB):
                rows = pl.ds(pl.multiple_of(seq * tokens + at * STEP + half * SUB, SUB), SUB)
                kept = keep[rows, :][:, 0:1]
                for number, lanes in enumerate(lane_blocks(channels)):
                    u = jnp.tanh(gates[0, rows, lanes] + bias[0:1, lanes])
                    f = sigmoid(gates[1, rows, lanes] + bias[1:2, lanes])
                    o = sigmoid(gates[2, rows, lanes] + bias[2:3, lanes])
                    upd[rows, lanes] = u
                    fgt[rows, lanes] = f
                    out[rows, lanes] = o
                    a, b = scan_down(f * kept, (1.0 - f) * u)
                    place = (seq * len(lane_blocks(channels)) + number) * 2
                    b = a * given[place + 1] + b
                    a = a * given[place]
                    scale[rows, lanes] = a
                    shift[rows, lanes] = b
                    given[place] = a[SUB - 1 : SUB]
                    given[place + 1] = b[SUB - 1 : SUB]
        return tuple(given)

    begin = []
    for seq in range(seqs):
        for lanes in lane_blocks(channels):
            width = lanes.stop - lanes.start
            begin += [jnp.ones((1, width), F32), jnp.zeros((1, width), F32)]
    end = lax.fori_loop(0, tokens // STEP, body, tuple(begin))
    place = 0
    for seq in range(seqs):
        for lanes in lane_blocks(channels):
            summary[seq : seq + 1, lanes] = end[place]
            summary[seqs + seq : seqs + seq + 1, lanes] = end[place + 1]
            place += 2


def back_pass(seqs, tokens, channels, upstream, keep, fgt, out, scale, shift, summary, row0):
    steps = tokens // STEP

    def body(index, carried):
        at = steps - 1 - index
        given = list(carried)
        for seq in range(seqs):
            whole = pl.ds(pl.multiple_of(seq * tokens + at * STEP, STEP), STEP)
            for number, lanes in enumerate(lane_blocks(channels)):
                ups = upstream[whole, lanes].astype(F32)
                place = (seq * len(lane_blocks(channels)) + number) * 2
                for half in reversed(range(STEP // SUB)):
                    rows = pl.ds(pl.multiple_of(seq * tokens + at * STEP + half * SUB, SUB), SUB)
                    kept = keep[rows, :][:, 0:1]
                    retain = fgt[rows, lanes] * kept
                    direct = ups[half * SUB : half * SUB + SUB] * out[rows, lanes]
                    a, b = scan_up(retain, retain * direct)
                    b = a * given[place + 1] + b
                    a = a * given[place]
                    scale[rows, lanes] = a
                    shift[rows, lanes] = b
                    given[place] = a[0:1]
                    given[place + 1] = b[0:1]
        return tuple(given)

    begin = []
    for seq in range(seqs):
        for lanes in lane_blocks(channels):
            width = lanes.stop - lanes.start
            begin += [jnp.ones((1, width), F32), jnp.zeros((1, width), F32)]
    end = lax.fori_loop(0, steps, body, tuple(begin))
    place = 0
    for seq in range(seqs):
        for lanes in lane_blocks(channels):
            summary[row0 + seq : row0 + seq + 1, lanes] = end[place]
            summary[row0 + seqs + seq : row0 + seqs + seq + 1, lanes] = end[place + 1]
            place += 2


def states_pass(seq, tokens, channels, entering, out, scale, shift, state, pooled):
    def body(at, none):
        rows = pl.ds(pl.multiple_of(seq * tokens + at * STEP, STEP), STEP)
        for lanes in lane_blocks(channels):
            value = scale[rows, lanes] * entering[seq : seq + 1, lanes] + shift[rows, lanes]
            state[rows, lanes] = value
            pooled[rows, lanes] = (out[rows, lanes] * value).astype(BF16)
        return none

    lax.fori_loop(0, tokens // STEP, body, 0)


def grads_pass(seqs, tokens, channels, message, entering, upstream, keep, upd, fgt, out, state, scale, shift, grads, planes, sums):
    steps = tokens // STEP
    sums[...] = jnp.zeros_like(sums)
    if grads.shape[1] > 3 * channels:
        grads[:, 3 * channels :] = jnp.zeros((grads.shape[0], grads.shape[1] - 3 * channels), BF16)
    for seq in range(seqs):
        for lanes in lane_blocks(channels):
            width = lanes.stop - lanes.start

            def body(index, later, seq=seq, lanes=lanes, width=width):
                at = steps - 1 - index
                whole = pl.ds(pl.multiple_of(seq * tokens + at * STEP, STEP), STEP)
                row = lax.broadcasted_iota(jnp.int32, (STEP, width), 0)
                kept = keep[whole, :][:, 0:1]
                ups = upstream[whole, lanes].astype(F32)
                u, f, o = upd[whole, lanes], fgt[whole, lanes], out[whole, lanes]
                states = state[whole, lanes]
                arriving = scale[whole, lanes] * message[seq : seq + 1, lanes] + shift[whole, lanes]
                adjoint = ups * o + jnp.where(row == STEP - 1, later, pltpu.roll(arriving, STEP - 1, 0))
                tile = pl.ds(pl.multiple_of(seq * tokens + jnp.maximum(at * STEP - SUB, 0), SUB), SUB)
                last = state[tile, lanes][SUB - 1 : SUB]
                first = jnp.where(at == 0, entering[seq : seq + 1, lanes], last)
                before = jnp.where(row == 0, first, pltpu.roll(states, 1, 0))
                given = [
                    adjoint * (1.0 - f) * (1.0 - u * u),
                    adjoint * (before * kept - u) * f * (1.0 - f),
                    ups * states * o * (1.0 - o),
                ]
                for gate, value in enumerate(given):
                    value = value.astype(BF16)
                    grads[whole, gate * channels + lanes.start : gate * channels + lanes.stop] = value
                    if planes is not None:
                        planes[gate, whole, lanes] = value
                    value = value.astype(F32)
                    total = value[:SUB]
                    for half in range(1, STEP // SUB):
                        total = total + value[half * SUB : half * SUB + SUB]
                    sums[gate, :, lanes] += total
                return arriving[0:1]

            lax.fori_loop(0, steps, body, message[seq : seq + 1, lanes])


def forward_kernel(seqs, tokens, channels, gates, bias, keep, initial, hidden, upd, fgt, out, state, entering, scale, shift, summary, slots, send_sems, recv_sems):
    greet("seq")
    first_pass(seqs, tokens, channels, gates, bias, keep, upd, fgt, out, scale, shift, summary)
    met("seq")
    copies = to_all(summary, slots, send_sems, recv_sems, "seq")
    for copy in copies:
        copy.wait()
    entering[...] = from_earlier(slots, initial[...], slice(0, seqs), slice(seqs, 2 * seqs), "seq")
    for seq in range(seqs):
        states_pass(seq, tokens, channels, entering, out, scale, shift, state, hidden)


def top_kernel(seqs, tokens, channels, gates, bias, keep, initial, cotangent, pooled, grads, planes, sums, upd, fgt, out, state, entering, message, scale, shift, back_scale, back_shift, summary, slots, send_sems, recv_sems):
    greet("seq")
    first_pass(seqs, tokens, channels, gates, bias, keep, upd, fgt, out, scale, shift, summary)
    back_pass(seqs, tokens, channels, cotangent, keep, fgt, out, back_scale, back_shift, summary, 2 * seqs)
    met("seq")
    copies = to_all(summary, slots, send_sems, recv_sems, "seq")
    for copy in copies:
        copy.wait()
    entering[...] = from_earlier(slots, initial[...], slice(0, seqs), slice(seqs, 2 * seqs), "seq")
    message[...] = from_later(
        slots, (seqs, channels), slice(2 * seqs, 3 * seqs), slice(3 * seqs, 4 * seqs), "seq"
    )
    for seq in range(seqs):
        states_pass(seq, tokens, channels, entering, out, scale, shift, state, pooled)
    grads_pass(seqs, tokens, channels, message, entering, cotangent, keep, upd, fgt, out, state, back_scale, back_shift, grads, planes, sums)


def pass_edges(seqs, tokens, grads, edges, arrived, edge_sems):
    count = lax.axis_size("seq")
    me = lax.axis_index("seq")
    row = lax.broadcasted_iota(jnp.int32, edges.shape, 0)
    firsts = jnp.zeros(edges.shape, F32)
    for seq in range(seqs):
        tile = grads[seq * tokens : seq * tokens + EDGE, :].astype(F32)
        firsts = jnp.where(row == seq, pltpu.roll(tile, seq, 0) if seq else tile, firsts)
    edges[...] = firsts.astype(BF16)
    copy = pltpu.make_async_remote_copy(
        src_ref=edges,
        dst_ref=arrived,
        send_sem=edge_sems.at[0],
        recv_sem=edge_sems.at[1],
        device_id={"seq": lax.rem(me + count - 1, count)},
        device_id_type=pl.DeviceIdType.MESH,
    )
    rows = slice(seqs * tokens, seqs * tokens + EDGE)

    @pl.when(me > 0)
    def _():
        copy.start()

    @pl.when(me < count - 1)
    def _():
        copy.wait_recv()
        grads[rows, :] = arrived[...]

    @pl.when(me == count - 1)
    def _():
        grads[rows, :] = jnp.zeros(edges.shape, BF16)

    @pl.when(me > 0)
    def _():
        copy.wait_send()


def backward_kernel(seqs, tokens, channels, upstream, keep, upd, fgt, out, state, entering, grads, sums, message, scale, shift, summary, slots, send_sems, recv_sems, edges, arrived, edge_sems):
    greet("seq")
    back_pass(seqs, tokens, channels, upstream, keep, fgt, out, scale, shift, summary, 0)
    met("seq")
    copies = to_all(summary, slots, send_sems, recv_sems, "seq")
    for copy in copies:
        copy.wait()
    message[...] = from_later(slots, (seqs, channels), slice(0, seqs), slice(seqs, 2 * seqs), "seq")
    grads_pass(seqs, tokens, channels, message, entering, upstream, keep, upd, fgt, out, state, scale, shift, grads, None, sums)
    pass_edges(seqs, tokens, grads, edges, arrived, edge_sems)


def neighbours():
    here = lax.axis_index("dp")
    beside = here + 1 - 2 * lax.rem(here, 2)
    return here, beside, lax.rem(here + 2, 4), lax.rem(beside + 2, 4)


def relay(value, every, plane_sems, kept_sem):
    here, beside, below, corner = neighbours()
    near = (beside, below)
    half = value.shape[0] // 2

    def over(src, owner, way):
        place = every.at[owner]
        return remote(src, place, plane_sems.at[0, way], plane_sems.at[1, way], "dp", near[way])

    def onward(owner, way):
        place = every.at[owner, pl.ds(way * half, half)]
        return remote(place, place, plane_sems.at[0, 2 + way], plane_sems.at[1, 2 + way], "dp", near[1 - way])

    def keep():
        return pltpu.make_async_copy(value, every.at[here], kept_sem)

    def start():
        for way in range(2):
            over(value, here, way).start()
        keep().start()

    def forward():
        for way in range(2):
            over(every.at[near[way]], near[way], way).wait_recv()
            onward(near[way], way).start()

    def finish():
        for way in range(2):
            over(value, here, way).wait_send()
            onward(near[way], way).wait_send()
            onward(corner, way).wait_recv()
        keep().wait()

    return start, forward, finish


def first_stage(seqs, tokens, channels, inputs, taps, bias, keep, initial, full_hidden, every, both, edges, weights, gates, hidden, state, entering, scale, shift, summary, slots, send_sems, recv_sems, weight_sems, plane_sems, kept_sem, pair_sems, edge_sems):
    axes = ("seq", "dp", "mp")
    line, at, mine = lax.axis_size("seq"), lax.axis_index("seq"), lax.axis_index("mp")
    after, before = lax.rem(at + 1, line), lax.rem(at + line - 1, line)
    greet(*axes)
    pl.semaphore_signal(
        pltpu.get_barrier_semaphore(),
        inc=1,
        device_id={"seq": before, "mp": 1 - mine},
        device_id_type=pl.DeviceIdType.MESH,
    )
    rows = seqs * tokens
    half = rows // 2
    gather_start, gather_forward, gather_finish = relay(inputs, every, plane_sems, kept_sem)

    def load(step):
        slot = lax.rem(step, 2)
        side = jnp.where(lax.rem(step // 3, 2) == 0, mine, 1 - mine)
        return pltpu.make_async_copy(
            taps.at[step // 6, lax.rem(step, 3), pl.ds(pl.multiple_of(side * channels, 128), channels), :],
            weights.at[slot],
            weight_sems.at[slot],
        )

    def lanes_of(core):
        return pl.ds(pl.multiple_of(core * channels, 128), channels)

    own = pltpu.make_async_copy(inputs, both.at[0, :, lanes_of(mine)], pair_sems.at[0])
    give = remote(inputs, both.at[0, :, lanes_of(mine)], pair_sems.at[1], pair_sems.at[2], "mp", 1 - mine)
    take = remote(inputs, both.at[0, :, lanes_of(1 - mine)], pair_sems.at[1], pair_sems.at[2], "mp", 1 - mine)

    def edge(seq, other, arriving=False):
        core = jnp.where(other, 1 - mine, mine)
        return pltpu.make_async_remote_copy(
            src_ref=inputs.at[seq * tokens + tokens - EDGE : seq * tokens + tokens],
            dst_ref=edges.at[core if arriving else mine, seq],
            send_sem=edge_sems.at[0, other, seq],
            recv_sem=edge_sems.at[1, other, seq],
            device_id={"seq": after, "mp": core},
            device_id_type=pl.DeviceIdType.MESH,
        )

    load(0).start()
    own.start()
    pl.semaphore_wait(pltpu.get_barrier_semaphore(), sum(lax.axis_size(axis) - 1 for axis in axes) + 1)
    give.start()

    @pl.when(at < line - 1)
    def _():
        for seq in range(seqs):
            for other in range(2):
                edge(seq, other).start()

    @pl.when(at == 0)
    def _():
        edges[...] = jnp.zeros(edges.shape, BF16)

    gather_start()
    own.wait()

    def shift_down():
        width = 2 * channels
        steps = tokens // STEP

        def body(index, none):
            seq, tile = index // steps, lax.rem(index, steps)
            row = lax.broadcasted_iota(jnp.int32, (STEP, width), 0)
            place = pl.ds(pl.multiple_of(index * STEP, STEP), STEP)
            ahead = pl.ds(pl.multiple_of(jnp.maximum(index - 1, 0) * STEP, STEP), STEP)
            last = both[0, ahead, :].astype(F32)[STEP - 1 : STEP]
            outer = jnp.concatenate([edges[0, seq], edges[1, seq]], 1).astype(F32)[EDGE - 1 : EDGE]
            moved = pltpu.roll(both[0, place, :].astype(F32), 1, 0)
            both[1, place, :] = jnp.where(row == 0, jnp.where(tile == 0, outer, last), moved).astype(BF16)
            return none

        lax.fori_loop(0, rows // STEP, body, 0)

    def body(step, none):
        @pl.when(step == 3)
        def _():
            take.wait_recv()

        @pl.when(step == 6)
        def _():
            @pl.when(at > 0)
            def _():
                for seq in range(seqs):
                    for other in range(2):
                        edge(seq, other, True).wait_recv()

            shift_down()

        load(step).wait()

        @pl.when(step < 11)
        def _():
            load(step + 1).start()

        gate, part = lax.rem(step, 3), lax.rem(step // 3, 2)
        columns = lanes_of(jnp.where(part == 0, mine, 1 - mine))
        for side in range(2):
            place = pl.ds(side * half, half)
            term = jnp.dot(
                both[step // 6, place, columns], weights[lax.rem(step, 2)], preferred_element_type=F32
            )
            gates[gate, place, :] = jnp.where(step < 3, term, gates[gate, place, :] + term)
        return none

    lax.fori_loop(0, 12, body, 0)
    upd, fgt, out = gates.at[0], gates.at[1], gates.at[2]
    first_pass(seqs, tokens, channels, gates, bias, keep, upd, fgt, out, scale, shift, summary)
    copies = to_all(summary, slots, send_sems, recv_sems, "seq")
    gather_forward()
    for copy in copies:
        copy.wait()
    entering[...] = from_earlier(slots, initial[...], slice(0, seqs), slice(seqs, 2 * seqs), "seq")
    sent = []
    for seq in range(seqs):
        states_pass(seq, tokens, channels, entering, out, scale, shift, state, hidden)
        part = pl.ds(seq * tokens, tokens)
        place = full_hidden.at[part, lanes_of(mine)]
        sent.append(pltpu.make_async_copy(hidden.at[part], place, pair_sems.at[3 + 3 * seq]))
        sent.append(remote(hidden.at[part], place, pair_sems.at[4 + 3 * seq], pair_sems.at[5 + 3 * seq], "mp", 1 - mine))
        for copy in sent[-2:]:
            copy.start()

    def finish():
        give.wait_send()

        @pl.when(at < line - 1)
        def _():
            for seq in range(seqs):
                for other in range(2):
                    edge(seq, other).wait_send()

        gather_finish()

    def hidden_here():
        for copy in sent:
            copy.wait()

    return hidden_here, finish


def upper_stage(seqs, tokens, channels, full_hidden, hidden_here, hidden, mix, bias, keep, initial, cotangent, pooled, grads, planes, sums, every, weights, gates, state, entering, message, scale, shift, back_scale, back_shift, summary, slots, send_sems, recv_sems, weight_sems, plane_sems, kept_sem):
    half = seqs * tokens // 2
    gather_start, gather_forward, gather_finish = relay(hidden, every, plane_sems, kept_sem)

    def load(step):
        slot = lax.rem(step, 2)
        return pltpu.make_async_copy(
            mix.at[step // 2, pl.ds(pl.multiple_of(lax.rem(step, 2) * channels, 128), channels), :],
            weights.at[slot],
            weight_sems.at[slot],
        )

    load(0).start()
    gather_start()
    hidden_here()

    def body(step, none):
        load(step).wait()

        @pl.when(step < 5)
        def _():
            load(step + 1).start()

        gate, part = step // 2, lax.rem(step, 2)
        columns = pl.ds(pl.multiple_of(part * channels, 128), channels)
        for side in range(2):
            place = pl.ds(side * half, half)
            term = jnp.dot(full_hidden[place, columns], weights[part], preferred_element_type=F32)
            gates[gate, place, :] = jnp.where(part == 0, term, gates[gate, place, :] + term)
        return none

    lax.fori_loop(0, 6, body, 0)
    upd, fgt, out = gates.at[0], gates.at[1], gates.at[2]
    first_pass(seqs, tokens, channels, gates, bias, keep, upd, fgt, out, scale, shift, summary)
    back_pass(seqs, tokens, channels, cotangent, keep, fgt, out, back_scale, back_shift, summary, 2 * seqs)
    copies = to_all(summary, slots, send_sems, recv_sems, "seq")
    gather_forward()
    for copy in copies:
        copy.wait()
    entering[...] = from_earlier(slots, initial[...], slice(0, seqs), slice(seqs, 2 * seqs), "seq")
    message[...] = from_later(
        slots, (seqs, channels), slice(2 * seqs, 3 * seqs), slice(3 * seqs, 4 * seqs), "seq"
    )
    for seq in range(seqs):
        states_pass(seq, tokens, channels, entering, out, scale, shift, state, pooled)
    grads_pass(seqs, tokens, channels, message, entering, cotangent, keep, upd, fgt, out, state, back_scale, back_shift, grads, planes, sums)
    return gather_finish


def lower_stage(seqs, tokens, channels, above, above_columns, mix, keep, upd, fgt, out, state, entering, grads, sums, swapped, weights, total, coming, message, scale, shift, summary, slots, send_sems, recv_sems, edges, arrived, edge_sems, weight_sems, pair_sems, swap_sems):
    mine = lax.axis_index("mp")
    width = swapped.shape[2]

    def load(step):
        side = jnp.where(step < 3, 1 - mine, mine)
        slot = lax.rem(step, 2)
        return pltpu.make_async_copy(
            mix.at[lax.rem(step, 3), pl.ds(pl.multiple_of(side * channels, 128), channels), :],
            weights.at[slot],
            weight_sems.at[slot],
        )

    load(0).start()
    plane = neighbours()
    swaps = []
    for steps in (3, 1, 2, 0):
        src = above_columns.at[:, pl.ds(pl.multiple_of(plane[steps] * width, 128), width)]
        dst = swapped.at[plane[0]]
        if steps:
            swaps.append(remote(src, dst, swap_sems.at[0, steps], swap_sems.at[1, steps], "dp", plane[steps]))
        else:
            swaps.append(pltpu.make_async_copy(src, dst, swap_sems.at[0, steps]))
        swaps[-1].start()
    give = remote(total.at[0], coming, pair_sems.at[0], pair_sems.at[1], "mp", 1 - mine)

    def body(step, none):
        load(step).wait()

        @pl.when(step < 5)
        def _():
            load(step + 1).start()

        side, gate = step // 3, lax.rem(step, 3)
        rows = above.shape[1] // 2
        for half in range(2):
            place = pl.ds(half * rows, rows)
            term = lax.dot_general(
                above[gate, place, :], weights[lax.rem(step, 2)], (((1,), (1,)), ((), ())), preferred_element_type=F32
            )
            total[side, place, :] = jnp.where(gate == 0, term, total[side, place, :] + term)

        @pl.when(step == 2)
        def _():
            give.start()

        return none

    lax.fori_loop(0, 6, body, 0)
    give.wait_recv()
    total[1] += coming[...]
    upstream = total.at[1]
    back_pass(seqs, tokens, channels, upstream, keep, fgt, out, scale, shift, summary, 0)
    copies = to_all(summary, slots, send_sems, recv_sems, "seq")
    for copy in copies:
        copy.wait()
    message[...] = from_later(slots, (seqs, channels), slice(0, seqs), slice(seqs, 2 * seqs), "seq")
    grads_pass(seqs, tokens, channels, message, entering, upstream, keep, upd, fgt, out, state, scale, shift, grads, None, sums)
    pass_edges(seqs, tokens, grads, edges, arrived, edge_sems)
    give.wait_send()
    for steps, copy in zip((3, 1, 2, 0), swaps):
        if steps:
            copy.wait_send()
            place = swapped.at[plane[steps]]
            remote(place, place, swap_sems.at[0, steps], swap_sems.at[1, steps], "dp", plane[steps]).wait_recv()
        else:
            copy.wait()


def front_kernel(seqs, tokens, channels, inputs, taps, mix, bias_one, bias_two, keep, initial_one, initial_two, cotangent, pooled, sums_one, sums_two, extended, every, every_hidden, swapped, both, edges, weights, gates_one, gates_two, hidden, full_hidden, planes, grads_two, coming, state_one, state_two, scale, shift, back_scale, back_shift, entering_one, entering_two, message, edge_out, edge_in, *refs):
    one, two, three = refs[:4], refs[4:8], refs[8:12]
    weight_sems, inputs_sems, inputs_kept, pair_sems, edge_sems, hidden_sems, hidden_kept, first_sems, give_sems, swap_sems = refs[12:]
    hidden_here, inputs_end = first_stage(
        seqs, tokens, channels, inputs, taps, bias_one, keep, initial_one, full_hidden, every, both, edges, weights,
        gates_one, hidden, state_one, entering_one, scale, shift, *one, weight_sems, inputs_sems, inputs_kept, pair_sems,
        edge_sems,
    )
    hidden_end = upper_stage(
        seqs, tokens, channels, full_hidden, hidden_here, hidden, mix, bias_two, keep, initial_two, cotangent, pooled,
        grads_two, planes, sums_two, every_hidden, weights, gates_two, state_two, entering_two, message, scale, shift,
        back_scale, back_shift, *two, weight_sems, hidden_sems, hidden_kept,
    )
    lower_stage(
        seqs, tokens, channels, planes, grads_two, mix, keep, gates_one.at[0], gates_one.at[1], gates_one.at[2],
        state_one, entering_one, extended, sums_one, swapped, weights, gates_two, coming, message, scale, shift, *three,
        edge_out, edge_in, first_sems, weight_sems, give_sems, swap_sems,
    )
    inputs_end()
    hidden_end()


def exchange_scratch(rows, channels):
    count = lax.axis_size("seq")
    return [
        pltpu.VMEM((rows, channels), F32),
        pltpu.VMEM((count - 1, rows, channels), F32),
        pltpu.SemaphoreType.DMA((count - 1,)),
        pltpu.SemaphoreType.DMA((count - 1,)),
    ]


def params(number):
    return pltpu.CompilerParams(collective_id=number, has_side_effects=True, vmem_limit_bytes=56 * 2**20)


def cost(elements, ops, moved):
    return pl.CostEstimate(flops=elements * ops, bytes_accessed=moved, transcendentals=elements * 3)


def pool_forward(seqs, tokens, gates, bias, keep, initial):
    channels = gates.shape[2]
    rows = seqs * tokens
    whole = jax.ShapeDtypeStruct((rows, channels), F32)
    return pl.pallas_call(
        functools.partial(forward_kernel, seqs, tokens, channels),
        out_shape=(
            jax.ShapeDtypeStruct((rows, channels), BF16),
            whole,
            whole,
            whole,
            whole,
            jax.ShapeDtypeStruct((seqs, channels), F32),
        ),
        in_specs=[VMEM] * 4,
        out_specs=[VMEM] * 6,
        scratch_shapes=[pltpu.VMEM((rows, channels), F32)] * 2 + exchange_scratch(2 * seqs, channels),
        compiler_params=params(1),
        cost_estimate=cost(rows * channels, 60, rows * channels * 30),
        name="pool_forward",
    )(gates, bias, keep, initial)


def pool_top(seqs, tokens, lanes, gates, bias, keep, initial, cotangent):
    channels = gates.shape[2]
    rows = seqs * tokens
    whole = pltpu.VMEM((rows, channels), F32)
    edge = pltpu.VMEM((seqs, channels), F32)
    return pl.pallas_call(
        functools.partial(top_kernel, seqs, tokens, channels),
        out_shape=(
            jax.ShapeDtypeStruct((rows, channels), BF16),
            jax.ShapeDtypeStruct((rows, lanes), BF16),
            jax.ShapeDtypeStruct((3, rows, channels), BF16),
            jax.ShapeDtypeStruct((3, SUB, channels), F32),
        ),
        in_specs=[VMEM] * 5,
        out_specs=[VMEM] * 4,
        scratch_shapes=[whole] * 4 + [edge] * 2 + [whole] * 4 + exchange_scratch(4 * seqs, channels),
        compiler_params=params(2),
        cost_estimate=cost(rows * channels, 120, rows * channels * 22),
        name="pool_top",
    )(gates, bias, keep, initial, cotangent)


def front(seqs, tokens, lanes, inputs, taps, mix, bias_one, bias_two, keep, initial_one, initial_two, cotangent):
    rows, channels = inputs.shape
    hbm = pl.BlockSpec(memory_space=pl.ANY)
    dma = pltpu.SemaphoreType.DMA
    whole = pltpu.VMEM((rows, channels), F32)
    few = pltpu.VMEM((seqs, channels), F32)
    return pl.pallas_call(
        functools.partial(front_kernel, seqs, tokens, channels),
        out_shape=(
            jax.ShapeDtypeStruct((rows, channels), BF16),
            jax.ShapeDtypeStruct((3, SUB, channels), F32),
            jax.ShapeDtypeStruct((3, SUB, channels), F32),
            jax.ShapeDtypeStruct((rows + EDGE, lanes), BF16),
            jax.ShapeDtypeStruct((4, rows, channels), BF16),
            jax.ShapeDtypeStruct((4, rows, channels), BF16),
            jax.ShapeDtypeStruct((4, rows, lanes // 4), BF16),
        ),
        in_specs=[hbm] * 3 + [VMEM] * 6,
        out_specs=[VMEM] * 4 + [hbm] * 3,
        scratch_shapes=[
            pltpu.VMEM((2, rows, 2 * channels), BF16),
            pltpu.VMEM((2, seqs, EDGE, channels), BF16),
            pltpu.VMEM((2, channels, channels), BF16),
            pltpu.VMEM((3, rows, channels), F32),
            pltpu.VMEM((3, rows, channels), F32),
            pltpu.VMEM((rows, channels), BF16),
            pltpu.VMEM((rows, 2 * channels), BF16),
            pltpu.VMEM((3, rows, channels), BF16),
            pltpu.VMEM((rows, lanes), BF16),
        ]
        + [whole] * 7
        + [few] * 3
        + [pltpu.VMEM((EDGE, lanes), BF16)] * 2
        + exchange_scratch(2 * seqs, channels)
        + exchange_scratch(4 * seqs, channels)
        + exchange_scratch(2 * seqs, channels)
        + [dma((2,)), dma((2, 4)), dma, dma((3 + 3 * seqs,)), dma((2, 2, seqs))]
        + [dma((2, 4)), dma, dma((2,)), dma((2,)), dma((2, 4))],
        compiler_params=pltpu.CompilerParams(
            collective_id=7, has_side_effects=True, vmem_limit_bytes=62 * 2**20
        ),
        cost_estimate=pl.CostEstimate(
            flops=48 * rows * channels * channels, bytes_accessed=rows * channels * 160, transcendentals=0
        ),
        name="front",
    )(inputs, taps, mix, bias_one, bias_two, keep, initial_one, initial_two, cotangent)


def pool_backward(seqs, tokens, lanes, upstream, keep, upd, fgt, out, state, entering):
    rows, channels = upstream.shape
    whole = pltpu.VMEM((rows, channels), F32)
    return pl.pallas_call(
        functools.partial(backward_kernel, seqs, tokens, channels),
        out_shape=(
            jax.ShapeDtypeStruct((rows + EDGE, lanes), BF16),
            jax.ShapeDtypeStruct((3, SUB, channels), F32),
        ),
        in_specs=[VMEM] * 7,
        out_specs=[VMEM] * 2,
        scratch_shapes=[pltpu.VMEM((seqs, channels), F32)]
        + [whole] * 2
        + exchange_scratch(2 * seqs, channels)
        + [pltpu.VMEM((EDGE, lanes), BF16)] * 2
        + [pltpu.SemaphoreType.DMA((2,))],
        compiler_params=params(3),
        cost_estimate=cost(rows * channels, 60, rows * channels * 26),
        name="pool_backward",
    )(upstream, keep, upd, fgt, out, state, entering)


def shift_up(seqs, tokens, value, edges, result):
    width = value.shape[1]
    steps = tokens // STEP

    def body(index, none):
        sequence, at = index // steps, lax.rem(index, steps)
        row = lax.broadcasted_iota(jnp.int32, (STEP, width), 0)
        rows = pl.ds(pl.multiple_of(index * STEP, STEP), STEP)
        after = jnp.minimum(index + 1, value.shape[0] // STEP - 1)
        first = value[pl.ds(pl.multiple_of(after * STEP, STEP), STEP), :].astype(F32)[0:1]
        edge = edges[sequence // seqs].astype(F32)
        edge = jnp.where(lax.rem(sequence, seqs) == 0, edge[0:1], edge[1:2])
        moved = pltpu.roll(value[rows, :].astype(F32), STEP - 1, 0)
        moved = jnp.where(row == STEP - 1, jnp.where(at == steps - 1, edge, first), moved)
        result[rows, :] = moved.astype(BF16)
        return none

    lax.fori_loop(0, value.shape[0] // STEP, body, 0)


def spread_kernel(seqs, tokens, parts, turn, tail, hidden, full, grads_two, grads_one, taps, sums, out, input_grad, sums_out, rows_full, grads, grads_edge, moved, own, ups, downs, acc, across, around, every, weights, leaving, coming, load_sems, swap_sems, up_sems, down_sems, line_send, line_recv, column_send, column_recv, kept_sems, plane_send, plane_recv, sums_sems, weight_sems, leaving_sems, coming_sems, result_sems, pair_sems, ready_sem):
    line, plane = lax.axis_size("seq"), lax.axis_size("dp")
    at, here = lax.axis_index("seq"), lax.axis_index("dp")
    unit = line * parts
    units = own.shape[0] // unit
    blocks = units // 3
    width = own.shape[1]
    block_rows = seqs * tokens
    half = unit // 2
    here, beside, below, across_from = neighbours()
    mine = lax.axis_index("mp")
    greet("seq", "dp", "mp")
    met("seq", "dp", "mp")

    def turned(u):
        return lax.rem(u, turn) == turn - 1

    def direct(u):
        return lax.rem(u, turn) != turn - 1

    wide = rows_full.shape[1] // 2

    def own_rows(value, number, way):
        place = rows_full.at[:, pl.ds(pl.multiple_of(mine * wide, 128), wide)]
        if way == 0:
            return pltpu.make_async_copy(value, place, load_sems.at[number])
        return remote(value, place, pair_sems.at[0, number], pair_sems.at[1, number], "mp", 1 - mine)

    def other_rows(number):
        place = rows_full.at[:, pl.ds(pl.multiple_of((1 - mine) * wide, 128), wide)]
        return remote(place, place, pair_sems.at[0, number], pair_sems.at[1, number], "mp", 1 - mine)

    def plane_rows(owner):
        return pl.ds(pl.multiple_of(owner * block_rows, 16), block_rows)

    def peer(steps):
        return (here, beside, below, across_from)[steps]

    def load_two():
        return pltpu.make_async_copy(grads_two, moved, load_sems.at[2])

    def swap(steps, edge, arriving=False):
        columns = pl.ds(pl.multiple_of(peer(steps) * width, 128), width)
        source = peer(steps) if arriving else here
        if edge:
            src, dst = grads_one.at[block_rows : block_rows + EDGE, columns], grads_edge.at[source]
        else:
            src, dst = grads_one.at[0:block_rows, columns], grads.at[plane_rows(source)]
        number = steps * 2 + edge
        if steps == 0:
            return pltpu.make_async_copy(src, dst, swap_sems.at[0, number])
        return remote(src, dst, swap_sems.at[0, number], swap_sems.at[1, number], "dp", peer(steps))

    def product(block, right):
        columns = pl.ds(pl.multiple_of(jnp.where(mine == 0, block, blocks - 1 - block) * unit, 128), unit)
        return lax.dot_general(
            rows_full[:, columns], right[...], (((0,), (0,)), ((), ())), preferred_element_type=F32
        ).astype(BF16)

    narrow = leaving.shape[2]
    pieces = wide // narrow

    def load_weights(step):
        first = jnp.where(step < pieces, (1 - mine) * pieces + step, mine * pieces + step - pieces) * narrow
        slot = lax.rem(step, 2)
        return pltpu.make_async_copy(
            taps.at[:, :, pl.ds(pl.multiple_of(first, narrow), narrow), :], weights.at[slot], weight_sems.at[slot]
        )

    def load_every():
        return pltpu.make_async_copy(grads_one, every, load_sems.at[3])

    def leave(step):
        slot = lax.rem(step, 2)
        return remote(leaving.at[slot], coming.at[step], leaving_sems.at[slot], coming_sems.at[step], "mp", 1 - mine)

    def result(step):
        return pltpu.make_async_copy(
            coming.at[step],
            input_grad.at[:, pl.ds(pl.multiple_of(step * narrow, narrow), narrow)],
            result_sems.at[step],
        )

    def input_terms(slot):
        channels = taps.shape[3]
        now = jnp.zeros((block_rows, narrow), F32)
        late = jnp.zeros((block_rows + EDGE, narrow), F32)
        for gate in range(3):
            lanes = slice(gate * channels, gate * channels + channels)
            now += lax.dot_general(
                every[:block_rows, lanes], weights[slot, 0, gate], (((1,), (1,)), ((), ())), preferred_element_type=F32
            )
            late += lax.dot_general(
                every[:, lanes], weights[slot, 1, gate], (((1,), (1,)), ((), ())), preferred_element_type=F32
            )
        row = lax.broadcasted_iota(jnp.int32, now.shape, 0)
        after = pltpu.roll(late[:block_rows], block_rows - 1, 0)
        for seq in range(seqs):
            after = jnp.where(
                row == seq * tokens + tokens - 1, late[block_rows + seq : block_rows + seq + 1], after
            )
        return now + after

    def whole(u):
        return pl.ds(pl.multiple_of(u * unit, unit), unit)

    def chunk(u, j):
        return pl.ds(pl.multiple_of(u * unit + j * parts, parts), parts)

    def up(src, u, j):
        number = u * (line - 1) + j - 1
        return remote(src, ups.at[u, j - 1], up_sems.at[0, number], up_sems.at[1, number], "seq", lax.rem(at + 1, line))

    def down(src, u, j):
        number = u * (line - 1) + j
        return remote(
            src, downs.at[u, j], down_sems.at[0, number], down_sems.at[1, number], "seq", lax.rem(at + line - 1, line)
        )

    def along(src, u, j, way, hop):
        return remote(
            src,
            out.at[here, chunk(u, j)],
            line_send.at[(u * 2 + way) * (line - 1) + hop],
            line_recv.at[u * line + j],
            "seq",
            lax.rem(at + (1 if way == 0 else line - 1), line),
        )

    at_end = (at == 0) | (at == line - 1)
    share = line // 2 * parts
    begin = jnp.where(at == 0, 0, line // 2) * parts

    def owner_of(u, j):
        return jnp.where(turned(u), (line - 1) * (j >= line // 2), j)

    def column(steps, u, way):
        number = (u // turn * 4 + steps) * 2 + way
        place = out.at[peer(steps), rows(u, way * share, share)]
        return remote(
            place,
            place,
            column_send.at[number],
            column_recv.at[number],
            "seq",
            lax.rem(at + (1 if way == 0 else line - 1), line),
        )

    def end_rows(u):
        return pl.ds(pl.multiple_of(u * unit + begin, parts), share)

    def keep_part(u):
        return pltpu.make_async_copy(own.at[end_rows(u)], out.at[here, end_rows(u)], kept_sems.at[u])

    def over_part(src, u, way):
        return remote(
            src,
            out.at[here, end_rows(u)],
            plane_send.at[u * 4 + way],
            plane_recv.at[u * 4 + way],
            "dp",
            (beside, below)[way],
        )

    def onward_part(owner, u, way):
        place = out.at[owner, pl.ds(pl.multiple_of(u * unit + begin + way * (share // 2), 16), share // 2)]
        return remote(
            place, place, plane_send.at[u * 4 + 2 + way], plane_recv.at[u * 4 + 2 + way], "dp", (below, beside)[way]
        )

    def keep(u):
        return pltpu.make_async_copy(own.at[chunk(u, at)], out.at[here, chunk(u, at)], kept_sems.at[u])

    def rows(u, first, count):
        return pl.ds(pl.multiple_of(u * unit + first, half), count)

    def over(u, way):
        place = out.at[here, rows(u, 0, unit)]
        return remote(place, place, plane_send.at[u * 4 + way], plane_recv.at[u * 4 + way], "dp", (beside, below)[way])

    def onward(u, way):
        place = out.at[(beside, below)[way], rows(u, way * half, half)]
        return remote(
            place, place, plane_send.at[u * 4 + 2 + way], plane_recv.at[u * 4 + 2 + way], "dp", (below, beside)[way]
        )

    def corner(u, way):
        place = out.at[across_from, rows(u, way * half, half)]
        return remote(place, place, plane_send.at[u * 4 + 2 + way], plane_recv.at[u * 4 + 2 + way], "dp", (below, beside)[way])

    def sums_copy(slots, me, count, axis, number, step):
        return remote(
            slots.at[me],
            slots.at[me],
            sums_sems.at[number, 0, step - 1],
            sums_sems.at[number, 1, step - 1],
            axis,
            lax.rem(me + step, count),
        )

    def sums_arrival(slots, me, count, axis, number, step):
        place = slots.at[lax.rem(me + count - step, count)]
        return remote(place, place, sums_sems.at[number, 0, step - 1], sums_sems.at[number, 1, step - 1], axis, lax.rem(me + step, count))

    for way in range(2):
        own_rows(hidden, 0, way).start()
    load_two().start()
    for steps in range(4):
        for edge in range(2):
            swap(steps, edge).start()
    load_every().start()
    load_weights(0).start()
    across[at] = sums[...]
    for step in range(1, line):
        sums_copy(across, at, line, "seq", 0, step).start()
    load_two().wait()
    own_rows(hidden, 0, 0).wait()

    def stage(index, none):
        @pl.when(index == 1)
        def _():
            for step in range(1, line):
                sums_arrival(across, at, line, "seq", 0, step).wait_recv()
            total = across[0]
            for other in range(1, line):
                total = total + across[other]
            around[here] = total
            for step in range(1, plane):
                sums_copy(around, here, plane, "dp", 1, step).start()

        @pl.when(index == 3)
        def _():
            for step in range(1, plane):
                sums_arrival(around, here, plane, "dp", 1, step).wait_recv()
            total = around[0]
            for other in range(1, plane):
                total = total + around[other]
            sums_out[...] = total

        @pl.when(index == wide // unit)
        def _():
            other_rows(0).wait_recv()

        @pl.when(index == blocks + 2 * (wide // unit))
        def _():
            other_rows(1).wait_recv()

        @pl.when(index < blocks)
        def _():
            own[whole(index), :] = product(index, moved)

        @pl.when(index == blocks - 1)
        def _():
            own_rows(hidden, 0, 1).wait_send()
            own_rows(full, 1, 0).start()
            pl.semaphore_signal(ready_sem, inc=1, device_id={"mp": 1 - mine}, device_id_type=pl.DeviceIdType.MESH)
            pl.semaphore_wait(ready_sem, 1)
            own_rows(full, 1, 1).start()

        @pl.when(index == blocks)
        def _():
            for steps in range(4):
                for edge in range(2):
                    if steps:
                        swap(steps, edge, True).wait_recv()
                    else:
                        swap(steps, edge).wait()
            shift_up(seqs, tokens, grads, grads_edge, moved)
            own_rows(full, 1, 0).wait()
            load_every().wait()

        @pl.when((index >= blocks) & (index < units) & (lax.rem(index - blocks, 2) == 0))
        def _():
            own[whole(index), :] = product((index - blocks) // 2, grads)

        @pl.when((index >= blocks) & (index < units) & (lax.rem(index - blocks, 2) == 1))
        def _():
            own[whole(index), :] = product((index - blocks) // 2, moved)

        k = index - blocks

        @pl.when((k >= 0) & (k < 2 * pieces))
        def _():
            load_weights(k).wait()

            @pl.when(k + 1 < 2 * pieces)
            def _():
                load_weights(k + 1).start()

            terms = input_terms(lax.rem(k, 2))

            @pl.when(k < pieces)
            def _():
                @pl.when(k >= 2)
                def _():
                    leave(k - 2).wait_send()

                leaving[lax.rem(k, 2)] = terms
                leave(k).start()

            @pl.when(k >= pieces)
            def _():
                leave(k - pieces).wait_recv()
                coming[k - pieces] += terms
                result(k - pieces).start()

        u = index - at

        @pl.when((u >= 0) & (u < units))
        def _():
            for j in range(line - 1, 0, -1):

                owner = owner_of(u, j)

                @pl.when((at == 0) & (at < owner))
                def _(j=j):
                    up(own.at[chunk(u, j)], u, j).start()

                @pl.when((at > 0) & (at <= owner))
                def _(j=j):
                    up(ups.at[u, j - 1], u, j).wait_recv()

                @pl.when((at > 0) & (at < owner))
                def _(j=j):
                    ups[u, j - 1] = (ups[u, j - 1].astype(F32) + own[chunk(u, j)].astype(F32)).astype(BF16)
                    up(ups.at[u, j - 1], u, j).start()

        v = index - (line - 1 - at)

        @pl.when((v >= 0) & (v < units))
        def _():
            for j in range(line - 1):

                owner = owner_of(v, j)

                @pl.when((at == line - 1) & (at > owner))
                def _(j=j):
                    down(own.at[chunk(v, j)], v, j).start()

                @pl.when((at < line - 1) & (at >= owner))
                def _(j=j):
                    down(downs.at[v, j], v, j).wait_recv()

                @pl.when((at < line - 1) & (at > owner))
                def _(j=j):
                    downs[v, j] = (downs[v, j].astype(F32) + own[chunk(v, j)].astype(F32)).astype(BF16)
                    down(downs.at[v, j], v, j).start()

        w = index - (line - 1)

        @pl.when((w >= 0) & (w < units) & direct(w))
        def _():
            acc[...] = own[chunk(w, at)].astype(F32)

            @pl.when(at > 0)
            def _():
                acc[...] += ups[w, at - 1].astype(F32)

            @pl.when(at < line - 1)
            def _():
                acc[...] += downs[w, at].astype(F32)

            own[chunk(w, at)] = acc[...].astype(BF16)
            keep(w).start()

            @pl.when(at < line - 1)
            def _():
                along(own.at[chunk(w, at)], w, at, 0, 0).start()

            @pl.when(at > 0)
            def _():
                along(own.at[chunk(w, at)], w, at, 1, 0).start()

        @pl.when((w >= 0) & (w < units) & turned(w))
        def _():
            @pl.when(at == 0)
            def _():
                for j in range(line // 2):
                    own[chunk(w, j)] = (own[chunk(w, j)].astype(F32) + downs[w, j].astype(F32)).astype(BF16)

            @pl.when(at == line - 1)
            def _():
                for j in range(line // 2, line):
                    own[chunk(w, j)] = (own[chunk(w, j)].astype(F32) + ups[w, j - 1].astype(F32)).astype(BF16)

            @pl.when(at_end)
            def _():
                keep_part(w).start()
                for way in range(2):
                    over_part(own.at[end_rows(w)], w, way).start()

        c = index - line

        @pl.when((c >= 0) & (c < units) & turned(c) & at_end)
        def _():
            keep_part(c).wait()
            for way in range(2):
                over_part(out.at[(beside, below)[way], end_rows(c)], c, way).wait_recv()
                onward_part((beside, below)[way], c, way).start()

        d = index - line - 1

        @pl.when((d >= 0) & (d < units) & turned(d) & at_end)
        def _():
            for way in range(2):
                onward_part(across_from, d, way).wait_recv()

        for steps in range(4):
            for way in range(2):
                hops = at if way == 0 else line - 1 - at
                e = d - steps - hops

                @pl.when((e >= 0) & (e < units) & turned(e))
                def _(e=e, steps=steps, way=way, hops=hops):
                    @pl.when(hops > 0)
                    def _():
                        column(steps, e, way).wait_recv()

                    @pl.when(hops < line - 1)
                    def _():
                        column(steps, e, way).start()

        for hop in range(1, line):
            x = index - (line - 1) - hop

            @pl.when((x >= 0) & (x < units) & direct(x))
            def _(x=x, hop=hop):
                @pl.when(at >= hop)
                def _():
                    src = out.at[here, chunk(x, at - hop)]
                    along(src, x, at - hop, 0, 0).wait_recv()
                    if hop < line - 1:

                        @pl.when(at < line - 1)
                        def _():
                            along(src, x, at - hop, 0, hop).start()

                @pl.when(at + hop < line)
                def _():
                    src = out.at[here, chunk(x, at + hop)]
                    along(src, x, at + hop, 1, 0).wait_recv()
                    if hop < line - 1:

                        @pl.when(at > 0)
                        def _():
                            along(src, x, at + hop, 1, hop).start()

        y = index - 2 * (line - 1)

        @pl.when((y >= 0) & (y < units) & direct(y))
        def _():
            keep(y).wait()

        @pl.when((y >= 0) & (y < units - tail) & direct(y))
        def _():
            over(y, 0).start()
            over(y, 1).start()

        z = y - LAG

        @pl.when((z >= 0) & (z < units - tail) & direct(z))
        def _():
            for way in range(2):
                place = out.at[(beside, below)[way], rows(z, 0, unit)]
                remote(place, place, plane_send.at[z * 4 + way], plane_recv.at[z * 4 + way], "dp", (beside, below)[way]).wait_recv()
                onward(z, way).start()

        t = z - LAG

        @pl.when((t >= 0) & (t < units - tail) & direct(t))
        def _():
            for way in range(2):
                corner(t, way).wait_recv()

        return none

    last_turned = units // turn * turn - 1
    lax.fori_loop(
        0, max(units + 2 * (line - 1), units - tail + 2 * (line - 1) + 2 * LAG, last_turned + 2 * line + 4), stage, 0
    )

    def settle(u, none):
        for j in range(1, line):

            @pl.when(at < owner_of(u, j))
            def _(j=j):
                up(ups.at[u, j - 1], u, j).wait_send()

        for j in range(line - 1):

            @pl.when(at > owner_of(u, j))
            def _(j=j):
                down(downs.at[u, j], u, j).wait_send()

        for hop in range(line - 1):

            @pl.when(direct(u) & (at >= hop) & (at < line - 1))
            def _(hop=hop):
                along(out.at[here, chunk(u, at - hop)], u, at - hop, 0, hop).wait_send()

            @pl.when(direct(u) & (at + hop < line) & (at > 0))
            def _(hop=hop):
                along(out.at[here, chunk(u, at + hop)], u, at + hop, 1, hop).wait_send()

        @pl.when(turned(u))
        def _():
            for steps in range(4):

                @pl.when(at < line - 1)
                def _(steps=steps):
                    column(steps, u, 0).wait_send()

                @pl.when(at > 0)
                def _(steps=steps):
                    column(steps, u, 1).wait_send()

        @pl.when(direct(u) & (u < units - tail))
        def _():
            for way in range(2):
                over(u, way).wait_send()
                onward(u, way).wait_send()

        @pl.when(turned(u) & at_end)
        def _():
            for way in range(2):
                over_part(out.at[here, end_rows(u)], u, way).wait_send()
                onward_part(here, u, way).wait_send()

        return none

    lax.fori_loop(0, units, settle, 0)
    for steps in range(1, 4):
        for edge in range(2):
            swap(steps, edge).wait_send()
    own_rows(full, 1, 1).wait_send()
    for step in range(pieces - 2, pieces):
        leave(step).wait_send()
    for step in range(pieces):
        result(step).wait()
    for step in range(1, line):
        sums_copy(across, at, line, "seq", 0, step).wait_send()
    for step in range(1, plane):
        sums_copy(around, here, plane, "dp", 1, step).wait_send()


def spread(seqs, tokens, hidden, full, grads_two, grads_one, taps, sums):
    line, plane = lax.axis_size("seq"), lax.axis_size("dp")
    width = grads_two.shape[1]
    rows = grads_two.shape[0] // plane
    depth = 2 * full.shape[1]
    units = 3 * depth // (line * PART)
    channels = taps.shape[3]
    narrow = depth // (units - units // 3)
    pieces = channels // narrow
    turns = units // TURN
    dma = pltpu.SemaphoreType.DMA
    hbm = pl.BlockSpec(memory_space=pl.ANY)
    return pl.pallas_call(
        functools.partial(spread_kernel, seqs, tokens, PART, TURN, TAIL),
        out_shape=(
            jax.ShapeDtypeStruct((plane, 3 * depth, width), BF16),
            jax.ShapeDtypeStruct((rows, channels), F32),
            jax.ShapeDtypeStruct(sums.shape, F32),
        ),
        in_specs=[hbm] * 5 + [VMEM],
        out_specs=[hbm, hbm, VMEM],
        scratch_shapes=[
            pltpu.VMEM((plane * rows, depth), BF16),
            pltpu.VMEM((plane * rows, width), BF16),
            pltpu.VMEM((plane, EDGE, width), BF16),
            pltpu.VMEM((plane * rows, width), BF16),
            pltpu.VMEM((3 * depth, width), BF16),
            pltpu.VMEM((units, line - 1, PART, width), BF16),
            pltpu.VMEM((units, line - 1, PART, width), BF16),
            pltpu.VMEM((PART, width), F32),
            pltpu.VMEM((line,) + sums.shape, F32),
            pltpu.VMEM((plane,) + sums.shape, F32),
            pltpu.VMEM(grads_one.shape, BF16),
            pltpu.VMEM((2, 2, 3, narrow, channels), BF16),
            pltpu.VMEM((2, rows, narrow), F32),
            pltpu.VMEM((pieces, rows, narrow), F32),
            dma((4,)),
            dma((2, 8)),
            dma((2, units * (line - 1))),
            dma((2, units * (line - 1))),
            dma((units * 2 * (line - 1),)),
            dma((units * line,)),
            dma((turns * 8,)),
            dma((turns * 8,)),
            dma((units,)),
            dma((units * 4,)),
            dma((units * 4,)),
            dma((2, 2, max(line, plane) - 1)),
            dma((2,)),
            dma((2,)),
            dma((pieces,)),
            dma((pieces,)),
            dma((2, 2)),
            pltpu.SemaphoreType.REGULAR,
        ],
        compiler_params=pltpu.CompilerParams(
            collective_id=4, has_side_effects=True, vmem_limit_bytes=62 * 2**20
        ),
        cost_estimate=pl.CostEstimate(
            flops=6 * plane * rows * depth * width, bytes_accessed=depth * width * 48, transcendentals=0
        ),
        name="spread",
    )(hidden, full, grads_two, grads_one, taps, sums)


def widen_kernel(blocks, core, given, *refs):
    out = refs[-1]
    per = given.shape[2] // 128
    for tile in range(3 * blocks):
        source, place = divmod(tile, per)
        gate, column = divmod(tile, blocks)
        out[0, gate, :, column * 128 : column * 128 + 128] = given[
            source, :, place * 128 : place * 128 + 128
        ].astype(F32)


def widen(gathered, first, taps, start, count, depth, channels, unit, core, into=None):
    plane, _, width = gathered.shape
    last = depth // unit - 1

    def source(tap, step, core):
        return (0, first + step * taps + tap, 0)

    def target(tap, step, core):
        block = start + step
        return (tap, 0, jnp.where(core[0] == 0, block, last - block), 0)

    given = (core, gathered) if into is None else (core, gathered, into)
    return pl.pallas_call(
        functools.partial(widen_kernel, channels // 128),
        grid_spec=pltpu.PrefetchScalarGridSpec(
            num_scalar_prefetch=1,
            grid=(taps, count),
            in_specs=[pl.BlockSpec((plane, unit, width), source)] + [pl.BlockSpec(memory_space=pl.ANY)] * (len(given) - 2),
            out_specs=pl.BlockSpec((1, 3, unit, channels), target),
        ),
        out_shape=jax.ShapeDtypeStruct((taps, 3, depth, channels), F32),
        input_output_aliases={} if into is None else {2: 0},
        compiler_params=pltpu.CompilerParams(vmem_limit_bytes=40 * 2**20),
        cost_estimate=pl.CostEstimate(
            flops=0, bytes_accessed=taps * count * unit * (plane * width * 2 + channels * 12), transcendentals=0
        ),
        name="widen",
    )(*given)


def shifted(value, axis, steps):
    count = lax.axis_size(axis)
    initial, last = (max(0, -steps), min(count, count - steps))
    return lax.ppermute(value, axis, [(source, source + steps) for source in range(initial, last)])


def gather_channels(value):
    count = lax.axis_size("mp")
    if count != 2:
        return lax.all_gather(value, "mp", axis=value.ndim - 1, tiled=True)
    other = lax.ppermute(value, "mp", [(0, 1), (1, 0)])
    second = lax.axis_index("mp") == 1
    return jnp.concatenate([jnp.where(second, other, value), jnp.where(second, value, other)], value.ndim - 1)


def sum_channels(terms):
    count = lax.axis_size("mp")
    if count != 2:
        return lax.psum_scatter(terms, "mp", scatter_dimension=1, tiled=True)
    width = terms.shape[1] // 2
    second = lax.axis_index("mp") == 1
    low, high = terms[:, :width], terms[:, width:]
    other = lax.ppermute(jnp.where(second, low, high), "mp", [(0, 1), (1, 0)])
    return jnp.where(second, high, low) + other


def dot(lhs, rhs, dims):
    return lax.dot_general(lhs, rhs, (dims, ((), ())), preferred_element_type=F32)


def reduce_weights(partial):
    shard = lax.psum_scatter(partial.astype(BF16), ("dp", "seq"), scatter_dimension=0, tiled=True)
    return lax.all_gather(shard, ("dp", "seq"), axis=0, tiled=True).astype(F32)


def local(inputs, starts, init_state, weight_one, bias_one, weight_two, bias_two, cotangent):
    seqs, tokens, channels = inputs.shape
    rows = seqs * tokens
    width = weight_one.shape[1]
    keep = jnp.broadcast_to((1 - starts).astype(F32).reshape(rows, 1), (rows, 128))
    taps = weight_one.transpose(0, 2, 1, 3)
    mix = weight_two.transpose(1, 0, 2)

    line, plane = lax.axis_size("seq"), lax.axis_size("dp")
    tiles = 3 * channels // 128
    spreads = plane == 4 and lax.axis_size("mp") == 2 and seqs == 2 and line % 2 == 0 and channels % 128 == 0
    spreads = spreads and width % (line * PART) == 0 and line > 1
    block = -(-tiles // plane) * 128
    lanes = plane * block if spreads else 3 * channels
    upstream = cotangent.reshape(rows, channels)
    if spreads:
        pooled_two, sums_one, sums_two, extended, every, every_hidden, swapped = front(
            seqs,
            tokens,
            lanes,
            inputs.reshape(rows, channels),
            taps,
            mix,
            bias_one,
            bias_two,
            keep,
            init_state[0],
            init_state[1],
            upstream,
        )
        sums = jnp.concatenate([jnp.sum(sums_one, 1), jnp.sum(sums_two, 1)])
        gathered, input_grad, sums = spread(
            seqs,
            tokens,
            every_hidden.reshape(plane * rows, channels),
            every.reshape(plane * rows, channels),
            swapped.reshape(plane * rows, block),
            extended,
            taps,
            sums,
        )
        unit = line * PART
        blocks = width // unit
        core = lax.axis_index("mp").reshape(1)
        behind = TAIL // 2
        kept = lax.dynamic_slice(
            gathered, (lax.axis_index("dp"), (3 * blocks - TAIL) * unit, 0), (1, TAIL * unit, block)
        )
        tail = lax.all_gather(kept, "dp", axis=0, tiled=True)
        weight_two_grad = widen(gathered, 0, 1, 0, blocks, width, channels, unit, core)
        weight_one_grad = widen(gathered, blocks, 2, 0, blocks - behind, width, channels, unit, core)
        weight_one_grad = widen(
            tail, 0, 2, blocks - behind, behind, width, channels, unit, core, weight_one_grad
        )
        weight_two_grad = weight_two_grad[0].transpose(1, 0, 2)
        weight_one_grad = weight_one_grad.transpose(0, 2, 1, 3)
    else:
        edge = gather_channels(shifted(inputs[:, -1], "seq", 1))
        full = gather_channels(inputs)
        previous = jnp.concatenate([edge[:, None], full[:, :-1]], 1).reshape(rows, width)
        full = full.reshape(rows, width)
        both = jnp.concatenate([full, previous], 1)
        gates_one = jnp.einsum(
            "tkd,kgdc->gtc", both.reshape(rows, 2, width), taps, preferred_element_type=F32
        )
        hidden, upd, fgt, out, state, entering = pool_forward(seqs, tokens, gates_one, bias_one, keep, init_state[0])
        full_hidden = gather_channels(hidden)
        gates_two = jnp.einsum("td,gdc->gtc", full_hidden, mix, preferred_element_type=F32)
        pooled_two, grad_two, planes_two, sums_two = pool_top(
            seqs, tokens, lanes, gates_two, bias_two, keep, init_state[1], upstream
        )
        hidden_terms = jnp.einsum("gtc,gdc->td", planes_two, mix, preferred_element_type=F32)
        hidden_grad = sum_channels(hidden_terms)
        extended, sums_one = pool_backward(seqs, tokens, lanes, hidden_grad, keep, upd, fgt, out, state, entering)
        grad_one = extended[:rows]
        input_terms = jnp.einsum(
            "tgc,kgdc->ktd", grad_one.reshape(rows, 3, channels), taps, preferred_element_type=F32
        ).reshape(2, seqs, tokens, width)
        late = input_terms[1]
        late = jnp.concatenate([late[:, 1:], shifted(late[:, 0], "seq", -1)[:, None]], 1)
        input_grad = sum_channels((input_terms[0] + late).reshape(rows, width))
        sums = jnp.concatenate([jnp.sum(sums_one, 1), jnp.sum(sums_two, 1)])
        sums = lax.psum(sums, ("dp", "seq"))
        weight_two_grad = reduce_weights(dot(full_hidden, grad_two, ((0,), (0,)))).reshape(width, 3, channels)
        weight_one_grad = jnp.stack(
            [
                reduce_weights(dot(full, grad_one, ((0,), (0,)))),
                reduce_weights(dot(previous, grad_one, ((0,), (0,)))),
            ]
        ).reshape(2, width, 3, channels)
    return (
        pooled_two.reshape(seqs, tokens, channels),
        input_grad.reshape(seqs, tokens, channels),
        weight_one_grad,
        sums[:3],
        weight_two_grad,
        sums[3:],
    )


def solution(mesh):
    return jax.shard_map(
        local,
        mesh=mesh,
        in_specs=(
            P("dp", "seq", "mp"),
            P("dp", "seq"),
            P(None, "dp", "mp"),
            P(None, None, None, "mp"),
            P(None, "mp"),
            P(None, None, "mp"),
            P(None, "mp"),
            P("dp", "seq", "mp"),
        ),
        out_specs=(
            P("dp", "seq", "mp"),
            P("dp", "seq", "mp"),
            P(None, None, None, "mp"),
            P(None, "mp"),
            P(None, None, "mp"),
            P(None, "mp"),
        ),
        check_vma=False,
    )
```
